32 devices in a mesh: dp: 2 (over y), ctx: 4 (over x, core), tensor: 4 (over z).
Axes of the slice: x: 2, y: 2, z: 4, core: 2. Of those that a mesh axis runs over, the one named last changes fastest.
Arguments:
- hidden_in: bfloat16 [8, 1024, 2048], P('dp', 'ctx'), may hold values from -6 to 6
- output_cotangent: bfloat16 [8, 1024, 2048], P('dp', 'ctx'), may hold values from -6 to 6
- adapter_index: int32 [8, 1], P('dp'), may hold values from 0 to 7
- mixing_weight: bfloat16 [2048, 3, 2048], P(('dp', 'ctx'), None, 'tensor'), may hold values from -0.125 to 0.125
- output_weight: bfloat16 [2048, 2048], P('tensor', ('dp', 'ctx')), may hold values from -2.5 to 2.5
- expand_weight: bfloat16 [2048, 8192], P(('dp', 'ctx'), 'tensor'), may hold values from -0.125 to 0.125
- contract_weight: bfloat16 [8192, 2048], P('tensor', ('dp', 'ctx')), may hold values from -0.0625 to 0.0625
- first_gain: float32 [2048], replicated, may hold values from 0.1 to 1.9
- first_shift: float32 [2048], replicated, may hold values from -3 to 3
- second_gain: float32 [2048], replicated, may hold values from 0.1 to 1.9
- second_shift: float32 [2048], replicated, may hold values from -3 to 3
- mixing_down: bfloat16 [8, 16, 2048], replicated, may hold values from -0.125 to 0.125
- mixing_up: bfloat16 [8, 16, 3, 2048], P(None, None, None, 'tensor'), may hold values from -0.75 to 0.75
- output_down: bfloat16 [8, 16, 2048], P(None, None, 'tensor'), may hold values from -2.5 to 2.5
- output_up: bfloat16 [8, 16, 2048], replicated, may hold values from -0.75 to 0.75
- expand_down: bfloat16 [8, 16, 2048], replicated, may hold values from -0.125 to 0.125
- expand_up: bfloat16 [8, 16, 8192], P(None, None, 'tensor'), may hold values from -0.75 to 0.75
- contract_down: bfloat16 [8, 16, 8192], P(None, None, 'tensor'), may hold values from -0.0625 to 0.0625
- contract_up: bfloat16 [8, 16, 2048], replicated, may hold values from -0.75 to 0.75
Outputs:
- hidden_out: bfloat16 [8, 1024, 2048], P('dp', 'ctx')
- input_grad: bfloat16 [8, 1024, 2048], P('dp', 'ctx')
- mixing_down_grad: float32 [8, 16, 2048], replicated
- mixing_up_grad: float32 [8, 16, 3, 2048], P(None, None, None, 'tensor')
- output_down_grad: float32 [8, 16, 2048], P(None, None, 'tensor')
- output_up_grad: float32 [8, 16, 2048], replicated
- expand_down_grad: float32 [8, 16, 2048], replicated
- expand_up_grad: float32 [8, 16, 8192], P(None, None, 'tensor')
- contract_down_grad: float32 [8, 16, 8192], P(None, None, 'tensor')
- contract_up_grad: float32 [8, 16, 2048], replicated
The draws below stay inside these ranges and needn't reach their ends.
Inputs may be any that keep to these rules, and one draw needn't show every extreme that they name: `adapter_index`: each of the 8 adapters serves at least one sequence.
All inputs are finite; a program needn't handle non-finite values.
Results may differ from the reference program's by a relative error of at most 0.025.
Values may be sent and summed in bfloat16 or wider, within the bound.
A program may use at most 256 MiB of HBM per device.

```python
import math
import jax
import jax.numpy as jnp
from jax import lax

D = 2048
HEADS = 16
HEAD_DIM = 128
FF = 8192
RANK = 16
NADAPT = 8
SEQS = 8
SEQ = 1024


def block_levels(stream_key, extent, pieces, least, high):
    level = 1.0
    for dim, blocks in pieces:
        heights = jax.random.uniform(jax.random.fold_in(jax.random.fold_in(stream_key, 6), dim), (blocks,), jnp.float32, least / len(pieces), high / len(pieces))
        level = level * jnp.repeat(jnp.exp(heights), extent[dim] // blocks).reshape((-1,) + (1,) * (len(extent) - 1 - dim))
    return level


def different_ones(key, rows, amount, top, lift):
    ranking = jax.random.permutation(jax.random.fold_in(key, 1), amount)
    pull = ranking
    for power in range(3):
        pull = pull * pull // amount
    pull = pull * lift // amount
    tickets = jax.random.randint(jax.random.fold_in(key, 2), (rows, amount), 0, 4096) + pull
    sure = jax.random.permutation(jax.random.fold_in(key, 3), rows)[jnp.arange(amount) % rows]
    tickets = jnp.where(jnp.arange(rows)[:, None] == sure[None, :], 1 << 14, tickets)
    merit = tickets * amount + jnp.arange(amount)
    return lax.top_k(merit.astype(jnp.int32), top)[1].astype(jnp.int32)


def normal_values(stream_key, extent, width, most, cuts=(), dtype=jnp.bfloat16):
    loudness = block_levels(stream_key, extent, cuts, -0.22, 0.18) if cuts else 1.0
    values = jax.random.normal(stream_key, extent, jnp.float32) * width * loudness
    return jnp.minimum(jnp.maximum(values, -most), most).astype(dtype)


def setup_inputs(seed: int = 0) -> dict:
    key_of = jax.random.split(jax.random.key(seed), 20)
    hidden_in = normal_values(key_of[0], (SEQS, SEQ, D), 1.0, 6.0, ((0, 2), (1, 4)))
    output_cotangent = normal_values(key_of[1], (SEQS, SEQ, D), 1.0, 6.0, ((0, 2), (1, 4)))
    adapter_index = different_ones(key_of[2], SEQS, NADAPT, 1, 0)
    mixing_weight = normal_values(key_of[3], (D, 3, D), D ** -0.5, 0.125, ((0, 8), (2, 4)))
    output_weight = normal_values(key_of[4], (D, D), (max(1, 3 * D // SEQ)) ** -0.5, 2.5, ((0, 4), (1, 8)))
    expand_weight = normal_values(key_of[5], (D, FF), D ** -0.5, 0.125, ((0, 8), (1, 4)))
    contract_weight = normal_values(key_of[6], (FF, D), FF ** -0.5, 0.0625, ((0, 4), (1, 8)))
    first_gain = jnp.clip(1.0 + 0.18 * jax.random.normal(key_of[7], (D,), jnp.float32), 0.1, 1.9)
    first_shift = normal_values(key_of[8], (D,), 0.5, 3.0, (), jnp.float32)
    second_gain = jnp.clip(1.0 + 0.18 * jax.random.normal(key_of[9], (D,), jnp.float32), 0.1, 1.9)
    second_shift = normal_values(key_of[10], (D,), 0.5, 3.0, (), jnp.float32)
    mixing_down = normal_values(key_of[11], (NADAPT, RANK, D), D ** -0.5, 0.125)
    mixing_up = normal_values(key_of[12], (NADAPT, RANK, 3, D), (4 * RANK) ** -0.5, 0.75, ((3, 4),))
    output_down = normal_values(key_of[13], (NADAPT, RANK, D), (max(1, 3 * D // SEQ)) ** -0.5, 2.5, ((2, 4),))
    output_up = normal_values(key_of[14], (NADAPT, RANK, D), (4 * RANK) ** -0.5, 0.75)
    expand_down = normal_values(key_of[15], (NADAPT, RANK, D), D ** -0.5, 0.125)
    expand_up = normal_values(key_of[16], (NADAPT, RANK, FF), (4 * RANK) ** -0.5, 0.75, ((2, 4),))
    contract_down = normal_values(key_of[17], (NADAPT, RANK, FF), FF ** -0.5, 0.0625, ((2, 4),))
    contract_up = normal_values(key_of[18], (NADAPT, RANK, D), (4 * RANK) ** -0.5, 0.75)
    return dict(hidden_in=hidden_in, output_cotangent=output_cotangent, adapter_index=adapter_index, mixing_weight=mixing_weight, output_weight=output_weight, expand_weight=expand_weight, contract_weight=contract_weight, first_gain=first_gain, first_shift=first_shift, second_gain=second_gain, second_shift=second_shift, mixing_down=mixing_down, mixing_up=mixing_up, output_down=output_down, output_up=output_up, expand_down=expand_down, expand_up=expand_up, contract_down=contract_down, contract_up=contract_up)


PRECISE = lax.Precision.HIGHEST

@jax.custom_vjp
def low(v):
    return lax.optimization_barrier(v.astype(jnp.bfloat16)).astype(jnp.float32)

@jax.custom_vjp
def low_back(v):
    return v

def low_keep(v):
    return (low(v), None)

def low_pass(kept, grad):
    return (grad,)

def back_keep(v):
    return (v, None)

def back_low(kept, grad):
    return (low(grad),)
low.defvjp(low_keep, low_pass)
low_back.defvjp(back_keep, back_low)

def both_ways(value):
    return low(low_back(value))

def smooth_gate(value):
    return 0.5 * value * (1.0 + jnp.tanh(0.7978845608028654 * (value + 0.044715 * value * value * value)))

def layer_norm(hidden, gain, shift):
    centred = hidden - lax.optimization_barrier(jnp.mean(hidden, axis=-1, keepdims=True))
    inverse = lax.rsqrt(lax.optimization_barrier(jnp.mean(centred * centred, axis=-1, keepdims=True)) + 1e-06)
    return centred * inverse * gain + shift

def attention(queries, key_rows, value_rows):
    block_rows = math.gcd(queries.shape[0], 512)
    score_scale = HEAD_DIM ** (-0.5)

    def one_block(query_block):
        scores = low_back(jnp.einsum('thd,khd->htk', query_block, key_rows, precision=PRECISE) * score_scale)
        largest = lax.optimization_barrier(jnp.max(scores, axis=-1, keepdims=True))
        raised = jnp.exp(scores - largest)
        probs = low(raised / lax.optimization_barrier(jnp.sum(raised, axis=-1, keepdims=True)))
        return jnp.einsum('htk,khd->thd', probs, value_rows, precision=PRECISE)
    blocks = queries.reshape((queries.shape[0] // block_rows, block_rows) + queries.shape[1:])
    return lax.map(jax.checkpoint(one_block), blocks).reshape(queries.shape)

def layer(hidden, frozen, picked):
    mixing, output, expand, contract, first_gain, first_shift, second_gain, second_shift = frozen
    mixing_down, mixing_up, output_down, output_up, expand_down, expand_up, contract_down, contract_up = picked
    hidden_low = low(hidden)
    mixing_rank = both_ways(jnp.dot(hidden_low, mixing_down.T, precision=PRECISE))
    projected = jnp.einsum('td,dcf->tcf', hidden_low, mixing, precision=PRECISE)
    projected = both_ways(projected + jnp.einsum('tr,rcf->tcf', mixing_rank, mixing_up, precision=PRECISE))
    shaped = (SEQ, HEADS, HEAD_DIM)
    attended = attention(projected[:, 0].reshape(shaped), projected[:, 1].reshape(shaped), projected[:, 2].reshape(shaped))
    context = both_ways(attended.reshape(SEQ, HEADS * HEAD_DIM))
    output_rank = both_ways(jnp.dot(context, output_down.T, precision=PRECISE))
    attn_total = low_back(jnp.dot(context, output, precision=PRECISE) + jnp.dot(output_rank, output_up, precision=PRECISE))
    first_out = layer_norm(hidden + attn_total, first_gain, first_shift)
    first_low = low(first_out)
    expand_rank = both_ways(jnp.dot(first_low, expand_down.T, precision=PRECISE))
    before = low_back(jnp.dot(first_low, expand, precision=PRECISE) + jnp.dot(expand_rank, expand_up, precision=PRECISE))
    active = low(smooth_gate(before))
    contract_rank = both_ways(jnp.dot(active, contract_down.T, precision=PRECISE))
    ffn_total = low_back(jnp.dot(active, contract, precision=PRECISE) + jnp.dot(contract_rank, contract_up, precision=PRECISE))
    return layer_norm(first_out + ffn_total, second_gain, second_shift)

def widen(value):
    return value.astype(jnp.float32)

def reference(hidden_in, output_cotangent, adapter_index, mixing_weight, output_weight, expand_weight, contract_weight, first_gain, first_shift, second_gain, second_shift, mixing_down, mixing_up, output_down, output_up, expand_down, expand_up, contract_down, contract_up):
    frozen = (widen(mixing_weight), widen(output_weight), widen(expand_weight), widen(contract_weight), widen(first_gain), widen(first_shift), widen(second_gain), widen(second_shift))
    tables = (widen(mixing_down), widen(mixing_up), widen(output_down), widen(output_up), widen(expand_down), widen(expand_up), widen(contract_down), widen(contract_up))

    def per_sequence(totals, inputs):
        hidden, cotangent, chosen = inputs

        def forward(hidden_wide, table_set):
            picked = tuple((lax.dynamic_index_in_dim(table, chosen, 0, keepdims=False) for table in table_set))
            return layer(hidden_wide, frozen, picked)
        result, pullback = jax.vjp(forward, widen(hidden), tables)
        grad_hidden, grad_tables = pullback(widen(cotangent))
        totals = tuple((total + extra for total, extra in zip(totals, grad_tables)))
        return (totals, (result.astype(jnp.bfloat16), grad_hidden.astype(jnp.bfloat16)))
    zeros = tuple((jnp.zeros(table.shape, jnp.float32) for table in tables))
    totals, (outputs, grads) = lax.scan(per_sequence, zeros, (hidden_in, output_cotangent, adapter_index[:, 0].astype(jnp.int32)))
    return (outputs, grads, totals[0], totals[1], totals[2], totals[3], totals[4], totals[5], totals[6], totals[7])
```

```python
import functools
import math

import jax
import jax.numpy as jnp
from jax import lax
from jax.experimental import pallas as pl
from jax.experimental.pallas import tpu as pltpu
from jax.sharding import PartitionSpec as P

HEAD_DIM = 128
NADAPT = 8
CHUNK_ROWS = 128


BF = jnp.bfloat16
F32 = jnp.float32
MESH_IDS = pl.DeviceIdType.MESH
RANK_ROWS = 16
GELU_C = 0.7978845608028654
GELU_A = 0.044715


def dot_nn(a, b):
    return lax.dot_general(a, b, (((1,), (0,)), ((), ())), preferred_element_type=F32)


def dot_nt(a, b):
    return lax.dot_general(a, b, (((1,), (1,)), ((), ())), preferred_element_type=F32)


def dot_tn(a, b):
    return lax.dot_general(a, b, (((0,), (0,)), ((), ())), preferred_element_type=F32)


def tile(index, size):
    return pl.ds(pl.multiple_of(index * size, size), size)


def middle_kernel(
    sizes,
    context,
    hidden,
    cotangent,
    w_out,
    w_exp,
    w_con,
    od,
    ou,
    ed,
    eu,
    cd,
    cu,
    gains,
    hidden_out,
    first_low,
    active,
    second_low,
    before_grad,
    attn_low,
    context_grad,
    out_rank,
    exp_rank,
    con_rank,
    con_rank_grad,
    exp_rank_grad,
    out_rank_grad,
    acc,
    red_up,
    red_down,
    normed,
    spreads,
    slope,
    second,
    stage_d,
    stage_f,
    rows_in,
    rank_buf,
    in_sem,
    out_sem,
    red_send,
    red_recv,
    cast_send,
    cast_recv,
):
    ranks, chunks, rows, per_seq, period = sizes
    half = rows // 2
    width = hidden.shape[1]
    units = w_exp.shape[1]
    heads = w_out.shape[0]
    block = min(16, half)
    tile_f = math.gcd(units, 256)
    tile_d = math.gcd(width, 256)
    tile_h = math.gcd(heads, 256)
    me = lax.axis_index("tensor")

    barrier = pltpu.get_barrier_semaphore()

    @pl.when(me > 0)
    def _():
        pl.semaphore_signal(barrier, inc=1, device_id={"tensor": me - 1}, device_id_type=MESH_IDS)

    @pl.when(me < ranks - 1)
    def _():
        pl.semaphore_signal(barrier, inc=1, device_id={"tensor": me + 1}, device_id_type=MESH_IDS)

    pl.semaphore_wait(
        barrier, jnp.minimum(me, 1) + jnp.minimum(ranks - 1 - me, 1)
    )

    def job_of(number, rounds):
        safe = jnp.maximum(number, 0)
        chunk = safe % period
        valid = (number >= 0) & (chunk < chunks) & (safe < rounds * period)
        return valid, jnp.minimum(chunk, chunks - 1)

    def comm(tick, way):
        upward = way == 0
        place = me if upward else ranks - 1 - me
        ahead = me + 1 if upward else me - 1
        behind = me - 1 if upward else me + 1
        red = red_up if upward else red_down
        part = pl.ds(way * half, half)

        def red_copy(c):
            return pltpu.make_async_remote_copy(
                src_ref=red.at[c],
                dst_ref=red.at[c],
                send_sem=red_send.at[way, c],
                recv_sem=red_recv.at[way, c],
                device_id={"tensor": ahead},
                device_id_type=MESH_IDS,
            )

        def cast_copy(c):
            return pltpu.make_async_remote_copy(
                src_ref=acc.at[c, part],
                dst_ref=acc.at[c, part],
                send_sem=cast_send.at[way, c],
                recv_sem=cast_recv.at[way, c],
                device_id={"tensor": behind},
                device_id_type=MESH_IDS,
            )

        old_red, c_old = job_of(tick - 2 - place, 3)

        @pl.when(old_red & (place < ranks - 1))
        def _():
            red_copy(c_old).wait_send()

        old_cast, c_cast = job_of(tick - 2 * ranks + place, 3)

        @pl.when(old_cast & (place > 0))
        def _():
            cast_copy(c_cast).wait_send()

        now_red, c = job_of(tick - 1 - place, 3)

        @pl.when(now_red & (place == 0))
        def _():
            red[c] = acc[c, part, :]

        @pl.when(now_red & (place > 0))
        def _():
            red_copy(c).wait_recv()

        @pl.when(now_red & (place > 0) & (place < ranks - 1))
        def _():
            @pl.loop(0, half // block)
            def _(i):
                rs = tile(i, block)
                own = acc[c, pl.ds(pl.multiple_of(way * half + i * block, block), block), :]
                red[c, rs, :] = (red[c, rs, :].astype(F32) + own.astype(F32)).astype(BF)

        @pl.when(now_red & (place < ranks - 1))
        def _():
            red_copy(c).start()

        @pl.when(now_red & (place == ranks - 1))
        def _():
            @pl.loop(0, half // block)
            def _(i):
                rs = tile(i, block)
                own_rs = pl.ds(pl.multiple_of(way * half + i * block, block), block)
                acc[c, own_rs, :] = (
                    red[c, rs, :].astype(F32) + acc[c, own_rs, :].astype(F32)
                ).astype(BF)

            cast_copy(c).start()

        now_cast, cc = job_of(tick - (2 * ranks - 1 - place), 3)

        @pl.when(now_cast & (place < ranks - 1))
        def _():
            cast_copy(cc).wait_recv()

        @pl.when(now_cast & (place > 0) & (place < ranks - 1))
        def _():
            cast_copy(cc).start()

    def rows_of(c):
        return tile(c, rows)

    def bring(source, c):
        return pltpu.make_async_copy(source.at[rows_of(c)], rows_in, in_sem)

    def keep(index, source, target, c):
        return pltpu.make_async_copy(source, target.at[rows_of(c)], out_sem.at[index])

    def mean(values):
        return jnp.sum(values, axis=-1, keepdims=True) * (1.0 / width)

    def attend_part(c, s):
        mine = context[rows_of(c), :]
        low = dot_nt(mine, od[s]).astype(BF)
        out_rank[rows_of(c), :] = low

        @pl.loop(0, width // tile_d)
        def _(i):
            cs = tile(i, tile_d)
            acc[c, :, cs] = (dot_nn(mine, w_out[:, cs]) + dot_nn(low, ou[s, :, cs])).astype(BF)

    def forward_first(c, s):
        bring(hidden, c).wait()

        @pl.loop(0, rows // block)
        def _(i):
            rs = tile(i, block)
            total = rows_in[rs, :].astype(F32) + acc[c, rs, :].astype(F32)
            centred = total - mean(total)
            spread = lax.rsqrt(mean(centred * centred) + 1e-06)
            n = centred * spread
            normed[c, rs, :] = n.astype(BF)
            spreads[c, rs, :] = jnp.broadcast_to(spread, (block, 128))
            stage_d[rs, :] = (n * gains[0:1, :] + gains[1:2, :]).astype(BF)

        low = dot_nt(stage_d[...], ed[s]).astype(BF)
        exp_rank[rows_of(c), :] = low
        rank_buf[...] = low

        @pl.loop(0, units // tile_f)
        def _(i):
            cs = tile(i, tile_f)
            b = dot_nn(stage_d[...], w_exp[:, cs]) + dot_nn(rank_buf[...], eu[s, :, cs])
            square = b * b
            t = jnp.tanh(GELU_C * b * (1.0 + GELU_A * square))
            upper = 0.5 * (1.0 + t)
            stage_f[:, cs] = (b * upper).astype(BF)
            slope[c, :, cs] = (
                upper
                + (0.5 * GELU_C) * b * (1.0 - t * t) * (1.0 + (3.0 * GELU_A) * square)
            ).astype(BF)

    def forward_second(c, s):
        low = dot_nt(stage_f[...], cd[s]).astype(BF)
        con_rank[rows_of(c), :] = low
        rank_buf[...] = low

        @pl.loop(0, width // tile_d)
        def _(i):
            cs = tile(i, tile_d)
            acc[c, :, cs] = (
                dot_nn(stage_f[...], w_con[:, cs]) + dot_nn(rank_buf[...], cu[s, :, cs])
            ).astype(BF)

        keep(0, stage_d, first_low, c).start()
        keep(1, stage_f, active, c).start()

    def back_first(c, s):
        bring(cotangent, c).wait()

        @pl.loop(0, rows // block)
        def _(i):
            rs = tile(i, block)
            first = normed[c, rs, :].astype(F32) * gains[0:1, :] + gains[1:2, :]
            total = first + acc[c, rs, :].astype(F32)
            centred = total - mean(total)
            spread = lax.rsqrt(mean(centred * centred) + 1e-06)
            n = centred * spread
            stage_d[rs, :] = (n * gains[2:3, :] + gains[3:4, :]).astype(BF)
            g = rows_in[rs, :].astype(F32) * gains[2:3, :]
            second[c, rs, :] = (spread * (g - mean(g) - n * mean(g * n))).astype(BF)

        low = dot_nt(second[c], cu[s]).astype(BF)
        con_rank_grad[rows_of(c), :] = low
        rank_buf[...] = low

        @pl.loop(0, units // tile_f)
        def _(i):
            cs = tile(i, tile_f)
            da = dot_nt(second[c], w_con[cs, :]) + dot_nn(rank_buf[...], cd[s, :, cs])
            stage_f[:, cs] = (da * slope[c, :, cs].astype(F32)).astype(BF)

    def back_second(c, s):
        low = dot_nt(stage_f[...], eu[s]).astype(BF)
        exp_rank_grad[rows_of(c), :] = low
        rank_buf[...] = low

        @pl.loop(0, width // tile_d)
        def _(i):
            cs = tile(i, tile_d)
            acc[c, :, cs] = (
                dot_nt(stage_f[...], w_exp[cs, :]) + dot_nn(rank_buf[...], ed[s, :, cs])
            ).astype(BF)

        keep(0, stage_d, hidden_out, c).start()
        keep(1, stage_f, before_grad, c).start()
        keep(2, second.at[c], second_low, c).start()

    def last_first(c, s):
        @pl.loop(0, rows // block)
        def _(i):
            rs = tile(i, block)
            n = normed[c, rs, :].astype(F32)
            g = (second[c, rs, :].astype(F32) + acc[c, rs, :].astype(F32)) * gains[0:1, :]
            spread = spreads[c, rs, 0:1]
            stage_d[rs, :] = (spread * (g - mean(g) - n * mean(g * n))).astype(BF)

    def last_second(c, s):
        low = dot_nt(stage_d[...], ou[s]).astype(BF)
        out_rank_grad[rows_of(c), :] = low
        rank_buf[...] = low

        @pl.loop(0, heads // tile_h)
        def _(i):
            cs = tile(i, tile_h)
            context_grad[rows_of(c), cs] = (
                dot_nt(stage_d[...], w_out[cs, :]) + dot_nn(rank_buf[...], od[s, :, cs])
            ).astype(BF)

        keep(0, stage_d, attn_low, c).start()

    @pl.loop(0, 3 * period + chunks)
    def _(tick):
        stage = tick // period
        valid, c = job_of(tick, 4)
        s = c // per_seq
        last_valid, last_c = job_of(tick - 1, 4)
        last_stage = jnp.maximum(tick - 1, 0) // period

        comm(tick, 0)

        @pl.when(last_valid & (last_stage >= 1))
        def _():
            keep(0, stage_d, first_low, last_c).wait()

        @pl.when(last_valid & (last_stage >= 1) & (last_stage <= 2))
        def _():
            keep(1, stage_f, active, last_c).wait()

        @pl.when(last_valid & (last_stage == 2))
        def _():
            keep(2, second.at[last_c], second_low, last_c).wait()

        pl.when(valid & (stage == 1))(lambda: forward_first(c, s))
        pl.when(valid & (stage == 2))(lambda: back_first(c, s))
        pl.when(valid & (stage == 3))(lambda: last_first(c, s))

        comm(tick, 1)

        pl.when(valid & (stage == 0))(lambda: attend_part(c, s))
        pl.when(valid & (stage == 1))(lambda: forward_second(c, s))
        pl.when(valid & (stage == 2))(lambda: back_second(c, s))
        pl.when(valid & (stage == 3))(lambda: last_second(c, s))

        next_valid, next_c = job_of(tick + 1, 4)
        next_stage = (tick + 1) // period
        pl.when(next_valid & (next_stage == 1))(lambda: bring(hidden, next_c).start())
        pl.when(next_valid & (next_stage == 2))(lambda: bring(cotangent, next_c).start())

    keep(0, stage_d, attn_low, chunks - 1).wait()


def middle(context, hidden, cotangent, w_out, w_exp, w_con, picked, gains, tok):
    od, ou, ed, eu, cd, cu = picked
    total, width = hidden.shape
    heads, units = w_out.shape[0], w_exp.shape[1]
    ranks = lax.axis_size("tensor")
    rank = od.shape[1]
    rows = math.gcd(tok, CHUNK_ROWS)
    chunks = total // rows
    period = max(chunks, 2 * ranks)
    sizes = (ranks, chunks, rows, tok // rows, period)
    vm = pl.BlockSpec(memory_space=pltpu.VMEM)
    hb = pl.BlockSpec(memory_space=pl.ANY)
    half = rows // 2

    def shape(*dims):
        return jax.ShapeDtypeStruct(dims, BF)

    return pl.pallas_call(
        functools.partial(middle_kernel, sizes),
        out_shape=(
            shape(total, width),
            shape(total, width),
            shape(total, units),
            shape(total, width),
            shape(total, units),
            shape(total, width),
            shape(total, heads),
        )
        + (shape(total, rank),) * 6,
        in_specs=[vm, hb, hb] + [vm] * 10,
        out_specs=(hb,) * 6 + (vm,) * 7,
        scratch_shapes=[
            pltpu.VMEM((chunks, rows, width), BF),
            pltpu.VMEM((chunks, half, width), BF),
            pltpu.VMEM((chunks, half, width), BF),
            pltpu.VMEM((chunks, rows, width), BF),
            pltpu.VMEM((chunks, rows, 128), F32),
            pltpu.VMEM((chunks, rows, units), BF),
            pltpu.VMEM((chunks, rows, width), BF),
            pltpu.VMEM((rows, width), BF),
            pltpu.VMEM((rows, units), BF),
            pltpu.VMEM((rows, width), BF),
            pltpu.VMEM((rows, rank), BF),
            pltpu.SemaphoreType.DMA(()),
            pltpu.SemaphoreType.DMA((3,)),
            pltpu.SemaphoreType.DMA((2, chunks)),
            pltpu.SemaphoreType.DMA((2, chunks)),
            pltpu.SemaphoreType.DMA((2, chunks)),
            pltpu.SemaphoreType.DMA((2, chunks)),
        ],
        compiler_params=pltpu.CompilerParams(
            collective_id=0, has_side_effects=True, vmem_limit_bytes=60 * 2**20
        ),
        cost_estimate=pl.CostEstimate(
            flops=8 * total * width * units + 4 * total * width * heads,
            bytes_accessed=16 * total * width,
            transcendentals=total * units,
        ),
    )(context, hidden, cotangent, w_out, w_exp, w_con, od, ou, ed, eu, cd, cu, gains)


def pick_rows(onehot_low, table):
    return jnp.einsum(
        "sn,n...->s...", onehot_low, table, preferred_element_type=jnp.float32
    ).astype(jnp.bfloat16)


def split_blocks(values, block_rows):
    return values.reshape((values.shape[0] // block_rows, block_rows) + values.shape[1:])


def attend_fold(queries, score_scale, state_now, shard_rows):
    key_rows, value_rows = shard_rows
    block_rows = math.gcd(key_rows.shape[0], 512)

    def attend_advance(state, pair):
        running_max, running_sum, weighted = state
        key_block, value_block = pair
        scores = (
            jnp.einsum("tshd,kshd->tshk", queries, key_block, preferred_element_type=jnp.float32)
            * score_scale
        )
        new_max = jnp.maximum(running_max, jnp.max(scores, axis=-1))
        factor = jnp.exp(running_max - new_max)
        raised = jnp.exp(scores - new_max[..., None])
        running_sum = running_sum * factor + jnp.sum(raised, axis=-1)
        weighted = weighted * factor[..., None] + jnp.einsum(
            "tshk,kshd->tshd",
            raised.astype(jnp.bfloat16),
            value_block,
            preferred_element_type=jnp.float32,
        )
        return ((new_max, running_sum, weighted), None)

    state_now, _ = lax.scan(
        attend_advance,
        state_now,
        (split_blocks(key_rows, block_rows), split_blocks(value_rows, block_rows)),
    )
    return state_now


def score_grads(
    query_block, grad_block, log_block, delta_block, key_block, value_block, score_scale
):
    scores = (
        jnp.einsum("tshd,kshd->tshk", query_block, key_block, preferred_element_type=jnp.float32)
        * score_scale
    )
    probs = jnp.exp(scores - log_block[..., None])
    dprobs = jnp.einsum(
        "tshd,kshd->tshk", grad_block, value_block, preferred_element_type=jnp.float32
    )
    dscores = (probs * (dprobs - delta_block[..., None])).astype(jnp.bfloat16)
    return (probs.astype(jnp.bfloat16), dscores)


def key_sweep(queries, grad_out, log_total, delta_rows, key_all, value_all, score_scale):
    block_rows = math.gcd(key_all.shape[0], 512)

    def key_advance(query_grad, pair):
        key_block, value_block = pair
        probs, dscores = score_grads(
            queries, grad_out, log_total, delta_rows, key_block, value_block, score_scale
        )
        query_grad = query_grad + score_scale * jnp.einsum(
            "tshk,kshd->tshd", dscores, key_block, preferred_element_type=jnp.float32
        )
        key_part = score_scale * jnp.einsum(
            "tshk,tshd->kshd", dscores, queries, preferred_element_type=jnp.float32
        )
        value_part = jnp.einsum(
            "tshk,tshd->kshd", probs, grad_out, preferred_element_type=jnp.float32
        )
        return (query_grad, (key_part, value_part))

    start_grad = jnp.zeros(queries.shape, jnp.float32)
    query_grad, (key_parts, value_parts) = lax.scan(
        key_advance,
        start_grad,
        (split_blocks(key_all, block_rows), split_blocks(value_all, block_rows)),
    )
    return (query_grad, key_parts.reshape(key_all.shape), value_parts.reshape(value_all.shape))


def per_device(
    hidden_in,
    output_cotangent,
    adapter_index,
    mixing_weight,
    output_weight,
    expand_weight,
    contract_weight,
    first_gain,
    first_shift,
    second_gain,
    second_shift,
    mixing_down,
    mixing_up,
    output_down,
    output_up,
    expand_down,
    expand_up,
    contract_down,
    contract_up,
):
    seq_count, tok_count, model_width = hidden_in.shape
    local_heads = mixing_weight.shape[2] // HEAD_DIM
    score_scale = HEAD_DIM ** (-0.5)
    head_shape = (tok_count, seq_count, local_heads, HEAD_DIM)
    adapter_ids = jnp.arange(NADAPT, dtype=jnp.int32)
    onehot = (adapter_index == adapter_ids[None, :]).astype(jnp.float32)
    onehot_low = onehot.astype(jnp.bfloat16)
    mixing_down_sel = pick_rows(onehot_low, mixing_down)
    mixing_up_sel = pick_rows(onehot_low, mixing_up)
    output_down_sel = pick_rows(onehot_low, output_down)
    output_up_sel = pick_rows(onehot_low, output_up)
    expand_down_sel = pick_rows(onehot_low, expand_down)
    expand_up_sel = pick_rows(onehot_low, expand_up)
    contract_down_sel = pick_rows(onehot_low, contract_down)
    contract_up_sel = pick_rows(onehot_low, contract_up)
    mixing_full, output_full = (
        lax.all_gather(mixing_weight, ("dp", "ctx"), axis=0, tiled=True),
        lax.all_gather(output_weight, ("dp", "ctx"), axis=1, tiled=True),
    )
    expand_full, contract_full = (
        lax.all_gather(expand_weight, ("dp", "ctx"), axis=0, tiled=True),
        lax.all_gather(contract_weight, ("dp", "ctx"), axis=1, tiled=True),
    )
    mixing_rank = jnp.einsum(
        "std,srd->str", hidden_in, mixing_down_sel, preferred_element_type=jnp.float32
    ).astype(jnp.bfloat16)
    projected = jnp.einsum(
        "std,dcf->tscf", hidden_in, mixing_full, preferred_element_type=jnp.float32
    )
    projected = projected + jnp.einsum(
        "str,srcf->tscf", mixing_rank, mixing_up_sel, preferred_element_type=jnp.float32
    )
    projected = projected.astype(jnp.bfloat16)
    queries = projected[:, :, 0].reshape(head_shape)
    key_rows = projected[:, :, 1].reshape(head_shape)
    value_rows = projected[:, :, 2].reshape(head_shape)
    start_state = (
        jnp.full(head_shape[:3], -1e30, jnp.float32),
        jnp.zeros(head_shape[:3], jnp.float32),
        jnp.zeros(head_shape, jnp.float32),
    )
    running_max, running_sum, weighted = attend_fold(
        queries,
        score_scale,
        start_state,
        (
            lax.all_gather(key_rows, "ctx", axis=0, tiled=True),
            lax.all_gather(value_rows, "ctx", axis=0, tiled=True),
        ),
    )
    attended = weighted / running_sum[..., None]
    log_total = running_max + jnp.log(running_sum)
    context = attended.reshape(tok_count, seq_count, -1).astype(jnp.bfloat16)
    rows_all = seq_count * tok_count
    context = context.swapaxes(0, 1).reshape(rows_all, -1)
    gains = jnp.stack([first_gain, first_shift, second_gain, second_shift])
    hidden_rows = hidden_in.reshape(rows_all, model_width)
    picked = (
        output_down_sel,
        output_up_sel,
        expand_down_sel,
        expand_up_sel,
        contract_down_sel,
        contract_up_sel,
    )
    (
        out_rows,
        first_low,
        active_low,
        second_low,
        before_low,
        attn_low,
        context_grad,
        output_rank,
        expand_rank,
        contract_rank,
        contract_rank_grad,
        expand_rank_grad,
        output_rank_grad,
    ) = middle(
        context,
        hidden_rows,
        output_cotangent.reshape(rows_all, model_width),
        output_full,
        expand_full,
        contract_full,
        picked,
        gains,
        tok_count,
    )
    shared = lax.psum(jnp.concatenate([output_rank, contract_rank, expand_rank_grad], axis=1), "tensor")
    rank = output_rank.shape[1]
    output_rank, contract_rank, expand_rank_grad = (
        shared[:, :rank],
        shared[:, rank : 2 * rank],
        shared[:, 2 * rank :],
    )
    row_hot = jnp.repeat(onehot_low, tok_count, axis=0)

    def table_grad(ranks, values):
        wide = (row_hot[:, :, None] * ranks[:, None, :]).reshape(rows_all, -1)
        part = jnp.einsum("nk,nd->kd", wide, values, preferred_element_type=jnp.float32)
        return part.astype(jnp.bfloat16).reshape(NADAPT, rank, values.shape[1])

    grad_out = context_grad.reshape(seq_count, tok_count, -1).swapaxes(0, 1).reshape(head_shape)
    delta_rows = jnp.sum(grad_out.astype(jnp.float32) * attended, axis=-1)
    key_all, value_all = (
        lax.all_gather(key_rows, "ctx", axis=0, tiled=True),
        lax.all_gather(value_rows, "ctx", axis=0, tiled=True),
    )
    query_grad, key_parts, value_parts = key_sweep(
        queries, grad_out, log_total, delta_rows, key_all, value_all, score_scale
    )
    key_grad, value_grad = (
        lax.psum_scatter(
            key_parts.astype(jnp.bfloat16), "ctx", scatter_dimension=0, tiled=True
        ).astype(jnp.float32),
        lax.psum_scatter(
            value_parts.astype(jnp.bfloat16), "ctx", scatter_dimension=0, tiled=True
        ).astype(jnp.float32),
    )
    grad_stack = jnp.stack([query_grad, key_grad, value_grad], axis=2).astype(jnp.bfloat16)
    grad_stack = grad_stack.reshape(tok_count, seq_count, 3, -1)
    rank_part = jnp.einsum(
        "tscf,srcf->str", grad_stack, mixing_up_sel, preferred_element_type=jnp.float32
    ).astype(jnp.bfloat16)
    input_part = jnp.einsum(
        "tscf,dcf->std", grad_stack, mixing_full, preferred_element_type=jnp.float32
    )
    input_part = input_part + jnp.einsum(
        "str,srd->std", rank_part, mixing_down_sel, preferred_element_type=jnp.float32
    )
    input_back = lax.psum(input_part.astype(jnp.bfloat16), "tensor").astype(jnp.float32)
    mixing_rank_low = lax.psum(rank_part, "tensor")
    input_low = (
        attn_low.reshape(hidden_in.shape).astype(jnp.float32) + input_back
    ).astype(jnp.bfloat16)
    grad_rows = grad_stack.swapaxes(0, 1).reshape(rows_all, -1)
    parts = (
        table_grad(mixing_rank_low.reshape(rows_all, rank), hidden_rows),
        table_grad(mixing_rank.reshape(rows_all, rank), grad_rows).reshape(
            (NADAPT, rank) + grad_stack.shape[2:]
        ),
        table_grad(output_rank_grad, context),
        table_grad(output_rank, attn_low),
        table_grad(expand_rank_grad, first_low),
        table_grad(expand_rank, before_low),
        table_grad(contract_rank_grad, active_low),
        table_grad(contract_rank, second_low),
    )
    summed = tuple(lax.psum(part, ("dp", "ctx")).astype(jnp.float32) for part in parts)
    return (out_rows.reshape(hidden_in.shape), input_low) + summed


def solution(mesh):
    return jax.shard_map(
        per_device,
        mesh=mesh,
        in_specs=(
            P("dp", "ctx", None),
            P("dp", "ctx", None),
            P("dp", None),
            P(("dp", "ctx"), None, "tensor"),
            P("tensor", ("dp", "ctx")),
            P(("dp", "ctx"), "tensor"),
            P("tensor", ("dp", "ctx")),
            P(),
            P(),
            P(),
            P(),
            P(),
            P(None, None, None, "tensor"),
            P(None, None, "tensor"),
            P(),
            P(),
            P(None, None, "tensor"),
            P(None, None, "tensor"),
            P(),
        ),
        out_specs=(
            P("dp", "ctx", None),
            P("dp", "ctx", None),
            P(),
            P(None, None, None, "tensor"),
            P(None, None, "tensor"),
            P(),
            P(),
            P(None, None, "tensor"),
            P(None, None, "tensor"),
            P(),
        ),
        check_vma=False,
    )
```

```python
import functools
import math

import jax
import jax.numpy as jnp
from jax import lax
from jax.experimental import pallas as pl
from jax.experimental.pallas import tpu as pltpu
from jax.sharding import PartitionSpec as P

HEAD_DIM = 128
NADAPT = 8
CHUNK_ROWS = 128
LAST_ROWS = 64
VMEM_BYTES = 62 * 2**20
VMEM_LAST = 48 * 2**20


BF = jnp.bfloat16
F32 = jnp.float32
MESH_IDS = pl.DeviceIdType.MESH
RANK_ROWS = 16
GELU_C = 0.7978845608028654
GELU_A = 0.044715


def dot_nn(a, b):
    return lax.dot_general(a, b, (((1,), (0,)), ((), ())), preferred_element_type=F32)


def dot_nt(a, b):
    return lax.dot_general(a, b, (((1,), (1,)), ((), ())), preferred_element_type=F32)


def dot_tn(a, b):
    return lax.dot_general(a, b, (((0,), (0,)), ((), ())), preferred_element_type=F32)


def tile(index, size):
    return pl.ds(pl.multiple_of(index * size, size), size)


def chain(
    ranks, half, block, me, acc, red_up, red_down, red_send, red_recv, cast_send, cast_recv, job_of
):
    def comm(tick, way):
        upward = way == 0
        place = me if upward else ranks - 1 - me
        ahead = me + 1 if upward else me - 1
        behind = me - 1 if upward else me + 1
        red = red_up if upward else red_down
        part = pl.ds(way * half, half)

        def red_copy(c):
            return pltpu.make_async_remote_copy(
                src_ref=red.at[c],
                dst_ref=red.at[c],
                send_sem=red_send.at[way, c],
                recv_sem=red_recv.at[way, c],
                device_id={"tensor": ahead},
                device_id_type=MESH_IDS,
            )

        def cast_copy(c):
            return pltpu.make_async_remote_copy(
                src_ref=acc.at[c, part],
                dst_ref=acc.at[c, part],
                send_sem=cast_send.at[way, c],
                recv_sem=cast_recv.at[way, c],
                device_id={"tensor": behind},
                device_id_type=MESH_IDS,
            )

        old_red, c_old = job_of(tick - 2 - place)

        @pl.when(old_red & (place < ranks - 1))
        def _():
            red_copy(c_old).wait_send()

        old_cast, c_cast = job_of(tick - 2 * ranks + place)

        @pl.when(old_cast & (place > 0))
        def _():
            cast_copy(c_cast).wait_send()

        now_red, c = job_of(tick - 1 - place)

        @pl.when(now_red & (place == 0))
        def _():
            red[c] = acc[c, part, :]

        @pl.when(now_red & (place > 0))
        def _():
            red_copy(c).wait_recv()

        @pl.when(now_red & (place > 0) & (place < ranks - 1))
        def _():
            @pl.loop(0, half // block)
            def _(i):
                rs = tile(i, block)
                own = acc[c, pl.ds(pl.multiple_of(way * half + i * block, block), block), :]
                red[c, rs, :] = (red[c, rs, :].astype(F32) + own.astype(F32)).astype(BF)

        @pl.when(now_red & (place < ranks - 1))
        def _():
            red_copy(c).start()

        @pl.when(now_red & (place == ranks - 1))
        def _():
            @pl.loop(0, half // block)
            def _(i):
                rs = tile(i, block)
                own_rs = pl.ds(pl.multiple_of(way * half + i * block, block), block)
                acc[c, own_rs, :] = (
                    red[c, rs, :].astype(F32) + acc[c, own_rs, :].astype(F32)
                ).astype(BF)

            cast_copy(c).start()

        now_cast, cc = job_of(tick - (2 * ranks - 1 - place))

        @pl.when(now_cast & (place < ranks - 1))
        def _():
            cast_copy(cc).wait_recv()

        @pl.when(now_cast & (place > 0) & (place < ranks - 1))
        def _():
            cast_copy(cc).start()
    return comm


def middle_kernel(
    sizes,
    local_qkv,
    hidden,
    cotangent,
    shard_out,
    shard_exp,
    shard_con,
    od,
    ou,
    ed,
    eu,
    cd,
    cu,
    gains,
    hidden_out,
    first_low,
    active,
    second_low,
    before_grad,
    attn_low,
    context_grad,
    out_rank,
    exp_rank,
    con_rank,
    con_rank_grad,
    exp_rank_grad,
    out_rank_grad,
    context,
    unit_qkv,
    unit_out,
    w_out,
    w_exp,
    w_con,
    acc,
    red_up,
    red_down,
    normed,
    spreads,
    slope,
    second,
    stage_d,
    stage_f,
    rows_in,
    rank_buf,
    in_sem,
    out_sem,
    red_send,
    red_recv,
    cast_send,
    cast_recv,
    peer_send,
    peer_recv,
    twin_send,
    twin_recv,
    own_sem,
    qkv_send,
    qkv_recv,
    ctx_send,
    ctx_recv,
    unit_sem,
):
    ranks, dps, ctxs, chunks, rows, per_seq, period = sizes
    half = rows // 2
    width = hidden.shape[1]
    hidden_units = w_exp.shape[1]
    heads = w_out.shape[0]
    block = min(16, half)
    tile_f = math.gcd(hidden_units, 256)
    tile_d = math.gcd(width, 256)
    tile_h = math.gcd(heads, 256)
    me = lax.axis_index("tensor")
    dp = lax.axis_index("dp")
    ctx = lax.axis_index("ctx")
    pairs = ctxs // 2
    core = ctx % 2
    chips = dps * pairs
    chip = dp * pairs + ctx // 2
    twin = {"ctx": ctx + 1 - 2 * core}
    lead = per_seq
    units, seq_all = unit_qkv.shape[0], unit_qkv.shape[2]
    tok = seq_all // ctxs
    local_heads = local_qkv.shape[1]

    def chip_block(step, which):
        row, column = step // pairs, step % pairs
        from_dp = (dp + dps - row) % dps
        from_chip = (ctx // 2 + pairs - column) % pairs
        return from_dp * ctxs + from_chip * 2 + which

    enter(me, ranks, [{"ctx": (ctx + d) % ctxs} for d in range(1, ctxs)]
          + [{"dp": (dp + e) % dps, "ctx": 2 * f + core}
             for e in range(1, dps) for f in range(pairs)])

    shards = (shard_out, shard_exp, shard_con)
    fulls = (w_out, w_exp, w_con)

    def block_of(w, index):
        if w == 1:
            return fulls[w].at[tile(index, shards[w].shape[0])]
        return fulls[w].at[:, tile(index, shards[w].shape[1])]

    def peer_copy(w, step):
        row, column = step // pairs, step % pairs
        block = block_of(w, chip_block(column, core))
        if row:
            target = {"dp": (dp + row) % dps}
        else:
            target = {"ctx": (ctx + 2 * column) % ctxs}
        own = block_of(w, chip_block(0, core))
        return pltpu.make_async_remote_copy(
            src_ref=block if row and column else shards[w],
            dst_ref=block if row else own,
            send_sem=peer_send.at[w, step],
            recv_sem=peer_recv.at[w, step],
            device_id=target,
            device_id_type=MESH_IDS,
        )

    def peer_arrival(w, step):
        row = step // pairs
        if row:
            target = {"dp": (dp + row) % dps}
        else:
            target = {"ctx": (ctx + 2 * step) % ctxs}
        return pltpu.make_async_remote_copy(
            src_ref=shards[w],
            dst_ref=block_of(w, chip_block(step, core)),
            send_sem=peer_send.at[w, step],
            recv_sem=peer_recv.at[w, step],
            device_id=target,
            device_id_type=MESH_IDS,
        )

    def twin_copy(w, step):
        block = block_of(w, chip_block(step, core))
        return pltpu.make_async_remote_copy(
            src_ref=shards[w] if step == 0 else block,
            dst_ref=block,
            send_sem=twin_send.at[w, step],
            recv_sem=twin_recv.at[w, step],
            device_id=twin,
            device_id_type=MESH_IDS,
        )

    def twin_arrival(w, step):
        block = block_of(w, chip_block(step, 1 - core))
        return pltpu.make_async_remote_copy(
            src_ref=block,
            dst_ref=block,
            send_sem=twin_send.at[w, step],
            recv_sem=twin_recv.at[w, step],
            device_id=twin,
            device_id_type=MESH_IDS,
        )

    def own_copy(w):
        return pltpu.make_async_copy(shards[w], block_of(w, chip_block(0, core)), own_sem.at[w])

    def weight_start(w):
        for step in list(range(pairs, chips, pairs)) + list(range(1, pairs)):
            peer_copy(w, step).start()
        twin_copy(w, 0).start()
        own_copy(w).start()

    def weight_relay(w):
        for step in range(1, pairs):
            peer_arrival(w, step).wait_recv()
            twin_copy(w, step).start()
            for row in range(1, dps):
                peer_copy(w, row * pairs + step).start()

    def weight_forward(w):
        for step in range(pairs, chips):
            peer_arrival(w, step).wait_recv()
            twin_copy(w, step).start()

    def weight_finish(w):
        own_copy(w).wait()
        for step in range(chips):
            twin_arrival(w, step).wait_recv()

    def weight_sent(w):
        for step in range(1, chips):
            peer_copy(w, step).wait_send()
        for step in range(chips):
            twin_copy(w, step).wait_send()

    def unit_place(device, u):
        return (device // local_heads) * units + u, device % local_heads

    def qkv_copy(u, step):
        peer = (ctx + step) % ctxs
        s, h = unit_place(peer, u)
        return pltpu.make_async_remote_copy(
            src_ref=local_qkv.at[s, h],
            dst_ref=unit_qkv.at[u, :, tile(ctx, tok)],
            send_sem=qkv_send.at[u, step],
            recv_sem=qkv_recv.at[u, step],
            device_id={"ctx": peer},
            device_id_type=MESH_IDS,
        )

    def qkv_arrival(u, step):
        return pltpu.make_async_remote_copy(
            src_ref=local_qkv.at[0, 0],
            dst_ref=unit_qkv.at[u, :, tile((ctx + ctxs - step) % ctxs, tok)],
            send_sem=qkv_send.at[u, step],
            recv_sem=qkv_recv.at[u, step],
            device_id={"ctx": (ctx + step) % ctxs},
            device_id_type=MESH_IDS,
        )

    def qkv_own(u):
        s, h = unit_place(ctx, u)
        return pltpu.make_async_copy(
            local_qkv.at[s, h], unit_qkv.at[u, :, tile(ctx, tok)], unit_sem.at[0, u]
        )

    def context_place(device, u):
        s, h = unit_place(device, u)
        return context.at[tile(s, tok), tile(h, HEAD_DIM)]

    def context_copy(u, step):
        peer = (ctx + step) % ctxs
        return pltpu.make_async_remote_copy(
            src_ref=unit_out.at[u, tile(peer, tok)],
            dst_ref=context_place(ctx, u),
            send_sem=ctx_send.at[u, step],
            recv_sem=ctx_recv.at[u, step],
            device_id={"ctx": peer},
            device_id_type=MESH_IDS,
        )

    def context_arrival(u, step):
        return pltpu.make_async_remote_copy(
            src_ref=unit_out.at[u, tile(ctx, tok)],
            dst_ref=context_place((ctx + ctxs - step) % ctxs, u),
            send_sem=ctx_send.at[u, step],
            recv_sem=ctx_recv.at[u, step],
            device_id={"ctx": (ctx + step) % ctxs},
            device_id_type=MESH_IDS,
        )

    def context_own(u):
        return pltpu.make_async_copy(
            unit_out.at[u, tile(ctx, tok)], context_place(ctx, u), unit_sem.at[1, u]
        )

    def attend(u):
        qkv_own(u).wait()
        for step in range(1, ctxs):
            qkv_arrival(u, step).wait_recv()
        part = math.gcd(seq_all, 256)

        @pl.loop(0, seq_all // part)
        def _(i):
            rs = tile(i, part)
            scores = dot_nt(unit_qkv[u, 0, rs, :], unit_qkv[u, 1]) * (HEAD_DIM ** (-0.5))
            largest = jnp.max(scores, axis=-1, keepdims=True)
            raised = jnp.exp(scores - largest)
            total = jnp.sum(raised, axis=-1, keepdims=True)
            mixed = dot_nn(raised.astype(BF), unit_qkv[u, 2])
            unit_out[u, rs, :] = (mixed / total).astype(BF)

        for step in range(1, ctxs):
            context_copy(u, step).start()
        context_own(u).start()

    def context_ready(u):
        context_own(u).wait()
        for step in range(1, ctxs):
            context_arrival(u, step).wait_recv()

    weight_start(0)
    for u in range(units):
        qkv_own(u).start()
        for step in range(1, ctxs):
            qkv_copy(u, step).start()
    weight_start(1)
    weight_start(2)
    weight_relay(0)

    def job_of(number, rounds):
        safe = jnp.maximum(number, 0)
        chunk = safe % period
        valid = (number >= 0) & (chunk < chunks) & (safe < rounds * period)
        return valid, jnp.minimum(chunk, chunks - 1)

    comm = chain(
        ranks,
        half,
        block,
        me,
        acc,
        red_up,
        red_down,
        red_send,
        red_recv,
        cast_send,
        cast_recv,
        lambda number: job_of(number, 3),
    )

    def rows_of(c):
        return tile(c, rows)

    def bring(source, c):
        return pltpu.make_async_copy(source.at[rows_of(c)], rows_in, in_sem)

    def keep(index, source, target, c):
        return pltpu.make_async_copy(source, target.at[rows_of(c)], out_sem.at[index])

    def mean(values):
        return jnp.sum(values, axis=-1, keepdims=True) * (1.0 / width)

    def attend_part(c, s):
        mine = context[rows_of(c), :]
        low = dot_nt(mine, od[s]).astype(BF)
        out_rank[rows_of(c), :] = low

        @pl.loop(0, width // tile_d)
        def _(i):
            cs = tile(i, tile_d)
            acc[c, :, cs] = (dot_nn(mine, w_out[:, cs]) + dot_nn(low, ou[s, :, cs])).astype(BF)

    def forward_first(c, s):
        bring(hidden, c).wait()

        @pl.loop(0, rows // block)
        def _(i):
            rs = tile(i, block)
            total = rows_in[rs, :].astype(F32) + acc[c, rs, :].astype(F32)
            centred = total - mean(total)
            spread = lax.rsqrt(mean(centred * centred) + 1e-06)
            n = centred * spread
            normed[c, rs, :] = n.astype(BF)
            spreads[c, rs, :] = jnp.broadcast_to(spread, (block, 128))
            stage_d[rs, :] = (n * gains[0:1, :] + gains[1:2, :]).astype(BF)

        low = dot_nt(stage_d[...], ed[s]).astype(BF)
        exp_rank[rows_of(c), :] = low
        rank_buf[...] = low

        @pl.loop(0, hidden_units // tile_f)
        def _(i):
            cs = tile(i, tile_f)
            b = dot_nn(stage_d[...], w_exp[:, cs]) + dot_nn(rank_buf[...], eu[s, :, cs])
            square = b * b
            t = jnp.tanh(GELU_C * b * (1.0 + GELU_A * square))
            upper = 0.5 * (1.0 + t)
            stage_f[:, cs] = (b * upper).astype(BF)
            slope[c, :, cs] = (
                upper
                + (0.5 * GELU_C) * b * (1.0 - t * t) * (1.0 + (3.0 * GELU_A) * square)
            ).astype(BF)

    def forward_second(c, s):
        low = dot_nt(stage_f[...], cd[s]).astype(BF)
        con_rank[rows_of(c), :] = low
        rank_buf[...] = low

        @pl.loop(0, width // tile_d)
        def _(i):
            cs = tile(i, tile_d)
            acc[c, :, cs] = (
                dot_nn(stage_f[...], w_con[:, cs]) + dot_nn(rank_buf[...], cu[s, :, cs])
            ).astype(BF)

        keep(0, stage_d, first_low, c).start()
        keep(1, stage_f, active, c).start()

    def back_first(c, s):
        bring(cotangent, c).wait()

        @pl.loop(0, rows // block)
        def _(i):
            rs = tile(i, block)
            first = normed[c, rs, :].astype(F32) * gains[0:1, :] + gains[1:2, :]
            total = first + acc[c, rs, :].astype(F32)
            centred = total - mean(total)
            spread = lax.rsqrt(mean(centred * centred) + 1e-06)
            n = centred * spread
            stage_d[rs, :] = (n * gains[2:3, :] + gains[3:4, :]).astype(BF)
            g = rows_in[rs, :].astype(F32) * gains[2:3, :]
            second[c, rs, :] = (spread * (g - mean(g) - n * mean(g * n))).astype(BF)

        low = dot_nt(second[c], cu[s]).astype(BF)
        con_rank_grad[rows_of(c), :] = low
        rank_buf[...] = low

        @pl.loop(0, hidden_units // tile_f)
        def _(i):
            cs = tile(i, tile_f)
            da = dot_nt(second[c], w_con[cs, :]) + dot_nn(rank_buf[...], cd[s, :, cs])
            stage_f[:, cs] = (da * slope[c, :, cs].astype(F32)).astype(BF)

    def back_second(c, s):
        low = dot_nt(stage_f[...], eu[s]).astype(BF)
        exp_rank_grad[rows_of(c), :] = low
        rank_buf[...] = low

        @pl.loop(0, width // tile_d)
        def _(i):
            cs = tile(i, tile_d)
            acc[c, :, cs] = (
                dot_nt(stage_f[...], w_exp[cs, :]) + dot_nn(rank_buf[...], ed[s, :, cs])
            ).astype(BF)

        keep(0, stage_d, hidden_out, c).start()
        keep(1, stage_f, before_grad, c).start()
        keep(2, second.at[c], second_low, c).start()

    def last_first(c, s):
        @pl.loop(0, rows // block)
        def _(i):
            rs = tile(i, block)
            n = normed[c, rs, :].astype(F32)
            g = (second[c, rs, :].astype(F32) + acc[c, rs, :].astype(F32)) * gains[0:1, :]
            spread = spreads[c, rs, 0:1]
            stage_d[rs, :] = (spread * (g - mean(g) - n * mean(g * n))).astype(BF)

    def last_second(c, s):
        low = dot_nt(stage_d[...], ou[s]).astype(BF)
        out_rank_grad[rows_of(c), :] = low
        rank_buf[...] = low

        @pl.loop(0, heads // tile_h)
        def _(i):
            cs = tile(i, tile_h)
            context_grad[rows_of(c), cs] = (
                dot_nt(stage_d[...], w_out[cs, :]) + dot_nn(rank_buf[...], od[s, :, cs])
            ).astype(BF)

        keep(0, stage_d, attn_low, c).start()

    @pl.loop(0, lead + 3 * period + chunks)
    def _(now):
        tick = now - lead
        stage = jnp.maximum(tick, 0) // period
        valid, c = job_of(tick, 4)
        s = c // per_seq
        last_valid, last_c = job_of(tick - 1, 4)
        last_stage = jnp.maximum(tick - 1, 0) // period

        comm(tick, 0)

        @pl.when(last_valid & (last_stage >= 1))
        def _():
            keep(0, stage_d, first_low, last_c).wait()

        @pl.when(last_valid & (last_stage >= 1) & (last_stage <= 2))
        def _():
            keep(1, stage_f, active, last_c).wait()

        @pl.when(last_valid & (last_stage == 2))
        def _():
            keep(2, second.at[last_c], second_low, last_c).wait()

        pl.when(now == 1)(lambda: weight_forward(0))

        @pl.when(now == lead + period - 4)
        def _():
            weight_relay(1)
            weight_relay(2)

        pl.when(now == lead + period - 1)(lambda: weight_forward(1))

        @pl.when(now == lead + period)
        def _():
            weight_forward(2)
            weight_finish(1)
            weight_finish(2)

        pl.when((now % per_seq == 0) & (now < units * per_seq))(lambda: attend(now // per_seq))
        pl.when(now == lead)(lambda: weight_finish(0))
        pl.when((tick >= 0) & (tick % per_seq == 0) & (tick < units * per_seq))(
            lambda: context_ready(s)
        )

        pl.when(valid & (stage == 1))(lambda: forward_first(c, s))
        pl.when(valid & (stage == 2))(lambda: back_first(c, s))
        pl.when(valid & (stage == 3))(lambda: last_first(c, s))

        comm(tick, 1)

        pl.when(valid & (stage == 0))(lambda: attend_part(c, s))
        pl.when(valid & (stage == 1))(lambda: forward_second(c, s))
        pl.when(valid & (stage == 2))(lambda: back_second(c, s))
        pl.when(valid & (stage == 3))(lambda: last_second(c, s))

        next_valid, next_c = job_of(tick + 1, 4)
        next_stage = jnp.maximum(tick + 1, 0) // period
        pl.when(next_valid & (next_stage == 1))(lambda: bring(hidden, next_c).start())
        pl.when(next_valid & (next_stage == 2))(lambda: bring(cotangent, next_c).start())

    keep(0, stage_d, attn_low, chunks - 1).wait()
    for w in range(3):
        weight_sent(w)
    for u in range(units):
        for step in range(1, ctxs):
            qkv_copy(u, step).wait_send()
            context_copy(u, step).wait_send()


def enter(me, ranks, others):
    barrier = pltpu.get_barrier_semaphore()

    @pl.when(me > 0)
    def _():
        pl.semaphore_signal(barrier, inc=1, device_id={"tensor": me - 1}, device_id_type=MESH_IDS)

    @pl.when(me < ranks - 1)
    def _():
        pl.semaphore_signal(barrier, inc=1, device_id={"tensor": me + 1}, device_id_type=MESH_IDS)

    for other in others:
        pl.semaphore_signal(barrier, inc=1, device_id=other, device_id_type=MESH_IDS)
    pl.semaphore_wait(
        barrier, len(others) + jnp.minimum(me, 1) + jnp.minimum(ranks - 1 - me, 1)
    )


def middle(local_qkv, hidden, cotangent, shards, picked, gains, tok):
    od, ou, ed, eu, cd, cu = picked
    total, width = hidden.shape
    heads, hidden_units = shards[0].shape[0], shards[1].shape[1]
    ranks, dps, ctxs = (lax.axis_size(name) for name in ("tensor", "dp", "ctx"))
    seqs, local_heads = local_qkv.shape[:2]
    units = seqs * local_heads // ctxs
    rank = od.shape[1]
    rows = math.gcd(tok, CHUNK_ROWS)
    chunks = total // rows
    period = max(chunks, 2 * ranks)
    sizes = (ranks, dps, ctxs, chunks, rows, tok // rows, period)
    chips = dps * ctxs // 2
    vm = pl.BlockSpec(memory_space=pltpu.VMEM)
    hb = pl.BlockSpec(memory_space=pl.ANY)
    half = rows // 2
    dma = pltpu.SemaphoreType.DMA

    def shape(*dims):
        return jax.ShapeDtypeStruct(dims, BF)

    return pl.pallas_call(
        functools.partial(middle_kernel, sizes),
        out_shape=(
            shape(total, width),
            shape(total, width),
            shape(total, hidden_units),
            shape(total, width),
            shape(total, hidden_units),
            shape(total, width),
            shape(total, heads),
        )
        + (shape(total, rank),) * 6
        + (
            shape(total, heads),
            shape(units, 3, tok * ctxs, HEAD_DIM),
            shape(units, tok * ctxs, HEAD_DIM),
        ),
        in_specs=[vm, hb, hb, hb, hb, hb] + [vm] * 7,
        out_specs=(hb,) * 6 + (vm,) * 10,
        scratch_shapes=[
            pltpu.VMEM((heads, width), BF),
            pltpu.VMEM((width, hidden_units), BF),
            pltpu.VMEM((hidden_units, width), BF),
            pltpu.VMEM((chunks, rows, width), BF),
            pltpu.VMEM((chunks, half, width), BF),
            pltpu.VMEM((chunks, half, width), BF),
            pltpu.VMEM((chunks, rows, width), BF),
            pltpu.VMEM((chunks, rows, 128), F32),
            pltpu.VMEM((chunks, rows, hidden_units), BF),
            pltpu.VMEM((chunks, rows, width), BF),
            pltpu.VMEM((rows, width), BF),
            pltpu.VMEM((rows, hidden_units), BF),
            pltpu.VMEM((rows, width), BF),
            pltpu.VMEM((rows, rank), BF),
            dma(()),
            dma((3,)),
            dma((2, chunks)),
            dma((2, chunks)),
            dma((2, chunks)),
            dma((2, chunks)),
            dma((3, chips)),
            dma((3, chips)),
            dma((3, chips)),
            dma((3, chips)),
            dma((3,)),
            dma((units, ctxs)),
            dma((units, ctxs)),
            dma((units, ctxs)),
            dma((units, ctxs)),
            dma((2, units)),
        ],
        compiler_params=pltpu.CompilerParams(
            collective_id=0, has_side_effects=True, vmem_limit_bytes=VMEM_BYTES
        ),
        cost_estimate=pl.CostEstimate(
            flops=8 * total * width * hidden_units + 4 * total * width * heads,
            bytes_accessed=16 * total * width,
            transcendentals=total * hidden_units,
        ),
    )(local_qkv, hidden, cotangent, *shards, od, ou, ed, eu, cd, cu, gains)


def mixing_kernel(
    sizes,
    context_grad,
    unit_qkv,
    unit_out,
    mixing,
    mu,
    md,
    attn_low,
    input_grad,
    grads,
    rank_part,
    unit_go,
    unit_grad,
    sum_k,
    sum_v,
    acc,
    red_up,
    red_down,
    stage_d,
    rows_in,
    rank_buf,
    in_sem,
    out_sem,
    red_send,
    red_recv,
    cast_send,
    cast_recv,
    go_send,
    go_recv,
    grad_send,
    grad_recv,
    unit_sem,
):
    ranks, ctxs, chunks, rows, per_seq, group = sizes
    half = rows // 2
    width = mixing.shape[0]
    heads = grads.shape[2]
    local_heads = heads // HEAD_DIM
    units, seq_all = unit_go.shape[0], unit_go.shape[1]
    tok = seq_all // ctxs
    block = min(16, half)
    tile_d = math.gcd(width, 256)
    scale = HEAD_DIM ** (-0.5)
    me = lax.axis_index("tensor")
    ctx = lax.axis_index("ctx")

    enter(me, ranks, [{"ctx": (ctx + d) % ctxs} for d in range(1, ctxs)])

    def unit_place(device, u):
        return (device // local_heads) * units + u, device % local_heads

    def go_copy(u, step):
        peer = (ctx + step) % ctxs
        s, h = unit_place(peer, u)
        return pltpu.make_async_remote_copy(
            src_ref=context_grad.at[tile(s, tok), tile(h, HEAD_DIM)],
            dst_ref=unit_go.at[u, tile(ctx, tok)],
            send_sem=go_send.at[u, step],
            recv_sem=go_recv.at[u, step],
            device_id={"ctx": peer},
            device_id_type=MESH_IDS,
        )

    def go_arrival(u, step):
        return pltpu.make_async_remote_copy(
            src_ref=context_grad.at[tile(0, tok), tile(0, HEAD_DIM)],
            dst_ref=unit_go.at[u, tile((ctx + ctxs - step) % ctxs, tok)],
            send_sem=go_send.at[u, step],
            recv_sem=go_recv.at[u, step],
            device_id={"ctx": (ctx + step) % ctxs},
            device_id_type=MESH_IDS,
        )

    def go_own(u):
        s, h = unit_place(ctx, u)
        return pltpu.make_async_copy(
            context_grad.at[tile(s, tok), tile(h, HEAD_DIM)],
            unit_go.at[u, tile(ctx, tok)],
            unit_sem.at[0, u],
        )

    def grads_place(device, u):
        s, h = unit_place(device, u)
        return grads.at[:, tile(s, tok), tile(h, HEAD_DIM)]

    def grad_copy(u, step):
        peer = (ctx + step) % ctxs
        return pltpu.make_async_remote_copy(
            src_ref=unit_grad.at[u, :, tile(peer, tok)],
            dst_ref=grads_place(ctx, u),
            send_sem=grad_send.at[u, step],
            recv_sem=grad_recv.at[u, step],
            device_id={"ctx": peer},
            device_id_type=MESH_IDS,
        )

    def grad_arrival(u, step):
        return pltpu.make_async_remote_copy(
            src_ref=unit_grad.at[u, :, tile(ctx, tok)],
            dst_ref=grads_place((ctx + ctxs - step) % ctxs, u),
            send_sem=grad_send.at[u, step],
            recv_sem=grad_recv.at[u, step],
            device_id={"ctx": (ctx + step) % ctxs},
            device_id_type=MESH_IDS,
        )

    def grad_own(u):
        return pltpu.make_async_copy(
            unit_grad.at[u, :, tile(ctx, tok)], grads_place(ctx, u), unit_sem.at[1, u]
        )

    def attend_back(u):
        go_own(u).wait()
        for step in range(1, ctxs):
            go_arrival(u, step).wait_recv()
        part = math.gcd(seq_all, 256)
        sum_k[...] = jnp.zeros_like(sum_k)
        sum_v[...] = jnp.zeros_like(sum_v)

        @pl.loop(0, seq_all // part)
        def _(i):
            rs = tile(i, part)
            queries = unit_qkv[u, 0, rs, :]
            go = unit_go[u, rs, :]
            scores = dot_nt(queries, unit_qkv[u, 1]) * scale
            raised = jnp.exp(scores - jnp.max(scores, axis=-1, keepdims=True))
            probs = raised * (1.0 / jnp.sum(raised, axis=-1, keepdims=True))
            delta = jnp.sum(
                go.astype(F32) * unit_out[u, rs, :].astype(F32), axis=-1, keepdims=True
            )
            dscores = (probs * (dot_nt(go, unit_qkv[u, 2]) - delta)).astype(BF)
            unit_grad[u, 0, rs, :] = (scale * dot_nn(dscores, unit_qkv[u, 1])).astype(BF)
            sum_k[...] += dot_tn(dscores, queries)
            sum_v[...] += dot_tn(probs.astype(BF), go)

        unit_grad[u, 1] = (scale * sum_k[...]).astype(BF)
        unit_grad[u, 2] = sum_v[...].astype(BF)
        for step in range(1, ctxs):
            grad_copy(u, step).start()
        grad_own(u).start()

    def grads_ready(u):
        grad_own(u).wait()
        for step in range(1, ctxs):
            grad_arrival(u, step).wait_recv()

    for u in range(units):
        go_own(u).start()
        for step in range(1, ctxs):
            go_copy(u, step).start()

    def job_of(number):
        return (number >= 0) & (number < chunks), jnp.clip(number, 0, chunks - 1)

    comm = chain(
        ranks, half, block, me, acc, red_up, red_down, red_send, red_recv, cast_send, cast_recv, job_of
    )

    def rows_of(c):
        return tile(c, rows)

    def bring(c):
        return pltpu.make_async_copy(attn_low.at[rows_of(c)], rows_in, in_sem)

    def keep(c):
        return pltpu.make_async_copy(stage_d, input_grad.at[rows_of(c)], out_sem)

    def back_part(c, s):
        rs = pl.ds(pl.multiple_of(c * rows, group * rows), group * rows)
        low = jnp.zeros((group * rows, mu.shape[1]), F32)
        for j in range(3):
            low = low + dot_nt(grads[j, rs, :], mu[s, :, pl.ds(j * heads, heads)])
        low = low.astype(BF)
        rank_part[rs, :] = low
        rank_buf[...] = low

        @pl.loop(0, width // tile_d)
        def _(i):
            cs = tile(i, tile_d)
            total = dot_nn(rank_buf[...], md[s, :, cs])
            for j in range(3):
                total = total + dot_nt(grads[j, rs, :], mixing[cs, pl.ds(j * heads, heads)])
            total = total.astype(BF)
            for k in range(group):
                acc[c + k, :, cs] = total[k * rows : (k + 1) * rows, :]

    def final_part(c):
        bring(c).wait()

        @pl.loop(0, rows // block)
        def _(i):
            rs = tile(i, block)
            stage_d[rs, :] = (rows_in[rs, :].astype(F32) + acc[c, rs, :].astype(F32)).astype(BF)

        keep(c).start()

    delay = 2 * ranks

    @pl.loop(0, per_seq + chunks + delay)
    def _(now):
        tick = now - per_seq
        valid, c = job_of(tick)
        final, c_final = job_of(tick - delay)
        before, c_before = job_of(tick - delay - 1)
        coming, c_coming = job_of(tick - delay + 1)
        s = c // per_seq

        comm(tick, 0)

        pl.when((now % per_seq == 0) & (now < units * per_seq))(lambda: attend_back(now // per_seq))
        pl.when((tick >= 0) & (tick % per_seq == 0) & (tick < units * per_seq))(
            lambda: grads_ready(s)
        )
        comm(tick, 1)

        pl.when(valid & (tick % group == 0))(lambda: back_part(c, s))

        pl.when(before)(lambda: keep(c_before).wait())
        pl.when(final)(lambda: final_part(c_final))
        pl.when(coming)(lambda: bring(c_coming).start())

    keep(chunks - 1).wait()
    for u in range(units):
        for step in range(1, ctxs):
            go_copy(u, step).wait_send()
            grad_copy(u, step).wait_send()


def mixing_back(context_grad, unit_qkv, unit_out, mixing, picked, attn_low):
    mu, md = picked
    total, width = attn_low.shape
    heads = context_grad.shape[1]
    ranks, ctxs = (lax.axis_size(name) for name in ("tensor", "ctx"))
    units, _, seq_all, _ = unit_qkv.shape
    tok = seq_all // ctxs
    rank = mu.shape[1]
    rows = math.gcd(tok, LAST_ROWS)
    chunks = total // rows
    per_seq = tok // rows
    group = math.gcd(per_seq, 2)
    half = rows // 2
    sizes = (ranks, ctxs, chunks, rows, per_seq, group)
    vm = pl.BlockSpec(memory_space=pltpu.VMEM)
    hb = pl.BlockSpec(memory_space=pl.ANY)
    dma = pltpu.SemaphoreType.DMA
    return pl.pallas_call(
        functools.partial(mixing_kernel, sizes),
        out_shape=(
            jax.ShapeDtypeStruct((total, width), BF),
            jax.ShapeDtypeStruct((3, total, heads), BF),
            jax.ShapeDtypeStruct((total, rank), BF),
        ),
        in_specs=[vm] * 6 + [hb],
        out_specs=(hb, vm, vm),
        scratch_shapes=[
            pltpu.VMEM((units, seq_all, HEAD_DIM), BF),
            pltpu.VMEM((units, 3, seq_all, HEAD_DIM), BF),
            pltpu.VMEM((seq_all, HEAD_DIM), F32),
            pltpu.VMEM((seq_all, HEAD_DIM), F32),
            pltpu.VMEM((chunks, rows, width), BF),
            pltpu.VMEM((chunks, half, width), BF),
            pltpu.VMEM((chunks, half, width), BF),
            pltpu.VMEM((rows, width), BF),
            pltpu.VMEM((rows, width), BF),
            pltpu.VMEM((group * rows, rank), BF),
            dma(()),
            dma(()),
            dma((2, chunks)),
            dma((2, chunks)),
            dma((2, chunks)),
            dma((2, chunks)),
            dma((units, ctxs)),
            dma((units, ctxs)),
            dma((units, ctxs)),
            dma((units, ctxs)),
            dma((2, units)),
        ],
        compiler_params=pltpu.CompilerParams(
            collective_id=1, has_side_effects=True, vmem_limit_bytes=VMEM_LAST
        ),
        cost_estimate=pl.CostEstimate(
            flops=6 * total * width * heads + 10 * units * seq_all * seq_all * HEAD_DIM,
            bytes_accessed=8 * total * width,
            transcendentals=units * seq_all * seq_all,
        ),
    )(context_grad, unit_qkv, unit_out, mixing, mu, md, attn_low)


def pick_rows(onehot_low, table):
    return jnp.einsum(
        "sn,n...->s...", onehot_low, table, preferred_element_type=jnp.float32
    ).astype(jnp.bfloat16)


def per_device(
    hidden_in,
    output_cotangent,
    adapter_index,
    mixing_weight,
    output_weight,
    expand_weight,
    contract_weight,
    first_gain,
    first_shift,
    second_gain,
    second_shift,
    mixing_down,
    mixing_up,
    output_down,
    output_up,
    expand_down,
    expand_up,
    contract_down,
    contract_up,
):
    seq_count, tok_count, model_width = hidden_in.shape
    local_heads = mixing_weight.shape[2] // HEAD_DIM
    local_width = mixing_weight.shape[2]
    rows_all = seq_count * tok_count
    adapter_ids = jnp.arange(NADAPT, dtype=jnp.int32)
    onehot_low = (adapter_index == adapter_ids[None, :]).astype(jnp.bfloat16)
    mixing_down_sel = pick_rows(onehot_low, mixing_down)
    mixing_up_sel = pick_rows(onehot_low, mixing_up)
    output_down_sel = pick_rows(onehot_low, output_down)
    output_up_sel = pick_rows(onehot_low, output_up)
    expand_down_sel = pick_rows(onehot_low, expand_down)
    expand_up_sel = pick_rows(onehot_low, expand_up)
    contract_down_sel = pick_rows(onehot_low, contract_down)
    contract_up_sel = pick_rows(onehot_low, contract_up)
    rank = mixing_down.shape[1]
    mixing_flat = mixing_weight.reshape(mixing_weight.shape[0], 3 * local_width)
    mixing_full = lax.all_gather(mixing_flat, ("dp", "ctx"), axis=0, tiled=True)
    hidden_rows = hidden_in.reshape(rows_all, model_width)
    mixing_rank = jnp.einsum(
        "std,srd->str", hidden_in, mixing_down_sel, preferred_element_type=jnp.float32
    ).astype(jnp.bfloat16)
    mixing_up_flat = mixing_up_sel.reshape(seq_count, rank, 3 * local_width)
    projected = jnp.einsum(
        "std,df->stf", hidden_in, mixing_full, preferred_element_type=jnp.float32
    )
    projected = projected + jnp.einsum(
        "str,srf->stf", mixing_rank, mixing_up_flat, preferred_element_type=jnp.float32
    )
    projected = projected.astype(jnp.bfloat16)
    local_qkv = projected.reshape(seq_count, tok_count, 3, local_heads, HEAD_DIM).transpose(
        0, 3, 2, 1, 4
    )
    gains = jnp.stack([first_gain, first_shift, second_gain, second_shift])
    (
        out_rows,
        first_low,
        active_low,
        second_low,
        before_low,
        attn_low,
        context_grad,
        output_rank,
        expand_rank,
        contract_rank,
        contract_rank_grad,
        expand_rank_grad,
        output_rank_grad,
        context,
        unit_qkv,
        unit_out,
    ) = middle(
        local_qkv,
        hidden_rows,
        output_cotangent.reshape(rows_all, model_width),
        (output_weight, expand_weight, contract_weight),
        (
            output_down_sel,
            output_up_sel,
            expand_down_sel,
            expand_up_sel,
            contract_down_sel,
            contract_up_sel,
        ),
        gains,
        tok_count,
    )
    input_rows, grads, mixing_rank_grad = mixing_back(
        context_grad, unit_qkv, unit_out, mixing_full, (mixing_up_flat, mixing_down_sel), attn_low
    )
    shared = lax.psum(
        jnp.concatenate([output_rank, contract_rank, expand_rank_grad], axis=1), "tensor"
    )
    output_rank, contract_rank, expand_rank_grad = (
        shared[:, :rank],
        shared[:, rank : 2 * rank],
        shared[:, 2 * rank :],
    )
    mixing_rank_grad = lax.psum(mixing_rank_grad, "tensor")
    row_hot = jnp.repeat(onehot_low, tok_count, axis=0)

    def table_grad(ranks, values):
        wide = (row_hot[:, :, None] * ranks[:, None, :]).reshape(rows_all, -1)
        part = jnp.einsum("nk,nd->kd", wide, values, preferred_element_type=jnp.float32)
        return part.astype(jnp.bfloat16).reshape(NADAPT, rank, values.shape[1])

    early = (
        table_grad(output_rank_grad, context),
        table_grad(output_rank, attn_low),
        table_grad(expand_rank_grad, first_low),
        table_grad(expand_rank, before_low),
        table_grad(contract_rank_grad, active_low),
        table_grad(contract_rank, second_low),
    )
    mixing_ranks = mixing_rank.reshape(rows_all, rank)
    late = (
        table_grad(mixing_rank_grad, hidden_rows),
        jnp.stack([table_grad(mixing_ranks, grads[j]) for j in range(3)], axis=2),
    )
    early = lax.psum(early, ("dp", "ctx"))
    late = lax.psum(late, ("dp", "ctx"))
    summed = tuple(part.astype(jnp.float32) for part in late + early)
    return (
        out_rows.reshape(hidden_in.shape),
        input_rows.reshape(hidden_in.shape),
    ) + summed


def solution(mesh):
    return jax.shard_map(
        per_device,
        mesh=mesh,
        in_specs=(
            P("dp", "ctx", None),
            P("dp", "ctx", None),
            P("dp", None),
            P(("dp", "ctx"), None, "tensor"),
            P("tensor", ("dp", "ctx")),
            P(("dp", "ctx"), "tensor"),
            P("tensor", ("dp", "ctx")),
            P(),
            P(),
            P(),
            P(),
            P(),
            P(None, None, None, "tensor"),
            P(None, None, "tensor"),
            P(),
            P(),
            P(None, None, "tensor"),
            P(None, None, "tensor"),
            P(),
        ),
        out_specs=(
            P("dp", "ctx", None),
            P("dp", "ctx", None),
            P(),
            P(None, None, None, "tensor"),
            P(None, None, "tensor"),
            P(),
            P(),
            P(None, None, "tensor"),
            P(None, None, "tensor"),
            P(),
        ),
        check_vma=False,
    )
```

```python
import functools
import math

import jax
import jax.numpy as jnp
from jax import lax
from jax.experimental import pallas as pl
from jax.experimental.pallas import tpu as pltpu
from jax.sharding import PartitionSpec as P

HEAD_DIM = 128
NADAPT = 8
CHUNK_ROWS = 128
LAST_ROWS = 64
VMEM_BYTES = 62 * 2**20
VMEM_LAST = 48 * 2**20
PIECES = 4


BF = jnp.bfloat16
F32 = jnp.float32
MESH_IDS = pl.DeviceIdType.MESH
RANK_ROWS = 16
GELU_C = 0.7978845608028654
GELU_A = 0.044715


def dot_nn(a, b):
    return lax.dot_general(a, b, (((1,), (0,)), ((), ())), preferred_element_type=F32)


def dot_nt(a, b):
    return lax.dot_general(a, b, (((1,), (1,)), ((), ())), preferred_element_type=F32)


def dot_tn(a, b):
    return lax.dot_general(a, b, (((0,), (0,)), ((), ())), preferred_element_type=F32)


def tile(index, size):
    return pl.ds(pl.multiple_of(index * size, size), size)


def chain(
    ranks, half, block, me, acc, red_up, red_down, red_send, red_recv, cast_send, cast_recv, job_of
):
    def comm(tick, way):
        upward = way == 0
        place = me if upward else ranks - 1 - me
        ahead = me + 1 if upward else me - 1
        behind = me - 1 if upward else me + 1
        red = red_up if upward else red_down
        part = pl.ds(way * half, half)

        def red_copy(c):
            return pltpu.make_async_remote_copy(
                src_ref=red.at[c],
                dst_ref=red.at[c],
                send_sem=red_send.at[way, c],
                recv_sem=red_recv.at[way, c],
                device_id={"tensor": ahead},
                device_id_type=MESH_IDS,
            )

        def cast_copy(c):
            return pltpu.make_async_remote_copy(
                src_ref=acc.at[c, part],
                dst_ref=acc.at[c, part],
                send_sem=cast_send.at[way, c],
                recv_sem=cast_recv.at[way, c],
                device_id={"tensor": behind},
                device_id_type=MESH_IDS,
            )

        old_red, c_old = job_of(tick - 2 - place)

        @pl.when(old_red & (place < ranks - 1))
        def _():
            red_copy(c_old).wait_send()

        old_cast, c_cast = job_of(tick - 2 * ranks + place)

        @pl.when(old_cast & (place > 0))
        def _():
            cast_copy(c_cast).wait_send()

        now_red, c = job_of(tick - 1 - place)

        @pl.when(now_red & (place == 0))
        def _():
            red[c] = acc[c, part, :]

        @pl.when(now_red & (place > 0))
        def _():
            red_copy(c).wait_recv()

        @pl.when(now_red & (place > 0) & (place < ranks - 1))
        def _():
            @pl.loop(0, half // block)
            def _(i):
                rs = tile(i, block)
                own = acc[c, pl.ds(pl.multiple_of(way * half + i * block, block), block), :]
                red[c, rs, :] = (red[c, rs, :].astype(F32) + own.astype(F32)).astype(BF)

        @pl.when(now_red & (place < ranks - 1))
        def _():
            red_copy(c).start()

        @pl.when(now_red & (place == ranks - 1))
        def _():
            @pl.loop(0, half // block)
            def _(i):
                rs = tile(i, block)
                own_rs = pl.ds(pl.multiple_of(way * half + i * block, block), block)
                acc[c, own_rs, :] = (
                    red[c, rs, :].astype(F32) + acc[c, own_rs, :].astype(F32)
                ).astype(BF)

            cast_copy(c).start()

        now_cast, cc = job_of(tick - (2 * ranks - 1 - place))

        @pl.when(now_cast & (place < ranks - 1))
        def _():
            cast_copy(cc).wait_recv()

        @pl.when(now_cast & (place > 0) & (place < ranks - 1))
        def _():
            cast_copy(cc).start()
    return comm


def middle_kernel(
    sizes,
    hidden,
    cotangent,
    shard_mix,
    shard_out,
    shard_exp,
    shard_con,
    md,
    mu,
    od,
    ou,
    ed,
    eu,
    cd,
    cu,
    gains,
    unit_rank,
    hidden_out,
    first_low,
    active,
    second_low,
    before_grad,
    attn_low,
    mixing,
    context_grad,
    part_ranks,
    full_ranks,
    context,
    unit_qkv,
    unit_out,
    local_qkv,
    w_out,
    w_exp,
    w_con,
    acc,
    red_up,
    red_down,
    stash,
    spreads,
    rank_in,
    stage_d,
    stage_f,
    rows_in,
    rank_buf,
    in_sem,
    out_sem,
    red_send,
    red_recv,
    cast_send,
    cast_recv,
    peer_send,
    peer_recv,
    twin_send,
    twin_recv,
    side_send,
    side_recv,
    own_sem,
    rank_send,
    rank_recv,
    mix_sem,
    qkv_send,
    qkv_recv,
    ctx_send,
    ctx_recv,
    unit_sem,
):
    ranks, dps, ctxs, chunks, rows, per_seq, period = sizes
    half = rows // 2
    width = hidden.shape[1]
    hidden_units = w_exp.shape[1]
    heads = w_out.shape[0]
    block = min(16, half)
    tile_f = math.gcd(hidden_units, 256)
    tile_d = math.gcd(width, 256)
    tile_h = math.gcd(heads, 256)
    me = lax.axis_index("tensor")
    dp = lax.axis_index("dp")
    ctx = lax.axis_index("ctx")
    pairs = ctxs // 2
    core = ctx % 2
    chips = dps * pairs
    chip = dp * pairs + ctx // 2
    twin = {"ctx": ctx + 1 - 2 * core}
    lead = per_seq
    units, seq_all = unit_qkv.shape[0], unit_qkv.shape[2]
    tok = seq_all // ctxs
    local_heads = local_qkv.shape[1]

    def chip_block(step, which):
        row, column = step // pairs, step % pairs
        from_dp = (dp + dps - row) % dps
        from_chip = (ctx // 2 + pairs - column) % pairs
        return from_dp * ctxs + from_chip * 2 + which

    total = chunks * rows
    enter(
        [{"tensor": (me + d) % ranks} for d in range(1, ranks)]
        + [{"ctx": (ctx + d) % ctxs} for d in range(1, ctxs)]
        + [{"dp": (dp + d) % dps} for d in range(1, dps)]
    )

    shards = (shard_mix, shard_out, shard_exp, shard_con)
    fulls = (stash, w_out, w_exp, w_con)
    mix_width = shard_mix.shape[1]
    mix_half = shard_mix.shape[0] // 2

    def piece_of(w, p):
        if w < 2:
            return shards[w]
        return shards[w].at[tile(p, shards[w].shape[0] // PIECES)]

    def block_of(w, index, p):
        deep, wide = shards[w].shape
        if w == 0:
            return stash.at[tile(index, deep), pl.ds(0, mix_width)]
        if w == 1:
            return w_out.at[:, tile(index, wide)]
        if w == 2:
            return w_exp.at[tile(index * PIECES + p, deep // PIECES)]
        return w_con.at[tile(p, deep // PIECES), tile(index, wide)]

    def mix_piece(step, lower):
        start = chip_block(step, core) * (2 * mix_half) + lower * mix_half
        return stash.at[pl.ds(pl.multiple_of(start, mix_half), mix_half), pl.ds(0, mix_width)]

    def peer_copy(w, step, p=0):
        row, column = step // pairs, step % pairs
        block = block_of(w, chip_block(column, core), p)
        if row:
            target = {"dp": (dp + row) % dps}
        else:
            target = {"ctx": (ctx + 2 * column) % ctxs}
        own = block_of(w, chip_block(0, core), p)
        if w == 0 and row and column:
            block = mix_piece(column, 0)
        return pltpu.make_async_remote_copy(
            src_ref=block if row and column else piece_of(w, p),
            dst_ref=block if row else own,
            send_sem=peer_send.at[w, step, p],
            recv_sem=peer_recv.at[w, step, p],
            device_id=target,
            device_id_type=MESH_IDS,
        )

    def peer_arrival(w, step, p=0):
        row = step // pairs
        if row:
            target = {"dp": (dp + row) % dps}
        else:
            target = {"ctx": (ctx + 2 * step) % ctxs}
        block = block_of(w, chip_block(step, core), p)
        if w == 0 and row and step % pairs:
            block = mix_piece(step, 0)
        return pltpu.make_async_remote_copy(
            src_ref=block,
            dst_ref=block,
            send_sem=peer_send.at[w, step, p],
            recv_sem=peer_recv.at[w, step, p],
            device_id=target,
            device_id_type=MESH_IDS,
        )

    def twin_copy(w, step, p=0):
        block = block_of(w, chip_block(step, core), p)
        return pltpu.make_async_remote_copy(
            src_ref=piece_of(w, p) if step == 0 else block,
            dst_ref=block,
            send_sem=twin_send.at[w, step, p],
            recv_sem=twin_recv.at[w, step, p],
            device_id=twin,
            device_id_type=MESH_IDS,
        )

    def twin_arrival(w, step, p=0):
        block = block_of(w, chip_block(step, 1 - core), p)
        return pltpu.make_async_remote_copy(
            src_ref=block,
            dst_ref=block,
            send_sem=twin_send.at[w, step, p],
            recv_sem=twin_recv.at[w, step, p],
            device_id=twin,
            device_id_type=MESH_IDS,
        )

    def own_copy(w, p=0):
        return pltpu.make_async_copy(piece_of(w, p), block_of(w, chip_block(0, core), p), own_sem.at[w, p])

    def side_copy(step):
        row, column = step // pairs, step % pairs
        piece = mix_piece(row * pairs, 1)
        return pltpu.make_async_remote_copy(
            src_ref=piece,
            dst_ref=piece,
            send_sem=side_send.at[step],
            recv_sem=side_recv.at[step],
            device_id={"ctx": (ctx + 2 * column) % ctxs},
            device_id_type=MESH_IDS,
        )

    def side_arrival(step):
        piece = mix_piece(step, 1)
        return pltpu.make_async_remote_copy(
            src_ref=piece,
            dst_ref=piece,
            send_sem=side_send.at[step],
            recv_sem=side_recv.at[step],
            device_id={"ctx": (ctx + 2 * (step % pairs)) % ctxs},
            device_id_type=MESH_IDS,
        )

    def across_start(w, p=0):
        for step in range(pairs, chips, pairs):
            peer_copy(w, step, p).start()
        twin_copy(w, 0, p).start()
        own_copy(w, p).start()

    def along_start(w, p=0):
        for step in range(1, pairs):
            peer_copy(w, step, p).start()

    def weight_relay(w, p=0):
        for step in range(1, pairs):
            peer_arrival(w, step, p).wait_recv()
            for row in range(1, dps):
                peer_copy(w, row * pairs + step, p).start()
            twin_copy(w, step, p).start()

    def weight_forward(w, p=0):
        for step in range(pairs, chips):
            peer_arrival(w, step, p).wait_recv()
            twin_copy(w, step, p).start()

    def mixing_gather():
        along_start(0)
        across_start(0)
        weight_relay(0)
        for row in range(1, dps):
            peer_arrival(0, row * pairs).wait_recv()
            for column in range(1, pairs):
                side_copy(row * pairs + column).start()
            twin_copy(0, row * pairs).start()
        for row in range(1, dps):
            for column in range(1, pairs):
                step = row * pairs + column
                peer_arrival(0, step).wait_recv()
                side_arrival(step).wait_recv()
                twin_copy(0, step).start()

    def weight_finish(w, p=0):
        own_copy(w, p).wait()
        for step in range(chips):
            twin_arrival(w, step, p).wait_recv()

    def side_sent():
        for row in range(1, dps):
            for column in range(1, pairs):
                side_copy(row * pairs + column).wait_send()

    def weight_sent(w, p=0):
        for step in range(1, chips):
            peer_copy(w, step, p).wait_send()
        for step in range(chips):
            twin_copy(w, step, p).wait_send()

    def unit_place(device, u):
        return (device // local_heads) * units + u, device % local_heads

    def qkv_copy(u, step):
        peer = (ctx + step) % ctxs
        s, h = unit_place(peer, u)
        return pltpu.make_async_remote_copy(
            src_ref=local_qkv.at[s, h],
            dst_ref=unit_qkv.at[u, :, tile(ctx, tok)],
            send_sem=qkv_send.at[u, step],
            recv_sem=qkv_recv.at[u, step],
            device_id={"ctx": peer},
            device_id_type=MESH_IDS,
        )

    def qkv_arrival(u, step):
        return pltpu.make_async_remote_copy(
            src_ref=local_qkv.at[0, 0],
            dst_ref=unit_qkv.at[u, :, tile((ctx + ctxs - step) % ctxs, tok)],
            send_sem=qkv_send.at[u, step],
            recv_sem=qkv_recv.at[u, step],
            device_id={"ctx": (ctx + step) % ctxs},
            device_id_type=MESH_IDS,
        )

    def qkv_own(u):
        s, h = unit_place(ctx, u)
        return pltpu.make_async_copy(
            local_qkv.at[s, h], unit_qkv.at[u, :, tile(ctx, tok)], unit_sem.at[0, u]
        )

    def context_place(device, u):
        s, h = unit_place(device, u)
        return context.at[tile(s, tok), tile(h, HEAD_DIM)]

    def context_copy(u, step):
        peer = (ctx + step) % ctxs
        return pltpu.make_async_remote_copy(
            src_ref=unit_out.at[u, tile(peer, tok)],
            dst_ref=context_place(ctx, u),
            send_sem=ctx_send.at[u, step],
            recv_sem=ctx_recv.at[u, step],
            device_id={"ctx": peer},
            device_id_type=MESH_IDS,
        )

    def context_arrival(u, step):
        return pltpu.make_async_remote_copy(
            src_ref=unit_out.at[u, tile(ctx, tok)],
            dst_ref=context_place((ctx + ctxs - step) % ctxs, u),
            send_sem=ctx_send.at[u, step],
            recv_sem=ctx_recv.at[u, step],
            device_id={"ctx": (ctx + step) % ctxs},
            device_id_type=MESH_IDS,
        )

    def context_own(u):
        return pltpu.make_async_copy(
            unit_out.at[u, tile(ctx, tok)], context_place(ctx, u), unit_sem.at[1, u]
        )

    def attend(u):
        qkv_own(u).wait()
        for step in range(1, ctxs):
            qkv_arrival(u, step).wait_recv()
        part = math.gcd(seq_all, 256)

        @pl.loop(0, seq_all // part)
        def _(i):
            rs = tile(i, part)
            scores = dot_nt(unit_qkv[u, 0, rs, :], unit_qkv[u, 1]) * (HEAD_DIM ** (-0.5))
            largest = jnp.max(scores, axis=-1, keepdims=True)
            raised = jnp.exp(scores - largest)
            total = jnp.sum(raised, axis=-1, keepdims=True)
            mixed = dot_nn(raised.astype(BF), unit_qkv[u, 2])
            unit_out[u, rs, :] = (mixed / total).astype(BF)

        for step in range(1, ctxs):
            context_copy(u, step).start()
        context_own(u).start()

    def context_ready(u):
        context_own(u).wait()
        for step in range(1, ctxs):
            context_arrival(u, step).wait_recv()

    def project_chunk(c):
        bring(hidden, c).wait()
        following = (c + 1) % chunks
        s = c // per_seq
        rs = tile(c % per_seq, rows)
        low = dot_nt(rows_in[...], md[s]).astype(BF)
        put_rank(3, c, low)
        rank_buf[...] = low
        heads_at_once = math.gcd(local_heads, 2)
        step = heads_at_once * HEAD_DIM

        @pl.loop(0, mix_width // step)
        def _(i):
            cs = tile(i, step)
            values = dot_nn(rows_in[...], stash[0:width, cs]) + dot_nn(rank_buf[...], mu[s, :, cs])
            values = values.astype(BF)
            first = i * heads_at_once
            for k in range(heads_at_once):
                local_qkv[s, (first + k) % local_heads, (first + k) // local_heads, rs, :] = values[
                    :, k * HEAD_DIM : (k + 1) * HEAD_DIM
                ]

        bring(hidden, following).start()

    def project(s):
        @pl.loop(0, per_seq)
        def _(i):
            project_chunk(s * per_seq + i)

    def send_unit(u):
        qkv_own(u).start()
        for step in range(1, ctxs):
            qkv_copy(u, step).start()

    def job_of(number, rounds):
        safe = jnp.maximum(number, 0)
        chunk = safe % period
        valid = (number >= 0) & (chunk < chunks) & (safe < rounds * period)
        return valid, jnp.minimum(chunk, chunks - 1)

    comm = chain(
        ranks,
        half,
        block,
        me,
        acc,
        red_up,
        red_down,
        red_send,
        red_recv,
        cast_send,
        cast_recv,
        lambda number: job_of(number, 3),
    )

    def rows_of(c):
        return tile(c, rows)

    def spot(t, c, i=None):
        start = t * total + c * rows
        if i is None:
            return pl.ds(pl.multiple_of(start, rows), rows)
        return pl.ds(pl.multiple_of(start + i * block, block), block)

    def mixing_keep():
        return pltpu.make_async_copy(
            stash.at[pl.ds(0, width), pl.ds(0, mix_width)], mixing, mix_sem
        )

    def bring(source, c):
        return pltpu.make_async_copy(source.at[rows_of(c)], rows_in, in_sem)

    def keep(index, source, target, c):
        return pltpu.make_async_copy(source, target.at[rows_of(c)], out_sem.at[index])

    def put_rank(t, c, low):
        part_ranks[t, :, tile(c, rows)] = dot_nt(unit_rank[...], low).astype(BF)

    def rank_copy(t, step):
        return pltpu.make_async_remote_copy(
            src_ref=part_ranks.at[t],
            dst_ref=rank_in.at[t, step],
            send_sem=rank_send.at[t, step],
            recv_sem=rank_recv.at[t, step],
            device_id={"tensor": (me + step) % ranks},
            device_id_type=MESH_IDS,
        )

    def mean(values):
        return jnp.sum(values, axis=-1, keepdims=True) * (1.0 / width)

    def attend_part(c, s):
        mine = context[rows_of(c), :]
        low = dot_nt(mine, od[s]).astype(BF)
        put_rank(0, c, low)

        @pl.loop(0, width // tile_d)
        def _(i):
            cs = tile(i, tile_d)
            acc[c, :, cs] = (dot_nn(mine, w_out[:, cs]) + dot_nn(low, ou[s, :, cs])).astype(BF)

    def forward_first(c, s):
        bring(hidden, c).wait()

        @pl.loop(0, rows // block)
        def _(i):
            rs = tile(i, block)
            total = rows_in[rs, :].astype(F32) + acc[c, rs, :].astype(F32)
            centred = total - mean(total)
            spread = lax.rsqrt(mean(centred * centred) + 1e-06)
            n = centred * spread
            stash[spot(0, c, i), :] = n.astype(BF)
            spreads[c, rs, :] = jnp.broadcast_to(spread, (block, 128))
            stage_d[rs, :] = (n * gains[0:1, :] + gains[1:2, :]).astype(BF)

        low = dot_nt(stage_d[...], ed[s]).astype(BF)
        put_rank(4, c, low)
        rank_buf[...] = low

        @pl.loop(0, hidden_units // tile_f)
        def _(i):
            cs = tile(i, tile_f)
            b = dot_nn(stage_d[...], w_exp[:, cs]) + dot_nn(rank_buf[...], eu[s, :, cs])
            square = b * b
            t = jnp.tanh(GELU_C * b * (1.0 + GELU_A * square))
            upper = 0.5 * (1.0 + t)
            stage_f[:, cs] = (b * upper).astype(BF)
            stash[spot(1, c), cs] = (
                upper
                + (0.5 * GELU_C) * b * (1.0 - t * t) * (1.0 + (3.0 * GELU_A) * square)
            ).astype(BF)

    def forward_second(c, s):
        low = dot_nt(stage_f[...], cd[s]).astype(BF)
        put_rank(1, c, low)
        rank_buf[...] = low

        @pl.loop(0, width // tile_d)
        def _(i):
            cs = tile(i, tile_d)
            acc[c, :, cs] = (
                dot_nn(stage_f[...], w_con[:, cs]) + dot_nn(rank_buf[...], cu[s, :, cs])
            ).astype(BF)

        keep(0, stage_d, first_low, c).start()
        keep(1, stage_f, active, c).start()

    def back_first(c, s):
        bring(cotangent, c).wait()

        @pl.loop(0, rows // block)
        def _(i):
            rs = tile(i, block)
            first = stash[spot(0, c, i), :].astype(F32) * gains[0:1, :] + gains[1:2, :]
            total = first + acc[c, rs, :].astype(F32)
            centred = total - mean(total)
            spread = lax.rsqrt(mean(centred * centred) + 1e-06)
            n = centred * spread
            stage_d[rs, :] = (n * gains[2:3, :] + gains[3:4, :]).astype(BF)
            g = rows_in[rs, :].astype(F32) * gains[2:3, :]
            stash[spot(2, c, i), :] = (spread * (g - mean(g) - n * mean(g * n))).astype(BF)

        low = dot_nt(stash[spot(2, c), :], cu[s]).astype(BF)
        put_rank(5, c, low)
        rank_buf[...] = low

        @pl.loop(0, hidden_units // tile_f)
        def _(i):
            cs = tile(i, tile_f)
            da = dot_nt(stash[spot(2, c), :], w_con[cs, :]) + dot_nn(rank_buf[...], cd[s, :, cs])
            stage_f[:, cs] = (da * stash[spot(1, c), cs].astype(F32)).astype(BF)

    def back_second(c, s):
        low = dot_nt(stage_f[...], eu[s]).astype(BF)
        put_rank(2, c, low)
        rank_buf[...] = low

        @pl.loop(0, width // tile_d)
        def _(i):
            cs = tile(i, tile_d)
            acc[c, :, cs] = (
                dot_nt(stage_f[...], w_exp[cs, :]) + dot_nn(rank_buf[...], ed[s, :, cs])
            ).astype(BF)

        keep(0, stage_d, hidden_out, c).start()
        keep(1, stage_f, before_grad, c).start()
        keep(2, stash.at[spot(2, c)], second_low, c).start()

    def last_first(c, s):
        @pl.loop(0, rows // block)
        def _(i):
            rs = tile(i, block)
            n = stash[spot(0, c, i), :].astype(F32)
            g = (stash[spot(2, c, i), :].astype(F32) + acc[c, rs, :].astype(F32)) * gains[0:1, :]
            spread = spreads[c, rs, 0:1]
            stage_d[rs, :] = (spread * (g - mean(g) - n * mean(g * n))).astype(BF)

    def last_second(c, s):
        low = dot_nt(stage_d[...], ou[s]).astype(BF)
        put_rank(6, c, low)
        rank_buf[...] = low

        @pl.loop(0, heads // tile_h)
        def _(i):
            cs = tile(i, tile_h)
            context_grad[rows_of(c), cs] = (
                dot_nt(stage_d[...], w_out[cs, :]) + dot_nn(rank_buf[...], od[s, :, cs])
            ).astype(BF)

        keep(0, stage_d, attn_low, c).start()

    seqs = chunks // per_seq
    flowing = units == seqs
    bring(hidden, 0).start()
    mixing_gather()
    weight_finish(0)
    along_start(1)
    across_start(1)
    mixing_keep().start()
    if flowing:
        for u in range(min(2, units)):
            project(u)
            send_unit(u)
    else:
        pl.loop(0, seqs)(project)
        for u in range(units):
            send_unit(u)
    weight_relay(1)

    @pl.loop(0, lead + 3 * period + chunks)
    def _(now):
        tick = now - lead
        stage = jnp.maximum(tick, 0) // period
        valid, c = job_of(tick, 4)
        s = c // per_seq
        last_valid, last_c = job_of(tick - 1, 4)
        last_stage = jnp.maximum(tick - 1, 0) // period

        comm(tick, 0)

        @pl.when(last_valid & (last_stage >= 1))
        def _():
            keep(0, stage_d, first_low, last_c).wait()

        @pl.when(last_valid & (last_stage >= 1) & (last_stage <= 2))
        def _():
            keep(1, stage_f, active, last_c).wait()

        @pl.when(last_valid & (last_stage == 2))
        def _():
            keep(2, stash.at[spot(2, last_c)], second_low, last_c).wait()

        pl.when(now == 1)(lambda: weight_forward(1))
        if flowing:

            @pl.when((now % per_seq == 0) & (now < (units - 2) * per_seq))
            def _():
                project(now // per_seq + 2)
                send_unit(now // per_seq + 2)

        @pl.when((now % per_seq == 0) & (now > 0) & (now <= PIECES * per_seq))
        def _():
            p = now // per_seq - 1
            weight_relay(2, p)
            weight_relay(3, p)

        @pl.when((now % per_seq == 0) & (now < PIECES * per_seq))
        def _():
            for w in (2, 3):
                along_start(w, now // per_seq)
                across_start(w, now // per_seq)

        @pl.when((now % per_seq == 1 % per_seq) & (now > per_seq) & (now <= PIECES * per_seq + 1))
        def _():
            p = (now - 1) // per_seq - 1
            weight_forward(2, p)
            weight_forward(3, p)

        @pl.when(now == lead + period)
        def _():
            for p in range(PIECES):
                weight_finish(2, p)
                weight_finish(3, p)

        pl.when((now % per_seq == 0) & (now < units * per_seq))(lambda: attend(now // per_seq))
        pl.when(now == lead)(lambda: weight_finish(1))

        @pl.when(now == lead + period - 2)
        def _():
            mixing_keep().wait()
            weight_sent(0)
            side_sent()

        for t in range(3):

            @pl.when(tick == (t + 1) * period)
            def _(t=t):
                for step in range(1, ranks):
                    rank_copy(t, step).start()

        pl.when((tick >= 0) & (tick % per_seq == 0) & (tick < units * per_seq))(
            lambda: context_ready(s)
        )

        pl.when(valid & (stage == 1))(lambda: forward_first(c, s))
        pl.when(valid & (stage == 2))(lambda: back_first(c, s))
        pl.when(valid & (stage == 3))(lambda: last_first(c, s))

        comm(tick, 1)

        pl.when(valid & (stage == 0))(lambda: attend_part(c, s))
        pl.when(valid & (stage == 1))(lambda: forward_second(c, s))
        pl.when(valid & (stage == 2))(lambda: back_second(c, s))
        pl.when(valid & (stage == 3))(lambda: last_second(c, s))

        next_valid, next_c = job_of(tick + 1, 4)
        next_stage = jnp.maximum(tick + 1, 0) // period
        pl.when(next_valid & (next_stage == 1) & (next_c > 0))(
            lambda: bring(hidden, next_c).start()
        )
        pl.when(next_valid & (next_stage == 2))(lambda: bring(cotangent, next_c).start())

    keep(0, stage_d, attn_low, chunks - 1).wait()
    for t in range(3):
        value = part_ranks[t].astype(F32)
        for step in range(1, ranks):
            rank_copy(t, step).wait_recv()
            value = value + rank_in[t, step].astype(F32)
        full_ranks[t] = value.astype(BF)
    for t in range(3):
        for step in range(1, ranks):
            rank_copy(t, step).wait_send()
    weight_sent(1)
    for p in range(PIECES):
        weight_sent(2, p)
        weight_sent(3, p)
    for u in range(units):
        for step in range(1, ctxs):
            qkv_copy(u, step).wait_send()
            context_copy(u, step).wait_send()


def enter(others):
    barrier = pltpu.get_barrier_semaphore()
    for other in others:
        pl.semaphore_signal(barrier, inc=1, device_id=other, device_id_type=MESH_IDS)
    pl.semaphore_wait(barrier, len(others))


def middle(hidden, cotangent, shards, picked, gains, tok):
    total, width = hidden.shape
    mix_width = shards[0].shape[1]
    heads, hidden_units = shards[1].shape[0], shards[2].shape[1]
    ranks, dps, ctxs = (lax.axis_size(name) for name in ("tensor", "dp", "ctx"))
    seqs, rank = picked[0].shape[:2]
    local_heads = heads // HEAD_DIM
    units = seqs * local_heads // ctxs
    rows = math.gcd(tok, CHUNK_ROWS)
    chunks = total // rows
    period = max(chunks, 2 * ranks)
    sizes = (ranks, dps, ctxs, chunks, rows, tok // rows, period)
    chips = dps * ctxs // 2
    vm = pl.BlockSpec(memory_space=pltpu.VMEM)
    hb = pl.BlockSpec(memory_space=pl.ANY)
    half = rows // 2
    dma = pltpu.SemaphoreType.DMA

    def shape(*dims):
        return jax.ShapeDtypeStruct(dims, BF)

    return pl.pallas_call(
        functools.partial(middle_kernel, sizes),
        out_shape=(
            shape(total, width),
            shape(total, width),
            shape(total, hidden_units),
            shape(total, width),
            shape(total, hidden_units),
            shape(total, width),
            shape(width, mix_width),
            shape(total, heads),
            shape(7, rank, total),
            shape(3, rank, total),
            shape(total, heads),
            shape(units, 3, tok * ctxs, HEAD_DIM),
            shape(units, tok * ctxs, HEAD_DIM),
        ),
        in_specs=[hb] * 6 + [vm] * 10,
        out_specs=(hb,) * 7 + (vm,) * 6,
        scratch_shapes=[
            pltpu.VMEM((seqs, local_heads, 3, tok, HEAD_DIM), BF),
            pltpu.VMEM((heads, width), BF),
            pltpu.VMEM((width, hidden_units), BF),
            pltpu.VMEM((hidden_units, width), BF),
            pltpu.VMEM((chunks, rows, width), BF),
            pltpu.VMEM((chunks, half, width), BF),
            pltpu.VMEM((chunks, half, width), BF),
            pltpu.VMEM((3 * total, width), BF),
            pltpu.VMEM((chunks, rows, 128), F32),
            pltpu.VMEM((3, ranks, rank, total), BF),
            pltpu.VMEM((rows, width), BF),
            pltpu.VMEM((rows, hidden_units), BF),
            pltpu.VMEM((rows, width), BF),
            pltpu.VMEM((rows, rank), BF),
            dma(()),
            dma((3,)),
            dma((2, chunks)),
            dma((2, chunks)),
            dma((2, chunks)),
            dma((2, chunks)),
            dma((4, chips, PIECES)),
            dma((4, chips, PIECES)),
            dma((4, chips, PIECES)),
            dma((4, chips, PIECES)),
            dma((chips,)),
            dma((chips,)),
            dma((4, PIECES)),
            dma((3, ranks)),
            dma((3, ranks)),
            dma(()),
            dma((units, ctxs)),
            dma((units, ctxs)),
            dma((units, ctxs)),
            dma((units, ctxs)),
            dma((2, units)),
        ],
        compiler_params=pltpu.CompilerParams(
            collective_id=0, has_side_effects=True, vmem_limit_bytes=VMEM_BYTES
        ),
        cost_estimate=pl.CostEstimate(
            flops=8 * total * width * hidden_units + 4 * total * width * heads,
            bytes_accessed=16 * total * width,
            transcendentals=total * hidden_units,
        ),
    )(hidden, cotangent, *shards, *picked, gains, jnp.eye(rank, dtype=BF))


def mixing_kernel(
    sizes,
    context_grad,
    unit_qkv,
    unit_out,
    mixing,
    mu,
    md,
    attn_low,
    unit_rank,
    input_grad,
    grads,
    full_rank,
    rank_part,
    rank_in,
    unit_go,
    unit_grad,
    sum_k,
    sum_v,
    acc,
    red_up,
    red_down,
    stage_d,
    rows_in,
    rank_buf,
    in_sem,
    out_sem,
    red_send,
    red_recv,
    cast_send,
    cast_recv,
    go_send,
    go_recv,
    grad_send,
    grad_recv,
    unit_sem,
    rank_send,
    rank_recv,
):
    ranks, ctxs, chunks, rows, per_seq, group = sizes
    half = rows // 2
    width = mixing.shape[0]
    heads = grads.shape[2]
    local_heads = heads // HEAD_DIM
    units, seq_all = unit_go.shape[0], unit_go.shape[1]
    tok = seq_all // ctxs
    block = min(16, half)
    tile_d = math.gcd(width, 256)
    scale = HEAD_DIM ** (-0.5)
    me = lax.axis_index("tensor")
    ctx = lax.axis_index("ctx")

    enter(
        [{"tensor": (me + d) % ranks} for d in range(1, ranks)]
        + [{"ctx": (ctx + d) % ctxs} for d in range(1, ctxs)]
    )

    def unit_place(device, u):
        return (device // local_heads) * units + u, device % local_heads

    def go_copy(u, step):
        peer = (ctx + step) % ctxs
        s, h = unit_place(peer, u)
        return pltpu.make_async_remote_copy(
            src_ref=context_grad.at[tile(s, tok), tile(h, HEAD_DIM)],
            dst_ref=unit_go.at[u, tile(ctx, tok)],
            send_sem=go_send.at[u, step],
            recv_sem=go_recv.at[u, step],
            device_id={"ctx": peer},
            device_id_type=MESH_IDS,
        )

    def go_arrival(u, step):
        return pltpu.make_async_remote_copy(
            src_ref=context_grad.at[tile(0, tok), tile(0, HEAD_DIM)],
            dst_ref=unit_go.at[u, tile((ctx + ctxs - step) % ctxs, tok)],
            send_sem=go_send.at[u, step],
            recv_sem=go_recv.at[u, step],
            device_id={"ctx": (ctx + step) % ctxs},
            device_id_type=MESH_IDS,
        )

    def go_own(u):
        s, h = unit_place(ctx, u)
        return pltpu.make_async_copy(
            context_grad.at[tile(s, tok), tile(h, HEAD_DIM)],
            unit_go.at[u, tile(ctx, tok)],
            unit_sem.at[0, u],
        )

    def grads_place(device, u):
        s, h = unit_place(device, u)
        return grads.at[:, tile(s, tok), tile(h, HEAD_DIM)]

    def grad_copy(u, step):
        peer = (ctx + step) % ctxs
        return pltpu.make_async_remote_copy(
            src_ref=unit_grad.at[u, :, tile(peer, tok)],
            dst_ref=grads_place(ctx, u),
            send_sem=grad_send.at[u, step],
            recv_sem=grad_recv.at[u, step],
            device_id={"ctx": peer},
            device_id_type=MESH_IDS,
        )

    def grad_arrival(u, step):
        return pltpu.make_async_remote_copy(
            src_ref=unit_grad.at[u, :, tile(ctx, tok)],
            dst_ref=grads_place((ctx + ctxs - step) % ctxs, u),
            send_sem=grad_send.at[u, step],
            recv_sem=grad_recv.at[u, step],
            device_id={"ctx": (ctx + step) % ctxs},
            device_id_type=MESH_IDS,
        )

    def grad_own(u):
        return pltpu.make_async_copy(
            unit_grad.at[u, :, tile(ctx, tok)], grads_place(ctx, u), unit_sem.at[1, u]
        )

    def attend_back(u):
        go_own(u).wait()
        for step in range(1, ctxs):
            go_arrival(u, step).wait_recv()
        part = math.gcd(seq_all, 256)
        sum_k[...] = jnp.zeros_like(sum_k)
        sum_v[...] = jnp.zeros_like(sum_v)

        @pl.loop(0, seq_all // part)
        def _(i):
            rs = tile(i, part)
            queries = unit_qkv[u, 0, rs, :]
            go = unit_go[u, rs, :]
            scores = dot_nt(queries, unit_qkv[u, 1]) * scale
            raised = jnp.exp(scores - jnp.max(scores, axis=-1, keepdims=True))
            probs = raised * (1.0 / jnp.sum(raised, axis=-1, keepdims=True))
            delta = jnp.sum(
                go.astype(F32) * unit_out[u, rs, :].astype(F32), axis=-1, keepdims=True
            )
            dscores = (probs * (dot_nt(go, unit_qkv[u, 2]) - delta)).astype(BF)
            unit_grad[u, 0, rs, :] = (scale * dot_nn(dscores, unit_qkv[u, 1])).astype(BF)
            sum_k[...] += dot_tn(dscores, queries)
            sum_v[...] += dot_tn(probs.astype(BF), go)

        unit_grad[u, 1] = (scale * sum_k[...]).astype(BF)
        unit_grad[u, 2] = sum_v[...].astype(BF)
        for step in range(1, ctxs):
            grad_copy(u, step).start()
        grad_own(u).start()

    def grads_ready(u):
        grad_own(u).wait()
        for step in range(1, ctxs):
            grad_arrival(u, step).wait_recv()

    for u in range(units):
        go_own(u).start()
        for step in range(1, ctxs):
            go_copy(u, step).start()

    def job_of(number):
        return (number >= 0) & (number < chunks), jnp.clip(number, 0, chunks - 1)

    comm = chain(
        ranks, half, block, me, acc, red_up, red_down, red_send, red_recv, cast_send, cast_recv, job_of
    )

    def rows_of(c):
        return tile(c, rows)

    def bring(c):
        return pltpu.make_async_copy(attn_low.at[rows_of(c)], rows_in, in_sem)

    def keep(c):
        return pltpu.make_async_copy(stage_d, input_grad.at[rows_of(c)], out_sem)

    def back_part(c, s):
        rs = pl.ds(pl.multiple_of(c * rows, group * rows), group * rows)
        low = jnp.zeros((group * rows, mu.shape[1]), F32)
        for j in range(3):
            low = low + dot_nt(grads[j, rs, :], mu[s, :, pl.ds(j * heads, heads)])
        low = low.astype(BF)
        rank_part[:, pl.ds(pl.multiple_of(c * rows, group * rows), group * rows)] = dot_nt(
            unit_rank[...], low
        ).astype(BF)
        rank_buf[...] = low

        @pl.loop(0, width // tile_d)
        def _(i):
            cs = tile(i, tile_d)
            total = dot_nn(rank_buf[...], md[s, :, cs])
            for j in range(3):
                total = total + dot_nt(grads[j, rs, :], mixing[cs, pl.ds(j * heads, heads)])
            total = total.astype(BF)
            for k in range(group):
                acc[c + k, :, cs] = total[k * rows : (k + 1) * rows, :]

    def final_part(c):
        bring(c).wait()

        @pl.loop(0, rows // block)
        def _(i):
            rs = tile(i, block)
            stage_d[rs, :] = (rows_in[rs, :].astype(F32) + acc[c, rs, :].astype(F32)).astype(BF)

        keep(c).start()

    def rank_copy(step):
        return pltpu.make_async_remote_copy(
            src_ref=rank_part,
            dst_ref=rank_in.at[step],
            send_sem=rank_send.at[step],
            recv_sem=rank_recv.at[step],
            device_id={"tensor": (me + step) % ranks},
            device_id_type=MESH_IDS,
        )

    delay = 2 * ranks

    @pl.loop(0, per_seq + chunks + delay)
    def _(now):
        tick = now - per_seq

        @pl.when(tick == chunks)
        def _():
            for step in range(1, ranks):
                rank_copy(step).start()

        valid, c = job_of(tick)
        final, c_final = job_of(tick - delay)
        before, c_before = job_of(tick - delay - 1)
        coming, c_coming = job_of(tick - delay + 1)
        s = c // per_seq

        comm(tick, 0)

        pl.when((now % per_seq == 0) & (now < units * per_seq))(lambda: attend_back(now // per_seq))
        pl.when((tick >= 0) & (tick % per_seq == 0) & (tick < units * per_seq))(
            lambda: grads_ready(s)
        )
        comm(tick, 1)

        pl.when(valid & (tick % group == 0))(lambda: back_part(c, s))

        pl.when(before)(lambda: keep(c_before).wait())
        pl.when(final)(lambda: final_part(c_final))
        pl.when(coming)(lambda: bring(c_coming).start())

    keep(chunks - 1).wait()
    value = rank_part[...].astype(F32)
    for step in range(1, ranks):
        rank_copy(step).wait_recv()
        value = value + rank_in[step].astype(F32)
    full_rank[...] = value.astype(BF)
    for step in range(1, ranks):
        rank_copy(step).wait_send()
    for u in range(units):
        for step in range(1, ctxs):
            go_copy(u, step).wait_send()
            grad_copy(u, step).wait_send()


def mixing_back(context_grad, unit_qkv, unit_out, mixing, picked, attn_low):
    mu, md = picked
    total, width = attn_low.shape
    heads = context_grad.shape[1]
    ranks, ctxs = (lax.axis_size(name) for name in ("tensor", "ctx"))
    units, _, seq_all, _ = unit_qkv.shape
    tok = seq_all // ctxs
    rank = mu.shape[1]
    rows = math.gcd(tok, LAST_ROWS)
    chunks = total // rows
    per_seq = tok // rows
    group = math.gcd(per_seq, 2)
    half = rows // 2
    sizes = (ranks, ctxs, chunks, rows, per_seq, group)
    vm = pl.BlockSpec(memory_space=pltpu.VMEM)
    hb = pl.BlockSpec(memory_space=pl.ANY)
    dma = pltpu.SemaphoreType.DMA
    return pl.pallas_call(
        functools.partial(mixing_kernel, sizes),
        out_shape=(
            jax.ShapeDtypeStruct((total, width), BF),
            jax.ShapeDtypeStruct((3, total, heads), BF),
            jax.ShapeDtypeStruct((rank, total), BF),
        ),
        in_specs=[vm] * 6 + [hb, vm],
        out_specs=(hb, vm, vm),
        scratch_shapes=[
            pltpu.VMEM((rank, total), BF),
            pltpu.VMEM((ranks, rank, total), BF),
            pltpu.VMEM((units, seq_all, HEAD_DIM), BF),
            pltpu.VMEM((units, 3, seq_all, HEAD_DIM), BF),
            pltpu.VMEM((seq_all, HEAD_DIM), F32),
            pltpu.VMEM((seq_all, HEAD_DIM), F32),
            pltpu.VMEM((chunks, rows, width), BF),
            pltpu.VMEM((chunks, half, width), BF),
            pltpu.VMEM((chunks, half, width), BF),
            pltpu.VMEM((rows, width), BF),
            pltpu.VMEM((rows, width), BF),
            pltpu.VMEM((group * rows, rank), BF),
            dma(()),
            dma(()),
            dma((2, chunks)),
            dma((2, chunks)),
            dma((2, chunks)),
            dma((2, chunks)),
            dma((units, ctxs)),
            dma((units, ctxs)),
            dma((units, ctxs)),
            dma((units, ctxs)),
            dma((2, units)),
            dma((ranks,)),
            dma((ranks,)),
        ],
        compiler_params=pltpu.CompilerParams(
            collective_id=1, has_side_effects=True, vmem_limit_bytes=VMEM_LAST
        ),
        cost_estimate=pl.CostEstimate(
            flops=6 * total * width * heads + 10 * units * seq_all * seq_all * HEAD_DIM,
            bytes_accessed=8 * total * width,
            transcendentals=units * seq_all * seq_all,
        ),
    )(context_grad, unit_qkv, unit_out, mixing, mu, md, attn_low, jnp.eye(rank, dtype=BF))


def pick_rows(onehot_low, table):
    return jnp.einsum(
        "sn,n...->s...", onehot_low, table, preferred_element_type=jnp.float32
    ).astype(jnp.bfloat16)


def per_device(
    hidden_in,
    output_cotangent,
    adapter_index,
    mixing_weight,
    output_weight,
    expand_weight,
    contract_weight,
    first_gain,
    first_shift,
    second_gain,
    second_shift,
    mixing_down,
    mixing_up,
    output_down,
    output_up,
    expand_down,
    expand_up,
    contract_down,
    contract_up,
):
    seq_count, tok_count, model_width = hidden_in.shape
    local_heads = mixing_weight.shape[2] // HEAD_DIM
    local_width = mixing_weight.shape[2]
    rows_all = seq_count * tok_count
    adapter_ids = jnp.arange(NADAPT, dtype=jnp.int32)
    onehot_low = (adapter_index == adapter_ids[None, :]).astype(jnp.bfloat16)
    mixing_down_sel = pick_rows(onehot_low, mixing_down)
    mixing_up_sel = pick_rows(onehot_low, mixing_up)
    output_down_sel = pick_rows(onehot_low, output_down)
    output_up_sel = pick_rows(onehot_low, output_up)
    expand_down_sel = pick_rows(onehot_low, expand_down)
    expand_up_sel = pick_rows(onehot_low, expand_up)
    contract_down_sel = pick_rows(onehot_low, contract_down)
    contract_up_sel = pick_rows(onehot_low, contract_up)
    rank = mixing_down.shape[1]
    mixing_flat = mixing_weight.reshape(mixing_weight.shape[0], 3 * local_width)
    hidden_rows = hidden_in.reshape(rows_all, model_width)
    mixing_up_flat = mixing_up_sel.reshape(seq_count, rank, 3 * local_width)
    gains = jnp.stack([first_gain, first_shift, second_gain, second_shift])
    (
        out_rows,
        first_low,
        active_low,
        second_low,
        before_low,
        attn_low,
        mixing_full,
        context_grad,
        part_ranks,
        full_ranks,
        context,
        unit_qkv,
        unit_out,
    ) = middle(
        hidden_rows,
        output_cotangent.reshape(rows_all, model_width),
        (mixing_flat, output_weight, expand_weight, contract_weight),
        (
            mixing_down_sel,
            mixing_up_flat,
            output_down_sel,
            output_up_sel,
            expand_down_sel,
            expand_up_sel,
            contract_down_sel,
            contract_up_sel,
        ),
        gains,
        tok_count,
    )
    row_hot = jnp.repeat(onehot_low.T, tok_count, axis=1)

    def table_grad(ranks, values):
        wide = (row_hot[:, None, :] * ranks[None, :, :]).reshape(-1, rows_all)
        part = jnp.einsum("kn,nd->kd", wide, values, preferred_element_type=jnp.float32)
        return part.astype(jnp.bfloat16).reshape(NADAPT, rank, values.shape[1])

    early = (
        table_grad(part_ranks[6], context),
        table_grad(full_ranks[0], attn_low),
        table_grad(full_ranks[2], first_low),
        table_grad(part_ranks[4], before_low),
        table_grad(part_ranks[5], active_low),
        table_grad(full_ranks[1], second_low),
    )
    early, context_grad = lax.optimization_barrier((early, context_grad))
    input_rows, grads, mixing_rank_grad = mixing_back(
        context_grad, unit_qkv, unit_out, mixing_full, (mixing_up_flat, mixing_down_sel), attn_low
    )
    early = lax.psum(early, ("dp", "ctx"))
    late = (
        table_grad(mixing_rank_grad, hidden_rows),
        jnp.stack([table_grad(part_ranks[3], grads[j]) for j in range(3)], axis=2),
    )
    late, early = lax.optimization_barrier((late, early))
    late = lax.psum(late, ("dp", "ctx"))
    summed = tuple(part.astype(jnp.float32) for part in late + early)
    return (
        out_rows.reshape(hidden_in.shape),
        input_rows.reshape(hidden_in.shape),
    ) + summed


def solution(mesh):
    return jax.shard_map(
        per_device,
        mesh=mesh,
        in_specs=(
            P("dp", "ctx", None),
            P("dp", "ctx", None),
            P("dp", None),
            P(("dp", "ctx"), None, "tensor"),
            P("tensor", ("dp", "ctx")),
            P(("dp", "ctx"), "tensor"),
            P("tensor", ("dp", "ctx")),
            P(),
            P(),
            P(),
            P(),
            P(),
            P(None, None, None, "tensor"),
            P(None, None, "tensor"),
            P(),
            P(),
            P(None, None, "tensor"),
            P(None, None, "tensor"),
            P(),
        ),
        out_specs=(
            P("dp", "ctx", None),
            P("dp", "ctx", None),
            P(),
            P(None, None, None, "tensor"),
            P(None, None, "tensor"),
            P(),
            P(),
            P(None, None, "tensor"),
            P(None, None, "tensor"),
            P(),
        ),
        check_vma=False,
    )
```

```python
import functools
import math

import jax
import jax.numpy as jnp
from jax import lax
from jax.experimental import pallas as pl
from jax.experimental.pallas import tpu as pltpu
from jax.sharding import PartitionSpec as P

HEAD_DIM = 128
NADAPT = 8
CHUNK_ROWS = 128
LAST_ROWS = 64
VMEM_BYTES = 62 * 2**20
VMEM_LAST = 48 * 2**20
PIECES = 4


BF = jnp.bfloat16
F32 = jnp.float32
MESH_IDS = pl.DeviceIdType.MESH
RANK_ROWS = 16
GELU_C = 0.7978845608028654
GELU_A = 0.044715


def dot_nn(a, b):
    return lax.dot_general(a, b, (((1,), (0,)), ((), ())), preferred_element_type=F32)


def dot_nt(a, b):
    return lax.dot_general(a, b, (((1,), (1,)), ((), ())), preferred_element_type=F32)


def dot_tn(a, b):
    return lax.dot_general(a, b, (((0,), (0,)), ((), ())), preferred_element_type=F32)


def tile(index, size):
    return pl.ds(pl.multiple_of(index * size, size), size)


def chain(
    ranks, half, block, me, acc, red_up, red_down, red_send, red_recv, cast_send, cast_recv, job_of
):
    def comm(tick, way):
        upward = way == 0
        place = me if upward else ranks - 1 - me
        ahead = me + 1 if upward else me - 1
        behind = me - 1 if upward else me + 1
        red = red_up if upward else red_down
        part = pl.ds(way * half, half)

        def red_copy(c):
            return pltpu.make_async_remote_copy(
                src_ref=red.at[c],
                dst_ref=red.at[c],
                send_sem=red_send.at[way, c],
                recv_sem=red_recv.at[way, c],
                device_id={"tensor": ahead},
                device_id_type=MESH_IDS,
            )

        def cast_copy(c):
            return pltpu.make_async_remote_copy(
                src_ref=acc.at[c, part],
                dst_ref=acc.at[c, part],
                send_sem=cast_send.at[way, c],
                recv_sem=cast_recv.at[way, c],
                device_id={"tensor": behind},
                device_id_type=MESH_IDS,
            )

        old_red, c_old = job_of(tick - 2 - place)

        @pl.when(old_red & (place < ranks - 1))
        def _():
            red_copy(c_old).wait_send()

        old_cast, c_cast = job_of(tick - 2 * ranks + place)

        @pl.when(old_cast & (place > 0))
        def _():
            cast_copy(c_cast).wait_send()

        now_red, c = job_of(tick - 1 - place)

        @pl.when(now_red & (place == 0))
        def _():
            red[c] = acc[c, part, :]

        @pl.when(now_red & (place > 0))
        def _():
            red_copy(c).wait_recv()

        @pl.when(now_red & (place > 0) & (place < ranks - 1))
        def _():
            @pl.loop(0, half // block)
            def _(i):
                rs = tile(i, block)
                own = acc[c, pl.ds(pl.multiple_of(way * half + i * block, block), block), :]
                red[c, rs, :] = (red[c, rs, :].astype(F32) + own.astype(F32)).astype(BF)

        @pl.when(now_red & (place < ranks - 1))
        def _():
            red_copy(c).start()

        @pl.when(now_red & (place == ranks - 1))
        def _():
            @pl.loop(0, half // block)
            def _(i):
                rs = tile(i, block)
                own_rs = pl.ds(pl.multiple_of(way * half + i * block, block), block)
                acc[c, own_rs, :] = (
                    red[c, rs, :].astype(F32) + acc[c, own_rs, :].astype(F32)
                ).astype(BF)

            cast_copy(c).start()

        now_cast, cc = job_of(tick - (2 * ranks - 1 - place))

        @pl.when(now_cast & (place < ranks - 1))
        def _():
            cast_copy(cc).wait_recv()

        @pl.when(now_cast & (place > 0) & (place < ranks - 1))
        def _():
            cast_copy(cc).start()
    return comm


def middle_kernel(
    sizes,
    hidden,
    cotangent,
    shard_mix,
    shard_out,
    shard_exp,
    shard_con,
    md,
    mu,
    od,
    ou,
    ed,
    eu,
    cd,
    cu,
    gains,
    unit_rank,
    hidden_out,
    first_low,
    active,
    second_low,
    before_grad,
    attn_low,
    mixing,
    context_grad,
    part_ranks,
    full_ranks,
    context,
    unit_qkv,
    unit_out,
    local_qkv,
    w_out,
    w_exp,
    w_con,
    acc,
    red_up,
    red_down,
    stash,
    spreads,
    rank_in,
    stage_d,
    stage_f,
    rows_in,
    rank_buf,
    in_sem,
    out_sem,
    red_send,
    red_recv,
    cast_send,
    cast_recv,
    peer_send,
    peer_recv,
    twin_send,
    twin_recv,
    side_send,
    side_recv,
    own_sem,
    rank_send,
    rank_recv,
    mix_sem,
    qkv_send,
    qkv_recv,
    ctx_send,
    ctx_recv,
    unit_sem,
):
    ranks, dps, ctxs, chunks, rows, per_seq, period = sizes
    half = rows // 2
    width = hidden.shape[1]
    hidden_units = w_exp.shape[1]
    heads = w_out.shape[0]
    block = min(16, half)
    tile_f = math.gcd(hidden_units, 256)
    tile_d = math.gcd(width, 256)
    tile_h = math.gcd(heads, 256)
    me = lax.axis_index("tensor")
    dp = lax.axis_index("dp")
    ctx = lax.axis_index("ctx")
    pairs = ctxs // 2
    core = ctx % 2
    chips = dps * pairs
    chip = dp * pairs + ctx // 2
    twin = {"ctx": ctx + 1 - 2 * core}
    lead = per_seq
    units, seq_all = unit_qkv.shape[0], unit_qkv.shape[2]
    tok = seq_all // ctxs
    local_heads = local_qkv.shape[1]

    def chip_block(step, which):
        row, column = step // pairs, step % pairs
        from_dp = (dp + dps - row) % dps
        from_chip = (ctx // 2 + pairs - column) % pairs
        return from_dp * ctxs + from_chip * 2 + which

    total = chunks * rows
    enter(
        [{"tensor": (me + d) % ranks} for d in range(1, ranks)]
        + [{"ctx": (ctx + d) % ctxs} for d in range(1, ctxs)]
        + [{"dp": (dp + d) % dps} for d in range(1, dps)]
    )

    shards = (shard_mix, shard_out, shard_exp, shard_con)
    fulls = (stash, w_out, w_exp, w_con)
    mix_width = shard_mix.shape[1]
    mix_half = shard_mix.shape[0] // 2

    def piece_of(w, p):
        if w < 2:
            return shards[w]
        return shards[w].at[tile(p, shards[w].shape[0] // PIECES)]

    def block_of(w, index, p):
        deep, wide = shards[w].shape
        if w == 0:
            return stash.at[tile(index, deep), pl.ds(0, mix_width)]
        if w == 1:
            return w_out.at[:, tile(index, wide)]
        if w == 2:
            return w_exp.at[tile(index * PIECES + p, deep // PIECES)]
        return w_con.at[tile(p, deep // PIECES), tile(index, wide)]

    def mix_piece(step, lower):
        start = chip_block(step, core) * (2 * mix_half) + lower * mix_half
        return stash.at[pl.ds(pl.multiple_of(start, mix_half), mix_half), pl.ds(0, mix_width)]

    def peer_copy(w, step, p=0):
        row, column = step // pairs, step % pairs
        block = block_of(w, chip_block(column, core), p)
        if row:
            target = {"dp": (dp + row) % dps}
        else:
            target = {"ctx": (ctx + 2 * column) % ctxs}
        own = block_of(w, chip_block(0, core), p)
        if w == 0 and row and column:
            block = mix_piece(column, 0)
        return pltpu.make_async_remote_copy(
            src_ref=block if row and column else piece_of(w, p),
            dst_ref=block if row else own,
            send_sem=peer_send.at[w, step, p],
            recv_sem=peer_recv.at[w, step, p],
            device_id=target,
            device_id_type=MESH_IDS,
        )

    def peer_arrival(w, step, p=0):
        row = step // pairs
        if row:
            target = {"dp": (dp + row) % dps}
        else:
            target = {"ctx": (ctx + 2 * step) % ctxs}
        block = block_of(w, chip_block(step, core), p)
        if w == 0 and row and step % pairs:
            block = mix_piece(step, 0)
        return pltpu.make_async_remote_copy(
            src_ref=block,
            dst_ref=block,
            send_sem=peer_send.at[w, step, p],
            recv_sem=peer_recv.at[w, step, p],
            device_id=target,
            device_id_type=MESH_IDS,
        )

    def twin_copy(w, step, p=0):
        block = block_of(w, chip_block(step, core), p)
        return pltpu.make_async_remote_copy(
            src_ref=piece_of(w, p) if step == 0 else block,
            dst_ref=block,
            send_sem=twin_send.at[w, step, p],
            recv_sem=twin_recv.at[w, step, p],
            device_id=twin,
            device_id_type=MESH_IDS,
        )

    def twin_arrival(w, step, p=0):
        block = block_of(w, chip_block(step, 1 - core), p)
        return pltpu.make_async_remote_copy(
            src_ref=block,
            dst_ref=block,
            send_sem=twin_send.at[w, step, p],
            recv_sem=twin_recv.at[w, step, p],
            device_id=twin,
            device_id_type=MESH_IDS,
        )

    def own_copy(w, p=0):
        return pltpu.make_async_copy(piece_of(w, p), block_of(w, chip_block(0, core), p), own_sem.at[w, p])

    def side_copy(step):
        row, column = step // pairs, step % pairs
        piece = mix_piece(row * pairs, 1)
        return pltpu.make_async_remote_copy(
            src_ref=piece,
            dst_ref=piece,
            send_sem=side_send.at[step],
            recv_sem=side_recv.at[step],
            device_id={"ctx": (ctx + 2 * column) % ctxs},
            device_id_type=MESH_IDS,
        )

    def side_arrival(step):
        piece = mix_piece(step, 1)
        return pltpu.make_async_remote_copy(
            src_ref=piece,
            dst_ref=piece,
            send_sem=side_send.at[step],
            recv_sem=side_recv.at[step],
            device_id={"ctx": (ctx + 2 * (step % pairs)) % ctxs},
            device_id_type=MESH_IDS,
        )

    def across_start(w, p=0):
        for step in range(pairs, chips, pairs):
            peer_copy(w, step, p).start()
        twin_copy(w, 0, p).start()
        own_copy(w, p).start()

    def along_start(w, p=0):
        for step in range(1, pairs):
            peer_copy(w, step, p).start()

    def weight_relay(w, p=0):
        for step in range(1, pairs):
            peer_arrival(w, step, p).wait_recv()
            for row in range(1, dps):
                peer_copy(w, row * pairs + step, p).start()
            twin_copy(w, step, p).start()

    def weight_forward(w, p=0):
        for step in range(pairs, chips):
            peer_arrival(w, step, p).wait_recv()
            twin_copy(w, step, p).start()

    def mixing_gather():
        along_start(0)
        across_start(0)
        weight_relay(0)
        for row in range(1, dps):
            peer_arrival(0, row * pairs).wait_recv()
            for column in range(1, pairs):
                side_copy(row * pairs + column).start()
            twin_copy(0, row * pairs).start()
        for row in range(1, dps):
            for column in range(1, pairs):
                step = row * pairs + column
                peer_arrival(0, step).wait_recv()
                side_arrival(step).wait_recv()
                twin_copy(0, step).start()

    def weight_finish(w, p=0):
        own_copy(w, p).wait()
        for step in range(chips):
            twin_arrival(w, step, p).wait_recv()

    def side_sent():
        for row in range(1, dps):
            for column in range(1, pairs):
                side_copy(row * pairs + column).wait_send()

    def weight_sent(w, p=0):
        for step in range(1, chips):
            peer_copy(w, step, p).wait_send()
        for step in range(chips):
            twin_copy(w, step, p).wait_send()

    def unit_place(device, u):
        return (device // local_heads) * units + u, device % local_heads

    def qkv_copy(u, step):
        peer = (ctx + step) % ctxs
        s, h = unit_place(peer, u)
        return pltpu.make_async_remote_copy(
            src_ref=local_qkv.at[s, h],
            dst_ref=unit_qkv.at[u, :, tile(ctx, tok)],
            send_sem=qkv_send.at[u, step],
            recv_sem=qkv_recv.at[u, step],
            device_id={"ctx": peer},
            device_id_type=MESH_IDS,
        )

    def qkv_arrival(u, step):
        return pltpu.make_async_remote_copy(
            src_ref=local_qkv.at[0, 0],
            dst_ref=unit_qkv.at[u, :, tile((ctx + ctxs - step) % ctxs, tok)],
            send_sem=qkv_send.at[u, step],
            recv_sem=qkv_recv.at[u, step],
            device_id={"ctx": (ctx + step) % ctxs},
            device_id_type=MESH_IDS,
        )

    def qkv_own(u):
        s, h = unit_place(ctx, u)
        return pltpu.make_async_copy(
            local_qkv.at[s, h], unit_qkv.at[u, :, tile(ctx, tok)], unit_sem.at[0, u]
        )

    def context_place(device, u):
        s, h = unit_place(device, u)
        return context.at[tile(s, tok), tile(h, HEAD_DIM)]

    def context_copy(u, step):
        peer = (ctx + step) % ctxs
        return pltpu.make_async_remote_copy(
            src_ref=unit_out.at[u, tile(peer, tok)],
            dst_ref=context_place(ctx, u),
            send_sem=ctx_send.at[u, step],
            recv_sem=ctx_recv.at[u, step],
            device_id={"ctx": peer},
            device_id_type=MESH_IDS,
        )

    def context_arrival(u, step):
        return pltpu.make_async_remote_copy(
            src_ref=unit_out.at[u, tile(ctx, tok)],
            dst_ref=context_place((ctx + ctxs - step) % ctxs, u),
            send_sem=ctx_send.at[u, step],
            recv_sem=ctx_recv.at[u, step],
            device_id={"ctx": (ctx + step) % ctxs},
            device_id_type=MESH_IDS,
        )

    def context_own(u):
        return pltpu.make_async_copy(
            unit_out.at[u, tile(ctx, tok)], context_place(ctx, u), unit_sem.at[1, u]
        )

    def attend(u):
        qkv_own(u).wait()
        for step in range(1, ctxs):
            qkv_arrival(u, step).wait_recv()
        part = math.gcd(seq_all, 256)

        @pl.loop(0, seq_all // part)
        def _(i):
            rs = tile(i, part)
            scores = dot_nt(unit_qkv[u, 0, rs, :], unit_qkv[u, 1]) * (HEAD_DIM ** (-0.5))
            largest = jnp.max(scores, axis=-1, keepdims=True)
            raised = jnp.exp(scores - largest)
            total = jnp.sum(raised, axis=-1, keepdims=True)
            mixed = dot_nn(raised.astype(BF), unit_qkv[u, 2])
            unit_out[u, rs, :] = (mixed / total).astype(BF)

        for step in range(1, ctxs):
            context_copy(u, step).start()
        context_own(u).start()

    def context_ready(u):
        context_own(u).wait()
        for step in range(1, ctxs):
            context_arrival(u, step).wait_recv()

    def project_chunk(c):
        bring(hidden, c).wait()
        following = (c + 1) % chunks
        s = c // per_seq
        rs = tile(c % per_seq, rows)
        low = dot_nt(rows_in[...], md[s]).astype(BF)
        put_rank(3, c, low)
        rank_buf[...] = low
        heads_at_once = math.gcd(local_heads, 2)
        step = heads_at_once * HEAD_DIM

        @pl.loop(0, mix_width // step)
        def _(i):
            cs = tile(i, step)
            values = dot_nn(rows_in[...], stash[0:width, cs]) + dot_nn(rank_buf[...], mu[s, :, cs])
            values = values.astype(BF)
            first = i * heads_at_once
            for k in range(heads_at_once):
                local_qkv[s, (first + k) % local_heads, (first + k) // local_heads, rs, :] = values[
                    :, k * HEAD_DIM : (k + 1) * HEAD_DIM
                ]

        bring(hidden, following).start()

    def project(s):
        @pl.loop(0, per_seq)
        def _(i):
            project_chunk(s * per_seq + i)

    def send_unit(u):
        qkv_own(u).start()
        for step in range(1, ctxs):
            qkv_copy(u, step).start()

    def job_of(number, rounds):
        safe = jnp.maximum(number, 0)
        chunk = safe % period
        valid = (number >= 0) & (chunk < chunks) & (safe < rounds * period)
        return valid, jnp.minimum(chunk, chunks - 1)

    comm = chain(
        ranks,
        half,
        block,
        me,
        acc,
        red_up,
        red_down,
        red_send,
        red_recv,
        cast_send,
        cast_recv,
        lambda number: job_of(number, 3),
    )

    def rows_of(c):
        return tile(c, rows)

    def spot(t, c, i=None):
        start = t * total + c * rows
        if i is None:
            return pl.ds(pl.multiple_of(start, rows), rows)
        return pl.ds(pl.multiple_of(start + i * block, block), block)

    def mixing_keep():
        return pltpu.make_async_copy(
            stash.at[pl.ds(0, width), pl.ds(0, mix_width)], mixing, mix_sem
        )

    def bring(source, c):
        return pltpu.make_async_copy(source.at[rows_of(c)], rows_in, in_sem)

    def keep(index, source, target, c):
        return pltpu.make_async_copy(source, target.at[rows_of(c)], out_sem.at[index])

    def put_rank(t, c, low):
        part_ranks[t, :, tile(c, rows)] = dot_nt(unit_rank[...], low).astype(BF)

    def rank_copy(t, step):
        return pltpu.make_async_remote_copy(
            src_ref=part_ranks.at[t],
            dst_ref=rank_in.at[t, step],
            send_sem=rank_send.at[t, step],
            recv_sem=rank_recv.at[t, step],
            device_id={"tensor": (me + step) % ranks},
            device_id_type=MESH_IDS,
        )

    def mean(values):
        return jnp.sum(values, axis=-1, keepdims=True) * (1.0 / width)

    def attend_part(c, s):
        mine = context[rows_of(c), :]
        low = dot_nt(mine, od[s]).astype(BF)
        put_rank(0, c, low)

        @pl.loop(0, width // tile_d)
        def _(i):
            cs = tile(i, tile_d)
            acc[c, :, cs] = (dot_nn(mine, w_out[:, cs]) + dot_nn(low, ou[s, :, cs])).astype(BF)

    def forward_first(c, s):
        bring(hidden, c).wait()

        @pl.loop(0, rows // block)
        def _(i):
            rs = tile(i, block)
            total = rows_in[rs, :].astype(F32) + acc[c, rs, :].astype(F32)
            centred = total - mean(total)
            spread = lax.rsqrt(mean(centred * centred) + 1e-06)
            n = centred * spread
            stash[spot(0, c, i), :] = n.astype(BF)
            spreads[c, rs, :] = jnp.broadcast_to(spread, (block, 128))
            stage_d[rs, :] = (n * gains[0:1, :] + gains[1:2, :]).astype(BF)

        low = dot_nt(stage_d[...], ed[s]).astype(BF)
        put_rank(4, c, low)
        rank_buf[...] = low

        @pl.loop(0, hidden_units // tile_f)
        def _(i):
            cs = tile(i, tile_f)
            b = dot_nn(stage_d[...], w_exp[:, cs]) + dot_nn(rank_buf[...], eu[s, :, cs])
            square = b * b
            t = jnp.tanh(GELU_C * b * (1.0 + GELU_A * square))
            upper = 0.5 * (1.0 + t)
            stage_f[:, cs] = (b * upper).astype(BF)
            stash[spot(1, c), cs] = (
                upper
                + (0.5 * GELU_C) * b * (1.0 - t * t) * (1.0 + (3.0 * GELU_A) * square)
            ).astype(BF)

    def forward_second(c, s):
        low = dot_nt(stage_f[...], cd[s]).astype(BF)
        put_rank(1, c, low)
        rank_buf[...] = low

        @pl.loop(0, width // tile_d)
        def _(i):
            cs = tile(i, tile_d)
            acc[c, :, cs] = (
                dot_nn(stage_f[...], w_con[:, cs]) + dot_nn(rank_buf[...], cu[s, :, cs])
            ).astype(BF)

        keep(0, stage_d, first_low, c).start()
        keep(1, stage_f, active, c).start()

    def back_first(c, s):
        bring(cotangent, c).wait()

        @pl.loop(0, rows // block)
        def _(i):
            rs = tile(i, block)
            first = stash[spot(0, c, i), :].astype(F32) * gains[0:1, :] + gains[1:2, :]
            total = first + acc[c, rs, :].astype(F32)
            centred = total - mean(total)
            spread = lax.rsqrt(mean(centred * centred) + 1e-06)
            n = centred * spread
            stage_d[rs, :] = (n * gains[2:3, :] + gains[3:4, :]).astype(BF)
            g = rows_in[rs, :].astype(F32) * gains[2:3, :]
            stash[spot(2, c, i), :] = (spread * (g - mean(g) - n * mean(g * n))).astype(BF)

        low = dot_nt(stash[spot(2, c), :], cu[s]).astype(BF)
        put_rank(5, c, low)
        rank_buf[...] = low

        @pl.loop(0, hidden_units // tile_f)
        def _(i):
            cs = tile(i, tile_f)
            da = dot_nt(stash[spot(2, c), :], w_con[cs, :]) + dot_nn(rank_buf[...], cd[s, :, cs])
            stage_f[:, cs] = (da * stash[spot(1, c), cs].astype(F32)).astype(BF)

    def back_second(c, s):
        low = dot_nt(stage_f[...], eu[s]).astype(BF)
        put_rank(2, c, low)
        rank_buf[...] = low

        @pl.loop(0, width // tile_d)
        def _(i):
            cs = tile(i, tile_d)
            acc[c, :, cs] = (
                dot_nt(stage_f[...], w_exp[cs, :]) + dot_nn(rank_buf[...], ed[s, :, cs])
            ).astype(BF)

        keep(0, stage_d, hidden_out, c).start()
        keep(1, stage_f, before_grad, c).start()
        keep(2, stash.at[spot(2, c)], second_low, c).start()

    def last_first(c, s):
        @pl.loop(0, rows // block)
        def _(i):
            rs = tile(i, block)
            n = stash[spot(0, c, i), :].astype(F32)
            g = (stash[spot(2, c, i), :].astype(F32) + acc[c, rs, :].astype(F32)) * gains[0:1, :]
            spread = spreads[c, rs, 0:1]
            stage_d[rs, :] = (spread * (g - mean(g) - n * mean(g * n))).astype(BF)

    def last_second(c, s):
        low = dot_nt(stage_d[...], ou[s]).astype(BF)
        put_rank(6, c, low)
        rank_buf[...] = low

        @pl.loop(0, heads // tile_h)
        def _(i):
            cs = tile(i, tile_h)
            context_grad[rows_of(c), cs] = (
                dot_nt(stage_d[...], w_out[cs, :]) + dot_nn(rank_buf[...], od[s, :, cs])
            ).astype(BF)

        keep(0, stage_d, attn_low, c).start()

    seqs = chunks // per_seq
    flowing = units == seqs
    bring(hidden, 0).start()
    mixing_gather()
    weight_finish(0)
    along_start(1)
    across_start(1)
    mixing_keep().start()
    if flowing:
        for u in range(min(2, units)):
            project(u)
            send_unit(u)
    else:
        pl.loop(0, seqs)(project)
        for u in range(units):
            send_unit(u)
    weight_relay(1)

    @pl.loop(0, lead + 3 * period + chunks)
    def _(now):
        tick = now - lead
        stage = jnp.maximum(tick, 0) // period
        valid, c = job_of(tick, 4)
        s = c // per_seq
        last_valid, last_c = job_of(tick - 1, 4)
        last_stage = jnp.maximum(tick - 1, 0) // period

        comm(tick, 0)

        @pl.when(last_valid & (last_stage >= 1))
        def _():
            keep(0, stage_d, first_low, last_c).wait()

        @pl.when(last_valid & (last_stage >= 1) & (last_stage <= 2))
        def _():
            keep(1, stage_f, active, last_c).wait()

        @pl.when(last_valid & (last_stage == 2))
        def _():
            keep(2, stash.at[spot(2, last_c)], second_low, last_c).wait()

        pl.when(now == 1)(lambda: weight_forward(1))
        if flowing:

            @pl.when((now % per_seq == 0) & (now < (units - 2) * per_seq))
            def _():
                project(now // per_seq + 2)
                send_unit(now // per_seq + 2)

        @pl.when((now % per_seq == 0) & (now > 0) & (now <= PIECES * per_seq))
        def _():
            p = now // per_seq - 1
            weight_relay(2, p)
            weight_relay(3, p)

        @pl.when((now % per_seq == 0) & (now < PIECES * per_seq))
        def _():
            for w in (2, 3):
                along_start(w, now // per_seq)
                across_start(w, now // per_seq)

        @pl.when((now % per_seq == 1 % per_seq) & (now > per_seq) & (now <= PIECES * per_seq + 1))
        def _():
            p = (now - 1) // per_seq - 1
            weight_forward(2, p)
            weight_forward(3, p)

        @pl.when(now == lead + period)
        def _():
            for p in range(PIECES):
                weight_finish(2, p)
                weight_finish(3, p)

        pl.when((now % per_seq == 0) & (now < units * per_seq))(lambda: attend(now // per_seq))
        pl.when(now == lead)(lambda: weight_finish(1))

        @pl.when(now == lead + period - 2)
        def _():
            mixing_keep().wait()
            weight_sent(0)
            side_sent()

        for t in range(3):

            @pl.when(tick == (t + 1) * period)
            def _(t=t):
                for step in range(1, ranks):
                    rank_copy(t, step).start()

        pl.when((tick >= 0) & (tick % per_seq == 0) & (tick < units * per_seq))(
            lambda: context_ready(s)
        )

        pl.when(valid & (stage == 1))(lambda: forward_first(c, s))
        pl.when(valid & (stage == 2))(lambda: back_first(c, s))
        pl.when(valid & (stage == 3))(lambda: last_first(c, s))

        comm(tick, 1)

        pl.when(valid & (stage == 0))(lambda: attend_part(c, s))
        pl.when(valid & (stage == 1))(lambda: forward_second(c, s))
        pl.when(valid & (stage == 2))(lambda: back_second(c, s))
        pl.when(valid & (stage == 3))(lambda: last_second(c, s))

        next_valid, next_c = job_of(tick + 1, 4)
        next_stage = jnp.maximum(tick + 1, 0) // period
        pl.when(next_valid & (next_stage == 1) & (next_c > 0))(
            lambda: bring(hidden, next_c).start()
        )
        pl.when(next_valid & (next_stage == 2))(lambda: bring(cotangent, next_c).start())

    keep(0, stage_d, attn_low, chunks - 1).wait()
    for t in range(3):
        value = part_ranks[t].astype(F32)
        for step in range(1, ranks):
            rank_copy(t, step).wait_recv()
            value = value + rank_in[t, step].astype(F32)
        full_ranks[t] = value.astype(BF)
    for t in range(3):
        for step in range(1, ranks):
            rank_copy(t, step).wait_send()
    weight_sent(1)
    for p in range(PIECES):
        weight_sent(2, p)
        weight_sent(3, p)
    for u in range(units):
        for step in range(1, ctxs):
            qkv_copy(u, step).wait_send()
            context_copy(u, step).wait_send()


def enter(others):
    barrier = pltpu.get_barrier_semaphore()
    for other in others:
        pl.semaphore_signal(barrier, inc=1, device_id=other, device_id_type=MESH_IDS)
    pl.semaphore_wait(barrier, len(others))


def middle(hidden, cotangent, shards, picked, gains, tok):
    total, width = hidden.shape
    mix_width = shards[0].shape[1]
    heads, hidden_units = shards[1].shape[0], shards[2].shape[1]
    ranks, dps, ctxs = (lax.axis_size(name) for name in ("tensor", "dp", "ctx"))
    seqs, rank = picked[0].shape[:2]
    local_heads = heads // HEAD_DIM
    units = seqs * local_heads // ctxs
    rows = math.gcd(tok, CHUNK_ROWS)
    chunks = total // rows
    period = max(chunks, 2 * ranks)
    sizes = (ranks, dps, ctxs, chunks, rows, tok // rows, period)
    chips = dps * ctxs // 2
    vm = pl.BlockSpec(memory_space=pltpu.VMEM)
    hb = pl.BlockSpec(memory_space=pl.ANY)
    half = rows // 2
    dma = pltpu.SemaphoreType.DMA

    def shape(*dims):
        return jax.ShapeDtypeStruct(dims, BF)

    return pl.pallas_call(
        functools.partial(middle_kernel, sizes),
        out_shape=(
            shape(total, width),
            shape(total, width),
            shape(total, hidden_units),
            shape(total, width),
            shape(total, hidden_units),
            shape(total, width),
            shape(width, mix_width),
            shape(total, heads),
            shape(7, rank, total),
            shape(3, rank, total),
            shape(total, heads),
            shape(units, 3, tok * ctxs, HEAD_DIM),
            shape(units, tok * ctxs, HEAD_DIM),
        ),
        in_specs=[hb] * 6 + [vm] * 10,
        out_specs=(hb,) * 7 + (vm,) * 6,
        scratch_shapes=[
            pltpu.VMEM((seqs, local_heads, 3, tok, HEAD_DIM), BF),
            pltpu.VMEM((heads, width), BF),
            pltpu.VMEM((width, hidden_units), BF),
            pltpu.VMEM((hidden_units, width), BF),
            pltpu.VMEM((chunks, rows, width), BF),
            pltpu.VMEM((chunks, half, width), BF),
            pltpu.VMEM((chunks, half, width), BF),
            pltpu.VMEM((3 * total, width), BF),
            pltpu.VMEM((chunks, rows, 128), F32),
            pltpu.VMEM((3, ranks, rank, total), BF),
            pltpu.VMEM((rows, width), BF),
            pltpu.VMEM((rows, hidden_units), BF),
            pltpu.VMEM((rows, width), BF),
            pltpu.VMEM((rows, rank), BF),
            dma(()),
            dma((3,)),
            dma((2, chunks)),
            dma((2, chunks)),
            dma((2, chunks)),
            dma((2, chunks)),
            dma((4, chips, PIECES)),
            dma((4, chips, PIECES)),
            dma((4, chips, PIECES)),
            dma((4, chips, PIECES)),
            dma((chips,)),
            dma((chips,)),
            dma((4, PIECES)),
            dma((3, ranks)),
            dma((3, ranks)),
            dma(()),
            dma((units, ctxs)),
            dma((units, ctxs)),
            dma((units, ctxs)),
            dma((units, ctxs)),
            dma((2, units)),
        ],
        compiler_params=pltpu.CompilerParams(
            collective_id=0, has_side_effects=True, vmem_limit_bytes=VMEM_BYTES
        ),
        cost_estimate=pl.CostEstimate(
            flops=8 * total * width * hidden_units + 4 * total * width * heads,
            bytes_accessed=16 * total * width,
            transcendentals=total * hidden_units,
        ),
    )(hidden, cotangent, *shards, *picked, gains, jnp.eye(rank, dtype=BF))


def mixing_kernel(
    sizes,
    context_grad,
    unit_qkv,
    unit_out,
    mixing,
    mu,
    md,
    attn_low,
    unit_rank,
    hidden,
    mix_rank,
    row_hot,
    input_grad,
    grads,
    table_sum,
    rank_part,
    rank_in,
    wide,
    table_part,
    table_in,
    unit_go,
    unit_grad,
    sum_k,
    sum_v,
    acc,
    red_up,
    red_down,
    stage_d,
    rows_in,
    rank_buf,
    in_sem,
    out_sem,
    red_send,
    red_recv,
    cast_send,
    cast_recv,
    go_send,
    go_recv,
    grad_send,
    grad_recv,
    unit_sem,
    rank_send,
    rank_recv,
    part_send,
    part_recv,
    whole_send,
    whole_recv,
):
    ranks, dps, ctxs, chunks, rows, per_seq, group = sizes
    half = rows // 2
    width = mixing.shape[0]
    heads = grads.shape[2]
    local_heads = heads // HEAD_DIM
    units, seq_all = unit_go.shape[0], unit_go.shape[1]
    tok = seq_all // ctxs
    block = min(16, half)
    tile_d = math.gcd(width, 256)
    scale = HEAD_DIM ** (-0.5)
    me = lax.axis_index("tensor")
    ctx = lax.axis_index("ctx")
    dp = lax.axis_index("dp")
    parts = dps * ctxs
    index = dp * ctxs + ctx
    rank = mu.shape[1]
    tables, _, part_width = table_part.shape
    segments = parts // NADAPT
    tile_g = math.gcd(part_width, 256)

    def part_place(step):
        other = (index + step) % parts
        return {"dp": other // ctxs, "ctx": other % ctxs}

    enter(
        [{"tensor": (me + d) % ranks} for d in range(1, ranks)]
        + [part_place(d) for d in range(1, parts)]
    )

    def unit_place(device, u):
        return (device // local_heads) * units + u, device % local_heads

    def go_copy(u, step):
        peer = (ctx + step) % ctxs
        s, h = unit_place(peer, u)
        return pltpu.make_async_remote_copy(
            src_ref=context_grad.at[tile(s, tok), tile(h, HEAD_DIM)],
            dst_ref=unit_go.at[u, tile(ctx, tok)],
            send_sem=go_send.at[u, step],
            recv_sem=go_recv.at[u, step],
            device_id={"ctx": peer},
            device_id_type=MESH_IDS,
        )

    def go_arrival(u, step):
        return pltpu.make_async_remote_copy(
            src_ref=context_grad.at[tile(0, tok), tile(0, HEAD_DIM)],
            dst_ref=unit_go.at[u, tile((ctx + ctxs - step) % ctxs, tok)],
            send_sem=go_send.at[u, step],
            recv_sem=go_recv.at[u, step],
            device_id={"ctx": (ctx + step) % ctxs},
            device_id_type=MESH_IDS,
        )

    def go_own(u):
        s, h = unit_place(ctx, u)
        return pltpu.make_async_copy(
            context_grad.at[tile(s, tok), tile(h, HEAD_DIM)],
            unit_go.at[u, tile(ctx, tok)],
            unit_sem.at[0, u],
        )

    def grads_place(device, u):
        s, h = unit_place(device, u)
        return grads.at[:, tile(s, tok), tile(h, HEAD_DIM)]

    def grad_copy(u, step):
        peer = (ctx + step) % ctxs
        return pltpu.make_async_remote_copy(
            src_ref=unit_grad.at[u, :, tile(peer, tok)],
            dst_ref=grads_place(ctx, u),
            send_sem=grad_send.at[u, step],
            recv_sem=grad_recv.at[u, step],
            device_id={"ctx": peer},
            device_id_type=MESH_IDS,
        )

    def grad_arrival(u, step):
        return pltpu.make_async_remote_copy(
            src_ref=unit_grad.at[u, :, tile(ctx, tok)],
            dst_ref=grads_place((ctx + ctxs - step) % ctxs, u),
            send_sem=grad_send.at[u, step],
            recv_sem=grad_recv.at[u, step],
            device_id={"ctx": (ctx + step) % ctxs},
            device_id_type=MESH_IDS,
        )

    def grad_own(u):
        return pltpu.make_async_copy(
            unit_grad.at[u, :, tile(ctx, tok)], grads_place(ctx, u), unit_sem.at[1, u]
        )

    def attend_back(u):
        go_own(u).wait()
        for step in range(1, ctxs):
            go_arrival(u, step).wait_recv()
        part = math.gcd(seq_all, 256)
        sum_k[...] = jnp.zeros_like(sum_k)
        sum_v[...] = jnp.zeros_like(sum_v)

        @pl.loop(0, seq_all // part)
        def _(i):
            rs = tile(i, part)
            queries = unit_qkv[u, 0, rs, :]
            go = unit_go[u, rs, :]
            scores = dot_nt(queries, unit_qkv[u, 1]) * scale
            raised = jnp.exp(scores - jnp.max(scores, axis=-1, keepdims=True))
            probs = raised * (1.0 / jnp.sum(raised, axis=-1, keepdims=True))
            delta = jnp.sum(
                go.astype(F32) * unit_out[u, rs, :].astype(F32), axis=-1, keepdims=True
            )
            dscores = (probs * (dot_nt(go, unit_qkv[u, 2]) - delta)).astype(BF)
            unit_grad[u, 0, rs, :] = (scale * dot_nn(dscores, unit_qkv[u, 1])).astype(BF)
            sum_k[...] += dot_tn(dscores, queries)
            sum_v[...] += dot_tn(probs.astype(BF), go)

        unit_grad[u, 1] = (scale * sum_k[...]).astype(BF)
        unit_grad[u, 2] = sum_v[...].astype(BF)
        for step in range(1, ctxs):
            grad_copy(u, step).start()
        grad_own(u).start()

    def grads_ready(u):
        grad_own(u).wait()
        for step in range(1, ctxs):
            grad_arrival(u, step).wait_recv()

    for u in range(units):
        go_own(u).start()
        for step in range(1, ctxs):
            go_copy(u, step).start()

    def job_of(number):
        return (number >= 0) & (number < chunks), jnp.clip(number, 0, chunks - 1)

    comm = chain(
        ranks, half, block, me, acc, red_up, red_down, red_send, red_recv, cast_send, cast_recv, job_of
    )

    def rows_of(c):
        return tile(c, rows)

    def bring(c):
        return pltpu.make_async_copy(attn_low.at[rows_of(c)], rows_in, in_sem)

    def keep(c):
        return pltpu.make_async_copy(stage_d, input_grad.at[rows_of(c)], out_sem)

    def back_part(c, s):
        rs = pl.ds(pl.multiple_of(c * rows, group * rows), group * rows)
        low = jnp.zeros((group * rows, mu.shape[1]), F32)
        for j in range(3):
            low = low + dot_nt(grads[j, rs, :], mu[s, :, pl.ds(j * heads, heads)])
        low = low.astype(BF)
        rank_part[:, pl.ds(pl.multiple_of(c * rows, group * rows), group * rows)] = dot_nt(
            unit_rank[...], low
        ).astype(BF)
        rank_buf[...] = low

        @pl.loop(0, width // tile_d)
        def _(i):
            cs = tile(i, tile_d)
            total = dot_nn(rank_buf[...], md[s, :, cs])
            for j in range(3):
                total = total + dot_nt(grads[j, rs, :], mixing[cs, pl.ds(j * heads, heads)])
            total = total.astype(BF)
            for k in range(group):
                acc[c + k, :, cs] = total[k * rows : (k + 1) * rows, :]

    def final_part(c):
        bring(c).wait()

        @pl.loop(0, rows // block)
        def _(i):
            rs = tile(i, block)
            stage_d[rs, :] = (rows_in[rs, :].astype(F32) + acc[c, rs, :].astype(F32)).astype(BF)

        keep(c).start()

    def rank_copy(step):
        return pltpu.make_async_remote_copy(
            src_ref=rank_part,
            dst_ref=rank_in.at[step],
            send_sem=rank_send.at[step],
            recv_sem=rank_recv.at[step],
            device_id={"tensor": (me + step) % ranks},
            device_id_type=MESH_IDS,
        )

    def part_copy(step):
        return pltpu.make_async_remote_copy(
            src_ref=table_part.at[(index + step) % parts],
            dst_ref=table_in.at[step],
            send_sem=part_send.at[step],
            recv_sem=part_recv.at[step],
            device_id=part_place(step),
            device_id_type=MESH_IDS,
        )

    def whole_copy(step):
        return pltpu.make_async_remote_copy(
            src_ref=table_sum.at[index],
            dst_ref=table_sum.at[index],
            send_sem=whole_send.at[step],
            recv_sem=whole_recv.at[step],
            device_id=part_place(step),
            device_id_type=MESH_IDS,
        )

    def whole_arrival(step):
        return pltpu.make_async_remote_copy(
            src_ref=table_sum.at[index],
            dst_ref=table_sum.at[(index + parts - step) % parts],
            send_sem=whole_send.at[step],
            recv_sem=whole_recv.at[step],
            device_id=part_place(step),
            device_id_type=MESH_IDS,
        )

    def put_table(column, values):
        segment = column // part_width
        cs = pl.ds(pl.multiple_of(column % part_width, tile_g), tile_g)
        for n in range(NADAPT):
            table_part[n * segments + segment, :, cs] = values[n * rank : (n + 1) * rank, :].astype(
                BF
            )

    def make_tables():
        value = rank_part[...].astype(F32)
        for step in range(1, ranks):
            rank_copy(step).wait_recv()
            value = value + rank_in[step].astype(F32)
        for n in range(NADAPT):
            hot = row_hot[n : n + 1, :]
            wide[0, pl.ds(n * rank, rank), :] = (value * hot).astype(BF)
            wide[1, pl.ds(n * rank, rank), :] = (mix_rank[...].astype(F32) * hot).astype(BF)

        @pl.loop(0, width // tile_g)
        def _(i):
            put_table(i * tile_g, dot_nn(wide[0], hidden[:, tile(i, tile_g)]))

        for j in range(3):

            @pl.loop(0, heads // tile_g)
            def _(i):
                put_table(
                    width + j * heads + i * tile_g, dot_nn(wide[1], grads[j, :, tile(i, tile_g)])
                )

        for step in range(1, parts):
            part_copy(step).start()

    def sum_tables():
        value = table_part[index].astype(F32)
        for step in range(1, parts):
            part_copy(step).wait_recv()
            value = value + table_in[step].astype(F32)
        table_sum[index] = value.astype(BF)
        for step in range(1, parts):
            whole_copy(step).start()

    delay = 2 * ranks

    @pl.loop(0, per_seq + chunks + delay)
    def _(now):
        tick = now - per_seq

        @pl.when(tick == chunks)
        def _():
            for step in range(1, ranks):
                rank_copy(step).start()

        valid, c = job_of(tick)
        final, c_final = job_of(tick - delay)
        before, c_before = job_of(tick - delay - 1)
        coming, c_coming = job_of(tick - delay + 1)
        s = c // per_seq

        comm(tick, 0)

        pl.when((now % per_seq == 0) & (now < units * per_seq))(lambda: attend_back(now // per_seq))
        pl.when((tick >= 0) & (tick % per_seq == 0) & (tick < units * per_seq))(
            lambda: grads_ready(s)
        )
        comm(tick, 1)

        pl.when(valid & (tick % group == 0))(lambda: back_part(c, s))

        pl.when(tick == chunks + 1)(make_tables)
        pl.when(tick == chunks + 4)(sum_tables)

        pl.when(before)(lambda: keep(c_before).wait())
        pl.when(final)(lambda: final_part(c_final))
        pl.when(coming)(lambda: bring(c_coming).start())

    keep(chunks - 1).wait()
    for step in range(1, ranks):
        rank_copy(step).wait_send()
    for step in range(1, parts):
        whole_arrival(step).wait_recv()
    for step in range(1, parts):
        part_copy(step).wait_send()
        whole_copy(step).wait_send()
    for u in range(units):
        for step in range(1, ctxs):
            go_copy(u, step).wait_send()
            grad_copy(u, step).wait_send()


def mixing_back(
    context_grad, unit_qkv, unit_out, mixing, picked, attn_low, hidden, mix_rank, row_hot
):
    mu, md = picked
    total, width = attn_low.shape
    heads = context_grad.shape[1]
    ranks, dps, ctxs = (lax.axis_size(name) for name in ("tensor", "dp", "ctx"))
    parts = dps * ctxs
    part_width = (width + 3 * heads) * NADAPT // parts
    units, _, seq_all, _ = unit_qkv.shape
    tok = seq_all // ctxs
    rank = mu.shape[1]
    rows = math.gcd(tok, LAST_ROWS)
    chunks = total // rows
    per_seq = tok // rows
    group = math.gcd(per_seq, 2)
    half = rows // 2
    sizes = (ranks, dps, ctxs, chunks, rows, per_seq, group)
    vm = pl.BlockSpec(memory_space=pltpu.VMEM)
    hb = pl.BlockSpec(memory_space=pl.ANY)
    dma = pltpu.SemaphoreType.DMA
    return pl.pallas_call(
        functools.partial(mixing_kernel, sizes),
        out_shape=(
            jax.ShapeDtypeStruct((total, width), BF),
            jax.ShapeDtypeStruct((3, total, heads), BF),
            jax.ShapeDtypeStruct((parts, rank, part_width), BF),
        ),
        in_specs=[vm] * 6 + [hb] + [vm] * 4,
        out_specs=(hb, vm, vm),
        scratch_shapes=[
            pltpu.VMEM((rank, total), BF),
            pltpu.VMEM((ranks, rank, total), BF),
            pltpu.VMEM((2, NADAPT * rank, total), BF),
            pltpu.VMEM((parts, rank, part_width), BF),
            pltpu.VMEM((parts, rank, part_width), BF),
            pltpu.VMEM((units, seq_all, HEAD_DIM), BF),
            pltpu.VMEM((units, 3, seq_all, HEAD_DIM), BF),
            pltpu.VMEM((seq_all, HEAD_DIM), F32),
            pltpu.VMEM((seq_all, HEAD_DIM), F32),
            pltpu.VMEM((chunks, rows, width), BF),
            pltpu.VMEM((chunks, half, width), BF),
            pltpu.VMEM((chunks, half, width), BF),
            pltpu.VMEM((rows, width), BF),
            pltpu.VMEM((rows, width), BF),
            pltpu.VMEM((group * rows, rank), BF),
            dma(()),
            dma(()),
            dma((2, chunks)),
            dma((2, chunks)),
            dma((2, chunks)),
            dma((2, chunks)),
            dma((units, ctxs)),
            dma((units, ctxs)),
            dma((units, ctxs)),
            dma((units, ctxs)),
            dma((2, units)),
            dma((ranks,)),
            dma((ranks,)),
            dma((parts,)),
            dma((parts,)),
            dma((parts,)),
            dma((parts,)),
        ],
        compiler_params=pltpu.CompilerParams(
            collective_id=1, has_side_effects=True, vmem_limit_bytes=VMEM_LAST
        ),
        cost_estimate=pl.CostEstimate(
            flops=6 * total * width * heads + 10 * units * seq_all * seq_all * HEAD_DIM,
            bytes_accessed=8 * total * width,
            transcendentals=units * seq_all * seq_all,
        ),
    )(
        context_grad,
        unit_qkv,
        unit_out,
        mixing,
        mu,
        md,
        attn_low,
        jnp.eye(rank, dtype=BF),
        hidden,
        mix_rank,
        row_hot,
    )


def pick_rows(onehot_low, table):
    return jnp.einsum(
        "sn,n...->s...", onehot_low, table, preferred_element_type=jnp.float32
    ).astype(jnp.bfloat16)


def per_device(
    hidden_in,
    output_cotangent,
    adapter_index,
    mixing_weight,
    output_weight,
    expand_weight,
    contract_weight,
    first_gain,
    first_shift,
    second_gain,
    second_shift,
    mixing_down,
    mixing_up,
    output_down,
    output_up,
    expand_down,
    expand_up,
    contract_down,
    contract_up,
):
    seq_count, tok_count, model_width = hidden_in.shape
    local_heads = mixing_weight.shape[2] // HEAD_DIM
    local_width = mixing_weight.shape[2]
    rows_all = seq_count * tok_count
    adapter_ids = jnp.arange(NADAPT, dtype=jnp.int32)
    onehot_low = (adapter_index == adapter_ids[None, :]).astype(jnp.bfloat16)
    mixing_down_sel = pick_rows(onehot_low, mixing_down)
    mixing_up_sel = pick_rows(onehot_low, mixing_up)
    output_down_sel = pick_rows(onehot_low, output_down)
    output_up_sel = pick_rows(onehot_low, output_up)
    expand_down_sel = pick_rows(onehot_low, expand_down)
    expand_up_sel = pick_rows(onehot_low, expand_up)
    contract_down_sel = pick_rows(onehot_low, contract_down)
    contract_up_sel = pick_rows(onehot_low, contract_up)
    rank = mixing_down.shape[1]
    mixing_flat = mixing_weight.reshape(mixing_weight.shape[0], 3 * local_width)
    hidden_rows = hidden_in.reshape(rows_all, model_width)
    mixing_up_flat = mixing_up_sel.reshape(seq_count, rank, 3 * local_width)
    gains = jnp.stack([first_gain, first_shift, second_gain, second_shift])
    (
        out_rows,
        first_low,
        active_low,
        second_low,
        before_low,
        attn_low,
        mixing_full,
        context_grad,
        part_ranks,
        full_ranks,
        context,
        unit_qkv,
        unit_out,
    ) = middle(
        hidden_rows,
        output_cotangent.reshape(rows_all, model_width),
        (mixing_flat, output_weight, expand_weight, contract_weight),
        (
            mixing_down_sel,
            mixing_up_flat,
            output_down_sel,
            output_up_sel,
            expand_down_sel,
            expand_up_sel,
            contract_down_sel,
            contract_up_sel,
        ),
        gains,
        tok_count,
    )
    row_hot = jnp.repeat(onehot_low.T, tok_count, axis=1)

    def table_grad(ranks, values):
        wide = (row_hot[:, None, :] * ranks[None, :, :]).reshape(-1, rows_all)
        part = jnp.einsum("kn,nd->kd", wide, values, preferred_element_type=jnp.float32)
        return part.astype(jnp.bfloat16).reshape(NADAPT, rank, values.shape[1])

    early = (
        table_grad(part_ranks[6], context),
        table_grad(full_ranks[0], attn_low),
        table_grad(full_ranks[2], first_low),
        table_grad(part_ranks[4], before_low),
        table_grad(part_ranks[5], active_low),
        table_grad(full_ranks[1], second_low),
    )
    early, context_grad = lax.optimization_barrier((early, context_grad))
    input_rows, _, late = mixing_back(
        context_grad,
        unit_qkv,
        unit_out,
        mixing_full,
        (mixing_up_flat, mixing_down_sel),
        attn_low,
        hidden_rows,
        part_ranks[3],
        row_hot.astype(jnp.float32),
    )
    early = lax.psum(early, ("dp", "ctx"))
    late = late.reshape(NADAPT, -1, rank, late.shape[2]).swapaxes(1, 2).reshape(NADAPT, rank, -1)
    late = (
        late[:, :, :model_width],
        late[:, :, model_width:].reshape(NADAPT, rank, 3, local_width),
    )
    summed = tuple(part.astype(jnp.float32) for part in late + early)
    return (
        out_rows.reshape(hidden_in.shape),
        input_rows.reshape(hidden_in.shape),
    ) + summed


def solution(mesh):
    return jax.shard_map(
        per_device,
        mesh=mesh,
        in_specs=(
            P("dp", "ctx", None),
            P("dp", "ctx", None),
            P("dp", None),
            P(("dp", "ctx"), None, "tensor"),
            P("tensor", ("dp", "ctx")),
            P(("dp", "ctx"), "tensor"),
            P("tensor", ("dp", "ctx")),
            P(),
            P(),
            P(),
            P(),
            P(),
            P(None, None, None, "tensor"),
            P(None, None, "tensor"),
            P(),
            P(),
            P(None, None, "tensor"),
            P(None, None, "tensor"),
            P(),
        ),
        out_specs=(
            P("dp", "ctx", None),
            P("dp", "ctx", None),
            P(),
            P(None, None, None, "tensor"),
            P(None, None, "tensor"),
            P(),
            P(),
            P(None, None, "tensor"),
            P(None, None, "tensor"),
            P(),
        ),
        check_vma=False,
    )
```

```python
import functools
import math

import jax
import jax.numpy as jnp
from jax import lax
from jax.experimental import pallas as pl
from jax.experimental.pallas import tpu as pltpu
from jax.sharding import PartitionSpec as P

HEAD_DIM = 128
NADAPT = 8
CHUNK_ROWS = 128
LAST_ROWS = 128
VMEM_BYTES = 62 * 2**20
VMEM_LAST = 56 * 2**20
PIECES = 4


BF = jnp.bfloat16
F32 = jnp.float32
MESH_IDS = pl.DeviceIdType.MESH
RANK_ROWS = 16
GELU_C = 0.7978845608028654
GELU_A = 0.044715


def dot_nn(a, b):
    return lax.dot_general(a, b, (((1,), (0,)), ((), ())), preferred_element_type=F32)


def dot_nt(a, b):
    return lax.dot_general(a, b, (((1,), (1,)), ((), ())), preferred_element_type=F32)


def dot_tn(a, b):
    return lax.dot_general(a, b, (((0,), (0,)), ((), ())), preferred_element_type=F32)


def tile(index, size):
    return pl.ds(pl.multiple_of(index * size, size), size)


def chain(
    ranks, half, block, me, acc, red_up, red_down, red_send, red_recv, cast_send, cast_recv, job_of
):
    def comm(tick, way):
        upward = way == 0
        place = me if upward else ranks - 1 - me
        ahead = me + 1 if upward else me - 1
        behind = me - 1 if upward else me + 1
        red = red_up if upward else red_down
        part = pl.ds(way * half, half)

        def red_copy(c):
            return pltpu.make_async_remote_copy(
                src_ref=red.at[c],
                dst_ref=red.at[c],
                send_sem=red_send.at[way, c],
                recv_sem=red_recv.at[way, c],
                device_id={"tensor": ahead},
                device_id_type=MESH_IDS,
            )

        def cast_copy(c):
            return pltpu.make_async_remote_copy(
                src_ref=acc.at[c, part],
                dst_ref=acc.at[c, part],
                send_sem=cast_send.at[way, c],
                recv_sem=cast_recv.at[way, c],
                device_id={"tensor": behind},
                device_id_type=MESH_IDS,
            )

        old_red, c_old = job_of(tick - 2 - place)

        @pl.when(old_red & (place < ranks - 1))
        def _():
            red_copy(c_old).wait_send()

        old_cast, c_cast = job_of(tick - 2 * ranks + place)

        @pl.when(old_cast & (place > 0))
        def _():
            cast_copy(c_cast).wait_send()

        now_red, c = job_of(tick - 1 - place)

        @pl.when(now_red & (place == 0))
        def _():
            red[c] = acc[c, part, :]

        @pl.when(now_red & (place > 0))
        def _():
            red_copy(c).wait_recv()

        @pl.when(now_red & (place > 0) & (place < ranks - 1))
        def _():
            @pl.loop(0, half // block)
            def _(i):
                rs = tile(i, block)
                own = acc[c, pl.ds(pl.multiple_of(way * half + i * block, block), block), :]
                red[c, rs, :] = (red[c, rs, :].astype(F32) + own.astype(F32)).astype(BF)

        @pl.when(now_red & (place < ranks - 1))
        def _():
            red_copy(c).start()

        @pl.when(now_red & (place == ranks - 1))
        def _():
            @pl.loop(0, half // block)
            def _(i):
                rs = tile(i, block)
                own_rs = pl.ds(pl.multiple_of(way * half + i * block, block), block)
                acc[c, own_rs, :] = (
                    red[c, rs, :].astype(F32) + acc[c, own_rs, :].astype(F32)
                ).astype(BF)

            cast_copy(c).start()

        now_cast, cc = job_of(tick - (2 * ranks - 1 - place))

        @pl.when(now_cast & (place < ranks - 1))
        def _():
            cast_copy(cc).wait_recv()

        @pl.when(now_cast & (place > 0) & (place < ranks - 1))
        def _():
            cast_copy(cc).start()
    return comm


def middle_kernel(
    sizes,
    hidden,
    cotangent,
    shard_mix,
    shard_out,
    shard_exp,
    shard_con,
    md,
    mu,
    od,
    ou,
    ed,
    eu,
    cd,
    cu,
    gains,
    unit_rank,
    picks,
    hidden_out,
    first_low,
    active,
    second_low,
    before_grad,
    attn_low,
    mixing,
    unit_go,
    part_ranks,
    full_ranks,
    context,
    unit_qkv,
    unit_out,
    context_grad,
    local_qkv,
    w_out,
    w_exp,
    w_con,
    acc,
    red_up,
    red_down,
    stash,
    spreads,
    rank_in,
    stage_d,
    stage_f,
    rows_in,
    rank_buf,
    in_sem,
    out_sem,
    red_send,
    red_recv,
    cast_send,
    cast_recv,
    peer_send,
    peer_recv,
    twin_send,
    twin_recv,
    side_send,
    side_recv,
    own_sem,
    rank_send,
    rank_recv,
    mix_sem,
    qkv_send,
    qkv_recv,
    ctx_send,
    ctx_recv,
    go_send,
    go_recv,
    unit_sem,
):
    ranks, dps, ctxs, chunks, rows, per_seq, period = sizes
    half = rows // 2
    width = hidden.shape[1]
    hidden_units = w_exp.shape[1]
    heads = w_out.shape[0]
    block = min(16, half)
    tile_f = math.gcd(hidden_units, 256)
    tile_d = math.gcd(width, 256)
    tile_h = math.gcd(heads, 256)
    me = lax.axis_index("tensor")
    dp = lax.axis_index("dp")
    ctx = lax.axis_index("ctx")
    pairs = ctxs // 2
    core = ctx % 2
    chips = dps * pairs
    chip = dp * pairs + ctx // 2
    twin = {"ctx": ctx + 1 - 2 * core}
    lead = per_seq
    units, seq_all = unit_qkv.shape[0], unit_qkv.shape[2]
    tok = seq_all // ctxs
    local_heads = local_qkv.shape[1]

    def chip_block(step, which):
        row, column = step // pairs, step % pairs
        from_dp = (dp + dps - row) % dps
        from_chip = (ctx // 2 + pairs - column) % pairs
        return from_dp * ctxs + from_chip * 2 + which

    total = chunks * rows
    enter(
        [{"tensor": (me + d) % ranks} for d in range(1, ranks)]
        + [{"ctx": (ctx + d) % ctxs} for d in range(1, ctxs)]
        + [{"dp": (dp + d) % dps} for d in range(1, dps)]
    )

    shards = (shard_mix, shard_out, shard_exp, shard_con)
    fulls = (stash, w_out, w_exp, w_con)
    mix_width = shard_mix.shape[1]
    mix_half = shard_mix.shape[0] // 2

    def piece_of(w, p):
        if w < 2:
            return shards[w]
        return shards[w].at[tile(p, shards[w].shape[0] // PIECES)]

    def block_of(w, index, p):
        deep, wide = shards[w].shape
        if w == 0:
            return stash.at[tile(index, deep), pl.ds(0, mix_width)]
        if w == 1:
            return w_out.at[:, tile(index, wide)]
        if w == 2:
            return w_exp.at[tile(index * PIECES + p, deep // PIECES)]
        return w_con.at[tile(p, deep // PIECES), tile(index, wide)]

    def mix_piece(step, lower):
        start = chip_block(step, core) * (2 * mix_half) + lower * mix_half
        return stash.at[pl.ds(pl.multiple_of(start, mix_half), mix_half), pl.ds(0, mix_width)]

    def peer_copy(w, step, p=0):
        row, column = step // pairs, step % pairs
        block = block_of(w, chip_block(column, core), p)
        if row:
            target = {"dp": (dp + row) % dps}
        else:
            target = {"ctx": (ctx + 2 * column) % ctxs}
        own = block_of(w, chip_block(0, core), p)
        if w == 0 and row and column:
            block = mix_piece(column, 0)
        return pltpu.make_async_remote_copy(
            src_ref=block if row and column else piece_of(w, p),
            dst_ref=block if row else own,
            send_sem=peer_send.at[w, step, p],
            recv_sem=peer_recv.at[w, step, p],
            device_id=target,
            device_id_type=MESH_IDS,
        )

    def peer_arrival(w, step, p=0):
        row = step // pairs
        if row:
            target = {"dp": (dp + row) % dps}
        else:
            target = {"ctx": (ctx + 2 * step) % ctxs}
        block = block_of(w, chip_block(step, core), p)
        if w == 0 and row and step % pairs:
            block = mix_piece(step, 0)
        return pltpu.make_async_remote_copy(
            src_ref=block,
            dst_ref=block,
            send_sem=peer_send.at[w, step, p],
            recv_sem=peer_recv.at[w, step, p],
            device_id=target,
            device_id_type=MESH_IDS,
        )

    def twin_copy(w, step, p=0):
        block = block_of(w, chip_block(step, core), p)
        return pltpu.make_async_remote_copy(
            src_ref=piece_of(w, p) if step == 0 else block,
            dst_ref=block,
            send_sem=twin_send.at[w, step, p],
            recv_sem=twin_recv.at[w, step, p],
            device_id=twin,
            device_id_type=MESH_IDS,
        )

    def twin_arrival(w, step, p=0):
        block = block_of(w, chip_block(step, 1 - core), p)
        return pltpu.make_async_remote_copy(
            src_ref=block,
            dst_ref=block,
            send_sem=twin_send.at[w, step, p],
            recv_sem=twin_recv.at[w, step, p],
            device_id=twin,
            device_id_type=MESH_IDS,
        )

    def own_copy(w, p=0):
        return pltpu.make_async_copy(piece_of(w, p), block_of(w, chip_block(0, core), p), own_sem.at[w, p])

    def side_copy(step):
        row, column = step // pairs, step % pairs
        piece = mix_piece(row * pairs, 1)
        return pltpu.make_async_remote_copy(
            src_ref=piece,
            dst_ref=piece,
            send_sem=side_send.at[step],
            recv_sem=side_recv.at[step],
            device_id={"ctx": (ctx + 2 * column) % ctxs},
            device_id_type=MESH_IDS,
        )

    def side_arrival(step):
        piece = mix_piece(step, 1)
        return pltpu.make_async_remote_copy(
            src_ref=piece,
            dst_ref=piece,
            send_sem=side_send.at[step],
            recv_sem=side_recv.at[step],
            device_id={"ctx": (ctx + 2 * (step % pairs)) % ctxs},
            device_id_type=MESH_IDS,
        )

    def across_start(w, p=0):
        for step in range(pairs, chips, pairs):
            peer_copy(w, step, p).start()
        twin_copy(w, 0, p).start()
        own_copy(w, p).start()

    def along_start(w, p=0):
        for step in range(1, pairs):
            peer_copy(w, step, p).start()

    def weight_relay(w, p=0):
        for step in range(1, pairs):
            peer_arrival(w, step, p).wait_recv()
            for row in range(1, dps):
                peer_copy(w, row * pairs + step, p).start()
            twin_copy(w, step, p).start()

    def weight_forward(w, p=0):
        for step in range(pairs, chips):
            peer_arrival(w, step, p).wait_recv()
            twin_copy(w, step, p).start()

    def mixing_gather():
        along_start(0)
        across_start(0)
        weight_relay(0)
        for row in range(1, dps):
            peer_arrival(0, row * pairs).wait_recv()
            for column in range(1, pairs):
                side_copy(row * pairs + column).start()
            twin_copy(0, row * pairs).start()
        for row in range(1, dps):
            for column in range(1, pairs):
                step = row * pairs + column
                peer_arrival(0, step).wait_recv()
                side_arrival(step).wait_recv()
                twin_copy(0, step).start()

    def weight_finish(w, p=0):
        own_copy(w, p).wait()
        for step in range(chips):
            twin_arrival(w, step, p).wait_recv()

    def side_sent():
        for row in range(1, dps):
            for column in range(1, pairs):
                side_copy(row * pairs + column).wait_send()

    def weight_sent(w, p=0):
        for step in range(1, chips):
            peer_copy(w, step, p).wait_send()
        for step in range(chips):
            twin_copy(w, step, p).wait_send()

    def unit_place(device, u):
        return (device // local_heads) * units + u, device % local_heads

    def qkv_copy(u, step):
        peer = (ctx + step) % ctxs
        s, h = unit_place(peer, u)
        return pltpu.make_async_remote_copy(
            src_ref=local_qkv.at[s, h],
            dst_ref=unit_qkv.at[u, :, tile(ctx, tok)],
            send_sem=qkv_send.at[u, step],
            recv_sem=qkv_recv.at[u, step],
            device_id={"ctx": peer},
            device_id_type=MESH_IDS,
        )

    def qkv_arrival(u, step):
        return pltpu.make_async_remote_copy(
            src_ref=local_qkv.at[0, 0],
            dst_ref=unit_qkv.at[u, :, tile((ctx + ctxs - step) % ctxs, tok)],
            send_sem=qkv_send.at[u, step],
            recv_sem=qkv_recv.at[u, step],
            device_id={"ctx": (ctx + step) % ctxs},
            device_id_type=MESH_IDS,
        )

    def qkv_own(u):
        s, h = unit_place(ctx, u)
        return pltpu.make_async_copy(
            local_qkv.at[s, h], unit_qkv.at[u, :, tile(ctx, tok)], unit_sem.at[0, u]
        )

    def context_place(device, u):
        s, h = unit_place(device, u)
        return context.at[tile(s, tok), tile(h, HEAD_DIM)]

    def context_copy(u, step):
        peer = (ctx + step) % ctxs
        return pltpu.make_async_remote_copy(
            src_ref=unit_out.at[u, tile(peer, tok)],
            dst_ref=context_place(ctx, u),
            send_sem=ctx_send.at[u, step],
            recv_sem=ctx_recv.at[u, step],
            device_id={"ctx": peer},
            device_id_type=MESH_IDS,
        )

    def context_arrival(u, step):
        return pltpu.make_async_remote_copy(
            src_ref=unit_out.at[u, tile(ctx, tok)],
            dst_ref=context_place((ctx + ctxs - step) % ctxs, u),
            send_sem=ctx_send.at[u, step],
            recv_sem=ctx_recv.at[u, step],
            device_id={"ctx": (ctx + step) % ctxs},
            device_id_type=MESH_IDS,
        )

    def context_own(u):
        return pltpu.make_async_copy(
            unit_out.at[u, tile(ctx, tok)], context_place(ctx, u), unit_sem.at[1, u]
        )

    def go_copy(u, step):
        peer = (ctx + step) % ctxs
        s, h = unit_place(peer, u)
        return pltpu.make_async_remote_copy(
            src_ref=context_grad.at[tile(s, tok), tile(h, HEAD_DIM)],
            dst_ref=unit_go.at[u, tile(ctx, tok)],
            send_sem=go_send.at[u, step],
            recv_sem=go_recv.at[u, step],
            device_id={"ctx": peer},
            device_id_type=MESH_IDS,
        )

    def go_arrival(u, step):
        return pltpu.make_async_remote_copy(
            src_ref=context_grad.at[tile(0, tok), tile(0, HEAD_DIM)],
            dst_ref=unit_go.at[u, tile((ctx + ctxs - step) % ctxs, tok)],
            send_sem=go_send.at[u, step],
            recv_sem=go_recv.at[u, step],
            device_id={"ctx": (ctx + step) % ctxs},
            device_id_type=MESH_IDS,
        )

    def go_own(u):
        s, h = unit_place(ctx, u)
        return pltpu.make_async_copy(
            context_grad.at[tile(s, tok), tile(h, HEAD_DIM)],
            unit_go.at[u, tile(ctx, tok)],
            unit_sem.at[2, u],
        )

    def go_start(u):
        for step in range(1, ctxs):
            go_copy(u, step).start()
        go_own(u).start()

    def attend(u):
        qkv_own(u).wait()
        for step in range(1, ctxs):
            qkv_arrival(u, step).wait_recv()
        part = math.gcd(seq_all, 256)

        @pl.loop(0, seq_all // part)
        def _(i):
            rs = tile(i, part)
            scores = dot_nt(unit_qkv[u, 0, rs, :], unit_qkv[u, 1]) * (HEAD_DIM ** (-0.5))
            largest = jnp.max(scores, axis=-1, keepdims=True)
            raised = jnp.exp(scores - largest)
            total = jnp.sum(raised, axis=-1, keepdims=True)
            mixed = dot_nn(raised.astype(BF), unit_qkv[u, 2])
            unit_out[u, rs, :] = (mixed / total).astype(BF)

        for step in range(1, ctxs):
            context_copy(u, step).start()
        context_own(u).start()

    def context_ready(u):
        context_own(u).wait()
        for step in range(1, ctxs):
            context_arrival(u, step).wait_recv()

    def project_chunk(c):
        bring(hidden, c).wait()
        following = (c + 1) % chunks
        s = c // per_seq
        rs = tile(c % per_seq, rows)
        low = dot_nt(rows_in[...], md[picks[s]]).astype(BF)
        put_rank(3, c, low)
        rank_buf[...] = low
        heads_at_once = math.gcd(local_heads, 2)
        step = heads_at_once * HEAD_DIM

        @pl.loop(0, mix_width // step)
        def _(i):
            cs = tile(i, step)
            values = dot_nn(rows_in[...], stash[0:width, cs]) + dot_nn(rank_buf[...], mu[picks[s], :, cs])
            values = values.astype(BF)
            first = i * heads_at_once
            for k in range(heads_at_once):
                local_qkv[s, (first + k) % local_heads, (first + k) // local_heads, rs, :] = values[
                    :, k * HEAD_DIM : (k + 1) * HEAD_DIM
                ]

        bring(hidden, following).start()

    def project(s):
        @pl.loop(0, per_seq)
        def _(i):
            project_chunk(s * per_seq + i)

    def send_unit(u):
        qkv_own(u).start()
        for step in range(1, ctxs):
            qkv_copy(u, step).start()

    def job_of(number, rounds):
        safe = jnp.maximum(number, 0)
        chunk = safe % period
        valid = (number >= 0) & (chunk < chunks) & (safe < rounds * period)
        return valid, jnp.minimum(chunk, chunks - 1)

    comm = chain(
        ranks,
        half,
        block,
        me,
        acc,
        red_up,
        red_down,
        red_send,
        red_recv,
        cast_send,
        cast_recv,
        lambda number: job_of(number, 3),
    )

    def rows_of(c):
        return tile(c, rows)

    def spot(t, c, i=None):
        start = t * total + c * rows
        if i is None:
            return pl.ds(pl.multiple_of(start, rows), rows)
        return pl.ds(pl.multiple_of(start + i * block, block), block)

    def mixing_keep():
        return pltpu.make_async_copy(
            stash.at[pl.ds(0, width), pl.ds(0, mix_width)], mixing, mix_sem
        )

    def bring(source, c):
        return pltpu.make_async_copy(source.at[rows_of(c)], rows_in, in_sem)

    def keep(index, source, target, c):
        return pltpu.make_async_copy(source, target.at[rows_of(c)], out_sem.at[index])

    def put_rank(t, c, low):
        part_ranks[t, :, tile(c, rows)] = dot_nt(unit_rank[...], low).astype(BF)

    def rank_copy(t, step):
        return pltpu.make_async_remote_copy(
            src_ref=part_ranks.at[t],
            dst_ref=rank_in.at[t, step],
            send_sem=rank_send.at[t, step],
            recv_sem=rank_recv.at[t, step],
            device_id={"tensor": (me + step) % ranks},
            device_id_type=MESH_IDS,
        )

    def mean(values):
        return jnp.sum(values, axis=-1, keepdims=True) * (1.0 / width)

    def attend_part(c, s):
        mine = context[rows_of(c), :]
        low = dot_nt(mine, od[picks[s]]).astype(BF)
        put_rank(0, c, low)

        @pl.loop(0, width // tile_d)
        def _(i):
            cs = tile(i, tile_d)
            acc[c, :, cs] = (dot_nn(mine, w_out[:, cs]) + dot_nn(low, ou[picks[s], :, cs])).astype(BF)

    def forward_first(c, s):
        bring(hidden, c).wait()

        @pl.loop(0, rows // block)
        def _(i):
            rs = tile(i, block)
            total = rows_in[rs, :].astype(F32) + acc[c, rs, :].astype(F32)
            centred = total - mean(total)
            spread = lax.rsqrt(mean(centred * centred) + 1e-06)
            n = centred * spread
            stash[spot(0, c, i), :] = n.astype(BF)
            spreads[c, rs, :] = jnp.broadcast_to(spread, (block, 128))
            stage_d[rs, :] = (n * gains[0:1, :] + gains[1:2, :]).astype(BF)

        low = dot_nt(stage_d[...], ed[picks[s]]).astype(BF)
        put_rank(4, c, low)
        rank_buf[...] = low

        @pl.loop(0, hidden_units // tile_f)
        def _(i):
            cs = tile(i, tile_f)
            b = dot_nn(stage_d[...], w_exp[:, cs]) + dot_nn(rank_buf[...], eu[picks[s], :, cs])
            square = b * b
            t = jnp.tanh(GELU_C * b * (1.0 + GELU_A * square))
            upper = 0.5 * (1.0 + t)
            stage_f[:, cs] = (b * upper).astype(BF)
            stash[spot(1, c), cs] = (
                upper
                + (0.5 * GELU_C) * b * (1.0 - t * t) * (1.0 + (3.0 * GELU_A) * square)
            ).astype(BF)

    def forward_second(c, s):
        low = dot_nt(stage_f[...], cd[picks[s]]).astype(BF)
        put_rank(1, c, low)
        rank_buf[...] = low

        @pl.loop(0, width // tile_d)
        def _(i):
            cs = tile(i, tile_d)
            acc[c, :, cs] = (
                dot_nn(stage_f[...], w_con[:, cs]) + dot_nn(rank_buf[...], cu[picks[s], :, cs])
            ).astype(BF)

        keep(0, stage_d, first_low, c).start()
        keep(1, stage_f, active, c).start()

    def back_first(c, s):
        bring(cotangent, c).wait()

        @pl.loop(0, rows // block)
        def _(i):
            rs = tile(i, block)
            first = stash[spot(0, c, i), :].astype(F32) * gains[0:1, :] + gains[1:2, :]
            total = first + acc[c, rs, :].astype(F32)
            centred = total - mean(total)
            spread = lax.rsqrt(mean(centred * centred) + 1e-06)
            n = centred * spread
            stage_d[rs, :] = (n * gains[2:3, :] + gains[3:4, :]).astype(BF)
            g = rows_in[rs, :].astype(F32) * gains[2:3, :]
            stash[spot(2, c, i), :] = (spread * (g - mean(g) - n * mean(g * n))).astype(BF)

        low = dot_nt(stash[spot(2, c), :], cu[picks[s]]).astype(BF)
        put_rank(5, c, low)
        rank_buf[...] = low

        @pl.loop(0, hidden_units // tile_f)
        def _(i):
            cs = tile(i, tile_f)
            da = dot_nt(stash[spot(2, c), :], w_con[cs, :]) + dot_nn(rank_buf[...], cd[picks[s], :, cs])
            stage_f[:, cs] = (da * stash[spot(1, c), cs].astype(F32)).astype(BF)

    def back_second(c, s):
        low = dot_nt(stage_f[...], eu[picks[s]]).astype(BF)
        put_rank(2, c, low)
        rank_buf[...] = low

        @pl.loop(0, width // tile_d)
        def _(i):
            cs = tile(i, tile_d)
            acc[c, :, cs] = (
                dot_nt(stage_f[...], w_exp[cs, :]) + dot_nn(rank_buf[...], ed[picks[s], :, cs])
            ).astype(BF)

        keep(0, stage_d, hidden_out, c).start()
        keep(1, stage_f, before_grad, c).start()
        keep(2, stash.at[spot(2, c)], second_low, c).start()

    def last_first(c, s):
        @pl.loop(0, rows // block)
        def _(i):
            rs = tile(i, block)
            n = stash[spot(0, c, i), :].astype(F32)
            g = (stash[spot(2, c, i), :].astype(F32) + acc[c, rs, :].astype(F32)) * gains[0:1, :]
            spread = spreads[c, rs, 0:1]
            stage_d[rs, :] = (spread * (g - mean(g) - n * mean(g * n))).astype(BF)

    def last_second(c, s):
        low = dot_nt(stage_d[...], ou[picks[s]]).astype(BF)
        put_rank(6, c, low)
        rank_buf[...] = low

        @pl.loop(0, heads // tile_h)
        def _(i):
            cs = tile(i, tile_h)
            context_grad[rows_of(c), cs] = (
                dot_nt(stage_d[...], w_out[cs, :]) + dot_nn(rank_buf[...], od[picks[s], :, cs])
            ).astype(BF)

        keep(0, stage_d, attn_low, c).start()

    seqs = chunks // per_seq
    flowing = units == seqs
    bring(hidden, 0).start()
    mixing_gather()
    weight_finish(0)
    along_start(1)
    across_start(1)
    mixing_keep().start()
    if flowing:
        for u in range(min(2, units)):
            project(u)
            send_unit(u)
    else:
        pl.loop(0, seqs)(project)
        for u in range(units):
            send_unit(u)
    weight_relay(1)

    @pl.loop(0, lead + 3 * period + chunks)
    def _(now):
        tick = now - lead
        stage = jnp.maximum(tick, 0) // period
        valid, c = job_of(tick, 4)
        s = c // per_seq
        last_valid, last_c = job_of(tick - 1, 4)
        last_stage = jnp.maximum(tick - 1, 0) // period

        comm(tick, 0)

        @pl.when(last_valid & (last_stage >= 1))
        def _():
            keep(0, stage_d, first_low, last_c).wait()

        @pl.when(last_valid & (last_stage >= 1) & (last_stage <= 2))
        def _():
            keep(1, stage_f, active, last_c).wait()

        @pl.when(last_valid & (last_stage == 2))
        def _():
            keep(2, stash.at[spot(2, last_c)], second_low, last_c).wait()

        pl.when(now == 1)(lambda: weight_forward(1))
        if flowing:

            @pl.when((now % per_seq == 0) & (now < (units - 2) * per_seq))
            def _():
                project(now // per_seq + 2)
                send_unit(now // per_seq + 2)

        @pl.when((now % per_seq == 0) & (now > 0) & (now <= PIECES * per_seq))
        def _():
            p = now // per_seq - 1
            weight_relay(2, p)
            weight_relay(3, p)

        @pl.when((now % per_seq == 0) & (now < PIECES * per_seq))
        def _():
            for w in (2, 3):
                along_start(w, now // per_seq)
                across_start(w, now // per_seq)

        @pl.when((now % per_seq == 1 % per_seq) & (now > per_seq) & (now <= PIECES * per_seq + 1))
        def _():
            p = (now - 1) // per_seq - 1
            weight_forward(2, p)
            weight_forward(3, p)

        @pl.when(now == lead + period)
        def _():
            for p in range(PIECES):
                weight_finish(2, p)
                weight_finish(3, p)

        pl.when((now % per_seq == 0) & (now < units * per_seq))(lambda: attend(now // per_seq))
        pl.when(now == lead)(lambda: weight_finish(1))

        @pl.when(now == lead + period - 2)
        def _():
            mixing_keep().wait()
            weight_sent(0)
            side_sent()

        for t in range(3):

            @pl.when(tick == (t + 1) * period)
            def _(t=t):
                for step in range(1, ranks):
                    rank_copy(t, step).start()

        pl.when((tick >= 0) & (tick % per_seq == 0) & (tick < units * per_seq))(
            lambda: context_ready(s)
        )

        pl.when(valid & (stage == 1))(lambda: forward_first(c, s))
        pl.when(valid & (stage == 2))(lambda: back_first(c, s))
        pl.when(valid & (stage == 3))(lambda: last_first(c, s))

        comm(tick, 1)

        pl.when(valid & (stage == 0))(lambda: attend_part(c, s))
        pl.when(valid & (stage == 1))(lambda: forward_second(c, s))
        pl.when(valid & (stage == 2))(lambda: back_second(c, s))
        pl.when(valid & (stage == 3))(lambda: last_second(c, s))
        if flowing:
            pl.when(valid & (stage == 3) & (c % per_seq == per_seq - 1))(lambda: go_start(s))

        next_valid, next_c = job_of(tick + 1, 4)
        next_stage = jnp.maximum(tick + 1, 0) // period
        pl.when(next_valid & (next_stage == 1) & (next_c > 0))(
            lambda: bring(hidden, next_c).start()
        )
        pl.when(next_valid & (next_stage == 2))(lambda: bring(cotangent, next_c).start())

    keep(0, stage_d, attn_low, chunks - 1).wait()
    for t in range(3):
        value = part_ranks[t].astype(F32)
        for step in range(1, ranks):
            rank_copy(t, step).wait_recv()
            value = value + rank_in[t, step].astype(F32)
        full_ranks[t] = value.astype(BF)
    for t in range(3):
        for step in range(1, ranks):
            rank_copy(t, step).wait_send()
    weight_sent(1)
    for p in range(PIECES):
        weight_sent(2, p)
        weight_sent(3, p)
    for u in range(units):
        if not flowing:
            go_start(u)
        for step in range(1, ctxs):
            qkv_copy(u, step).wait_send()
            context_copy(u, step).wait_send()
    for u in range(units):
        go_own(u).wait()
        for step in range(1, ctxs):
            go_arrival(u, step).wait_recv()
            go_copy(u, step).wait_send()


def enter(others):
    barrier = pltpu.get_barrier_semaphore()
    for other in others:
        pl.semaphore_signal(barrier, inc=1, device_id=other, device_id_type=MESH_IDS)
    pl.semaphore_wait(barrier, len(others))


def middle(hidden, cotangent, shards, picked, gains, tok, picks):
    total, width = hidden.shape
    mix_width = shards[0].shape[1]
    heads, hidden_units = shards[1].shape[0], shards[2].shape[1]
    ranks, dps, ctxs = (lax.axis_size(name) for name in ("tensor", "dp", "ctx"))
    seqs, rank = picks.shape[0], picked[0].shape[1]
    local_heads = heads // HEAD_DIM
    units = seqs * local_heads // ctxs
    rows = math.gcd(tok, CHUNK_ROWS)
    chunks = total // rows
    period = max(chunks, 2 * ranks)
    sizes = (ranks, dps, ctxs, chunks, rows, tok // rows, period)
    chips = dps * ctxs // 2
    vm = pl.BlockSpec(memory_space=pltpu.VMEM)
    hb = pl.BlockSpec(memory_space=pl.ANY)
    sm = pl.BlockSpec(memory_space=pltpu.SMEM)
    half = rows // 2
    dma = pltpu.SemaphoreType.DMA

    def shape(*dims):
        return jax.ShapeDtypeStruct(dims, BF)

    return pl.pallas_call(
        functools.partial(middle_kernel, sizes),
        out_shape=(
            shape(total, width),
            shape(total, width),
            shape(total, hidden_units),
            shape(total, width),
            shape(total, hidden_units),
            shape(total, width),
            shape(width, mix_width),
            shape(units, tok * ctxs, HEAD_DIM),
            shape(7, rank, total),
            shape(3, rank, total),
            shape(total, heads),
            shape(units, 3, tok * ctxs, HEAD_DIM),
            shape(units, tok * ctxs, HEAD_DIM),
        ),
        in_specs=[hb] * 6 + [vm] * 10 + [sm],
        out_specs=(hb,) * 7 + (vm,) * 6,
        scratch_shapes=[
            pltpu.VMEM((total, heads), BF),
            pltpu.VMEM((seqs, local_heads, 3, tok, HEAD_DIM), BF),
            pltpu.VMEM((heads, width), BF),
            pltpu.VMEM((width, hidden_units), BF),
            pltpu.VMEM((hidden_units, width), BF),
            pltpu.VMEM((chunks, rows, width), BF),
            pltpu.VMEM((chunks, half, width), BF),
            pltpu.VMEM((chunks, half, width), BF),
            pltpu.VMEM((3 * total, width), BF),
            pltpu.VMEM((chunks, rows, 128), F32),
            pltpu.VMEM((3, ranks, rank, total), BF),
            pltpu.VMEM((rows, width), BF),
            pltpu.VMEM((rows, hidden_units), BF),
            pltpu.VMEM((rows, width), BF),
            pltpu.VMEM((rows, rank), BF),
            dma(()),
            dma((3,)),
            dma((2, chunks)),
            dma((2, chunks)),
            dma((2, chunks)),
            dma((2, chunks)),
            dma((4, chips, PIECES)),
            dma((4, chips, PIECES)),
            dma((4, chips, PIECES)),
            dma((4, chips, PIECES)),
            dma((chips,)),
            dma((chips,)),
            dma((4, PIECES)),
            dma((3, ranks)),
            dma((3, ranks)),
            dma(()),
            dma((units, ctxs)),
            dma((units, ctxs)),
            dma((units, ctxs)),
            dma((units, ctxs)),
            dma((units, ctxs)),
            dma((units, ctxs)),
            dma((3, units)),
        ],
        compiler_params=pltpu.CompilerParams(
            collective_id=0, has_side_effects=True, vmem_limit_bytes=VMEM_BYTES
        ),
        cost_estimate=pl.CostEstimate(
            flops=8 * total * width * hidden_units + 4 * total * width * heads,
            bytes_accessed=16 * total * width,
            transcendentals=total * hidden_units,
        ),
    )(hidden, cotangent, *shards, *picked, gains, jnp.eye(rank, dtype=BF), picks)


def mixing_kernel(
    sizes,
    unit_go,
    unit_qkv,
    unit_out,
    mixing_far,
    mu,
    md,
    attn_low,
    unit_rank,
    hidden_far,
    mix_rank,
    row_hot,
    picks,
    input_grad,
    table_sum,
    grads,
    mixing,
    hidden,
    rank_part,
    rank_in,
    wide,
    table_part,
    table_in,
    unit_grad,
    sum_k,
    sum_v,
    acc,
    red_up,
    red_down,
    stage_d,
    rows_in,
    rank_buf,
    in_sem,
    out_sem,
    red_send,
    red_recv,
    cast_send,
    cast_recv,
    far_sem,
    grad_send,
    grad_recv,
    unit_sem,
    rank_send,
    rank_recv,
    part_send,
    part_recv,
    whole_send,
    whole_recv,
):
    ranks, dps, ctxs, chunks, rows, per_seq, group = sizes
    half = rows // 2
    width = mixing.shape[0]
    heads = grads.shape[2]
    local_heads = heads // HEAD_DIM
    units, seq_all = unit_go.shape[0], unit_go.shape[1]
    tok = seq_all // ctxs
    block = min(16, half)
    tile_d = math.gcd(width, 256)
    scale = HEAD_DIM ** (-0.5)
    me = lax.axis_index("tensor")
    ctx = lax.axis_index("ctx")
    dp = lax.axis_index("dp")
    parts = dps * ctxs
    index = dp * ctxs + ctx
    rank = mu.shape[1]
    tables, _, part_width = table_part.shape
    segments = parts // NADAPT
    tile_g = math.gcd(part_width, 256)

    def part_place(step):
        other = (index + step) % parts
        return {"dp": other // ctxs, "ctx": other % ctxs}

    enter(
        [{"tensor": (me + d) % ranks} for d in range(1, ranks)]
        + [part_place(d) for d in range(1, parts)]
    )

    def unit_place(device, u):
        return (device // local_heads) * units + u, device % local_heads

    def mixing_load():
        return pltpu.make_async_copy(mixing_far, mixing, far_sem.at[0])

    def hidden_load():
        return pltpu.make_async_copy(hidden_far, hidden, far_sem.at[1])

    def grads_place(device, u):
        s, h = unit_place(device, u)
        return grads.at[:, tile(s, tok), tile(h, HEAD_DIM)]

    def grad_copy(u, step):
        peer = (ctx + step) % ctxs
        return pltpu.make_async_remote_copy(
            src_ref=unit_grad.at[u, :, tile(peer, tok)],
            dst_ref=grads_place(ctx, u),
            send_sem=grad_send.at[u, step],
            recv_sem=grad_recv.at[u, step],
            device_id={"ctx": peer},
            device_id_type=MESH_IDS,
        )

    def grad_arrival(u, step):
        return pltpu.make_async_remote_copy(
            src_ref=unit_grad.at[u, :, tile(ctx, tok)],
            dst_ref=grads_place((ctx + ctxs - step) % ctxs, u),
            send_sem=grad_send.at[u, step],
            recv_sem=grad_recv.at[u, step],
            device_id={"ctx": (ctx + step) % ctxs},
            device_id_type=MESH_IDS,
        )

    def grad_own(u):
        return pltpu.make_async_copy(
            unit_grad.at[u, :, tile(ctx, tok)], grads_place(ctx, u), unit_sem.at[u]
        )

    def attend_back(u):
        part = math.gcd(seq_all, 256)
        sum_k[...] = jnp.zeros_like(sum_k)
        sum_v[...] = jnp.zeros_like(sum_v)

        @pl.loop(0, seq_all // part)
        def _(i):
            rs = tile(i, part)
            queries = unit_qkv[u, 0, rs, :]
            go = unit_go[u, rs, :]
            scores = dot_nt(queries, unit_qkv[u, 1]) * scale
            raised = jnp.exp(scores - jnp.max(scores, axis=-1, keepdims=True))
            probs = raised * (1.0 / jnp.sum(raised, axis=-1, keepdims=True))
            delta = jnp.sum(
                go.astype(F32) * unit_out[u, rs, :].astype(F32), axis=-1, keepdims=True
            )
            dscores = (probs * (dot_nt(go, unit_qkv[u, 2]) - delta)).astype(BF)
            unit_grad[u, 0, rs, :] = (scale * dot_nn(dscores, unit_qkv[u, 1])).astype(BF)
            sum_k[...] += dot_tn(dscores, queries)
            sum_v[...] += dot_tn(probs.astype(BF), go)

        unit_grad[u, 1] = (scale * sum_k[...]).astype(BF)
        unit_grad[u, 2] = sum_v[...].astype(BF)
        for step in range(1, ctxs):
            grad_copy(u, step).start()
        grad_own(u).start()

    def grads_ready(u):
        grad_own(u).wait()
        for step in range(1, ctxs):
            grad_arrival(u, step).wait_recv()

    mixing_load().start()
    hidden_load().start()

    def job_of(number):
        return (number >= 0) & (number < chunks), jnp.clip(number, 0, chunks - 1)

    comm = chain(
        ranks, half, block, me, acc, red_up, red_down, red_send, red_recv, cast_send, cast_recv, job_of
    )

    def rows_of(c):
        return tile(c, rows)

    def bring(c):
        return pltpu.make_async_copy(attn_low.at[rows_of(c)], rows_in, in_sem)

    def keep(c):
        return pltpu.make_async_copy(stage_d, input_grad.at[rows_of(c)], out_sem)

    def back_part(c, s):
        rs = pl.ds(pl.multiple_of(c * rows, group * rows), group * rows)
        low = jnp.zeros((group * rows, mu.shape[1]), F32)
        for j in range(3):
            low = low + dot_nt(grads[j, rs, :], mu[picks[s], :, pl.ds(j * heads, heads)])
        low = low.astype(BF)
        rank_part[:, pl.ds(pl.multiple_of(c * rows, group * rows), group * rows)] = dot_nt(
            unit_rank[...], low
        ).astype(BF)
        rank_buf[...] = low

        @pl.loop(0, width // tile_d)
        def _(i):
            cs = tile(i, tile_d)
            total = dot_nn(rank_buf[...], md[picks[s], :, cs])
            for j in range(3):
                total = total + dot_nt(grads[j, rs, :], mixing[cs, pl.ds(j * heads, heads)])
            total = total.astype(BF)
            for k in range(group):
                acc[c + k, :, cs] = total[k * rows : (k + 1) * rows, :]

    def final_part(c):
        bring(c).wait()

        @pl.loop(0, rows // block)
        def _(i):
            rs = tile(i, block)
            stage_d[rs, :] = (rows_in[rs, :].astype(F32) + acc[c, rs, :].astype(F32)).astype(BF)

        keep(c).start()

    def rank_copy(step):
        return pltpu.make_async_remote_copy(
            src_ref=rank_part,
            dst_ref=rank_in.at[step],
            send_sem=rank_send.at[step],
            recv_sem=rank_recv.at[step],
            device_id={"tensor": (me + step) % ranks},
            device_id_type=MESH_IDS,
        )

    def part_copy(step):
        return pltpu.make_async_remote_copy(
            src_ref=table_part.at[(index + step) % parts],
            dst_ref=table_in.at[step],
            send_sem=part_send.at[step],
            recv_sem=part_recv.at[step],
            device_id=part_place(step),
            device_id_type=MESH_IDS,
        )

    def whole_copy(step):
        return pltpu.make_async_remote_copy(
            src_ref=table_sum.at[index],
            dst_ref=table_sum.at[index],
            send_sem=whole_send.at[step],
            recv_sem=whole_recv.at[step],
            device_id=part_place(step),
            device_id_type=MESH_IDS,
        )

    def whole_arrival(step):
        return pltpu.make_async_remote_copy(
            src_ref=table_sum.at[index],
            dst_ref=table_sum.at[(index + parts - step) % parts],
            send_sem=whole_send.at[step],
            recv_sem=whole_recv.at[step],
            device_id=part_place(step),
            device_id_type=MESH_IDS,
        )

    def put_table(column, values):
        segment = column // part_width
        cs = pl.ds(pl.multiple_of(column % part_width, tile_g), tile_g)
        for n in range(NADAPT):
            table_part[n * segments + segment, :, cs] = values[n * rank : (n + 1) * rank, :].astype(
                BF
            )

    def make_tables():
        value = rank_part[...].astype(F32)
        for step in range(1, ranks):
            rank_copy(step).wait_recv()
            value = value + rank_in[step].astype(F32)
        for n in range(NADAPT):
            hot = row_hot[n : n + 1, :]
            wide[0, pl.ds(n * rank, rank), :] = (value * hot).astype(BF)
            wide[1, pl.ds(n * rank, rank), :] = (mix_rank[...].astype(F32) * hot).astype(BF)

        @pl.loop(0, width // tile_g)
        def _(i):
            put_table(i * tile_g, dot_nn(wide[0], hidden[:, tile(i, tile_g)]))

        for j in range(3):

            @pl.loop(0, heads // tile_g)
            def _(i):
                put_table(
                    width + j * heads + i * tile_g, dot_nn(wide[1], grads[j, :, tile(i, tile_g)])
                )

        for step in range(1, parts):
            part_copy(step).start()

    def sum_tables():
        value = table_part[index].astype(F32)
        for step in range(1, parts):
            part_copy(step).wait_recv()
            value = value + table_in[step].astype(F32)
        table_sum[index] = value.astype(BF)
        for step in range(1, parts):
            whole_copy(step).start()

    delay = 2 * ranks

    @pl.loop(0, per_seq + chunks + delay)
    def _(now):
        tick = now - per_seq

        @pl.when(tick == chunks)
        def _():
            for step in range(1, ranks):
                rank_copy(step).start()

        valid, c = job_of(tick)
        final, c_final = job_of(tick - delay)
        before, c_before = job_of(tick - delay - 1)
        coming, c_coming = job_of(tick - delay + 1)
        s = c // per_seq

        comm(tick, 0)

        pl.when((now % per_seq == 0) & (now < units * per_seq))(lambda: attend_back(now // per_seq))
        pl.when((tick >= 0) & (tick % per_seq == 0) & (tick < units * per_seq))(
            lambda: grads_ready(s)
        )
        comm(tick, 1)

        pl.when(tick == 0)(lambda: mixing_load().wait())
        pl.when(valid & (tick % group == 0))(lambda: back_part(c, s))

        @pl.when(tick == chunks + 1)
        def _():
            hidden_load().wait()
            make_tables()

        pl.when(tick == chunks + 4)(sum_tables)

        pl.when(before)(lambda: keep(c_before).wait())
        pl.when(final)(lambda: final_part(c_final))
        pl.when(coming)(lambda: bring(c_coming).start())

    keep(chunks - 1).wait()
    for step in range(1, ranks):
        rank_copy(step).wait_send()
    for step in range(1, parts):
        whole_arrival(step).wait_recv()
    for step in range(1, parts):
        part_copy(step).wait_send()
        whole_copy(step).wait_send()
    for u in range(units):
        for step in range(1, ctxs):
            grad_copy(u, step).wait_send()


def mixing_back(
    unit_go, unit_qkv, unit_out, mixing, picked, attn_low, hidden, mix_rank, row_hot, picks
):
    mu, md = picked
    total, width = attn_low.shape
    heads = mixing.shape[1] // 3
    ranks, dps, ctxs = (lax.axis_size(name) for name in ("tensor", "dp", "ctx"))
    parts = dps * ctxs
    part_width = (width + 3 * heads) * NADAPT // parts
    units, _, seq_all, _ = unit_qkv.shape
    tok = seq_all // ctxs
    rank = mu.shape[1]
    rows = math.gcd(tok, LAST_ROWS)
    chunks = total // rows
    per_seq = tok // rows
    group = math.gcd(per_seq, 2)
    half = rows // 2
    sizes = (ranks, dps, ctxs, chunks, rows, per_seq, group)
    vm = pl.BlockSpec(memory_space=pltpu.VMEM)
    hb = pl.BlockSpec(memory_space=pl.ANY)
    sm = pl.BlockSpec(memory_space=pltpu.SMEM)
    dma = pltpu.SemaphoreType.DMA
    return pl.pallas_call(
        functools.partial(mixing_kernel, sizes),
        out_shape=(
            jax.ShapeDtypeStruct((total, width), BF),
            jax.ShapeDtypeStruct((parts, rank, part_width), BF),
        ),
        in_specs=[vm] * 3 + [hb] + [vm] * 2 + [hb, vm, hb] + [vm] * 2 + [sm],
        out_specs=(hb, vm),
        scratch_shapes=[
            pltpu.VMEM((3, total, heads), BF),
            pltpu.VMEM((width, 3 * heads), BF),
            pltpu.VMEM((total, width), BF),
            pltpu.VMEM((rank, total), BF),
            pltpu.VMEM((ranks, rank, total), BF),
            pltpu.VMEM((2, NADAPT * rank, total), BF),
            pltpu.VMEM((parts, rank, part_width), BF),
            pltpu.VMEM((parts, rank, part_width), BF),
            pltpu.VMEM((units, 3, seq_all, HEAD_DIM), BF),
            pltpu.VMEM((seq_all, HEAD_DIM), F32),
            pltpu.VMEM((seq_all, HEAD_DIM), F32),
            pltpu.VMEM((chunks, rows, width), BF),
            pltpu.VMEM((chunks, half, width), BF),
            pltpu.VMEM((chunks, half, width), BF),
            pltpu.VMEM((rows, width), BF),
            pltpu.VMEM((rows, width), BF),
            pltpu.VMEM((group * rows, rank), BF),
            dma(()),
            dma(()),
            dma((2, chunks)),
            dma((2, chunks)),
            dma((2, chunks)),
            dma((2, chunks)),
            dma((2,)),
            dma((units, ctxs)),
            dma((units, ctxs)),
            dma((units,)),
            dma((ranks,)),
            dma((ranks,)),
            dma((parts,)),
            dma((parts,)),
            dma((parts,)),
            dma((parts,)),
        ],
        compiler_params=pltpu.CompilerParams(
            collective_id=1, has_side_effects=True, vmem_limit_bytes=VMEM_LAST
        ),
        cost_estimate=pl.CostEstimate(
            flops=6 * total * width * heads + 10 * units * seq_all * seq_all * HEAD_DIM,
            bytes_accessed=8 * total * width,
            transcendentals=units * seq_all * seq_all,
        ),
    )(
        unit_go,
        unit_qkv,
        unit_out,
        mixing,
        mu,
        md,
        attn_low,
        jnp.eye(rank, dtype=BF),
        hidden,
        mix_rank,
        row_hot,
        picks,
    )


def per_device(
    hidden_in,
    output_cotangent,
    adapter_index,
    mixing_weight,
    output_weight,
    expand_weight,
    contract_weight,
    first_gain,
    first_shift,
    second_gain,
    second_shift,
    mixing_down,
    mixing_up,
    output_down,
    output_up,
    expand_down,
    expand_up,
    contract_down,
    contract_up,
):
    seq_count, tok_count, model_width = hidden_in.shape
    local_heads = mixing_weight.shape[2] // HEAD_DIM
    local_width = mixing_weight.shape[2]
    rows_all = seq_count * tok_count
    adapter_ids = jnp.arange(NADAPT, dtype=jnp.int32)
    onehot_low = (adapter_index == adapter_ids[None, :]).astype(jnp.bfloat16)
    picks = adapter_index.reshape(-1)
    rank = mixing_down.shape[1]
    mixing_flat = mixing_weight.reshape(mixing_weight.shape[0], 3 * local_width)
    hidden_rows = hidden_in.reshape(rows_all, model_width)
    mixing_up_flat = mixing_up.reshape(NADAPT, rank, 3 * local_width)
    gains = jnp.stack([first_gain, first_shift, second_gain, second_shift])
    (
        out_rows,
        first_low,
        active_low,
        second_low,
        before_low,
        attn_low,
        mixing_full,
        unit_go,
        part_ranks,
        full_ranks,
        context,
        unit_qkv,
        unit_out,
    ) = middle(
        hidden_rows,
        output_cotangent.reshape(rows_all, model_width),
        (mixing_flat, output_weight, expand_weight, contract_weight),
        (
            mixing_down,
            mixing_up_flat,
            output_down,
            output_up,
            expand_down,
            expand_up,
            contract_down,
            contract_up,
        ),
        gains,
        tok_count,
        picks,
    )
    row_hot = jnp.repeat(onehot_low.T, tok_count, axis=1)

    def table_grad(ranks, values):
        wide = (row_hot[:, None, :] * ranks[None, :, :]).reshape(-1, rows_all)
        part = jnp.einsum("kn,nd->kd", wide, values, preferred_element_type=jnp.float32)
        return part.astype(jnp.bfloat16).reshape(NADAPT, rank, values.shape[1])

    early = (
        table_grad(part_ranks[6], context),
        table_grad(full_ranks[0], attn_low),
        table_grad(full_ranks[2], first_low),
        table_grad(part_ranks[4], before_low),
        table_grad(part_ranks[5], active_low),
        table_grad(full_ranks[1], second_low),
    )
    early, unit_go = lax.optimization_barrier((early, unit_go))
    input_rows, late = mixing_back(
        unit_go,
        unit_qkv,
        unit_out,
        mixing_full,
        (mixing_up_flat, mixing_down),
        attn_low,
        hidden_rows,
        part_ranks[3],
        row_hot.astype(jnp.float32),
        picks,
    )
    early = lax.psum(early, ("dp", "ctx"))
    late = late.reshape(NADAPT, -1, rank, late.shape[2]).swapaxes(1, 2).reshape(NADAPT, rank, -1)
    late = (
        late[:, :, :model_width],
        late[:, :, model_width:].reshape(NADAPT, rank, 3, local_width),
    )
    summed = tuple(part.astype(jnp.float32) for part in late + early)
    return (
        out_rows.reshape(hidden_in.shape),
        input_rows.reshape(hidden_in.shape),
    ) + summed


def solution(mesh):
    return jax.shard_map(
        per_device,
        mesh=mesh,
        in_specs=(
            P("dp", "ctx", None),
            P("dp", "ctx", None),
            P("dp", None),
            P(("dp", "ctx"), None, "tensor"),
            P("tensor", ("dp", "ctx")),
            P(("dp", "ctx"), "tensor"),
            P("tensor", ("dp", "ctx")),
            P(),
            P(),
            P(),
            P(),
            P(),
            P(None, None, None, "tensor"),
            P(None, None, "tensor"),
            P(),
            P(),
            P(None, None, "tensor"),
            P(None, None, "tensor"),
            P(),
        ),
        out_specs=(
            P("dp", "ctx", None),
            P("dp", "ctx", None),
            P(),
            P(None, None, None, "tensor"),
            P(None, None, "tensor"),
            P(),
            P(),
            P(None, None, "tensor"),
            P(None, None, "tensor"),
            P(),
        ),
        check_vma=False,
    )
```

```python
import functools
import math

import jax
import jax.numpy as jnp
from jax import lax
from jax.experimental import pallas as pl
from jax.experimental.pallas import tpu as pltpu
from jax.sharding import PartitionSpec as P

HEAD_DIM = 128
NADAPT = 8
CHUNK_ROWS = 128
LAST_ROWS = 128
VMEM_BYTES = 62 * 2**20
VMEM_LAST = 56 * 2**20
PIECES = 4


BF = jnp.bfloat16
F32 = jnp.float32
MESH_IDS = pl.DeviceIdType.MESH
RANK_ROWS = 16
GELU_C = 0.7978845608028654
GELU_A = 0.044715


def dot_nn(a, b):
    return lax.dot_general(a, b, (((1,), (0,)), ((), ())), preferred_element_type=F32)


def dot_nt(a, b):
    return lax.dot_general(a, b, (((1,), (1,)), ((), ())), preferred_element_type=F32)


def dot_tn(a, b):
    return lax.dot_general(a, b, (((0,), (0,)), ((), ())), preferred_element_type=F32)


def tile(index, size):
    return pl.ds(pl.multiple_of(index * size, size), size)


def chain(
    ranks, half, block, me, acc, red_up, red_down, red_send, red_recv, cast_send, cast_recv, job_of
):
    def comm(tick, way):
        upward = way == 0
        place = me if upward else ranks - 1 - me
        ahead = me + 1 if upward else me - 1
        behind = me - 1 if upward else me + 1
        red = red_up if upward else red_down
        part = pl.ds(way * half, half)

        def red_copy(c):
            return pltpu.make_async_remote_copy(
                src_ref=red.at[c],
                dst_ref=red.at[c],
                send_sem=red_send.at[way, c],
                recv_sem=red_recv.at[way, c],
                device_id={"tensor": ahead},
                device_id_type=MESH_IDS,
            )

        def cast_copy(c):
            return pltpu.make_async_remote_copy(
                src_ref=acc.at[c, part],
                dst_ref=acc.at[c, part],
                send_sem=cast_send.at[way, c],
                recv_sem=cast_recv.at[way, c],
                device_id={"tensor": behind},
                device_id_type=MESH_IDS,
            )

        old_red, c_old = job_of(tick - 2 - place)

        @pl.when(old_red & (place < ranks - 1))
        def _():
            red_copy(c_old).wait_send()

        old_cast, c_cast = job_of(tick - 2 * ranks + place)

        @pl.when(old_cast & (place > 0))
        def _():
            cast_copy(c_cast).wait_send()

        now_red, c = job_of(tick - 1 - place)

        @pl.when(now_red & (place == 0))
        def _():
            red[c] = acc[c, part, :]

        @pl.when(now_red & (place > 0))
        def _():
            red_copy(c).wait_recv()

        @pl.when(now_red & (place > 0) & (place < ranks - 1))
        def _():
            @pl.loop(0, half // block)
            def _(i):
                rs = tile(i, block)
                own = acc[c, pl.ds(pl.multiple_of(way * half + i * block, block), block), :]
                red[c, rs, :] = (red[c, rs, :].astype(F32) + own.astype(F32)).astype(BF)

        @pl.when(now_red & (place < ranks - 1))
        def _():
            red_copy(c).start()

        @pl.when(now_red & (place == ranks - 1))
        def _():
            @pl.loop(0, half // block)
            def _(i):
                rs = tile(i, block)
                own_rs = pl.ds(pl.multiple_of(way * half + i * block, block), block)
                acc[c, own_rs, :] = (
                    red[c, rs, :].astype(F32) + acc[c, own_rs, :].astype(F32)
                ).astype(BF)

            cast_copy(c).start()

        now_cast, cc = job_of(tick - (2 * ranks - 1 - place))

        @pl.when(now_cast & (place < ranks - 1))
        def _():
            cast_copy(cc).wait_recv()

        @pl.when(now_cast & (place > 0) & (place < ranks - 1))
        def _():
            cast_copy(cc).start()
    return comm


def middle_kernel(
    sizes,
    hidden,
    cotangent,
    shard_mix,
    shard_out,
    shard_exp,
    shard_con,
    md,
    mu,
    od,
    ou,
    ed,
    eu,
    cd,
    cu,
    gains,
    unit_rank,
    picks,
    hidden_out,
    first_low,
    active,
    second_low,
    before_grad,
    attn_low,
    mixing,
    unit_go,
    part_ranks,
    full_ranks,
    context,
    unit_qkv,
    unit_out,
    context_grad,
    local_qkv,
    w_out,
    w_exp,
    w_con,
    acc,
    red_up,
    red_down,
    stash,
    spreads,
    rank_in,
    stage_d,
    stage_f,
    rows_in,
    rank_buf,
    in_sem,
    out_sem,
    red_send,
    red_recv,
    cast_send,
    cast_recv,
    peer_send,
    peer_recv,
    twin_send,
    twin_recv,
    side_send,
    side_recv,
    own_sem,
    rank_send,
    rank_recv,
    mix_sem,
    qkv_send,
    qkv_recv,
    ctx_send,
    ctx_recv,
    go_send,
    go_recv,
    unit_sem,
):
    ranks, dps, ctxs, chunks, rows, per_seq, period = sizes
    half = rows // 2
    width = hidden.shape[1]
    hidden_units = w_exp.shape[1]
    heads = w_out.shape[0]
    block = min(16, half)
    tile_f = math.gcd(hidden_units, 256)
    tile_d = math.gcd(width, 256)
    tile_h = math.gcd(heads, 256)
    me = lax.axis_index("tensor")
    dp = lax.axis_index("dp")
    ctx = lax.axis_index("ctx")
    pairs = ctxs // 2
    core = ctx % 2
    chips = dps * pairs
    chip = dp * pairs + ctx // 2
    twin = {"ctx": ctx + 1 - 2 * core}
    lead = per_seq
    units, seq_all = unit_qkv.shape[0], unit_qkv.shape[2]
    tok = seq_all // ctxs
    local_heads = local_qkv.shape[1]

    def chip_block(step, which):
        row, column = step // pairs, step % pairs
        from_dp = (dp + dps - row) % dps
        from_chip = (ctx // 2 + pairs - column) % pairs
        return from_dp * ctxs + from_chip * 2 + which

    total = chunks * rows
    enter(
        [{"tensor": (me + d) % ranks} for d in range(1, ranks)]
        + [{"ctx": (ctx + d) % ctxs} for d in range(1, ctxs)]
        + [{"dp": (dp + d) % dps} for d in range(1, dps)]
    )

    shards = (shard_mix, shard_out, shard_exp, shard_con)
    fulls = (stash, w_out, w_exp, w_con)
    mix_width = shard_mix.shape[1]
    mix_half = shard_mix.shape[0] // 2

    def piece_of(w, p):
        if w < 2:
            return shards[w]
        return shards[w].at[tile(p, shards[w].shape[0] // PIECES)]

    def block_of(w, index, p):
        deep, wide = shards[w].shape
        if w == 0:
            return stash.at[tile(index, deep), pl.ds(0, mix_width)]
        if w == 1:
            return w_out.at[:, tile(index, wide)]
        if w == 2:
            return w_exp.at[tile(index * PIECES + p, deep // PIECES)]
        return w_con.at[tile(p, deep // PIECES), tile(index, wide)]

    def mix_piece(step, lower):
        start = chip_block(step, core) * (2 * mix_half) + lower * mix_half
        return stash.at[pl.ds(pl.multiple_of(start, mix_half), mix_half), pl.ds(0, mix_width)]

    def peer_copy(w, step, p=0):
        row, column = step // pairs, step % pairs
        block = block_of(w, chip_block(column, core), p)
        if row:
            target = {"dp": (dp + row) % dps}
        else:
            target = {"ctx": (ctx + 2 * column) % ctxs}
        own = block_of(w, chip_block(0, core), p)
        if w == 0 and row and column:
            block = mix_piece(column, 0)
        return pltpu.make_async_remote_copy(
            src_ref=block if row and column else piece_of(w, p),
            dst_ref=block if row else own,
            send_sem=peer_send.at[w, step, p],
            recv_sem=peer_recv.at[w, step, p],
            device_id=target,
            device_id_type=MESH_IDS,
        )

    def peer_arrival(w, step, p=0):
        row = step // pairs
        if row:
            target = {"dp": (dp + row) % dps}
        else:
            target = {"ctx": (ctx + 2 * step) % ctxs}
        block = block_of(w, chip_block(step, core), p)
        if w == 0 and row and step % pairs:
            block = mix_piece(step, 0)
        return pltpu.make_async_remote_copy(
            src_ref=block,
            dst_ref=block,
            send_sem=peer_send.at[w, step, p],
            recv_sem=peer_recv.at[w, step, p],
            device_id=target,
            device_id_type=MESH_IDS,
        )

    def twin_copy(w, step, p=0):
        block = block_of(w, chip_block(step, core), p)
        return pltpu.make_async_remote_copy(
            src_ref=piece_of(w, p) if step == 0 else block,
            dst_ref=block,
            send_sem=twin_send.at[w, step, p],
            recv_sem=twin_recv.at[w, step, p],
            device_id=twin,
            device_id_type=MESH_IDS,
        )

    def twin_arrival(w, step, p=0):
        block = block_of(w, chip_block(step, 1 - core), p)
        return pltpu.make_async_remote_copy(
            src_ref=block,
            dst_ref=block,
            send_sem=twin_send.at[w, step, p],
            recv_sem=twin_recv.at[w, step, p],
            device_id=twin,
            device_id_type=MESH_IDS,
        )

    def own_copy(w, p=0):
        return pltpu.make_async_copy(piece_of(w, p), block_of(w, chip_block(0, core), p), own_sem.at[w, p])

    def side_copy(step):
        row, column = step // pairs, step % pairs
        piece = mix_piece(row * pairs, 1)
        return pltpu.make_async_remote_copy(
            src_ref=piece,
            dst_ref=piece,
            send_sem=side_send.at[step],
            recv_sem=side_recv.at[step],
            device_id={"ctx": (ctx + 2 * column) % ctxs},
            device_id_type=MESH_IDS,
        )

    def side_arrival(step):
        piece = mix_piece(step, 1)
        return pltpu.make_async_remote_copy(
            src_ref=piece,
            dst_ref=piece,
            send_sem=side_send.at[step],
            recv_sem=side_recv.at[step],
            device_id={"ctx": (ctx + 2 * (step % pairs)) % ctxs},
            device_id_type=MESH_IDS,
        )

    def across_start(w, p=0):
        for step in range(pairs, chips, pairs):
            peer_copy(w, step, p).start()
        twin_copy(w, 0, p).start()
        own_copy(w, p).start()

    def along_start(w, p=0):
        for step in range(1, pairs):
            peer_copy(w, step, p).start()

    def weight_relay(w, p=0):
        for step in range(1, pairs):
            peer_arrival(w, step, p).wait_recv()
            for row in range(1, dps):
                peer_copy(w, row * pairs + step, p).start()
            twin_copy(w, step, p).start()

    def weight_forward(w, p=0):
        for step in range(pairs, chips):
            peer_arrival(w, step, p).wait_recv()
            twin_copy(w, step, p).start()

    def mixing_gather():
        along_start(0)
        across_start(0)
        weight_relay(0)
        for row in range(1, dps):
            peer_arrival(0, row * pairs).wait_recv()
            for column in range(1, pairs):
                side_copy(row * pairs + column).start()
            twin_copy(0, row * pairs).start()
        for row in range(1, dps):
            for column in range(1, pairs):
                step = row * pairs + column
                peer_arrival(0, step).wait_recv()
                side_arrival(step).wait_recv()
                twin_copy(0, step).start()

    def weight_finish(w, p=0):
        own_copy(w, p).wait()
        for step in range(chips):
            twin_arrival(w, step, p).wait_recv()

    def side_sent():
        for row in range(1, dps):
            for column in range(1, pairs):
                side_copy(row * pairs + column).wait_send()

    def weight_sent(w, p=0):
        for step in range(1, chips):
            peer_copy(w, step, p).wait_send()
        for step in range(chips):
            twin_copy(w, step, p).wait_send()

    def unit_place(device, u):
        return (device // local_heads) * units + u, device % local_heads

    def qkv_copy(u, step):
        peer = (ctx + step) % ctxs
        s, h = unit_place(peer, u)
        return pltpu.make_async_remote_copy(
            src_ref=local_qkv.at[s, h],
            dst_ref=unit_qkv.at[u, :, tile(ctx, tok)],
            send_sem=qkv_send.at[u, step],
            recv_sem=qkv_recv.at[u, step],
            device_id={"ctx": peer},
            device_id_type=MESH_IDS,
        )

    def qkv_arrival(u, step):
        return pltpu.make_async_remote_copy(
            src_ref=local_qkv.at[0, 0],
            dst_ref=unit_qkv.at[u, :, tile((ctx + ctxs - step) % ctxs, tok)],
            send_sem=qkv_send.at[u, step],
            recv_sem=qkv_recv.at[u, step],
            device_id={"ctx": (ctx + step) % ctxs},
            device_id_type=MESH_IDS,
        )

    def qkv_own(u):
        s, h = unit_place(ctx, u)
        return pltpu.make_async_copy(
            local_qkv.at[s, h], unit_qkv.at[u, :, tile(ctx, tok)], unit_sem.at[0, u]
        )

    def context_place(device, u):
        s, h = unit_place(device, u)
        return context.at[tile(s, tok), tile(h, HEAD_DIM)]

    def context_copy(u, step):
        peer = (ctx + step) % ctxs
        return pltpu.make_async_remote_copy(
            src_ref=unit_out.at[u, tile(peer, tok)],
            dst_ref=context_place(ctx, u),
            send_sem=ctx_send.at[u, step],
            recv_sem=ctx_recv.at[u, step],
            device_id={"ctx": peer},
            device_id_type=MESH_IDS,
        )

    def context_arrival(u, step):
        return pltpu.make_async_remote_copy(
            src_ref=unit_out.at[u, tile(ctx, tok)],
            dst_ref=context_place((ctx + ctxs - step) % ctxs, u),
            send_sem=ctx_send.at[u, step],
            recv_sem=ctx_recv.at[u, step],
            device_id={"ctx": (ctx + step) % ctxs},
            device_id_type=MESH_IDS,
        )

    def context_own(u):
        return pltpu.make_async_copy(
            unit_out.at[u, tile(ctx, tok)], context_place(ctx, u), unit_sem.at[1, u]
        )

    def go_copy(u, step):
        peer = (ctx + step) % ctxs
        s, h = unit_place(peer, u)
        return pltpu.make_async_remote_copy(
            src_ref=context_grad.at[tile(s, tok), tile(h, HEAD_DIM)],
            dst_ref=unit_go.at[u, tile(ctx, tok)],
            send_sem=go_send.at[u, step],
            recv_sem=go_recv.at[u, step],
            device_id={"ctx": peer},
            device_id_type=MESH_IDS,
        )

    def go_arrival(u, step):
        return pltpu.make_async_remote_copy(
            src_ref=context_grad.at[tile(0, tok), tile(0, HEAD_DIM)],
            dst_ref=unit_go.at[u, tile((ctx + ctxs - step) % ctxs, tok)],
            send_sem=go_send.at[u, step],
            recv_sem=go_recv.at[u, step],
            device_id={"ctx": (ctx + step) % ctxs},
            device_id_type=MESH_IDS,
        )

    def go_own(u):
        s, h = unit_place(ctx, u)
        return pltpu.make_async_copy(
            context_grad.at[tile(s, tok), tile(h, HEAD_DIM)],
            unit_go.at[u, tile(ctx, tok)],
            unit_sem.at[2, u],
        )

    def go_start(u):
        for step in range(1, ctxs):
            go_copy(u, step).start()
        go_own(u).start()

    def attend(u):
        qkv_own(u).wait()
        for step in range(1, ctxs):
            qkv_arrival(u, step).wait_recv()
        part = math.gcd(seq_all, 256)

        @pl.loop(0, seq_all // part)
        def _(i):
            rs = tile(i, part)
            scores = dot_nt(unit_qkv[u, 0, rs, :], unit_qkv[u, 1]) * (HEAD_DIM ** (-0.5))
            largest = jnp.max(scores, axis=-1, keepdims=True)
            raised = jnp.exp(scores - largest)
            total = jnp.sum(raised, axis=-1, keepdims=True)
            mixed = dot_nn(raised.astype(BF), unit_qkv[u, 2])
            unit_out[u, rs, :] = (mixed / total).astype(BF)

        for step in range(1, ctxs):
            context_copy(u, step).start()
        context_own(u).start()

    def context_ready(u):
        context_own(u).wait()
        for step in range(1, ctxs):
            context_arrival(u, step).wait_recv()

    def project_chunk(c):
        bring(hidden, c).wait()
        following = (c + 1) % chunks
        s = c // per_seq
        rs = tile(c % per_seq, rows)
        low = dot_nt(rows_in[...], md[picks[s]]).astype(BF)
        put_rank(3, c, low)
        rank_buf[...] = low
        heads_at_once = math.gcd(local_heads, 2)
        step = heads_at_once * HEAD_DIM

        @pl.loop(0, mix_width // step)
        def _(i):
            cs = tile(i, step)
            values = dot_nn(rows_in[...], stash[0:width, cs]) + dot_nn(rank_buf[...], mu[picks[s], :, cs])
            values = values.astype(BF)
            first = i * heads_at_once
            for k in range(heads_at_once):
                local_qkv[s, (first + k) % local_heads, (first + k) // local_heads, rs, :] = values[
                    :, k * HEAD_DIM : (k + 1) * HEAD_DIM
                ]

        bring(hidden, following).start()

    def project(s):
        @pl.loop(0, per_seq)
        def _(i):
            project_chunk(s * per_seq + i)

    def send_unit(u):
        qkv_own(u).start()
        for step in range(1, ctxs):
            qkv_copy(u, step).start()

    def job_of(number, rounds):
        safe = jnp.maximum(number, 0)
        chunk = safe % period
        valid = (number >= 0) & (chunk < chunks) & (safe < rounds * period)
        return valid, jnp.minimum(chunk, chunks - 1)

    comm = chain(
        ranks,
        half,
        block,
        me,
        acc,
        red_up,
        red_down,
        red_send,
        red_recv,
        cast_send,
        cast_recv,
        lambda number: job_of(number, 3),
    )

    def rows_of(c):
        return tile(c, rows)

    def spot(t, c, i=None):
        start = t * total + c * rows
        if i is None:
            return pl.ds(pl.multiple_of(start, rows), rows)
        return pl.ds(pl.multiple_of(start + i * block, block), block)

    def mixing_keep():
        return pltpu.make_async_copy(
            stash.at[pl.ds(0, width), pl.ds(0, mix_width)], mixing, mix_sem
        )

    def bring(source, c):
        return pltpu.make_async_copy(source.at[rows_of(c)], rows_in, in_sem)

    def keep(index, source, target, c):
        return pltpu.make_async_copy(source, target.at[rows_of(c)], out_sem.at[index])

    def put_rank(t, c, low):
        part_ranks[t, :, tile(c, rows)] = dot_nt(unit_rank[...], low).astype(BF)

    def rank_copy(t, step):
        return pltpu.make_async_remote_copy(
            src_ref=part_ranks.at[t],
            dst_ref=rank_in.at[t, step],
            send_sem=rank_send.at[t, step],
            recv_sem=rank_recv.at[t, step],
            device_id={"tensor": (me + step) % ranks},
            device_id_type=MESH_IDS,
        )

    def mean(values):
        return jnp.sum(values, axis=-1, keepdims=True) * (1.0 / width)

    def attend_part(c, s):
        mine = context[rows_of(c), :]
        low = dot_nt(mine, od[picks[s]]).astype(BF)
        put_rank(0, c, low)

        @pl.loop(0, width // tile_d)
        def _(i):
            cs = tile(i, tile_d)
            acc[c, :, cs] = (dot_nn(mine, w_out[:, cs]) + dot_nn(low, ou[picks[s], :, cs])).astype(BF)

    def forward_first(c, s):
        bring(hidden, c).wait()

        @pl.loop(0, rows // block)
        def _(i):
            rs = tile(i, block)
            total = rows_in[rs, :].astype(F32) + acc[c, rs, :].astype(F32)
            centred = total - mean(total)
            spread = lax.rsqrt(mean(centred * centred) + 1e-06)
            n = centred * spread
            stash[spot(0, c, i), :] = n.astype(BF)
            spreads[c, rs, :] = jnp.broadcast_to(spread, (block, 128))
            stage_d[rs, :] = (n * gains[0:1, :] + gains[1:2, :]).astype(BF)

        low = dot_nt(stage_d[...], ed[picks[s]]).astype(BF)
        put_rank(4, c, low)
        rank_buf[...] = low

        @pl.loop(0, hidden_units // tile_f)
        def _(i):
            cs = tile(i, tile_f)
            b = dot_nn(stage_d[...], w_exp[:, cs]) + dot_nn(rank_buf[...], eu[picks[s], :, cs])
            square = b * b
            t = jnp.tanh(GELU_C * b * (1.0 + GELU_A * square))
            upper = 0.5 * (1.0 + t)
            stage_f[:, cs] = (b * upper).astype(BF)
            stash[spot(1, c), cs] = (
                upper
                + (0.5 * GELU_C) * b * (1.0 - t * t) * (1.0 + (3.0 * GELU_A) * square)
            ).astype(BF)

    def forward_second(c, s):
        low = dot_nt(stage_f[...], cd[picks[s]]).astype(BF)
        put_rank(1, c, low)
        rank_buf[...] = low

        @pl.loop(0, width // tile_d)
        def _(i):
            cs = tile(i, tile_d)
            acc[c, :, cs] = (
                dot_nn(stage_f[...], w_con[:, cs]) + dot_nn(rank_buf[...], cu[picks[s], :, cs])
            ).astype(BF)

        keep(0, stage_d, first_low, c).start()
        keep(1, stage_f, active, c).start()

    def back_first(c, s):
        bring(cotangent, c).wait()

        @pl.loop(0, rows // block)
        def _(i):
            rs = tile(i, block)
            first = stash[spot(0, c, i), :].astype(F32) * gains[0:1, :] + gains[1:2, :]
            total = first + acc[c, rs, :].astype(F32)
            centred = total - mean(total)
            spread = lax.rsqrt(mean(centred * centred) + 1e-06)
            n = centred * spread
            stage_d[rs, :] = (n * gains[2:3, :] + gains[3:4, :]).astype(BF)
            g = rows_in[rs, :].astype(F32) * gains[2:3, :]
            stash[spot(2, c, i), :] = (spread * (g - mean(g) - n * mean(g * n))).astype(BF)

        low = dot_nt(stash[spot(2, c), :], cu[picks[s]]).astype(BF)
        put_rank(5, c, low)
        rank_buf[...] = low

        @pl.loop(0, hidden_units // tile_f)
        def _(i):
            cs = tile(i, tile_f)
            da = dot_nt(stash[spot(2, c), :], w_con[cs, :]) + dot_nn(rank_buf[...], cd[picks[s], :, cs])
            stage_f[:, cs] = (da * stash[spot(1, c), cs].astype(F32)).astype(BF)

    def back_second(c, s):
        low = dot_nt(stage_f[...], eu[picks[s]]).astype(BF)
        put_rank(2, c, low)
        rank_buf[...] = low

        @pl.loop(0, width // tile_d)
        def _(i):
            cs = tile(i, tile_d)
            acc[c, :, cs] = (
                dot_nt(stage_f[...], w_exp[cs, :]) + dot_nn(rank_buf[...], ed[picks[s], :, cs])
            ).astype(BF)

        keep(0, stage_d, hidden_out, c).start()
        keep(1, stage_f, before_grad, c).start()
        keep(2, stash.at[spot(2, c)], second_low, c).start()

    def last_first(c, s):
        @pl.loop(0, rows // block)
        def _(i):
            rs = tile(i, block)
            n = stash[spot(0, c, i), :].astype(F32)
            g = (stash[spot(2, c, i), :].astype(F32) + acc[c, rs, :].astype(F32)) * gains[0:1, :]
            spread = spreads[c, rs, 0:1]
            stage_d[rs, :] = (spread * (g - mean(g) - n * mean(g * n))).astype(BF)

    def last_second(c, s):
        low = dot_nt(stage_d[...], ou[picks[s]]).astype(BF)
        put_rank(6, c, low)
        rank_buf[...] = low

        @pl.loop(0, heads // tile_h)
        def _(i):
            cs = tile(i, tile_h)
            context_grad[rows_of(c), cs] = (
                dot_nt(stage_d[...], w_out[cs, :]) + dot_nn(rank_buf[...], od[picks[s], :, cs])
            ).astype(BF)

        keep(0, stage_d, attn_low, c).start()

    seqs = chunks // per_seq
    flowing = units == seqs
    bring(hidden, 0).start()
    mixing_gather()
    weight_finish(0)
    along_start(1)
    across_start(1)
    mixing_keep().start()
    if flowing:
        for u in range(min(2, units)):
            project(u)
            send_unit(u)
    else:
        pl.loop(0, seqs)(project)
        for u in range(units):
            send_unit(u)
    weight_relay(1)

    @pl.loop(0, lead + 3 * period + chunks)
    def _(now):
        tick = now - lead
        stage = jnp.maximum(tick, 0) // period
        valid, c = job_of(tick, 4)
        s = c // per_seq
        last_valid, last_c = job_of(tick - 1, 4)
        last_stage = jnp.maximum(tick - 1, 0) // period

        comm(tick, 0)

        @pl.when(last_valid & (last_stage >= 1))
        def _():
            keep(0, stage_d, first_low, last_c).wait()

        @pl.when(last_valid & (last_stage >= 1) & (last_stage <= 2))
        def _():
            keep(1, stage_f, active, last_c).wait()

        @pl.when(last_valid & (last_stage == 2))
        def _():
            keep(2, stash.at[spot(2, last_c)], second_low, last_c).wait()

        pl.when(now == 1)(lambda: weight_forward(1))
        pl.when((now % per_seq == 0) & (now < units * per_seq))(lambda: attend(now // per_seq))
        if flowing:

            @pl.when((now % per_seq == 1) & (now < (units - 2) * per_seq))
            def _():
                project(now // per_seq + 2)
                send_unit(now // per_seq + 2)

        @pl.when((now % per_seq == 1) & (now > per_seq) & (now <= PIECES * per_seq + 1))
        def _():
            p = now // per_seq - 1
            weight_relay(2, p)
            weight_relay(3, p)

        @pl.when((now % per_seq == 1) & (now < PIECES * per_seq))
        def _():
            for w in (2, 3):
                along_start(w, now // per_seq)
                across_start(w, now // per_seq)

        @pl.when((now % per_seq == 0) & (now > per_seq) & (now <= (PIECES + 1) * per_seq))
        def _():
            p = now // per_seq - 2
            weight_forward(2, p)
            weight_forward(3, p)

        @pl.when(now == lead + period)
        def _():
            for p in range(PIECES):
                weight_finish(2, p)
                weight_finish(3, p)

        pl.when(now == lead)(lambda: weight_finish(1))

        @pl.when(now == lead + period - 2)
        def _():
            mixing_keep().wait()
            weight_sent(0)
            side_sent()

        for t in range(3):

            @pl.when(tick == (t + 1) * period)
            def _(t=t):
                for step in range(1, ranks):
                    rank_copy(t, step).start()

        pl.when((tick >= 0) & (tick % per_seq == 0) & (tick < units * per_seq))(
            lambda: context_ready(s)
        )

        pl.when(valid & (stage == 1))(lambda: forward_first(c, s))
        pl.when(valid & (stage == 2))(lambda: back_first(c, s))
        pl.when(valid & (stage == 3))(lambda: last_first(c, s))

        comm(tick, 1)

        pl.when(valid & (stage == 0))(lambda: attend_part(c, s))
        pl.when(valid & (stage == 1))(lambda: forward_second(c, s))
        pl.when(valid & (stage == 2))(lambda: back_second(c, s))
        pl.when(valid & (stage == 3))(lambda: last_second(c, s))
        if flowing:
            pl.when(valid & (stage == 3) & (c % per_seq == per_seq - 1))(lambda: go_start(s))

        next_valid, next_c = job_of(tick + 1, 4)
        next_stage = jnp.maximum(tick + 1, 0) // period
        pl.when(next_valid & (next_stage == 1) & (next_c > 0))(
            lambda: bring(hidden, next_c).start()
        )
        pl.when(next_valid & (next_stage == 2))(lambda: bring(cotangent, next_c).start())

    keep(0, stage_d, attn_low, chunks - 1).wait()
    for t in range(3):
        value = part_ranks[t].astype(F32)
        for step in range(1, ranks):
            rank_copy(t, step).wait_recv()
            value = value + rank_in[t, step].astype(F32)
        full_ranks[t] = value.astype(BF)
    for t in range(3):
        for step in range(1, ranks):
            rank_copy(t, step).wait_send()
    weight_sent(1)
    for p in range(PIECES):
        weight_sent(2, p)
        weight_sent(3, p)
    for u in range(units):
        if not flowing:
            go_start(u)
        for step in range(1, ctxs):
            qkv_copy(u, step).wait_send()
            context_copy(u, step).wait_send()
    for u in range(units):
        go_own(u).wait()
        for step in range(1, ctxs):
            go_arrival(u, step).wait_recv()
            go_copy(u, step).wait_send()


def enter(others):
    barrier = pltpu.get_barrier_semaphore()
    for other in others:
        pl.semaphore_signal(barrier, inc=1, device_id=other, device_id_type=MESH_IDS)
    pl.semaphore_wait(barrier, len(others))


def middle(hidden, cotangent, shards, picked, gains, tok, picks):
    total, width = hidden.shape
    mix_width = shards[0].shape[1]
    heads, hidden_units = shards[1].shape[0], shards[2].shape[1]
    ranks, dps, ctxs = (lax.axis_size(name) for name in ("tensor", "dp", "ctx"))
    seqs, rank = picks.shape[0], picked[0].shape[1]
    local_heads = heads // HEAD_DIM
    units = seqs * local_heads // ctxs
    rows = math.gcd(tok, CHUNK_ROWS)
    chunks = total // rows
    period = max(chunks, 2 * ranks)
    sizes = (ranks, dps, ctxs, chunks, rows, tok // rows, period)
    chips = dps * ctxs // 2
    vm = pl.BlockSpec(memory_space=pltpu.VMEM)
    hb = pl.BlockSpec(memory_space=pl.ANY)
    sm = pl.BlockSpec(memory_space=pltpu.SMEM)
    half = rows // 2
    dma = pltpu.SemaphoreType.DMA

    def shape(*dims):
        return jax.ShapeDtypeStruct(dims, BF)

    return pl.pallas_call(
        functools.partial(middle_kernel, sizes),
        out_shape=(
            shape(total, width),
            shape(total, width),
            shape(total, hidden_units),
            shape(total, width),
            shape(total, hidden_units),
            shape(total, width),
            shape(width, mix_width),
            shape(units, tok * ctxs, HEAD_DIM),
            shape(7, rank, total),
            shape(3, rank, total),
            shape(total, heads),
            shape(units, 3, tok * ctxs, HEAD_DIM),
            shape(units, tok * ctxs, HEAD_DIM),
        ),
        in_specs=[hb] * 6 + [vm] * 10 + [sm],
        out_specs=(hb,) * 7 + (vm,) * 6,
        scratch_shapes=[
            pltpu.VMEM((total, heads), BF),
            pltpu.VMEM((seqs, local_heads, 3, tok, HEAD_DIM), BF),
            pltpu.VMEM((heads, width), BF),
            pltpu.VMEM((width, hidden_units), BF),
            pltpu.VMEM((hidden_units, width), BF),
            pltpu.VMEM((chunks, rows, width), BF),
            pltpu.VMEM((chunks, half, width), BF),
            pltpu.VMEM((chunks, half, width), BF),
            pltpu.VMEM((3 * total, width), BF),
            pltpu.VMEM((chunks, rows, 128), F32),
            pltpu.VMEM((3, ranks, rank, total), BF),
            pltpu.VMEM((rows, width), BF),
            pltpu.VMEM((rows, hidden_units), BF),
            pltpu.VMEM((rows, width), BF),
            pltpu.VMEM((rows, rank), BF),
            dma(()),
            dma((3,)),
            dma((2, chunks)),
            dma((2, chunks)),
            dma((2, chunks)),
            dma((2, chunks)),
            dma((4, chips, PIECES)),
            dma((4, chips, PIECES)),
            dma((4, chips, PIECES)),
            dma((4, chips, PIECES)),
            dma((chips,)),
            dma((chips,)),
            dma((4, PIECES)),
            dma((3, ranks)),
            dma((3, ranks)),
            dma(()),
            dma((units, ctxs)),
            dma((units, ctxs)),
            dma((units, ctxs)),
            dma((units, ctxs)),
            dma((units, ctxs)),
            dma((units, ctxs)),
            dma((3, units)),
        ],
        compiler_params=pltpu.CompilerParams(
            collective_id=0, has_side_effects=True, vmem_limit_bytes=VMEM_BYTES
        ),
        cost_estimate=pl.CostEstimate(
            flops=8 * total * width * hidden_units + 4 * total * width * heads,
            bytes_accessed=16 * total * width,
            transcendentals=total * hidden_units,
        ),
    )(hidden, cotangent, *shards, *picked, gains, jnp.eye(rank, dtype=BF), picks)


def mixing_kernel(
    sizes,
    unit_go,
    unit_qkv,
    unit_out,
    mixing_far,
    mu,
    md,
    attn_low,
    unit_rank,
    hidden_far,
    mix_rank,
    row_hot,
    picks,
    input_grad,
    table_sum,
    grads,
    mixing,
    hidden,
    rank_part,
    rank_in,
    wide,
    table_part,
    table_in,
    unit_grad,
    sum_k,
    sum_v,
    acc,
    red_up,
    red_down,
    stage_d,
    rows_in,
    rank_buf,
    in_sem,
    out_sem,
    red_send,
    red_recv,
    cast_send,
    cast_recv,
    far_sem,
    grad_send,
    grad_recv,
    unit_sem,
    rank_send,
    rank_recv,
    part_send,
    part_recv,
    whole_send,
    whole_recv,
):
    ranks, dps, ctxs, chunks, rows, per_seq, group = sizes
    half = rows // 2
    width = mixing.shape[0]
    heads = grads.shape[2]
    local_heads = heads // HEAD_DIM
    units, seq_all = unit_go.shape[0], unit_go.shape[1]
    tok = seq_all // ctxs
    block = min(16, half)
    tile_d = math.gcd(width, 256)
    scale = HEAD_DIM ** (-0.5)
    me = lax.axis_index("tensor")
    ctx = lax.axis_index("ctx")
    dp = lax.axis_index("dp")
    parts = dps * ctxs
    index = dp * ctxs + ctx
    rank = mu.shape[1]
    tables, _, part_width = table_part.shape
    segments = parts // NADAPT
    tile_g = math.gcd(part_width, 256)

    def part_place(step):
        other = (index + step) % parts
        return {"dp": other // ctxs, "ctx": other % ctxs}

    enter(
        [{"tensor": (me + d) % ranks} for d in range(1, ranks)]
        + [part_place(d) for d in range(1, parts)]
    )

    def unit_place(device, u):
        return (device // local_heads) * units + u, device % local_heads

    def mixing_load():
        return pltpu.make_async_copy(mixing_far, mixing, far_sem.at[0])

    def hidden_load():
        return pltpu.make_async_copy(hidden_far, hidden, far_sem.at[1])

    def grads_place(device, u):
        s, h = unit_place(device, u)
        return grads.at[:, tile(s, tok), tile(h, HEAD_DIM)]

    def grad_copy(u, step):
        peer = (ctx + step) % ctxs
        return pltpu.make_async_remote_copy(
            src_ref=unit_grad.at[u, :, tile(peer, tok)],
            dst_ref=grads_place(ctx, u),
            send_sem=grad_send.at[u, step],
            recv_sem=grad_recv.at[u, step],
            device_id={"ctx": peer},
            device_id_type=MESH_IDS,
        )

    def grad_arrival(u, step):
        return pltpu.make_async_remote_copy(
            src_ref=unit_grad.at[u, :, tile(ctx, tok)],
            dst_ref=grads_place((ctx + ctxs - step) % ctxs, u),
            send_sem=grad_send.at[u, step],
            recv_sem=grad_recv.at[u, step],
            device_id={"ctx": (ctx + step) % ctxs},
            device_id_type=MESH_IDS,
        )

    def grad_own(u):
        return pltpu.make_async_copy(
            unit_grad.at[u, :, tile(ctx, tok)], grads_place(ctx, u), unit_sem.at[u]
        )

    def attend_back(u):
        part = math.gcd(seq_all, 256)
        sum_k[...] = jnp.zeros_like(sum_k)
        sum_v[...] = jnp.zeros_like(sum_v)

        @pl.loop(0, seq_all // part)
        def _(i):
            rs = tile(i, part)
            queries = unit_qkv[u, 0, rs, :]
            go = unit_go[u, rs, :]
            scores = dot_nt(queries, unit_qkv[u, 1]) * scale
            raised = jnp.exp(scores - jnp.max(scores, axis=-1, keepdims=True))
            probs = raised * (1.0 / jnp.sum(raised, axis=-1, keepdims=True))
            delta = jnp.sum(
                go.astype(F32) * unit_out[u, rs, :].astype(F32), axis=-1, keepdims=True
            )
            dscores = (probs * (dot_nt(go, unit_qkv[u, 2]) - delta)).astype(BF)
            unit_grad[u, 0, rs, :] = (scale * dot_nn(dscores, unit_qkv[u, 1])).astype(BF)
            sum_k[...] += dot_tn(dscores, queries)
            sum_v[...] += dot_tn(probs.astype(BF), go)

        unit_grad[u, 1] = (scale * sum_k[...]).astype(BF)
        unit_grad[u, 2] = sum_v[...].astype(BF)
        for step in range(1, ctxs):
            grad_copy(u, step).start()
        grad_own(u).start()

    def grads_ready(u):
        grad_own(u).wait()
        for step in range(1, ctxs):
            grad_arrival(u, step).wait_recv()

    mixing_load().start()
    hidden_load().start()

    def job_of(number):
        return (number >= 0) & (number < chunks), jnp.clip(number, 0, chunks - 1)

    comm = chain(
        ranks, half, block, me, acc, red_up, red_down, red_send, red_recv, cast_send, cast_recv, job_of
    )

    def rows_of(c):
        return tile(c, rows)

    def bring(c):
        return pltpu.make_async_copy(attn_low.at[rows_of(c)], rows_in, in_sem)

    def keep(c):
        return pltpu.make_async_copy(stage_d, input_grad.at[rows_of(c)], out_sem)

    def back_part(c, s):
        rs = pl.ds(pl.multiple_of(c * rows, group * rows), group * rows)
        low = jnp.zeros((group * rows, mu.shape[1]), F32)
        for j in range(3):
            low = low + dot_nt(grads[j, rs, :], mu[picks[s], :, pl.ds(j * heads, heads)])
        low = low.astype(BF)
        rank_part[:, pl.ds(pl.multiple_of(c * rows, group * rows), group * rows)] = dot_nt(
            unit_rank[...], low
        ).astype(BF)
        rank_buf[...] = low

        @pl.loop(0, width // tile_d)
        def _(i):
            cs = tile(i, tile_d)
            total = dot_nn(rank_buf[...], md[picks[s], :, cs])
            for j in range(3):
                total = total + dot_nt(grads[j, rs, :], mixing[cs, pl.ds(j * heads, heads)])
            total = total.astype(BF)
            for k in range(group):
                acc[c + k, :, cs] = total[k * rows : (k + 1) * rows, :]

    def final_part(c):
        bring(c).wait()

        @pl.loop(0, rows // block)
        def _(i):
            rs = tile(i, block)
            stage_d[rs, :] = (rows_in[rs, :].astype(F32) + acc[c, rs, :].astype(F32)).astype(BF)

        keep(c).start()

    def rank_copy(step):
        return pltpu.make_async_remote_copy(
            src_ref=rank_part,
            dst_ref=rank_in.at[step],
            send_sem=rank_send.at[step],
            recv_sem=rank_recv.at[step],
            device_id={"tensor": (me + step) % ranks},
            device_id_type=MESH_IDS,
        )

    def part_copy(step):
        return pltpu.make_async_remote_copy(
            src_ref=table_part.at[(index + step) % parts],
            dst_ref=table_in.at[step],
            send_sem=part_send.at[step],
            recv_sem=part_recv.at[step],
            device_id=part_place(step),
            device_id_type=MESH_IDS,
        )

    def whole_copy(step):
        return pltpu.make_async_remote_copy(
            src_ref=table_sum.at[index],
            dst_ref=table_sum.at[index],
            send_sem=whole_send.at[step],
            recv_sem=whole_recv.at[step],
            device_id=part_place(step),
            device_id_type=MESH_IDS,
        )

    def whole_arrival(step):
        return pltpu.make_async_remote_copy(
            src_ref=table_sum.at[index],
            dst_ref=table_sum.at[(index + parts - step) % parts],
            send_sem=whole_send.at[step],
            recv_sem=whole_recv.at[step],
            device_id=part_place(step),
            device_id_type=MESH_IDS,
        )

    def put_table(column, values):
        segment = column // part_width
        cs = pl.ds(pl.multiple_of(column % part_width, tile_g), tile_g)
        for n in range(NADAPT):
            table_part[n * segments + segment, :, cs] = values[n * rank : (n + 1) * rank, :].astype(
                BF
            )

    def make_tables():
        value = rank_part[...].astype(F32)
        for step in range(1, ranks):
            rank_copy(step).wait_recv()
            value = value + rank_in[step].astype(F32)
        for n in range(NADAPT):
            hot = row_hot[n : n + 1, :]
            wide[0, pl.ds(n * rank, rank), :] = (value * hot).astype(BF)
            wide[1, pl.ds(n * rank, rank), :] = (mix_rank[...].astype(F32) * hot).astype(BF)

        @pl.loop(0, width // tile_g)
        def _(i):
            put_table(i * tile_g, dot_nn(wide[0], hidden[:, tile(i, tile_g)]))

        for j in range(3):

            @pl.loop(0, heads // tile_g)
            def _(i):
                put_table(
                    width + j * heads + i * tile_g, dot_nn(wide[1], grads[j, :, tile(i, tile_g)])
                )

        for step in range(1, parts):
            part_copy(step).start()

    def sum_tables():
        value = table_part[index].astype(F32)
        for step in range(1, parts):
            part_copy(step).wait_recv()
            value = value + table_in[step].astype(F32)
        table_sum[index] = value.astype(BF)
        for step in range(1, parts):
            whole_copy(step).start()

    delay = 2 * ranks

    @pl.loop(0, per_seq + chunks + delay)
    def _(now):
        tick = now - per_seq

        @pl.when(tick == chunks)
        def _():
            for step in range(1, ranks):
                rank_copy(step).start()

        valid, c = job_of(tick)
        final, c_final = job_of(tick - delay)
        before, c_before = job_of(tick - delay - 1)
        coming, c_coming = job_of(tick - delay + 1)
        s = c // per_seq

        comm(tick, 0)

        pl.when((now % per_seq == 0) & (now < units * per_seq))(lambda: attend_back(now // per_seq))
        pl.when((tick >= 0) & (tick % per_seq == 0) & (tick < units * per_seq))(
            lambda: grads_ready(s)
        )
        comm(tick, 1)

        pl.when(tick == 0)(lambda: mixing_load().wait())
        pl.when(valid & (tick % group == 0))(lambda: back_part(c, s))

        @pl.when(tick == chunks + 1)
        def _():
            hidden_load().wait()
            make_tables()

        pl.when(tick == chunks + 4)(sum_tables)

        pl.when(before)(lambda: keep(c_before).wait())
        pl.when(final)(lambda: final_part(c_final))
        pl.when(coming)(lambda: bring(c_coming).start())

    keep(chunks - 1).wait()
    for step in range(1, ranks):
        rank_copy(step).wait_send()
    for step in range(1, parts):
        whole_arrival(step).wait_recv()
    for step in range(1, parts):
        part_copy(step).wait_send()
        whole_copy(step).wait_send()
    for u in range(units):
        for step in range(1, ctxs):
            grad_copy(u, step).wait_send()


def mixing_back(
    unit_go, unit_qkv, unit_out, mixing, picked, attn_low, hidden, mix_rank, row_hot, picks
):
    mu, md = picked
    total, width = attn_low.shape
    heads = mixing.shape[1] // 3
    ranks, dps, ctxs = (lax.axis_size(name) for name in ("tensor", "dp", "ctx"))
    parts = dps * ctxs
    part_width = (width + 3 * heads) * NADAPT // parts
    units, _, seq_all, _ = unit_qkv.shape
    tok = seq_all // ctxs
    rank = mu.shape[1]
    rows = math.gcd(tok, LAST_ROWS)
    chunks = total // rows
    per_seq = tok // rows
    group = math.gcd(per_seq, 2)
    half = rows // 2
    sizes = (ranks, dps, ctxs, chunks, rows, per_seq, group)
    vm = pl.BlockSpec(memory_space=pltpu.VMEM)
    hb = pl.BlockSpec(memory_space=pl.ANY)
    sm = pl.BlockSpec(memory_space=pltpu.SMEM)
    dma = pltpu.SemaphoreType.DMA
    return pl.pallas_call(
        functools.partial(mixing_kernel, sizes),
        out_shape=(
            jax.ShapeDtypeStruct((total, width), BF),
            jax.ShapeDtypeStruct((parts, rank, part_width), BF),
        ),
        in_specs=[vm] * 3 + [hb] + [vm] * 2 + [hb, vm, hb] + [vm] * 2 + [sm],
        out_specs=(hb, vm),
        scratch_shapes=[
            pltpu.VMEM((3, total, heads), BF),
            pltpu.VMEM((width, 3 * heads), BF),
            pltpu.VMEM((total, width), BF),
            pltpu.VMEM((rank, total), BF),
            pltpu.VMEM((ranks, rank, total), BF),
            pltpu.VMEM((2, NADAPT * rank, total), BF),
            pltpu.VMEM((parts, rank, part_width), BF),
            pltpu.VMEM((parts, rank, part_width), BF),
            pltpu.VMEM((units, 3, seq_all, HEAD_DIM), BF),
            pltpu.VMEM((seq_all, HEAD_DIM), F32),
            pltpu.VMEM((seq_all, HEAD_DIM), F32),
            pltpu.VMEM((chunks, rows, width), BF),
            pltpu.VMEM((chunks, half, width), BF),
            pltpu.VMEM((chunks, half, width), BF),
            pltpu.VMEM((rows, width), BF),
            pltpu.VMEM((rows, width), BF),
            pltpu.VMEM((group * rows, rank), BF),
            dma(()),
            dma(()),
            dma((2, chunks)),
            dma((2, chunks)),
            dma((2, chunks)),
            dma((2, chunks)),
            dma((2,)),
            dma((units, ctxs)),
            dma((units, ctxs)),
            dma((units,)),
            dma((ranks,)),
            dma((ranks,)),
            dma((parts,)),
            dma((parts,)),
            dma((parts,)),
            dma((parts,)),
        ],
        compiler_params=pltpu.CompilerParams(
            collective_id=1, has_side_effects=True, vmem_limit_bytes=VMEM_LAST
        ),
        cost_estimate=pl.CostEstimate(
            flops=6 * total * width * heads + 10 * units * seq_all * seq_all * HEAD_DIM,
            bytes_accessed=8 * total * width,
            transcendentals=units * seq_all * seq_all,
        ),
    )(
        unit_go,
        unit_qkv,
        unit_out,
        mixing,
        mu,
        md,
        attn_low,
        jnp.eye(rank, dtype=BF),
        hidden,
        mix_rank,
        row_hot,
        picks,
    )


def per_device(
    hidden_in,
    output_cotangent,
    adapter_index,
    mixing_weight,
    output_weight,
    expand_weight,
    contract_weight,
    first_gain,
    first_shift,
    second_gain,
    second_shift,
    mixing_down,
    mixing_up,
    output_down,
    output_up,
    expand_down,
    expand_up,
    contract_down,
    contract_up,
):
    seq_count, tok_count, model_width = hidden_in.shape
    local_heads = mixing_weight.shape[2] // HEAD_DIM
    local_width = mixing_weight.shape[2]
    rows_all = seq_count * tok_count
    adapter_ids = jnp.arange(NADAPT, dtype=jnp.int32)
    onehot_low = (adapter_index == adapter_ids[None, :]).astype(jnp.bfloat16)
    picks = adapter_index.reshape(-1)
    rank = mixing_down.shape[1]
    mixing_flat = mixing_weight.reshape(mixing_weight.shape[0], 3 * local_width)
    hidden_rows = hidden_in.reshape(rows_all, model_width)
    mixing_up_flat = mixing_up.reshape(NADAPT, rank, 3 * local_width)
    gains = jnp.stack([first_gain, first_shift, second_gain, second_shift])
    (
        out_rows,
        first_low,
        active_low,
        second_low,
        before_low,
        attn_low,
        mixing_full,
        unit_go,
        part_ranks,
        full_ranks,
        context,
        unit_qkv,
        unit_out,
    ) = middle(
        hidden_rows,
        output_cotangent.reshape(rows_all, model_width),
        (mixing_flat, output_weight, expand_weight, contract_weight),
        (
            mixing_down,
            mixing_up_flat,
            output_down,
            output_up,
            expand_down,
            expand_up,
            contract_down,
            contract_up,
        ),
        gains,
        tok_count,
        picks,
    )
    row_hot = jnp.repeat(onehot_low.T, tok_count, axis=1)

    def table_grad(ranks, values):
        wide = (row_hot[:, None, :] * ranks[None, :, :]).reshape(-1, rows_all)
        part = jnp.einsum("kn,nd->kd", wide, values, preferred_element_type=jnp.float32)
        return part.astype(jnp.bfloat16).reshape(NADAPT, rank, values.shape[1])

    early = (
        table_grad(part_ranks[6], context),
        table_grad(full_ranks[0], attn_low),
        table_grad(full_ranks[2], first_low),
        table_grad(part_ranks[4], before_low),
        table_grad(part_ranks[5], active_low),
        table_grad(full_ranks[1], second_low),
    )
    early, unit_go = lax.optimization_barrier((early, unit_go))
    input_rows, late = mixing_back(
        unit_go,
        unit_qkv,
        unit_out,
        mixing_full,
        (mixing_up_flat, mixing_down),
        attn_low,
        hidden_rows,
        part_ranks[3],
        row_hot.astype(jnp.float32),
        picks,
    )
    early = lax.psum(early, ("dp", "ctx"))
    late = late.reshape(NADAPT, -1, rank, late.shape[2]).swapaxes(1, 2).reshape(NADAPT, rank, -1)
    late = (
        late[:, :, :model_width],
        late[:, :, model_width:].reshape(NADAPT, rank, 3, local_width),
    )
    summed = tuple(part.astype(jnp.float32) for part in late + early)
    return (
        out_rows.reshape(hidden_in.shape),
        input_rows.reshape(hidden_in.shape),
    ) + summed


def solution(mesh):
    return jax.shard_map(
        per_device,
        mesh=mesh,
        in_specs=(
            P("dp", "ctx", None),
            P("dp", "ctx", None),
            P("dp", None),
            P(("dp", "ctx"), None, "tensor"),
            P("tensor", ("dp", "ctx")),
            P(("dp", "ctx"), "tensor"),
            P("tensor", ("dp", "ctx")),
            P(),
            P(),
            P(),
            P(),
            P(),
            P(None, None, None, "tensor"),
            P(None, None, "tensor"),
            P(),
            P(),
            P(None, None, "tensor"),
            P(None, None, "tensor"),
            P(),
        ),
        out_specs=(
            P("dp", "ctx", None),
            P("dp", "ctx", None),
            P(),
            P(None, None, None, "tensor"),
            P(None, None, "tensor"),
            P(),
            P(),
            P(None, None, "tensor"),
            P(None, None, "tensor"),
            P(),
        ),
        check_vma=False,
    )
```

```python
import functools
import math

import jax
import jax.numpy as jnp
from jax import lax
from jax.experimental import pallas as pl
from jax.experimental.pallas import tpu as pltpu
from jax.sharding import PartitionSpec as P

HEAD_DIM = 128
NADAPT = 8
CHUNK_ROWS = 128
LAST_ROWS = 128
VMEM_BYTES = 62 * 2**20
VMEM_LAST = 56 * 2**20
PIECES = 4
EARLY_AT = 3


BF = jnp.bfloat16
F32 = jnp.float32
MESH_IDS = pl.DeviceIdType.MESH
RANK_ROWS = 16
GELU_C = 0.7978845608028654
GELU_A = 0.044715


def dot_nn(a, b):
    return lax.dot_general(a, b, (((1,), (0,)), ((), ())), preferred_element_type=F32)


def dot_nt(a, b):
    return lax.dot_general(a, b, (((1,), (1,)), ((), ())), preferred_element_type=F32)


def dot_tn(a, b):
    return lax.dot_general(a, b, (((0,), (0,)), ((), ())), preferred_element_type=F32)


def tile(index, size):
    return pl.ds(pl.multiple_of(index * size, size), size)


def chain(
    ranks, half, block, me, acc, red_up, red_down, red_send, red_recv, cast_send, cast_recv, job_of
):
    def comm(tick, way):
        upward = way == 0
        place = me if upward else ranks - 1 - me
        ahead = me + 1 if upward else me - 1
        behind = me - 1 if upward else me + 1
        red = red_up if upward else red_down
        part = pl.ds(way * half, half)

        def red_copy(c):
            return pltpu.make_async_remote_copy(
                src_ref=red.at[c],
                dst_ref=red.at[c],
                send_sem=red_send.at[way, c],
                recv_sem=red_recv.at[way, c],
                device_id={"tensor": ahead},
                device_id_type=MESH_IDS,
            )

        def cast_copy(c):
            return pltpu.make_async_remote_copy(
                src_ref=acc.at[c, part],
                dst_ref=acc.at[c, part],
                send_sem=cast_send.at[way, c],
                recv_sem=cast_recv.at[way, c],
                device_id={"tensor": behind},
                device_id_type=MESH_IDS,
            )

        old_red, c_old = job_of(tick - 2 - place)

        @pl.when(old_red & (place < ranks - 1))
        def _():
            red_copy(c_old).wait_send()

        old_cast, c_cast = job_of(tick - 2 * ranks + place)

        @pl.when(old_cast & (place > 0))
        def _():
            cast_copy(c_cast).wait_send()

        now_red, c = job_of(tick - 1 - place)

        @pl.when(now_red & (place == 0))
        def _():
            red[c] = acc[c, part, :]

        @pl.when(now_red & (place > 0))
        def _():
            red_copy(c).wait_recv()

        @pl.when(now_red & (place > 0) & (place < ranks - 1))
        def _():
            @pl.loop(0, half // block)
            def _(i):
                rs = tile(i, block)
                own = acc[c, pl.ds(pl.multiple_of(way * half + i * block, block), block), :]
                red[c, rs, :] = (red[c, rs, :].astype(F32) + own.astype(F32)).astype(BF)

        @pl.when(now_red & (place < ranks - 1))
        def _():
            red_copy(c).start()

        @pl.when(now_red & (place == ranks - 1))
        def _():
            @pl.loop(0, half // block)
            def _(i):
                rs = tile(i, block)
                own_rs = pl.ds(pl.multiple_of(way * half + i * block, block), block)
                acc[c, own_rs, :] = (
                    red[c, rs, :].astype(F32) + acc[c, own_rs, :].astype(F32)
                ).astype(BF)

            cast_copy(c).start()

        now_cast, cc = job_of(tick - (2 * ranks - 1 - place))

        @pl.when(now_cast & (place < ranks - 1))
        def _():
            cast_copy(cc).wait_recv()

        @pl.when(now_cast & (place > 0) & (place < ranks - 1))
        def _():
            cast_copy(cc).start()
    return comm


def attention_back(unit_qkv, unit_go, unit_out, unit_grad, sum_k, sum_v, u, v):
    seq_all = unit_qkv.shape[2]
    scale = HEAD_DIM ** (-0.5)
    part = math.gcd(seq_all, 256)
    sum_k[...] = jnp.zeros_like(sum_k)
    sum_v[...] = jnp.zeros_like(sum_v)

    @pl.loop(0, seq_all // part)
    def _(i):
        rs = tile(i, part)
        queries = unit_qkv[u, 0, rs, :]
        go = unit_go[u, rs, :]
        scores = dot_nt(queries, unit_qkv[u, 1]) * scale
        raised = jnp.exp(scores - jnp.max(scores, axis=-1, keepdims=True))
        probs = raised * (1.0 / jnp.sum(raised, axis=-1, keepdims=True))
        delta = jnp.sum(
            go.astype(F32) * unit_out[u, rs, :].astype(F32), axis=-1, keepdims=True
        )
        dscores = (probs * (dot_nt(go, unit_qkv[u, 2]) - delta)).astype(BF)
        unit_grad[v, 0, rs, :] = (scale * dot_nn(dscores, unit_qkv[u, 1])).astype(BF)
        sum_k[...] += dot_tn(dscores, queries)
        sum_v[...] += dot_tn(probs.astype(BF), go)

    unit_grad[v, 1] = (scale * sum_k[...]).astype(BF)
    unit_grad[v, 2] = sum_v[...].astype(BF)


def early_units(total, tok, units):
    rows = math.gcd(tok, CHUNK_ROWS)
    return int(units == total // tok and tok // rows >= 2 and units >= 2)


def middle_kernel(
    sizes,
    hidden,
    cotangent,
    shard_mix,
    shard_out,
    shard_exp,
    shard_con,
    md,
    mu,
    od,
    ou,
    ed,
    eu,
    cd,
    cu,
    gains,
    unit_rank,
    picks,
    hidden_out,
    first_low,
    active,
    second_low,
    before_grad,
    attn_low,
    mixing,
    unit_go,
    early_grads,
    part_ranks,
    full_ranks,
    context,
    unit_qkv,
    unit_out,
    context_grad,
    unit_grad,
    sum_k,
    sum_v,
    local_qkv,
    w_out,
    w_exp,
    w_con,
    acc,
    red_up,
    red_down,
    stash,
    spreads,
    rank_in,
    stage_d,
    stage_f,
    rows_in,
    rank_buf,
    in_sem,
    out_sem,
    red_send,
    red_recv,
    cast_send,
    cast_recv,
    peer_send,
    peer_recv,
    twin_send,
    twin_recv,
    side_send,
    side_recv,
    own_sem,
    rank_send,
    rank_recv,
    mix_sem,
    qkv_send,
    qkv_recv,
    ctx_send,
    ctx_recv,
    go_send,
    go_recv,
    early_send,
    early_recv,
    unit_sem,
):
    ranks, dps, ctxs, chunks, rows, per_seq, period = sizes
    half = rows // 2
    width = hidden.shape[1]
    hidden_units = w_exp.shape[1]
    heads = w_out.shape[0]
    block = min(16, half)
    tile_f = math.gcd(hidden_units, 256)
    tile_d = math.gcd(width, 256)
    tile_h = math.gcd(heads, 256)
    me = lax.axis_index("tensor")
    dp = lax.axis_index("dp")
    ctx = lax.axis_index("ctx")
    pairs = ctxs // 2
    core = ctx % 2
    chips = dps * pairs
    chip = dp * pairs + ctx // 2
    twin = {"ctx": ctx + 1 - 2 * core}
    lead = per_seq
    units, seq_all = unit_qkv.shape[0], unit_qkv.shape[2]
    tok = seq_all // ctxs
    local_heads = local_qkv.shape[1]

    def chip_block(step, which):
        row, column = step // pairs, step % pairs
        from_dp = (dp + dps - row) % dps
        from_chip = (ctx // 2 + pairs - column) % pairs
        return from_dp * ctxs + from_chip * 2 + which

    total = chunks * rows
    enter(
        [{"tensor": (me + d) % ranks} for d in range(1, ranks)]
        + [{"ctx": (ctx + d) % ctxs} for d in range(1, ctxs)]
        + [{"dp": (dp + d) % dps} for d in range(1, dps)]
    )

    shards = (shard_mix, shard_out, shard_exp, shard_con)
    fulls = (stash, w_out, w_exp, w_con)
    mix_width = shard_mix.shape[1]
    mix_half = shard_mix.shape[0] // 2

    def piece_of(w, p):
        if w < 2:
            return shards[w]
        return shards[w].at[tile(p, shards[w].shape[0] // PIECES)]

    def block_of(w, index, p):
        deep, wide = shards[w].shape
        if w == 0:
            return stash.at[tile(index, deep), pl.ds(0, mix_width)]
        if w == 1:
            return w_out.at[:, tile(index, wide)]
        if w == 2:
            return w_exp.at[tile(index * PIECES + p, deep // PIECES)]
        return w_con.at[tile(p, deep // PIECES), tile(index, wide)]

    def mix_piece(step, lower):
        start = chip_block(step, core) * (2 * mix_half) + lower * mix_half
        return stash.at[pl.ds(pl.multiple_of(start, mix_half), mix_half), pl.ds(0, mix_width)]

    def peer_copy(w, step, p=0):
        row, column = step // pairs, step % pairs
        block = block_of(w, chip_block(column, core), p)
        if row:
            target = {"dp": (dp + row) % dps}
        else:
            target = {"ctx": (ctx + 2 * column) % ctxs}
        own = block_of(w, chip_block(0, core), p)
        if w == 0 and row and column:
            block = mix_piece(column, 0)
        return pltpu.make_async_remote_copy(
            src_ref=block if row and column else piece_of(w, p),
            dst_ref=block if row else own,
            send_sem=peer_send.at[w, step, p],
            recv_sem=peer_recv.at[w, step, p],
            device_id=target,
            device_id_type=MESH_IDS,
        )

    def peer_arrival(w, step, p=0):
        row = step // pairs
        if row:
            target = {"dp": (dp + row) % dps}
        else:
            target = {"ctx": (ctx + 2 * step) % ctxs}
        block = block_of(w, chip_block(step, core), p)
        if w == 0 and row and step % pairs:
            block = mix_piece(step, 0)
        return pltpu.make_async_remote_copy(
            src_ref=block,
            dst_ref=block,
            send_sem=peer_send.at[w, step, p],
            recv_sem=peer_recv.at[w, step, p],
            device_id=target,
            device_id_type=MESH_IDS,
        )

    def twin_copy(w, step, p=0):
        block = block_of(w, chip_block(step, core), p)
        return pltpu.make_async_remote_copy(
            src_ref=piece_of(w, p) if step == 0 else block,
            dst_ref=block,
            send_sem=twin_send.at[w, step, p],
            recv_sem=twin_recv.at[w, step, p],
            device_id=twin,
            device_id_type=MESH_IDS,
        )

    def twin_arrival(w, step, p=0):
        block = block_of(w, chip_block(step, 1 - core), p)
        return pltpu.make_async_remote_copy(
            src_ref=block,
            dst_ref=block,
            send_sem=twin_send.at[w, step, p],
            recv_sem=twin_recv.at[w, step, p],
            device_id=twin,
            device_id_type=MESH_IDS,
        )

    def own_copy(w, p=0):
        return pltpu.make_async_copy(piece_of(w, p), block_of(w, chip_block(0, core), p), own_sem.at[w, p])

    def side_copy(step):
        row, column = step // pairs, step % pairs
        piece = mix_piece(row * pairs, 1)
        return pltpu.make_async_remote_copy(
            src_ref=piece,
            dst_ref=piece,
            send_sem=side_send.at[step],
            recv_sem=side_recv.at[step],
            device_id={"ctx": (ctx + 2 * column) % ctxs},
            device_id_type=MESH_IDS,
        )

    def side_arrival(step):
        piece = mix_piece(step, 1)
        return pltpu.make_async_remote_copy(
            src_ref=piece,
            dst_ref=piece,
            send_sem=side_send.at[step],
            recv_sem=side_recv.at[step],
            device_id={"ctx": (ctx + 2 * (step % pairs)) % ctxs},
            device_id_type=MESH_IDS,
        )

    def across_start(w, p=0):
        for step in range(pairs, chips, pairs):
            peer_copy(w, step, p).start()
        twin_copy(w, 0, p).start()
        own_copy(w, p).start()

    def along_start(w, p=0):
        for step in range(1, pairs):
            peer_copy(w, step, p).start()

    def weight_relay(w, p=0):
        for step in range(1, pairs):
            peer_arrival(w, step, p).wait_recv()
            for row in range(1, dps):
                peer_copy(w, row * pairs + step, p).start()
            twin_copy(w, step, p).start()

    def weight_forward(w, p=0):
        for step in range(pairs, chips):
            peer_arrival(w, step, p).wait_recv()
            twin_copy(w, step, p).start()

    def mixing_gather():
        along_start(0)
        across_start(0)
        weight_relay(0)
        for row in range(1, dps):
            peer_arrival(0, row * pairs).wait_recv()
            for column in range(1, pairs):
                side_copy(row * pairs + column).start()
            twin_copy(0, row * pairs).start()
        for row in range(1, dps):
            for column in range(1, pairs):
                step = row * pairs + column
                peer_arrival(0, step).wait_recv()
                side_arrival(step).wait_recv()
                twin_copy(0, step).start()

    def weight_finish(w, p=0):
        own_copy(w, p).wait()
        for step in range(chips):
            twin_arrival(w, step, p).wait_recv()

    def side_sent():
        for row in range(1, dps):
            for column in range(1, pairs):
                side_copy(row * pairs + column).wait_send()

    def weight_sent(w, p=0):
        for step in range(1, chips):
            peer_copy(w, step, p).wait_send()
        for step in range(chips):
            twin_copy(w, step, p).wait_send()

    def unit_place(device, u):
        return (device // local_heads) * units + u, device % local_heads

    def qkv_copy(u, step):
        peer = (ctx + step) % ctxs
        s, h = unit_place(peer, u)
        return pltpu.make_async_remote_copy(
            src_ref=local_qkv.at[s, h],
            dst_ref=unit_qkv.at[u, :, tile(ctx, tok)],
            send_sem=qkv_send.at[u, step],
            recv_sem=qkv_recv.at[u, step],
            device_id={"ctx": peer},
            device_id_type=MESH_IDS,
        )

    def qkv_arrival(u, step):
        return pltpu.make_async_remote_copy(
            src_ref=local_qkv.at[0, 0],
            dst_ref=unit_qkv.at[u, :, tile((ctx + ctxs - step) % ctxs, tok)],
            send_sem=qkv_send.at[u, step],
            recv_sem=qkv_recv.at[u, step],
            device_id={"ctx": (ctx + step) % ctxs},
            device_id_type=MESH_IDS,
        )

    def qkv_own(u):
        s, h = unit_place(ctx, u)
        return pltpu.make_async_copy(
            local_qkv.at[s, h], unit_qkv.at[u, :, tile(ctx, tok)], unit_sem.at[0, u]
        )

    def context_place(device, u):
        s, h = unit_place(device, u)
        return context.at[tile(s, tok), tile(h, HEAD_DIM)]

    def context_copy(u, step):
        peer = (ctx + step) % ctxs
        return pltpu.make_async_remote_copy(
            src_ref=unit_out.at[u, tile(peer, tok)],
            dst_ref=context_place(ctx, u),
            send_sem=ctx_send.at[u, step],
            recv_sem=ctx_recv.at[u, step],
            device_id={"ctx": peer},
            device_id_type=MESH_IDS,
        )

    def context_arrival(u, step):
        return pltpu.make_async_remote_copy(
            src_ref=unit_out.at[u, tile(ctx, tok)],
            dst_ref=context_place((ctx + ctxs - step) % ctxs, u),
            send_sem=ctx_send.at[u, step],
            recv_sem=ctx_recv.at[u, step],
            device_id={"ctx": (ctx + step) % ctxs},
            device_id_type=MESH_IDS,
        )

    def context_own(u):
        return pltpu.make_async_copy(
            unit_out.at[u, tile(ctx, tok)], context_place(ctx, u), unit_sem.at[1, u]
        )

    def go_copy(u, step):
        peer = (ctx + step) % ctxs
        s, h = unit_place(peer, u)
        return pltpu.make_async_remote_copy(
            src_ref=context_grad.at[tile(s, tok), tile(h, HEAD_DIM)],
            dst_ref=unit_go.at[u, tile(ctx, tok)],
            send_sem=go_send.at[u, step],
            recv_sem=go_recv.at[u, step],
            device_id={"ctx": peer},
            device_id_type=MESH_IDS,
        )

    def go_arrival(u, step):
        return pltpu.make_async_remote_copy(
            src_ref=context_grad.at[tile(0, tok), tile(0, HEAD_DIM)],
            dst_ref=unit_go.at[u, tile((ctx + ctxs - step) % ctxs, tok)],
            send_sem=go_send.at[u, step],
            recv_sem=go_recv.at[u, step],
            device_id={"ctx": (ctx + step) % ctxs},
            device_id_type=MESH_IDS,
        )

    def go_own(u):
        s, h = unit_place(ctx, u)
        return pltpu.make_async_copy(
            context_grad.at[tile(s, tok), tile(h, HEAD_DIM)],
            unit_go.at[u, tile(ctx, tok)],
            unit_sem.at[2, u],
        )

    def go_start(u):
        for step in range(1, ctxs):
            go_copy(u, step).start()
        go_own(u).start()

    early = early_units(total, tok, units)

    def go_ready(u):
        go_own(u).wait()
        for step in range(1, ctxs):
            go_arrival(u, step).wait_recv()

    def early_place(device):
        return early_grads.at[:, :, tile(unit_place(device, 0)[1], HEAD_DIM)]

    def early_copy(step):
        peer = (ctx + step) % ctxs
        return pltpu.make_async_remote_copy(
            src_ref=unit_grad.at[0, :, tile(peer, tok)],
            dst_ref=early_place(ctx),
            send_sem=early_send.at[step],
            recv_sem=early_recv.at[step],
            device_id={"ctx": peer},
            device_id_type=MESH_IDS,
        )

    def early_arrival(step):
        return pltpu.make_async_remote_copy(
            src_ref=unit_grad.at[0, :, tile(ctx, tok)],
            dst_ref=early_place((ctx + ctxs - step) % ctxs),
            send_sem=early_send.at[step],
            recv_sem=early_recv.at[step],
            device_id={"ctx": (ctx + step) % ctxs},
            device_id_type=MESH_IDS,
        )

    def early_own():
        return pltpu.make_async_copy(
            unit_grad.at[0, :, tile(ctx, tok)], early_place(ctx), unit_sem.at[3, 0]
        )

    def early_back():
        go_ready(0)
        attention_back(unit_qkv, unit_go, unit_out, unit_grad, sum_k, sum_v, 0, 0)
        for step in range(1, ctxs):
            early_copy(step).start()
        early_own().start()

    def attend(u):
        qkv_own(u).wait()
        for step in range(1, ctxs):
            qkv_arrival(u, step).wait_recv()
        part = math.gcd(seq_all, 256)

        @pl.loop(0, seq_all // part)
        def _(i):
            rs = tile(i, part)
            scores = dot_nt(unit_qkv[u, 0, rs, :], unit_qkv[u, 1]) * (HEAD_DIM ** (-0.5))
            largest = jnp.max(scores, axis=-1, keepdims=True)
            raised = jnp.exp(scores - largest)
            total = jnp.sum(raised, axis=-1, keepdims=True)
            mixed = dot_nn(raised.astype(BF), unit_qkv[u, 2])
            unit_out[u, rs, :] = (mixed / total).astype(BF)

        for step in range(1, ctxs):
            context_copy(u, step).start()
        context_own(u).start()

    def context_ready(u):
        context_own(u).wait()
        for step in range(1, ctxs):
            context_arrival(u, step).wait_recv()

    def project_chunk(c):
        bring(hidden, c).wait()
        following = (c + 1) % chunks
        s = c // per_seq
        rs = tile(c % per_seq, rows)
        low = dot_nt(rows_in[...], md[picks[s]]).astype(BF)
        put_rank(3, c, low)
        rank_buf[...] = low
        heads_at_once = math.gcd(local_heads, 2)
        step = heads_at_once * HEAD_DIM

        @pl.loop(0, mix_width // step)
        def _(i):
            cs = tile(i, step)
            values = dot_nn(rows_in[...], stash[0:width, cs]) + dot_nn(rank_buf[...], mu[picks[s], :, cs])
            values = values.astype(BF)
            first = i * heads_at_once
            for k in range(heads_at_once):
                local_qkv[s, (first + k) % local_heads, (first + k) // local_heads, rs, :] = values[
                    :, k * HEAD_DIM : (k + 1) * HEAD_DIM
                ]

        bring(hidden, following).start()

    def project(s):
        @pl.loop(0, per_seq)
        def _(i):
            project_chunk(s * per_seq + i)

    def send_unit(u):
        qkv_own(u).start()
        for step in range(1, ctxs):
            qkv_copy(u, step).start()

    def job_of(number, rounds):
        safe = jnp.maximum(number, 0)
        chunk = safe % period
        valid = (number >= 0) & (chunk < chunks) & (safe < rounds * period)
        return valid, jnp.minimum(chunk, chunks - 1)

    comm = chain(
        ranks,
        half,
        block,
        me,
        acc,
        red_up,
        red_down,
        red_send,
        red_recv,
        cast_send,
        cast_recv,
        lambda number: job_of(number, 3),
    )

    def rows_of(c):
        return tile(c, rows)

    def spot(t, c, i=None):
        start = t * total + c * rows
        if i is None:
            return pl.ds(pl.multiple_of(start, rows), rows)
        return pl.ds(pl.multiple_of(start + i * block, block), block)

    def mixing_keep():
        return pltpu.make_async_copy(
            stash.at[pl.ds(0, width), pl.ds(0, mix_width)], mixing, mix_sem
        )

    def bring(source, c):
        return pltpu.make_async_copy(source.at[rows_of(c)], rows_in, in_sem)

    def keep(index, source, target, c):
        return pltpu.make_async_copy(source, target.at[rows_of(c)], out_sem.at[index])

    def put_rank(t, c, low):
        part_ranks[t, :, tile(c, rows)] = dot_nt(unit_rank[...], low).astype(BF)

    def rank_copy(t, step):
        return pltpu.make_async_remote_copy(
            src_ref=part_ranks.at[t],
            dst_ref=rank_in.at[t, step],
            send_sem=rank_send.at[t, step],
            recv_sem=rank_recv.at[t, step],
            device_id={"tensor": (me + step) % ranks},
            device_id_type=MESH_IDS,
        )

    def mean(values):
        return jnp.sum(values, axis=-1, keepdims=True) * (1.0 / width)

    def attend_part(c, s):
        mine = context[rows_of(c), :]
        low = dot_nt(mine, od[picks[s]]).astype(BF)
        put_rank(0, c, low)

        @pl.loop(0, width // tile_d)
        def _(i):
            cs = tile(i, tile_d)
            acc[c, :, cs] = (dot_nn(mine, w_out[:, cs]) + dot_nn(low, ou[picks[s], :, cs])).astype(BF)

    def forward_first(c, s):
        bring(hidden, c).wait()

        @pl.loop(0, rows // block)
        def _(i):
            rs = tile(i, block)
            total = rows_in[rs, :].astype(F32) + acc[c, rs, :].astype(F32)
            centred = total - mean(total)
            spread = lax.rsqrt(mean(centred * centred) + 1e-06)
            n = centred * spread
            stash[spot(0, c, i), :] = n.astype(BF)
            spreads[c, rs, :] = jnp.broadcast_to(spread, (block, 128))
            stage_d[rs, :] = (n * gains[0:1, :] + gains[1:2, :]).astype(BF)

        low = dot_nt(stage_d[...], ed[picks[s]]).astype(BF)
        put_rank(4, c, low)
        rank_buf[...] = low

        @pl.loop(0, hidden_units // tile_f)
        def _(i):
            cs = tile(i, tile_f)
            b = dot_nn(stage_d[...], w_exp[:, cs]) + dot_nn(rank_buf[...], eu[picks[s], :, cs])
            square = b * b
            t = jnp.tanh(GELU_C * b * (1.0 + GELU_A * square))
            upper = 0.5 * (1.0 + t)
            stage_f[:, cs] = (b * upper).astype(BF)
            stash[spot(1, c), cs] = (
                upper
                + (0.5 * GELU_C) * b * (1.0 - t * t) * (1.0 + (3.0 * GELU_A) * square)
            ).astype(BF)

    def forward_second(c, s):
        low = dot_nt(stage_f[...], cd[picks[s]]).astype(BF)
        put_rank(1, c, low)
        rank_buf[...] = low

        @pl.loop(0, width // tile_d)
        def _(i):
            cs = tile(i, tile_d)
            acc[c, :, cs] = (
                dot_nn(stage_f[...], w_con[:, cs]) + dot_nn(rank_buf[...], cu[picks[s], :, cs])
            ).astype(BF)

        keep(0, stage_d, first_low, c).start()
        keep(1, stage_f, active, c).start()

    def back_first(c, s):
        bring(cotangent, c).wait()

        @pl.loop(0, rows // block)
        def _(i):
            rs = tile(i, block)
            first = stash[spot(0, c, i), :].astype(F32) * gains[0:1, :] + gains[1:2, :]
            total = first + acc[c, rs, :].astype(F32)
            centred = total - mean(total)
            spread = lax.rsqrt(mean(centred * centred) + 1e-06)
            n = centred * spread
            stage_d[rs, :] = (n * gains[2:3, :] + gains[3:4, :]).astype(BF)
            g = rows_in[rs, :].astype(F32) * gains[2:3, :]
            stash[spot(2, c, i), :] = (spread * (g - mean(g) - n * mean(g * n))).astype(BF)

        low = dot_nt(stash[spot(2, c), :], cu[picks[s]]).astype(BF)
        put_rank(5, c, low)
        rank_buf[...] = low

        @pl.loop(0, hidden_units // tile_f)
        def _(i):
            cs = tile(i, tile_f)
            da = dot_nt(stash[spot(2, c), :], w_con[cs, :]) + dot_nn(rank_buf[...], cd[picks[s], :, cs])
            stage_f[:, cs] = (da * stash[spot(1, c), cs].astype(F32)).astype(BF)

    def back_second(c, s):
        low = dot_nt(stage_f[...], eu[picks[s]]).astype(BF)
        put_rank(2, c, low)
        rank_buf[...] = low

        @pl.loop(0, width // tile_d)
        def _(i):
            cs = tile(i, tile_d)
            acc[c, :, cs] = (
                dot_nt(stage_f[...], w_exp[cs, :]) + dot_nn(rank_buf[...], ed[picks[s], :, cs])
            ).astype(BF)

        keep(0, stage_d, hidden_out, c).start()
        keep(1, stage_f, before_grad, c).start()
        keep(2, stash.at[spot(2, c)], second_low, c).start()

    def last_first(c, s):
        @pl.loop(0, rows // block)
        def _(i):
            rs = tile(i, block)
            n = stash[spot(0, c, i), :].astype(F32)
            g = (stash[spot(2, c, i), :].astype(F32) + acc[c, rs, :].astype(F32)) * gains[0:1, :]
            spread = spreads[c, rs, 0:1]
            stage_d[rs, :] = (spread * (g - mean(g) - n * mean(g * n))).astype(BF)

    def last_second(c, s):
        low = dot_nt(stage_d[...], ou[picks[s]]).astype(BF)
        put_rank(6, c, low)
        rank_buf[...] = low

        @pl.loop(0, heads // tile_h)
        def _(i):
            cs = tile(i, tile_h)
            context_grad[rows_of(c), cs] = (
                dot_nt(stage_d[...], w_out[cs, :]) + dot_nn(rank_buf[...], od[picks[s], :, cs])
            ).astype(BF)

        keep(0, stage_d, attn_low, c).start()

    seqs = chunks // per_seq
    flowing = units == seqs
    bring(hidden, 0).start()
    mixing_gather()
    weight_finish(0)
    along_start(1)
    across_start(1)
    mixing_keep().start()
    if flowing:
        for u in range(min(2, units)):
            project(u)
            send_unit(u)
    else:
        pl.loop(0, seqs)(project)
        for u in range(units):
            send_unit(u)
    weight_relay(1)

    @pl.loop(0, lead + 3 * period + chunks)
    def _(now):
        tick = now - lead
        stage = jnp.maximum(tick, 0) // period
        valid, c = job_of(tick, 4)
        s = c // per_seq
        last_valid, last_c = job_of(tick - 1, 4)
        last_stage = jnp.maximum(tick - 1, 0) // period

        comm(tick, 0)

        @pl.when(last_valid & (last_stage >= 1))
        def _():
            keep(0, stage_d, first_low, last_c).wait()

        @pl.when(last_valid & (last_stage >= 1) & (last_stage <= 2))
        def _():
            keep(1, stage_f, active, last_c).wait()

        @pl.when(last_valid & (last_stage == 2))
        def _():
            keep(2, stash.at[spot(2, last_c)], second_low, last_c).wait()

        pl.when(now == 1)(lambda: weight_forward(1))
        pl.when((now % per_seq == 0) & (now < units * per_seq))(lambda: attend(now // per_seq))
        if flowing:

            @pl.when((now % per_seq == 1) & (now < (units - 2) * per_seq))
            def _():
                project(now // per_seq + 2)
                send_unit(now // per_seq + 2)

        @pl.when((now % per_seq == 1) & (now > per_seq) & (now <= PIECES * per_seq + 1))
        def _():
            p = now // per_seq - 1
            weight_relay(2, p)
            weight_relay(3, p)

        @pl.when((now % per_seq == 1) & (now < PIECES * per_seq))
        def _():
            for w in (2, 3):
                along_start(w, now // per_seq)
                across_start(w, now // per_seq)

        @pl.when((now % per_seq == 0) & (now > per_seq) & (now <= (PIECES + 1) * per_seq))
        def _():
            p = now // per_seq - 2
            weight_forward(2, p)
            weight_forward(3, p)

        @pl.when(now == lead + period)
        def _():
            for p in range(PIECES):
                weight_finish(2, p)
                weight_finish(3, p)

        pl.when(now == lead)(lambda: weight_finish(1))

        @pl.when(now == lead + period - 2)
        def _():
            mixing_keep().wait()
            weight_sent(0)
            side_sent()

        for t in range(3):

            @pl.when(tick == (t + 1) * period)
            def _(t=t):
                for step in range(1, ranks):
                    rank_copy(t, step).start()

        pl.when((tick >= 0) & (tick % per_seq == 0) & (tick < units * per_seq))(
            lambda: context_ready(s)
        )

        pl.when(valid & (stage == 1))(lambda: forward_first(c, s))
        pl.when(valid & (stage == 2))(lambda: back_first(c, s))
        pl.when(valid & (stage == 3))(lambda: last_first(c, s))

        comm(tick, 1)

        pl.when(valid & (stage == 0))(lambda: attend_part(c, s))
        pl.when(valid & (stage == 1))(lambda: forward_second(c, s))
        pl.when(valid & (stage == 2))(lambda: back_second(c, s))
        pl.when(valid & (stage == 3))(lambda: last_second(c, s))
        if flowing:
            pl.when(valid & (stage == 3) & (c % per_seq == per_seq - 1))(lambda: go_start(s))
        if early:
            pl.when(tick == 3 * period + EARLY_AT)(early_back)

        next_valid, next_c = job_of(tick + 1, 4)
        next_stage = jnp.maximum(tick + 1, 0) // period
        pl.when(next_valid & (next_stage == 1) & (next_c > 0))(
            lambda: bring(hidden, next_c).start()
        )
        pl.when(next_valid & (next_stage == 2))(lambda: bring(cotangent, next_c).start())

    keep(0, stage_d, attn_low, chunks - 1).wait()
    for t in range(3):
        value = part_ranks[t].astype(F32)
        for step in range(1, ranks):
            rank_copy(t, step).wait_recv()
            value = value + rank_in[t, step].astype(F32)
        full_ranks[t] = value.astype(BF)
    for t in range(3):
        for step in range(1, ranks):
            rank_copy(t, step).wait_send()
    weight_sent(1)
    for p in range(PIECES):
        weight_sent(2, p)
        weight_sent(3, p)
    for u in range(units):
        if not flowing:
            go_start(u)
        for step in range(1, ctxs):
            qkv_copy(u, step).wait_send()
            context_copy(u, step).wait_send()
    for u in range(units):
        if u >= early:
            go_ready(u)
        for step in range(1, ctxs):
            go_copy(u, step).wait_send()
    if early:
        early_own().wait()
        for step in range(1, ctxs):
            early_arrival(step).wait_recv()
            early_copy(step).wait_send()


def enter(others):
    barrier = pltpu.get_barrier_semaphore()
    for other in others:
        pl.semaphore_signal(barrier, inc=1, device_id=other, device_id_type=MESH_IDS)
    pl.semaphore_wait(barrier, len(others))


def middle(hidden, cotangent, shards, picked, gains, tok, picks):
    total, width = hidden.shape
    mix_width = shards[0].shape[1]
    heads, hidden_units = shards[1].shape[0], shards[2].shape[1]
    ranks, dps, ctxs = (lax.axis_size(name) for name in ("tensor", "dp", "ctx"))
    seqs, rank = picks.shape[0], picked[0].shape[1]
    local_heads = heads // HEAD_DIM
    units = seqs * local_heads // ctxs
    rows = math.gcd(tok, CHUNK_ROWS)
    chunks = total // rows
    period = max(chunks, 2 * ranks)
    sizes = (ranks, dps, ctxs, chunks, rows, tok // rows, period)
    chips = dps * ctxs // 2
    vm = pl.BlockSpec(memory_space=pltpu.VMEM)
    hb = pl.BlockSpec(memory_space=pl.ANY)
    sm = pl.BlockSpec(memory_space=pltpu.SMEM)
    half = rows // 2
    dma = pltpu.SemaphoreType.DMA

    def shape(*dims):
        return jax.ShapeDtypeStruct(dims, BF)

    return pl.pallas_call(
        functools.partial(middle_kernel, sizes),
        out_shape=(
            shape(total, width),
            shape(total, width),
            shape(total, hidden_units),
            shape(total, width),
            shape(total, hidden_units),
            shape(total, width),
            shape(width, mix_width),
            shape(units, tok * ctxs, HEAD_DIM),
            shape(3, tok, heads),
            shape(7, rank, total),
            shape(3, rank, total),
            shape(total, heads),
            shape(units, 3, tok * ctxs, HEAD_DIM),
            shape(units, tok * ctxs, HEAD_DIM),
        ),
        in_specs=[hb] * 6 + [vm] * 10 + [sm],
        out_specs=(hb,) * 7 + (vm,) * 7,
        scratch_shapes=[
            pltpu.VMEM((total, heads), BF),
            pltpu.VMEM((1, 3, tok * ctxs, HEAD_DIM), BF),
            pltpu.VMEM((tok * ctxs, HEAD_DIM), F32),
            pltpu.VMEM((tok * ctxs, HEAD_DIM), F32),
            pltpu.VMEM((seqs, local_heads, 3, tok, HEAD_DIM), BF),
            pltpu.VMEM((heads, width), BF),
            pltpu.VMEM((width, hidden_units), BF),
            pltpu.VMEM((hidden_units, width), BF),
            pltpu.VMEM((chunks, rows, width), BF),
            pltpu.VMEM((chunks, half, width), BF),
            pltpu.VMEM((chunks, half, width), BF),
            pltpu.VMEM((3 * total, width), BF),
            pltpu.VMEM((chunks, rows, 128), F32),
            pltpu.VMEM((3, ranks, rank, total), BF),
            pltpu.VMEM((rows, width), BF),
            pltpu.VMEM((rows, hidden_units), BF),
            pltpu.VMEM((rows, width), BF),
            pltpu.VMEM((rows, rank), BF),
            dma(()),
            dma((3,)),
            dma((2, chunks)),
            dma((2, chunks)),
            dma((2, chunks)),
            dma((2, chunks)),
            dma((4, chips, PIECES)),
            dma((4, chips, PIECES)),
            dma((4, chips, PIECES)),
            dma((4, chips, PIECES)),
            dma((chips,)),
            dma((chips,)),
            dma((4, PIECES)),
            dma((3, ranks)),
            dma((3, ranks)),
            dma(()),
            dma((units, ctxs)),
            dma((units, ctxs)),
            dma((units, ctxs)),
            dma((units, ctxs)),
            dma((units, ctxs)),
            dma((units, ctxs)),
            dma((ctxs,)),
            dma((ctxs,)),
            dma((4, units)),
        ],
        compiler_params=pltpu.CompilerParams(
            collective_id=0, has_side_effects=True, vmem_limit_bytes=VMEM_BYTES
        ),
        cost_estimate=pl.CostEstimate(
            flops=8 * total * width * hidden_units + 4 * total * width * heads,
            bytes_accessed=16 * total * width,
            transcendentals=total * hidden_units,
        ),
    )(hidden, cotangent, *shards, *picked, gains, jnp.eye(rank, dtype=BF), picks)


def mixing_kernel(
    sizes,
    unit_go,
    unit_qkv,
    unit_out,
    mixing_far,
    mu,
    md,
    attn_low,
    unit_rank,
    early_grads,
    hidden_far,
    mix_rank,
    row_hot,
    picks,
    input_grad,
    table_sum,
    grads,
    mixing,
    hidden,
    rank_part,
    rank_in,
    wide,
    table_part,
    table_in,
    unit_grad,
    sum_k,
    sum_v,
    acc,
    red_up,
    red_down,
    stage_d,
    rows_in,
    rank_buf,
    in_sem,
    out_sem,
    red_send,
    red_recv,
    cast_send,
    cast_recv,
    far_sem,
    grad_send,
    grad_recv,
    unit_sem,
    rank_send,
    rank_recv,
    part_send,
    part_recv,
    whole_send,
    whole_recv,
):
    ranks, dps, ctxs, chunks, rows, per_seq, group = sizes
    half = rows // 2
    width = mixing.shape[0]
    heads = grads.shape[2]
    local_heads = heads // HEAD_DIM
    units, seq_all = unit_go.shape[0], unit_go.shape[1]
    tok = seq_all // ctxs
    block = min(16, half)
    tile_d = math.gcd(width, 256)
    scale = HEAD_DIM ** (-0.5)
    me = lax.axis_index("tensor")
    ctx = lax.axis_index("ctx")
    dp = lax.axis_index("dp")
    parts = dps * ctxs
    index = dp * ctxs + ctx
    rank = mu.shape[1]
    tables, _, part_width = table_part.shape
    segments = parts // NADAPT
    tile_g = math.gcd(part_width, 256)

    def part_place(step):
        other = (index + step) % parts
        return {"dp": other // ctxs, "ctx": other % ctxs}

    enter(
        [{"tensor": (me + d) % ranks} for d in range(1, ranks)]
        + [part_place(d) for d in range(1, parts)]
    )

    def unit_place(device, u):
        return (device // local_heads) * units + u, device % local_heads

    def mixing_load():
        return pltpu.make_async_copy(mixing_far, mixing, far_sem.at[0])

    def early_load():
        return pltpu.make_async_copy(early_grads, grads.at[:, pl.ds(0, tok)], far_sem.at[2])

    def hidden_load():
        return pltpu.make_async_copy(hidden_far, hidden, far_sem.at[1])

    def grads_place(device, u):
        s, h = unit_place(device, u)
        return grads.at[:, tile(s, tok), tile(h, HEAD_DIM)]

    def grad_copy(u, step):
        peer = (ctx + step) % ctxs
        return pltpu.make_async_remote_copy(
            src_ref=unit_grad.at[u, :, tile(peer, tok)],
            dst_ref=grads_place(ctx, u),
            send_sem=grad_send.at[u, step],
            recv_sem=grad_recv.at[u, step],
            device_id={"ctx": peer},
            device_id_type=MESH_IDS,
        )

    def grad_arrival(u, step):
        return pltpu.make_async_remote_copy(
            src_ref=unit_grad.at[u, :, tile(ctx, tok)],
            dst_ref=grads_place((ctx + ctxs - step) % ctxs, u),
            send_sem=grad_send.at[u, step],
            recv_sem=grad_recv.at[u, step],
            device_id={"ctx": (ctx + step) % ctxs},
            device_id_type=MESH_IDS,
        )

    def grad_own(u):
        return pltpu.make_async_copy(
            unit_grad.at[u, :, tile(ctx, tok)], grads_place(ctx, u), unit_sem.at[u]
        )

    def attend_back(u):
        attention_back(unit_qkv, unit_go, unit_out, unit_grad, sum_k, sum_v, u, u)
        for step in range(1, ctxs):
            grad_copy(u, step).start()
        grad_own(u).start()

    def grads_ready(u):
        grad_own(u).wait()
        for step in range(1, ctxs):
            grad_arrival(u, step).wait_recv()

    early = early_units(chunks * rows, tok, units)
    lead = per_seq * (1 - early)
    if early:
        early_load().start()
    mixing_load().start()
    hidden_load().start()

    def job_of(number):
        return (number >= 0) & (number < chunks), jnp.clip(number, 0, chunks - 1)

    comm = chain(
        ranks, half, block, me, acc, red_up, red_down, red_send, red_recv, cast_send, cast_recv, job_of
    )

    def rows_of(c):
        return tile(c, rows)

    def bring(c):
        return pltpu.make_async_copy(attn_low.at[rows_of(c)], rows_in, in_sem)

    def keep(c):
        return pltpu.make_async_copy(stage_d, input_grad.at[rows_of(c)], out_sem)

    def back_part(c, s):
        rs = pl.ds(pl.multiple_of(c * rows, group * rows), group * rows)
        low = jnp.zeros((group * rows, mu.shape[1]), F32)
        for j in range(3):
            low = low + dot_nt(grads[j, rs, :], mu[picks[s], :, pl.ds(j * heads, heads)])
        low = low.astype(BF)
        rank_part[:, pl.ds(pl.multiple_of(c * rows, group * rows), group * rows)] = dot_nt(
            unit_rank[...], low
        ).astype(BF)
        rank_buf[...] = low

        @pl.loop(0, width // tile_d)
        def _(i):
            cs = tile(i, tile_d)
            total = dot_nn(rank_buf[...], md[picks[s], :, cs])
            for j in range(3):
                total = total + dot_nt(grads[j, rs, :], mixing[cs, pl.ds(j * heads, heads)])
            total = total.astype(BF)
            for k in range(group):
                acc[c + k, :, cs] = total[k * rows : (k + 1) * rows, :]

    def final_part(c):
        bring(c).wait()

        @pl.loop(0, rows // block)
        def _(i):
            rs = tile(i, block)
            stage_d[rs, :] = (rows_in[rs, :].astype(F32) + acc[c, rs, :].astype(F32)).astype(BF)

        keep(c).start()

    def rank_copy(step):
        return pltpu.make_async_remote_copy(
            src_ref=rank_part,
            dst_ref=rank_in.at[step],
            send_sem=rank_send.at[step],
            recv_sem=rank_recv.at[step],
            device_id={"tensor": (me + step) % ranks},
            device_id_type=MESH_IDS,
        )

    def part_copy(step):
        return pltpu.make_async_remote_copy(
            src_ref=table_part.at[(index + step) % parts],
            dst_ref=table_in.at[step],
            send_sem=part_send.at[step],
            recv_sem=part_recv.at[step],
            device_id=part_place(step),
            device_id_type=MESH_IDS,
        )

    def whole_copy(step):
        return pltpu.make_async_remote_copy(
            src_ref=table_sum.at[index],
            dst_ref=table_sum.at[index],
            send_sem=whole_send.at[step],
            recv_sem=whole_recv.at[step],
            device_id=part_place(step),
            device_id_type=MESH_IDS,
        )

    def whole_arrival(step):
        return pltpu.make_async_remote_copy(
            src_ref=table_sum.at[index],
            dst_ref=table_sum.at[(index + parts - step) % parts],
            send_sem=whole_send.at[step],
            recv_sem=whole_recv.at[step],
            device_id=part_place(step),
            device_id_type=MESH_IDS,
        )

    def put_table(column, values):
        segment = column // part_width
        cs = pl.ds(pl.multiple_of(column % part_width, tile_g), tile_g)
        for n in range(NADAPT):
            table_part[n * segments + segment, :, cs] = values[n * rank : (n + 1) * rank, :].astype(
                BF
            )

    def make_tables():
        value = rank_part[...].astype(F32)
        for step in range(1, ranks):
            rank_copy(step).wait_recv()
            value = value + rank_in[step].astype(F32)
        for n in range(NADAPT):
            hot = row_hot[n : n + 1, :]
            wide[0, pl.ds(n * rank, rank), :] = (value * hot).astype(BF)
            wide[1, pl.ds(n * rank, rank), :] = (mix_rank[...].astype(F32) * hot).astype(BF)

        @pl.loop(0, width // tile_g)
        def _(i):
            put_table(i * tile_g, dot_nn(wide[0], hidden[:, tile(i, tile_g)]))

        for j in range(3):

            @pl.loop(0, heads // tile_g)
            def _(i):
                put_table(
                    width + j * heads + i * tile_g, dot_nn(wide[1], grads[j, :, tile(i, tile_g)])
                )

        for step in range(1, parts):
            part_copy(step).start()

    def sum_tables():
        value = table_part[index].astype(F32)
        for step in range(1, parts):
            part_copy(step).wait_recv()
            value = value + table_in[step].astype(F32)
        table_sum[index] = value.astype(BF)
        for step in range(1, parts):
            whole_copy(step).start()

    delay = 2 * ranks

    @pl.loop(0, lead + chunks + delay)
    def _(now):
        tick = now - lead

        @pl.when(tick == chunks)
        def _():
            for step in range(1, ranks):
                rank_copy(step).start()

        valid, c = job_of(tick)
        final, c_final = job_of(tick - delay)
        before, c_before = job_of(tick - delay - 1)
        coming, c_coming = job_of(tick - delay + 1)
        s = c // per_seq

        comm(tick, 0)

        pl.when(
            (tick >= early * per_seq) & (tick % per_seq == 0) & (tick < units * per_seq)
        )(lambda: grads_ready(s))
        if not early:
            pl.when((now % per_seq == 0) & (now < units * per_seq))(
                lambda: attend_back(now // per_seq)
            )
        comm(tick, 1)
        if early:
            pl.when((now % per_seq == 0) & (now < (units - 1) * per_seq))(
                lambda: attend_back(now // per_seq + 1)
            )
            pl.when(tick == 0)(lambda: early_load().wait())

        pl.when(tick == 0)(lambda: mixing_load().wait())
        pl.when(valid & (tick % group == 0))(lambda: back_part(c, s))

        @pl.when(tick == chunks + 1)
        def _():
            hidden_load().wait()
            make_tables()

        pl.when(tick == chunks + 4)(sum_tables)

        pl.when(before)(lambda: keep(c_before).wait())
        pl.when(final)(lambda: final_part(c_final))
        pl.when(coming)(lambda: bring(c_coming).start())

    keep(chunks - 1).wait()
    for step in range(1, ranks):
        rank_copy(step).wait_send()
    for step in range(1, parts):
        whole_arrival(step).wait_recv()
    for step in range(1, parts):
        part_copy(step).wait_send()
        whole_copy(step).wait_send()
    for u in range(early, units):
        for step in range(1, ctxs):
            grad_copy(u, step).wait_send()


def mixing_back(
    unit_go, early_grads, unit_qkv, unit_out, mixing, picked, attn_low, hidden, mix_rank, row_hot, picks
):
    mu, md = picked
    total, width = attn_low.shape
    heads = mixing.shape[1] // 3
    ranks, dps, ctxs = (lax.axis_size(name) for name in ("tensor", "dp", "ctx"))
    parts = dps * ctxs
    part_width = (width + 3 * heads) * NADAPT // parts
    units, _, seq_all, _ = unit_qkv.shape
    tok = seq_all // ctxs
    rank = mu.shape[1]
    rows = math.gcd(tok, LAST_ROWS)
    chunks = total // rows
    per_seq = tok // rows
    group = math.gcd(per_seq, 2)
    half = rows // 2
    sizes = (ranks, dps, ctxs, chunks, rows, per_seq, group)
    vm = pl.BlockSpec(memory_space=pltpu.VMEM)
    hb = pl.BlockSpec(memory_space=pl.ANY)
    sm = pl.BlockSpec(memory_space=pltpu.SMEM)
    dma = pltpu.SemaphoreType.DMA
    return pl.pallas_call(
        functools.partial(mixing_kernel, sizes),
        out_shape=(
            jax.ShapeDtypeStruct((total, width), BF),
            jax.ShapeDtypeStruct((parts, rank, part_width), BF),
        ),
        in_specs=[vm] * 3 + [hb] + [vm] * 2 + [hb, vm, hb, hb] + [vm] * 2 + [sm],
        out_specs=(hb, vm),
        scratch_shapes=[
            pltpu.VMEM((3, total, heads), BF),
            pltpu.VMEM((width, 3 * heads), BF),
            pltpu.VMEM((total, width), BF),
            pltpu.VMEM((rank, total), BF),
            pltpu.VMEM((ranks, rank, total), BF),
            pltpu.VMEM((2, NADAPT * rank, total), BF),
            pltpu.VMEM((parts, rank, part_width), BF),
            pltpu.VMEM((parts, rank, part_width), BF),
            pltpu.VMEM((units, 3, seq_all, HEAD_DIM), BF),
            pltpu.VMEM((seq_all, HEAD_DIM), F32),
            pltpu.VMEM((seq_all, HEAD_DIM), F32),
            pltpu.VMEM((chunks, rows, width), BF),
            pltpu.VMEM((chunks, half, width), BF),
            pltpu.VMEM((chunks, half, width), BF),
            pltpu.VMEM((rows, width), BF),
            pltpu.VMEM((rows, width), BF),
            pltpu.VMEM((group * rows, rank), BF),
            dma(()),
            dma(()),
            dma((2, chunks)),
            dma((2, chunks)),
            dma((2, chunks)),
            dma((2, chunks)),
            dma((3,)),
            dma((units, ctxs)),
            dma((units, ctxs)),
            dma((units,)),
            dma((ranks,)),
            dma((ranks,)),
            dma((parts,)),
            dma((parts,)),
            dma((parts,)),
            dma((parts,)),
        ],
        compiler_params=pltpu.CompilerParams(
            collective_id=1, has_side_effects=True, vmem_limit_bytes=VMEM_LAST
        ),
        cost_estimate=pl.CostEstimate(
            flops=6 * total * width * heads + 10 * units * seq_all * seq_all * HEAD_DIM,
            bytes_accessed=8 * total * width,
            transcendentals=units * seq_all * seq_all,
        ),
    )(
        unit_go,
        unit_qkv,
        unit_out,
        mixing,
        mu,
        md,
        attn_low,
        jnp.eye(rank, dtype=BF),
        early_grads,
        hidden,
        mix_rank,
        row_hot,
        picks,
    )


def per_device(
    hidden_in,
    output_cotangent,
    adapter_index,
    mixing_weight,
    output_weight,
    expand_weight,
    contract_weight,
    first_gain,
    first_shift,
    second_gain,
    second_shift,
    mixing_down,
    mixing_up,
    output_down,
    output_up,
    expand_down,
    expand_up,
    contract_down,
    contract_up,
):
    seq_count, tok_count, model_width = hidden_in.shape
    local_heads = mixing_weight.shape[2] // HEAD_DIM
    local_width = mixing_weight.shape[2]
    rows_all = seq_count * tok_count
    adapter_ids = jnp.arange(NADAPT, dtype=jnp.int32)
    onehot_low = (adapter_index == adapter_ids[None, :]).astype(jnp.bfloat16)
    picks = adapter_index.reshape(-1)
    rank = mixing_down.shape[1]
    mixing_flat = mixing_weight.reshape(mixing_weight.shape[0], 3 * local_width)
    hidden_rows = hidden_in.reshape(rows_all, model_width)
    mixing_up_flat = mixing_up.reshape(NADAPT, rank, 3 * local_width)
    gains = jnp.stack([first_gain, first_shift, second_gain, second_shift])
    (
        out_rows,
        first_low,
        active_low,
        second_low,
        before_low,
        attn_low,
        mixing_full,
        unit_go,
        early_grads,
        part_ranks,
        full_ranks,
        context,
        unit_qkv,
        unit_out,
    ) = middle(
        hidden_rows,
        output_cotangent.reshape(rows_all, model_width),
        (mixing_flat, output_weight, expand_weight, contract_weight),
        (
            mixing_down,
            mixing_up_flat,
            output_down,
            output_up,
            expand_down,
            expand_up,
            contract_down,
            contract_up,
        ),
        gains,
        tok_count,
        picks,
    )
    row_hot = jnp.repeat(onehot_low.T, tok_count, axis=1)

    def table_grad(ranks, values):
        wide = (row_hot[:, None, :] * ranks[None, :, :]).reshape(-1, rows_all)
        part = jnp.einsum("kn,nd->kd", wide, values, preferred_element_type=jnp.float32)
        return part.astype(jnp.bfloat16).reshape(NADAPT, rank, values.shape[1])

    early = (
        table_grad(part_ranks[6], context),
        table_grad(full_ranks[0], attn_low),
        table_grad(full_ranks[2], first_low),
        table_grad(part_ranks[4], before_low),
        table_grad(part_ranks[5], active_low),
        table_grad(full_ranks[1], second_low),
    )
    early, unit_go = lax.optimization_barrier((early, unit_go))
    input_rows, late = mixing_back(
        unit_go,
        early_grads,
        unit_qkv,
        unit_out,
        mixing_full,
        (mixing_up_flat, mixing_down),
        attn_low,
        hidden_rows,
        part_ranks[3],
        row_hot.astype(jnp.float32),
        picks,
    )
    early = lax.psum(early, ("dp", "ctx"))
    late = late.reshape(NADAPT, -1, rank, late.shape[2]).swapaxes(1, 2).reshape(NADAPT, rank, -1)
    late = (
        late[:, :, :model_width],
        late[:, :, model_width:].reshape(NADAPT, rank, 3, local_width),
    )
    summed = tuple(part.astype(jnp.float32) for part in late + early)
    return (
        out_rows.reshape(hidden_in.shape),
        input_rows.reshape(hidden_in.shape),
    ) + summed


def solution(mesh):
    return jax.shard_map(
        per_device,
        mesh=mesh,
        in_specs=(
            P("dp", "ctx", None),
            P("dp", "ctx", None),
            P("dp", None),
            P(("dp", "ctx"), None, "tensor"),
            P("tensor", ("dp", "ctx")),
            P(("dp", "ctx"), "tensor"),
            P("tensor", ("dp", "ctx")),
            P(),
            P(),
            P(),
            P(),
            P(),
            P(None, None, None, "tensor"),
            P(None, None, "tensor"),
            P(),
            P(),
            P(None, None, "tensor"),
            P(None, None, "tensor"),
            P(),
        ),
        out_specs=(
            P("dp", "ctx", None),
            P("dp", "ctx", None),
            P(),
            P(None, None, None, "tensor"),
            P(None, None, "tensor"),
            P(),
            P(),
            P(None, None, "tensor"),
            P(None, None, "tensor"),
            P(),
        ),
        check_vma=False,
    )
```

```python
import functools
import math

import jax
import jax.numpy as jnp
from jax import lax
from jax.experimental import pallas as pl
from jax.experimental.pallas import tpu as pltpu
from jax.sharding import PartitionSpec as P

HEAD_DIM = 128
NADAPT = 8
CHUNK_ROWS = 128
LAST_ROWS = 128
VMEM_BYTES = 62 * 2**20
VMEM_LAST = 56 * 2**20
PIECES = 4
EARLY_AT = 3


BF = jnp.bfloat16
F32 = jnp.float32
MESH_IDS = pl.DeviceIdType.MESH
RANK_ROWS = 16
GELU_C = 0.7978845608028654
GELU_A = 0.044715


def dot_nn(a, b):
    return lax.dot_general(a, b, (((1,), (0,)), ((), ())), preferred_element_type=F32)


def dot_nt(a, b):
    return lax.dot_general(a, b, (((1,), (1,)), ((), ())), preferred_element_type=F32)


def dot_tn(a, b):
    return lax.dot_general(a, b, (((0,), (0,)), ((), ())), preferred_element_type=F32)


def tile(index, size):
    return pl.ds(pl.multiple_of(index * size, size), size)


def chain(
    ranks, half, block, me, acc, red_up, red_down, red_send, red_recv, cast_send, cast_recv, job_of
):
    def comm(tick, way):
        upward = way == 0
        place = me if upward else ranks - 1 - me
        ahead = me + 1 if upward else me - 1
        behind = me - 1 if upward else me + 1
        red = red_up if upward else red_down
        part = pl.ds(way * half, half)

        def red_copy(c):
            return pltpu.make_async_remote_copy(
                src_ref=red.at[c],
                dst_ref=red.at[c],
                send_sem=red_send.at[way, c],
                recv_sem=red_recv.at[way, c],
                device_id={"tensor": ahead},
                device_id_type=MESH_IDS,
            )

        def cast_copy(c):
            return pltpu.make_async_remote_copy(
                src_ref=acc.at[c, part],
                dst_ref=acc.at[c, part],
                send_sem=cast_send.at[way, c],
                recv_sem=cast_recv.at[way, c],
                device_id={"tensor": behind},
                device_id_type=MESH_IDS,
            )

        old_red, c_old = job_of(tick - 2 - place)

        @pl.when(old_red & (place < ranks - 1))
        def _():
            red_copy(c_old).wait_send()

        old_cast, c_cast = job_of(tick - 2 * ranks + place)

        @pl.when(old_cast & (place > 0))
        def _():
            cast_copy(c_cast).wait_send()

        now_red, c = job_of(tick - 1 - place)

        @pl.when(now_red & (place == 0))
        def _():
            red[c] = acc[c, part, :]

        @pl.when(now_red & (place > 0))
        def _():
            red_copy(c).wait_recv()

        @pl.when(now_red & (place > 0) & (place < ranks - 1))
        def _():
            @pl.loop(0, half // block)
            def _(i):
                rs = tile(i, block)
                own = acc[c, pl.ds(pl.multiple_of(way * half + i * block, block), block), :]
                red[c, rs, :] = (red[c, rs, :].astype(F32) + own.astype(F32)).astype(BF)

        @pl.when(now_red & (place < ranks - 1))
        def _():
            red_copy(c).start()

        @pl.when(now_red & (place == ranks - 1))
        def _():
            @pl.loop(0, half // block)
            def _(i):
                rs = tile(i, block)
                own_rs = pl.ds(pl.multiple_of(way * half + i * block, block), block)
                acc[c, own_rs, :] = (
                    red[c, rs, :].astype(F32) + acc[c, own_rs, :].astype(F32)
                ).astype(BF)

            cast_copy(c).start()

        now_cast, cc = job_of(tick - (2 * ranks - 1 - place))

        @pl.when(now_cast & (place < ranks - 1))
        def _():
            cast_copy(cc).wait_recv()

        @pl.when(now_cast & (place > 0) & (place < ranks - 1))
        def _():
            cast_copy(cc).start()
    return comm


def attention_back(unit_qkv, unit_go, unit_out, unit_grad, sum_k, sum_v, u, v):
    seq_all = unit_qkv.shape[2]
    scale = HEAD_DIM ** (-0.5)
    part = math.gcd(seq_all, 256)
    sum_k[...] = jnp.zeros_like(sum_k)
    sum_v[...] = jnp.zeros_like(sum_v)

    @pl.loop(0, seq_all // part)
    def _(i):
        rs = tile(i, part)
        queries = unit_qkv[u, 0, rs, :]
        go = unit_go[u, rs, :]
        scores = dot_nt(queries, unit_qkv[u, 1]) * scale
        raised = jnp.exp(scores - jnp.max(scores, axis=-1, keepdims=True))
        probs = raised * (1.0 / jnp.sum(raised, axis=-1, keepdims=True))
        delta = jnp.sum(
            go.astype(F32) * unit_out[u, rs, :].astype(F32), axis=-1, keepdims=True
        )
        dscores = (probs * (dot_nt(go, unit_qkv[u, 2]) - delta)).astype(BF)
        unit_grad[v, 0, rs, :] = (scale * dot_nn(dscores, unit_qkv[u, 1])).astype(BF)
        sum_k[...] += dot_tn(dscores, queries)
        sum_v[...] += dot_tn(probs.astype(BF), go)

    unit_grad[v, 1] = (scale * sum_k[...]).astype(BF)
    unit_grad[v, 2] = sum_v[...].astype(BF)


def early_units(total, tok, units):
    rows = math.gcd(tok, CHUNK_ROWS)
    return int(units == total // tok and tok // rows >= 2 and units >= 2)


def middle_kernel(
    sizes,
    hidden,
    cotangent,
    shard_mix,
    shard_out,
    shard_exp,
    shard_con,
    md,
    mu,
    od,
    ou,
    ed,
    eu,
    cd,
    cu,
    gains,
    unit_rank,
    picks,
    hidden_out,
    first_low,
    active,
    second_low,
    before_grad,
    attn_low,
    mixing,
    unit_go,
    early_grads,
    part_ranks,
    full_ranks,
    context,
    unit_qkv,
    unit_out,
    context_grad,
    unit_grad,
    sum_k,
    sum_v,
    local_qkv,
    w_out,
    w_exp,
    w_con,
    acc,
    red_up,
    red_down,
    stash,
    spreads,
    rank_in,
    stage_d,
    stage_f,
    rows_in,
    rank_buf,
    in_sem,
    out_sem,
    red_send,
    red_recv,
    cast_send,
    cast_recv,
    peer_send,
    peer_recv,
    twin_send,
    twin_recv,
    side_send,
    side_recv,
    own_sem,
    rank_send,
    rank_recv,
    mix_sem,
    qkv_send,
    qkv_recv,
    ctx_send,
    ctx_recv,
    go_send,
    go_recv,
    early_send,
    early_recv,
    unit_sem,
):
    ranks, dps, ctxs, chunks, rows, per_seq, period = sizes
    half = rows // 2
    width = hidden.shape[1]
    hidden_units = w_exp.shape[1]
    heads = w_out.shape[0]
    block = min(16, half)
    tile_f = math.gcd(hidden_units, 256)
    tile_d = math.gcd(width, 256)
    tile_h = math.gcd(heads, 256)
    me = lax.axis_index("tensor")
    dp = lax.axis_index("dp")
    ctx = lax.axis_index("ctx")
    pairs = ctxs // 2
    core = ctx % 2
    chips = dps * pairs
    chip = dp * pairs + ctx // 2
    twin = {"ctx": ctx + 1 - 2 * core}
    lead = per_seq
    units, seq_all = unit_qkv.shape[0], unit_qkv.shape[2]
    tok = seq_all // ctxs
    local_heads = local_qkv.shape[1]

    def chip_block(step, which):
        row, column = step // pairs, step % pairs
        from_dp = (dp + dps - row) % dps
        from_chip = (ctx // 2 + pairs - column) % pairs
        return from_dp * ctxs + from_chip * 2 + which

    total = chunks * rows
    enter(
        [{"tensor": (me + d) % ranks} for d in range(1, ranks)]
        + [{"ctx": (ctx + d) % ctxs} for d in range(1, ctxs)]
        + [{"dp": (dp + d) % dps} for d in range(1, dps)]
    )

    shards = (shard_mix, shard_out, shard_exp, shard_con)
    fulls = (stash, w_out, w_exp, w_con)
    mix_width = shard_mix.shape[1]
    mix_half = shard_mix.shape[0] // 2

    def piece_of(w, p):
        if w < 2:
            return shards[w]
        return shards[w].at[tile(p, shards[w].shape[0] // PIECES)]

    def block_of(w, index, p):
        deep, wide = shards[w].shape
        if w == 0:
            return stash.at[tile(index, deep), pl.ds(0, mix_width)]
        if w == 1:
            return w_out.at[:, tile(index, wide)]
        if w == 2:
            return w_exp.at[tile(index * PIECES + p, deep // PIECES)]
        return w_con.at[tile(p, deep // PIECES), tile(index, wide)]

    def mix_piece(step, lower):
        start = chip_block(step, core) * (2 * mix_half) + lower * mix_half
        return stash.at[pl.ds(pl.multiple_of(start, mix_half), mix_half), pl.ds(0, mix_width)]

    def peer_copy(w, step, p=0):
        row, column = step // pairs, step % pairs
        block = block_of(w, chip_block(column, core), p)
        if row:
            target = {"dp": (dp + row) % dps}
        else:
            target = {"ctx": (ctx + 2 * column) % ctxs}
        own = block_of(w, chip_block(0, core), p)
        if w == 0 and row and column:
            block = mix_piece(column, 0)
        return pltpu.make_async_remote_copy(
            src_ref=block if row and column else piece_of(w, p),
            dst_ref=block if row else own,
            send_sem=peer_send.at[w, step, p],
            recv_sem=peer_recv.at[w, step, p],
            device_id=target,
            device_id_type=MESH_IDS,
        )

    def peer_arrival(w, step, p=0):
        row = step // pairs
        if row:
            target = {"dp": (dp + row) % dps}
        else:
            target = {"ctx": (ctx + 2 * step) % ctxs}
        block = block_of(w, chip_block(step, core), p)
        if w == 0 and row and step % pairs:
            block = mix_piece(step, 0)
        return pltpu.make_async_remote_copy(
            src_ref=block,
            dst_ref=block,
            send_sem=peer_send.at[w, step, p],
            recv_sem=peer_recv.at[w, step, p],
            device_id=target,
            device_id_type=MESH_IDS,
        )

    def twin_copy(w, step, p=0):
        block = block_of(w, chip_block(step, core), p)
        return pltpu.make_async_remote_copy(
            src_ref=piece_of(w, p) if step == 0 else block,
            dst_ref=block,
            send_sem=twin_send.at[w, step, p],
            recv_sem=twin_recv.at[w, step, p],
            device_id=twin,
            device_id_type=MESH_IDS,
        )

    def twin_arrival(w, step, p=0):
        block = block_of(w, chip_block(step, 1 - core), p)
        return pltpu.make_async_remote_copy(
            src_ref=block,
            dst_ref=block,
            send_sem=twin_send.at[w, step, p],
            recv_sem=twin_recv.at[w, step, p],
            device_id=twin,
            device_id_type=MESH_IDS,
        )

    def own_copy(w, p=0):
        return pltpu.make_async_copy(piece_of(w, p), block_of(w, chip_block(0, core), p), own_sem.at[w, p])

    def side_copy(step):
        row, column = step // pairs, step % pairs
        piece = mix_piece(row * pairs, 1)
        return pltpu.make_async_remote_copy(
            src_ref=piece,
            dst_ref=piece,
            send_sem=side_send.at[step],
            recv_sem=side_recv.at[step],
            device_id={"ctx": (ctx + 2 * column) % ctxs},
            device_id_type=MESH_IDS,
        )

    def side_arrival(step):
        piece = mix_piece(step, 1)
        return pltpu.make_async_remote_copy(
            src_ref=piece,
            dst_ref=piece,
            send_sem=side_send.at[step],
            recv_sem=side_recv.at[step],
            device_id={"ctx": (ctx + 2 * (step % pairs)) % ctxs},
            device_id_type=MESH_IDS,
        )

    def across_start(w, p=0):
        for step in range(pairs, chips, pairs):
            peer_copy(w, step, p).start()
        twin_copy(w, 0, p).start()
        own_copy(w, p).start()

    def along_start(w, p=0):
        for step in range(1, pairs):
            peer_copy(w, step, p).start()

    def weight_relay(w, p=0):
        for step in range(1, pairs):
            peer_arrival(w, step, p).wait_recv()
            for row in range(1, dps):
                peer_copy(w, row * pairs + step, p).start()
            twin_copy(w, step, p).start()

    def weight_forward(w, p=0):
        for step in range(pairs, chips):
            peer_arrival(w, step, p).wait_recv()
            twin_copy(w, step, p).start()

    def mixing_gather():
        along_start(0)
        across_start(0)
        weight_relay(0)
        for row in range(1, dps):
            peer_arrival(0, row * pairs).wait_recv()
            for column in range(1, pairs):
                side_copy(row * pairs + column).start()
            twin_copy(0, row * pairs).start()
        for row in range(1, dps):
            for column in range(1, pairs):
                step = row * pairs + column
                peer_arrival(0, step).wait_recv()
                side_arrival(step).wait_recv()
                twin_copy(0, step).start()

    def weight_finish(w, p=0):
        own_copy(w, p).wait()
        for step in range(chips):
            twin_arrival(w, step, p).wait_recv()

    def side_sent():
        for row in range(1, dps):
            for column in range(1, pairs):
                side_copy(row * pairs + column).wait_send()

    def weight_sent(w, p=0):
        for step in range(1, chips):
            peer_copy(w, step, p).wait_send()
        for step in range(chips):
            twin_copy(w, step, p).wait_send()

    def unit_place(device, u):
        return (device // local_heads) * units + u, device % local_heads

    def qkv_copy(u, step):
        peer = (ctx + step) % ctxs
        s, h = unit_place(peer, u)
        return pltpu.make_async_remote_copy(
            src_ref=local_qkv.at[s, h],
            dst_ref=unit_qkv.at[u, :, tile(ctx, tok)],
            send_sem=qkv_send.at[u, step],
            recv_sem=qkv_recv.at[u, step],
            device_id={"ctx": peer},
            device_id_type=MESH_IDS,
        )

    def qkv_arrival(u, step):
        return pltpu.make_async_remote_copy(
            src_ref=local_qkv.at[0, 0],
            dst_ref=unit_qkv.at[u, :, tile((ctx + ctxs - step) % ctxs, tok)],
            send_sem=qkv_send.at[u, step],
            recv_sem=qkv_recv.at[u, step],
            device_id={"ctx": (ctx + step) % ctxs},
            device_id_type=MESH_IDS,
        )

    def qkv_own(u):
        s, h = unit_place(ctx, u)
        return pltpu.make_async_copy(
            local_qkv.at[s, h], unit_qkv.at[u, :, tile(ctx, tok)], unit_sem.at[0, u]
        )

    def context_place(device, u):
        s, h = unit_place(device, u)
        return context.at[tile(s, tok), tile(h, HEAD_DIM)]

    def context_copy(u, step):
        peer = (ctx + step) % ctxs
        return pltpu.make_async_remote_copy(
            src_ref=unit_out.at[u, tile(peer, tok)],
            dst_ref=context_place(ctx, u),
            send_sem=ctx_send.at[u, step],
            recv_sem=ctx_recv.at[u, step],
            device_id={"ctx": peer},
            device_id_type=MESH_IDS,
        )

    def context_arrival(u, step):
        return pltpu.make_async_remote_copy(
            src_ref=unit_out.at[u, tile(ctx, tok)],
            dst_ref=context_place((ctx + ctxs - step) % ctxs, u),
            send_sem=ctx_send.at[u, step],
            recv_sem=ctx_recv.at[u, step],
            device_id={"ctx": (ctx + step) % ctxs},
            device_id_type=MESH_IDS,
        )

    def context_own(u):
        return pltpu.make_async_copy(
            unit_out.at[u, tile(ctx, tok)], context_place(ctx, u), unit_sem.at[1, u]
        )

    def go_copy(u, step):
        peer = (ctx + step) % ctxs
        s, h = unit_place(peer, u)
        return pltpu.make_async_remote_copy(
            src_ref=context_grad.at[tile(s, tok), tile(h, HEAD_DIM)],
            dst_ref=unit_go.at[u, tile(ctx, tok)],
            send_sem=go_send.at[u, step],
            recv_sem=go_recv.at[u, step],
            device_id={"ctx": peer},
            device_id_type=MESH_IDS,
        )

    def go_arrival(u, step):
        return pltpu.make_async_remote_copy(
            src_ref=context_grad.at[tile(0, tok), tile(0, HEAD_DIM)],
            dst_ref=unit_go.at[u, tile((ctx + ctxs - step) % ctxs, tok)],
            send_sem=go_send.at[u, step],
            recv_sem=go_recv.at[u, step],
            device_id={"ctx": (ctx + step) % ctxs},
            device_id_type=MESH_IDS,
        )

    def go_own(u):
        s, h = unit_place(ctx, u)
        return pltpu.make_async_copy(
            context_grad.at[tile(s, tok), tile(h, HEAD_DIM)],
            unit_go.at[u, tile(ctx, tok)],
            unit_sem.at[2, u],
        )

    def go_start(u):
        for step in range(1, ctxs):
            go_copy(u, step).start()
        go_own(u).start()

    early = early_units(total, tok, units)

    def go_ready(u):
        go_own(u).wait()
        for step in range(1, ctxs):
            go_arrival(u, step).wait_recv()

    def early_place(device):
        return early_grads.at[:, :, tile(unit_place(device, 0)[1], HEAD_DIM)]

    def early_copy(step):
        peer = (ctx + step) % ctxs
        return pltpu.make_async_remote_copy(
            src_ref=unit_grad.at[0, :, tile(peer, tok)],
            dst_ref=early_place(ctx),
            send_sem=early_send.at[step],
            recv_sem=early_recv.at[step],
            device_id={"ctx": peer},
            device_id_type=MESH_IDS,
        )

    def early_arrival(step):
        return pltpu.make_async_remote_copy(
            src_ref=unit_grad.at[0, :, tile(ctx, tok)],
            dst_ref=early_place((ctx + ctxs - step) % ctxs),
            send_sem=early_send.at[step],
            recv_sem=early_recv.at[step],
            device_id={"ctx": (ctx + step) % ctxs},
            device_id_type=MESH_IDS,
        )

    def early_own():
        return pltpu.make_async_copy(
            unit_grad.at[0, :, tile(ctx, tok)], early_place(ctx), unit_sem.at[3, 0]
        )

    def early_back():
        go_ready(0)
        attention_back(unit_qkv, unit_go, unit_out, unit_grad, sum_k, sum_v, 0, 0)
        for step in range(1, ctxs):
            early_copy(step).start()
        early_own().start()

    def attend(u):
        qkv_own(u).wait()
        for step in range(1, ctxs):
            qkv_arrival(u, step).wait_recv()
        part = math.gcd(seq_all, 256)

        @pl.loop(0, seq_all // part)
        def _(i):
            rs = tile(i, part)
            scores = dot_nt(unit_qkv[u, 0, rs, :], unit_qkv[u, 1]) * (HEAD_DIM ** (-0.5))
            largest = jnp.max(scores, axis=-1, keepdims=True)
            raised = jnp.exp(scores - largest)
            total = jnp.sum(raised, axis=-1, keepdims=True)
            mixed = dot_nn(raised.astype(BF), unit_qkv[u, 2])
            unit_out[u, rs, :] = (mixed / total).astype(BF)

        for step in range(1, ctxs):
            context_copy(u, step).start()
        context_own(u).start()

    def context_ready(u):
        context_own(u).wait()
        for step in range(1, ctxs):
            context_arrival(u, step).wait_recv()

    def project_chunk(c):
        bring(hidden, c).wait()
        following = (c + 1) % chunks
        s = c // per_seq
        rs = tile(c % per_seq, rows)
        low = dot_nt(rows_in[...], md[picks[s]]).astype(BF)
        put_rank(3, c, low)
        rank_buf[...] = low
        heads_at_once = math.gcd(local_heads, 2)
        step = heads_at_once * HEAD_DIM

        @pl.loop(0, mix_width // step)
        def _(i):
            cs = tile(i, step)
            values = dot_nn(rows_in[...], stash[0:width, cs]) + dot_nn(rank_buf[...], mu[picks[s], :, cs])
            values = values.astype(BF)
            first = i * heads_at_once
            for k in range(heads_at_once):
                local_qkv[s, (first + k) % local_heads, (first + k) // local_heads, rs, :] = values[
                    :, k * HEAD_DIM : (k + 1) * HEAD_DIM
                ]

        bring(hidden, following).start()

    def project(s):
        @pl.loop(0, per_seq)
        def _(i):
            project_chunk(s * per_seq + i)

    def send_unit(u):
        qkv_own(u).start()
        for step in range(1, ctxs):
            qkv_copy(u, step).start()

    def job_of(number, rounds):
        safe = jnp.maximum(number, 0)
        chunk = safe % period
        valid = (number >= 0) & (chunk < chunks) & (safe < rounds * period)
        return valid, jnp.minimum(chunk, chunks - 1)

    comm = chain(
        ranks,
        half,
        block,
        me,
        acc,
        red_up,
        red_down,
        red_send,
        red_recv,
        cast_send,
        cast_recv,
        lambda number: job_of(number, 3),
    )

    def rows_of(c):
        return tile(c, rows)

    def spot(t, c, i=None):
        start = t * total + c * rows
        if i is None:
            return pl.ds(pl.multiple_of(start, rows), rows)
        return pl.ds(pl.multiple_of(start + i * block, block), block)

    def mixing_keep():
        return pltpu.make_async_copy(
            stash.at[pl.ds(0, width), pl.ds(0, mix_width)], mixing, mix_sem
        )

    def bring(source, c):
        return pltpu.make_async_copy(source.at[rows_of(c)], rows_in, in_sem)

    def keep(index, source, target, c):
        return pltpu.make_async_copy(source, target.at[rows_of(c)], out_sem.at[index])

    def put_rank(t, c, low):
        part_ranks[t, :, tile(c, rows)] = dot_nt(unit_rank[...], low).astype(BF)

    def rank_copy(t, step):
        return pltpu.make_async_remote_copy(
            src_ref=part_ranks.at[t],
            dst_ref=rank_in.at[t, step],
            send_sem=rank_send.at[t, step],
            recv_sem=rank_recv.at[t, step],
            device_id={"tensor": (me + step) % ranks},
            device_id_type=MESH_IDS,
        )

    def mean(values):
        return jnp.sum(values, axis=-1, keepdims=True) * (1.0 / width)

    def attend_part(c, s):
        mine = context[rows_of(c), :]
        low = dot_nt(mine, od[picks[s]]).astype(BF)
        put_rank(0, c, low)

        @pl.loop(0, width // tile_d)
        def _(i):
            cs = tile(i, tile_d)
            acc[c, :, cs] = (dot_nn(mine, w_out[:, cs]) + dot_nn(low, ou[picks[s], :, cs])).astype(BF)

    def forward_first(c, s):
        bring(hidden, c).wait()

        @pl.loop(0, rows // block)
        def _(i):
            rs = tile(i, block)
            total = rows_in[rs, :].astype(F32) + acc[c, rs, :].astype(F32)
            centred = total - mean(total)
            spread = lax.rsqrt(mean(centred * centred) + 1e-06)
            n = centred * spread
            stash[spot(0, c, i), :] = n.astype(BF)
            spreads[c, rs, :] = jnp.broadcast_to(spread, (block, 128))
            stage_d[rs, :] = (n * gains[0:1, :] + gains[1:2, :]).astype(BF)

        low = dot_nt(stage_d[...], ed[picks[s]]).astype(BF)
        put_rank(4, c, low)
        rank_buf[...] = low

        @pl.loop(0, hidden_units // tile_f)
        def _(i):
            cs = tile(i, tile_f)
            b = dot_nn(stage_d[...], w_exp[:, cs]) + dot_nn(rank_buf[...], eu[picks[s], :, cs])
            square = b * b
            t = jnp.tanh(GELU_C * b * (1.0 + GELU_A * square))
            upper = 0.5 * (1.0 + t)
            stage_f[:, cs] = (b * upper).astype(BF)
            stash[spot(1, c), cs] = (
                upper
                + (0.5 * GELU_C) * b * (1.0 - t * t) * (1.0 + (3.0 * GELU_A) * square)
            ).astype(BF)

    def forward_second(c, s):
        low = dot_nt(stage_f[...], cd[picks[s]]).astype(BF)
        put_rank(1, c, low)
        rank_buf[...] = low

        @pl.loop(0, width // tile_d)
        def _(i):
            cs = tile(i, tile_d)
            acc[c, :, cs] = (
                dot_nn(stage_f[...], w_con[:, cs]) + dot_nn(rank_buf[...], cu[picks[s], :, cs])
            ).astype(BF)

        keep(0, stage_d, first_low, c).start()
        keep(1, stage_f, active, c).start()

    def back_first(c, s):
        bring(cotangent, c).wait()

        @pl.loop(0, rows // block)
        def _(i):
            rs = tile(i, block)
            first = stash[spot(0, c, i), :].astype(F32) * gains[0:1, :] + gains[1:2, :]
            total = first + acc[c, rs, :].astype(F32)
            centred = total - mean(total)
            spread = lax.rsqrt(mean(centred * centred) + 1e-06)
            n = centred * spread
            stage_d[rs, :] = (n * gains[2:3, :] + gains[3:4, :]).astype(BF)
            g = rows_in[rs, :].astype(F32) * gains[2:3, :]
            stash[spot(2, c, i), :] = (spread * (g - mean(g) - n * mean(g * n))).astype(BF)

        low = dot_nt(stash[spot(2, c), :], cu[picks[s]]).astype(BF)
        put_rank(5, c, low)
        rank_buf[...] = low

        @pl.loop(0, hidden_units // tile_f)
        def _(i):
            cs = tile(i, tile_f)
            da = dot_nt(stash[spot(2, c), :], w_con[cs, :]) + dot_nn(rank_buf[...], cd[picks[s], :, cs])
            stage_f[:, cs] = (da * stash[spot(1, c), cs].astype(F32)).astype(BF)

    def back_second(c, s):
        low = dot_nt(stage_f[...], eu[picks[s]]).astype(BF)
        put_rank(2, c, low)
        rank_buf[...] = low

        @pl.loop(0, width // tile_d)
        def _(i):
            cs = tile(i, tile_d)
            acc[c, :, cs] = (
                dot_nt(stage_f[...], w_exp[cs, :]) + dot_nn(rank_buf[...], ed[picks[s], :, cs])
            ).astype(BF)

        keep(0, stage_d, hidden_out, c).start()
        keep(1, stage_f, before_grad, c).start()
        keep(2, stash.at[spot(2, c)], second_low, c).start()

    def last_first(c, s):
        @pl.loop(0, rows // block)
        def _(i):
            rs = tile(i, block)
            n = stash[spot(0, c, i), :].astype(F32)
            g = (stash[spot(2, c, i), :].astype(F32) + acc[c, rs, :].astype(F32)) * gains[0:1, :]
            spread = spreads[c, rs, 0:1]
            stage_d[rs, :] = (spread * (g - mean(g) - n * mean(g * n))).astype(BF)

    def last_second(c, s):
        low = dot_nt(stage_d[...], ou[picks[s]]).astype(BF)
        put_rank(6, c, low)
        rank_buf[...] = low

        @pl.loop(0, heads // tile_h)
        def _(i):
            cs = tile(i, tile_h)
            context_grad[rows_of(c), cs] = (
                dot_nt(stage_d[...], w_out[cs, :]) + dot_nn(rank_buf[...], od[picks[s], :, cs])
            ).astype(BF)

        keep(0, stage_d, attn_low, c).start()

    seqs = chunks // per_seq
    flowing = units == seqs
    bring(hidden, 0).start()
    mixing_gather()
    weight_finish(0)
    along_start(1)
    across_start(1)
    mixing_keep().start()
    if flowing:
        for u in range(min(2, units)):
            project(u)
            send_unit(u)
    else:
        pl.loop(0, seqs)(project)
        for u in range(units):
            send_unit(u)
    weight_relay(1)

    @pl.loop(0, lead + 3 * period + chunks)
    def _(now):
        tick = now - lead
        stage = jnp.maximum(tick, 0) // period
        valid, c = job_of(tick, 4)
        s = c // per_seq
        last_valid, last_c = job_of(tick - 1, 4)
        last_stage = jnp.maximum(tick - 1, 0) // period

        comm(tick, 0)

        @pl.when(last_valid & (last_stage >= 1))
        def _():
            keep(0, stage_d, first_low, last_c).wait()

        @pl.when(last_valid & (last_stage >= 1) & (last_stage <= 2))
        def _():
            keep(1, stage_f, active, last_c).wait()

        @pl.when(last_valid & (last_stage == 2))
        def _():
            keep(2, stash.at[spot(2, last_c)], second_low, last_c).wait()

        pl.when(now == 1)(lambda: weight_forward(1))
        pl.when((now % per_seq == 0) & (now < units * per_seq))(lambda: attend(now // per_seq))
        if flowing:

            @pl.when((now % per_seq == 1) & (now < (units - 2) * per_seq))
            def _():
                project(now // per_seq + 2)
                send_unit(now // per_seq + 2)

        @pl.when((now % per_seq == 1) & (now > per_seq) & (now <= PIECES * per_seq + 1))
        def _():
            p = now // per_seq - 1
            weight_relay(2, p)
            weight_relay(3, p)

        @pl.when((now % per_seq == 1) & (now < PIECES * per_seq))
        def _():
            for w in (2, 3):
                along_start(w, now // per_seq)
                across_start(w, now // per_seq)

        @pl.when((now % per_seq == 0) & (now > per_seq) & (now <= (PIECES + 1) * per_seq))
        def _():
            p = now // per_seq - 2
            weight_forward(2, p)
            weight_forward(3, p)

        @pl.when(now == lead + period)
        def _():
            for p in range(PIECES):
                weight_finish(2, p)
                weight_finish(3, p)

        pl.when(now == lead)(lambda: weight_finish(1))

        @pl.when(now == lead + period - 2)
        def _():
            mixing_keep().wait()
            weight_sent(0)
            side_sent()

        for t in range(3):

            @pl.when(tick == (t + 1) * period)
            def _(t=t):
                for step in range(1, ranks):
                    rank_copy(t, step).start()

        pl.when((tick >= 0) & (tick % per_seq == 0) & (tick < units * per_seq))(
            lambda: context_ready(s)
        )

        pl.when(valid & (stage == 1))(lambda: forward_first(c, s))
        pl.when(valid & (stage == 2))(lambda: back_first(c, s))
        pl.when(valid & (stage == 3))(lambda: last_first(c, s))

        comm(tick, 1)

        pl.when(valid & (stage == 0))(lambda: attend_part(c, s))
        pl.when(valid & (stage == 1))(lambda: forward_second(c, s))
        pl.when(valid & (stage == 2))(lambda: back_second(c, s))
        pl.when(valid & (stage == 3))(lambda: last_second(c, s))
        if flowing:
            pl.when(valid & (stage == 3) & (c % per_seq == per_seq - 1))(lambda: go_start(s))
        if early:
            pl.when(tick == 3 * period + EARLY_AT)(early_back)

        next_valid, next_c = job_of(tick + 1, 4)
        next_stage = jnp.maximum(tick + 1, 0) // period
        pl.when(next_valid & (next_stage == 1) & (next_c > 0))(
            lambda: bring(hidden, next_c).start()
        )
        pl.when(next_valid & (next_stage == 2))(lambda: bring(cotangent, next_c).start())

    keep(0, stage_d, attn_low, chunks - 1).wait()
    for t in range(3):
        value = part_ranks[t].astype(F32)
        for step in range(1, ranks):
            rank_copy(t, step).wait_recv()
            value = value + rank_in[t, step].astype(F32)
        full_ranks[t] = value.astype(BF)
    for t in range(3):
        for step in range(1, ranks):
            rank_copy(t, step).wait_send()
    weight_sent(1)
    for p in range(PIECES):
        weight_sent(2, p)
        weight_sent(3, p)
    for u in range(units):
        if not flowing:
            go_start(u)
        for step in range(1, ctxs):
            qkv_copy(u, step).wait_send()
            context_copy(u, step).wait_send()
    for u in range(units):
        if u >= early:
            go_ready(u)
        for step in range(1, ctxs):
            go_copy(u, step).wait_send()
    if early:
        early_own().wait()
        for step in range(1, ctxs):
            early_arrival(step).wait_recv()
            early_copy(step).wait_send()


def enter(others):
    barrier = pltpu.get_barrier_semaphore()
    for other in others:
        pl.semaphore_signal(barrier, inc=1, device_id=other, device_id_type=MESH_IDS)
    pl.semaphore_wait(barrier, len(others))


def middle(hidden, cotangent, shards, picked, gains, tok, picks):
    total, width = hidden.shape
    mix_width = shards[0].shape[1]
    heads, hidden_units = shards[1].shape[0], shards[2].shape[1]
    ranks, dps, ctxs = (lax.axis_size(name) for name in ("tensor", "dp", "ctx"))
    seqs, rank = picks.shape[0], picked[0].shape[1]
    local_heads = heads // HEAD_DIM
    units = seqs * local_heads // ctxs
    rows = math.gcd(tok, CHUNK_ROWS)
    chunks = total // rows
    period = max(chunks, 2 * ranks)
    sizes = (ranks, dps, ctxs, chunks, rows, tok // rows, period)
    chips = dps * ctxs // 2
    vm = pl.BlockSpec(memory_space=pltpu.VMEM)
    hb = pl.BlockSpec(memory_space=pl.ANY)
    sm = pl.BlockSpec(memory_space=pltpu.SMEM)
    half = rows // 2
    dma = pltpu.SemaphoreType.DMA

    def shape(*dims):
        return jax.ShapeDtypeStruct(dims, BF)

    return pl.pallas_call(
        functools.partial(middle_kernel, sizes),
        out_shape=(
            shape(total, width),
            shape(total, width),
            shape(total, hidden_units),
            shape(total, width),
            shape(total, hidden_units),
            shape(total, width),
            shape(width, mix_width),
            shape(units, tok * ctxs, HEAD_DIM),
            shape(3, tok, heads),
            shape(7, rank, total),
            shape(3, rank, total),
            shape(total, heads),
            shape(units, 3, tok * ctxs, HEAD_DIM),
            shape(units, tok * ctxs, HEAD_DIM),
        ),
        in_specs=[hb] * 6 + [vm] * 10 + [sm],
        out_specs=(hb,) * 7 + (vm,) * 7,
        scratch_shapes=[
            pltpu.VMEM((total, heads), BF),
            pltpu.VMEM((1, 3, tok * ctxs, HEAD_DIM), BF),
            pltpu.VMEM((tok * ctxs, HEAD_DIM), F32),
            pltpu.VMEM((tok * ctxs, HEAD_DIM), F32),
            pltpu.VMEM((seqs, local_heads, 3, tok, HEAD_DIM), BF),
            pltpu.VMEM((heads, width), BF),
            pltpu.VMEM((width, hidden_units), BF),
            pltpu.VMEM((hidden_units, width), BF),
            pltpu.VMEM((chunks, rows, width), BF),
            pltpu.VMEM((chunks, half, width), BF),
            pltpu.VMEM((chunks, half, width), BF),
            pltpu.VMEM((3 * total, width), BF),
            pltpu.VMEM((chunks, rows, 128), F32),
            pltpu.VMEM((3, ranks, rank, total), BF),
            pltpu.VMEM((rows, width), BF),
            pltpu.VMEM((rows, hidden_units), BF),
            pltpu.VMEM((rows, width), BF),
            pltpu.VMEM((rows, rank), BF),
            dma(()),
            dma((3,)),
            dma((2, chunks)),
            dma((2, chunks)),
            dma((2, chunks)),
            dma((2, chunks)),
            dma((4, chips, PIECES)),
            dma((4, chips, PIECES)),
            dma((4, chips, PIECES)),
            dma((4, chips, PIECES)),
            dma((chips,)),
            dma((chips,)),
            dma((4, PIECES)),
            dma((3, ranks)),
            dma((3, ranks)),
            dma(()),
            dma((units, ctxs)),
            dma((units, ctxs)),
            dma((units, ctxs)),
            dma((units, ctxs)),
            dma((units, ctxs)),
            dma((units, ctxs)),
            dma((ctxs,)),
            dma((ctxs,)),
            dma((4, units)),
        ],
        compiler_params=pltpu.CompilerParams(
            collective_id=0, has_side_effects=True, vmem_limit_bytes=VMEM_BYTES
        ),
        cost_estimate=pl.CostEstimate(
            flops=8 * total * width * hidden_units + 4 * total * width * heads,
            bytes_accessed=16 * total * width,
            transcendentals=total * hidden_units,
        ),
    )(hidden, cotangent, *shards, *picked, gains, jnp.eye(rank, dtype=BF), picks)


def mixing_kernel(
    sizes,
    unit_go,
    unit_qkv,
    unit_out,
    mixing_far,
    mu,
    md,
    attn_low,
    unit_rank,
    early_grads,
    hidden_far,
    mix_rank,
    row_hot,
    picks,
    input_grad,
    table_sum,
    grads,
    mixing,
    hidden,
    rank_part,
    rank_in,
    wide,
    table_part,
    table_in,
    unit_grad,
    sum_k,
    sum_v,
    acc,
    red_up,
    red_down,
    stage_d,
    rows_in,
    rank_buf,
    in_sem,
    out_sem,
    red_send,
    red_recv,
    cast_send,
    cast_recv,
    far_sem,
    grad_send,
    grad_recv,
    unit_sem,
    rank_send,
    rank_recv,
    part_send,
    part_recv,
    whole_send,
    whole_recv,
):
    ranks, dps, ctxs, chunks, rows, per_seq, group = sizes
    half = rows // 2
    width = mixing.shape[0]
    heads = grads.shape[2]
    local_heads = heads // HEAD_DIM
    units, seq_all = unit_go.shape[0], unit_go.shape[1]
    tok = seq_all // ctxs
    block = min(16, half)
    tile_d = math.gcd(width, 256)
    scale = HEAD_DIM ** (-0.5)
    me = lax.axis_index("tensor")
    ctx = lax.axis_index("ctx")
    dp = lax.axis_index("dp")
    parts = dps * ctxs
    index = dp * ctxs + ctx
    rank = mu.shape[1]
    tables, _, part_width = table_part.shape
    segments = parts // NADAPT
    tile_g = math.gcd(part_width, 256)

    def part_place(step):
        other = (index + step) % parts
        return {"dp": other // ctxs, "ctx": other % ctxs}

    enter(
        [{"tensor": (me + d) % ranks} for d in range(1, ranks)]
        + [part_place(d) for d in range(1, parts)]
    )

    def unit_place(device, u):
        return (device // local_heads) * units + u, device % local_heads

    def mixing_load():
        return pltpu.make_async_copy(mixing_far, mixing, far_sem.at[0])

    def early_load():
        return pltpu.make_async_copy(early_grads, grads.at[:, pl.ds(0, tok)], far_sem.at[2])

    def hidden_load():
        return pltpu.make_async_copy(hidden_far, hidden, far_sem.at[1])

    def grads_place(device, u):
        s, h = unit_place(device, u)
        return grads.at[:, tile(s, tok), tile(h, HEAD_DIM)]

    def grad_copy(u, step):
        peer = (ctx + step) % ctxs
        return pltpu.make_async_remote_copy(
            src_ref=unit_grad.at[u, :, tile(peer, tok)],
            dst_ref=grads_place(ctx, u),
            send_sem=grad_send.at[u, step],
            recv_sem=grad_recv.at[u, step],
            device_id={"ctx": peer},
            device_id_type=MESH_IDS,
        )

    def grad_arrival(u, step):
        return pltpu.make_async_remote_copy(
            src_ref=unit_grad.at[u, :, tile(ctx, tok)],
            dst_ref=grads_place((ctx + ctxs - step) % ctxs, u),
            send_sem=grad_send.at[u, step],
            recv_sem=grad_recv.at[u, step],
            device_id={"ctx": (ctx + step) % ctxs},
            device_id_type=MESH_IDS,
        )

    def grad_own(u):
        return pltpu.make_async_copy(
            unit_grad.at[u, :, tile(ctx, tok)], grads_place(ctx, u), unit_sem.at[u]
        )

    def attend_back(u):
        attention_back(unit_qkv, unit_go, unit_out, unit_grad, sum_k, sum_v, u, u)
        for step in range(1, ctxs):
            grad_copy(u, step).start()
        grad_own(u).start()

    def grads_ready(u):
        grad_own(u).wait()
        for step in range(1, ctxs):
            grad_arrival(u, step).wait_recv()

    early = early_units(chunks * rows, tok, units)
    lead = per_seq * (1 - early)
    if early:
        early_load().start()
    mixing_load().start()
    hidden_load().start()

    def job_of(number):
        return (number >= 0) & (number < chunks), jnp.clip(number, 0, chunks - 1)

    comm = chain(
        ranks, half, block, me, acc, red_up, red_down, red_send, red_recv, cast_send, cast_recv, job_of
    )

    def rows_of(c):
        return tile(c, rows)

    def bring(c):
        return pltpu.make_async_copy(attn_low.at[rows_of(c)], rows_in, in_sem)

    def keep(c):
        return pltpu.make_async_copy(stage_d, input_grad.at[rows_of(c)], out_sem)

    def back_part(c, s):
        rs = pl.ds(pl.multiple_of(c * rows, group * rows), group * rows)
        low = jnp.zeros((group * rows, mu.shape[1]), F32)
        for j in range(3):
            low = low + dot_nt(grads[j, rs, :], mu[picks[s], :, pl.ds(j * heads, heads)])
        low = low.astype(BF)
        rank_part[:, pl.ds(pl.multiple_of(c * rows, group * rows), group * rows)] = dot_nt(
            unit_rank[...], low
        ).astype(BF)
        rank_buf[...] = low

        @pl.loop(0, width // tile_d)
        def _(i):
            cs = tile(i, tile_d)
            total = dot_nn(rank_buf[...], md[picks[s], :, cs])
            for j in range(3):
                total = total + dot_nt(grads[j, rs, :], mixing[cs, pl.ds(j * heads, heads)])
            total = total.astype(BF)
            for k in range(group):
                acc[c + k, :, cs] = total[k * rows : (k + 1) * rows, :]

    def final_part(c):
        bring(c).wait()

        @pl.loop(0, rows // block)
        def _(i):
            rs = tile(i, block)
            stage_d[rs, :] = (rows_in[rs, :].astype(F32) + acc[c, rs, :].astype(F32)).astype(BF)

        keep(c).start()

    def rank_copy(step):
        return pltpu.make_async_remote_copy(
            src_ref=rank_part,
            dst_ref=rank_in.at[step],
            send_sem=rank_send.at[step],
            recv_sem=rank_recv.at[step],
            device_id={"tensor": (me + step) % ranks},
            device_id_type=MESH_IDS,
        )

    def part_copy(step):
        return pltpu.make_async_remote_copy(
            src_ref=table_part.at[(index + step) % parts],
            dst_ref=table_in.at[step],
            send_sem=part_send.at[step],
            recv_sem=part_recv.at[step],
            device_id=part_place(step),
            device_id_type=MESH_IDS,
        )

    def whole_copy(step):
        return pltpu.make_async_remote_copy(
            src_ref=table_sum.at[index],
            dst_ref=table_sum.at[index],
            send_sem=whole_send.at[step],
            recv_sem=whole_recv.at[step],
            device_id=part_place(step),
            device_id_type=MESH_IDS,
        )

    def whole_arrival(step):
        return pltpu.make_async_remote_copy(
            src_ref=table_sum.at[index],
            dst_ref=table_sum.at[(index + parts - step) % parts],
            send_sem=whole_send.at[step],
            recv_sem=whole_recv.at[step],
            device_id=part_place(step),
            device_id_type=MESH_IDS,
        )

    def put_table(column, values):
        segment = column // part_width
        cs = pl.ds(pl.multiple_of(column % part_width, tile_g), tile_g)
        for n in range(NADAPT):
            table_part[n * segments + segment, :, cs] = values[n * rank : (n + 1) * rank, :].astype(
                BF
            )

    def make_tables():
        value = rank_part[...].astype(F32)
        for step in range(1, ranks):
            rank_copy(step).wait_recv()
            value = value + rank_in[step].astype(F32)
        for n in range(NADAPT):
            hot = row_hot[n : n + 1, :]
            wide[0, pl.ds(n * rank, rank), :] = (value * hot).astype(BF)
            wide[1, pl.ds(n * rank, rank), :] = (mix_rank[...].astype(F32) * hot).astype(BF)

        @pl.loop(0, width // tile_g)
        def _(i):
            put_table(i * tile_g, dot_nn(wide[0], hidden[:, tile(i, tile_g)]))

        for j in range(3):

            @pl.loop(0, heads // tile_g)
            def _(i):
                put_table(
                    width + j * heads + i * tile_g, dot_nn(wide[1], grads[j, :, tile(i, tile_g)])
                )

        for step in range(1, parts):
            part_copy(step).start()

    def sum_tables():
        value = table_part[index].astype(F32)
        for step in range(1, parts):
            part_copy(step).wait_recv()
            value = value + table_in[step].astype(F32)
        table_sum[index] = value.astype(BF)
        for step in range(1, parts):
            whole_copy(step).start()

    delay = max(2 * ranks - 1, 4)

    @pl.loop(0, lead + chunks + delay)
    def _(now):
        tick = now - lead

        @pl.when(tick == chunks)
        def _():
            for step in range(1, ranks):
                rank_copy(step).start()

        valid, c = job_of(tick)
        final, c_final = job_of(tick - delay)
        before, c_before = job_of(tick - delay - 1)
        coming, c_coming = job_of(tick - delay + 1)
        s = c // per_seq

        comm(tick, 0)

        pl.when(
            (tick >= early * per_seq) & (tick % per_seq == 0) & (tick < units * per_seq)
        )(lambda: grads_ready(s))
        if not early:
            pl.when((now % per_seq == 0) & (now < units * per_seq))(
                lambda: attend_back(now // per_seq)
            )
        comm(tick, 1)
        if early:
            pl.when((now % per_seq == 0) & (now < (units - 1) * per_seq))(
                lambda: attend_back(now // per_seq + 1)
            )
            pl.when(tick == 0)(lambda: early_load().wait())

        pl.when(tick == 0)(lambda: mixing_load().wait())
        pl.when(valid & (tick % group == 0))(lambda: back_part(c, s))

        @pl.when(tick == chunks + 1)
        def _():
            hidden_load().wait()
            make_tables()

        pl.when(tick == chunks + 3)(sum_tables)

        pl.when(before)(lambda: keep(c_before).wait())
        pl.when(final)(lambda: final_part(c_final))
        pl.when(coming)(lambda: bring(c_coming).start())

    keep(chunks - 1).wait()
    for step in range(1, ranks):
        rank_copy(step).wait_send()
    for step in range(1, parts):
        whole_arrival(step).wait_recv()
    for step in range(1, parts):
        part_copy(step).wait_send()
        whole_copy(step).wait_send()
    for u in range(early, units):
        for step in range(1, ctxs):
            grad_copy(u, step).wait_send()


def mixing_back(
    unit_go, early_grads, unit_qkv, unit_out, mixing, picked, attn_low, hidden, mix_rank, row_hot, picks
):
    mu, md = picked
    total, width = attn_low.shape
    heads = mixing.shape[1] // 3
    ranks, dps, ctxs = (lax.axis_size(name) for name in ("tensor", "dp", "ctx"))
    parts = dps * ctxs
    part_width = (width + 3 * heads) * NADAPT // parts
    units, _, seq_all, _ = unit_qkv.shape
    tok = seq_all // ctxs
    rank = mu.shape[1]
    rows = math.gcd(tok, LAST_ROWS)
    chunks = total // rows
    per_seq = tok // rows
    group = math.gcd(per_seq, 2)
    half = rows // 2
    sizes = (ranks, dps, ctxs, chunks, rows, per_seq, group)
    vm = pl.BlockSpec(memory_space=pltpu.VMEM)
    hb = pl.BlockSpec(memory_space=pl.ANY)
    sm = pl.BlockSpec(memory_space=pltpu.SMEM)
    dma = pltpu.SemaphoreType.DMA
    return pl.pallas_call(
        functools.partial(mixing_kernel, sizes),
        out_shape=(
            jax.ShapeDtypeStruct((total, width), BF),
            jax.ShapeDtypeStruct((parts, rank, part_width), BF),
        ),
        in_specs=[vm] * 3 + [hb] + [vm] * 2 + [hb, vm, hb, hb] + [vm] * 2 + [sm],
        out_specs=(hb, vm),
        scratch_shapes=[
            pltpu.VMEM((3, total, heads), BF),
            pltpu.VMEM((width, 3 * heads), BF),
            pltpu.VMEM((total, width), BF),
            pltpu.VMEM((rank, total), BF),
            pltpu.VMEM((ranks, rank, total), BF),
            pltpu.VMEM((2, NADAPT * rank, total), BF),
            pltpu.VMEM((parts, rank, part_width), BF),
            pltpu.VMEM((parts, rank, part_width), BF),
            pltpu.VMEM((units, 3, seq_all, HEAD_DIM), BF),
            pltpu.VMEM((seq_all, HEAD_DIM), F32),
            pltpu.VMEM((seq_all, HEAD_DIM), F32),
            pltpu.VMEM((chunks, rows, width), BF),
            pltpu.VMEM((chunks, half, width), BF),
            pltpu.VMEM((chunks, half, width), BF),
            pltpu.VMEM((rows, width), BF),
            pltpu.VMEM((rows, width), BF),
            pltpu.VMEM((group * rows, rank), BF),
            dma(()),
            dma(()),
            dma((2, chunks)),
            dma((2, chunks)),
            dma((2, chunks)),
            dma((2, chunks)),
            dma((3,)),
            dma((units, ctxs)),
            dma((units, ctxs)),
            dma((units,)),
            dma((ranks,)),
            dma((ranks,)),
            dma((parts,)),
            dma((parts,)),
            dma((parts,)),
            dma((parts,)),
        ],
        compiler_params=pltpu.CompilerParams(
            collective_id=1, has_side_effects=True, vmem_limit_bytes=VMEM_LAST
        ),
        cost_estimate=pl.CostEstimate(
            flops=6 * total * width * heads + 10 * units * seq_all * seq_all * HEAD_DIM,
            bytes_accessed=8 * total * width,
            transcendentals=units * seq_all * seq_all,
        ),
    )(
        unit_go,
        unit_qkv,
        unit_out,
        mixing,
        mu,
        md,
        attn_low,
        jnp.eye(rank, dtype=BF),
        early_grads,
        hidden,
        mix_rank,
        row_hot,
        picks,
    )


def per_device(
    hidden_in,
    output_cotangent,
    adapter_index,
    mixing_weight,
    output_weight,
    expand_weight,
    contract_weight,
    first_gain,
    first_shift,
    second_gain,
    second_shift,
    mixing_down,
    mixing_up,
    output_down,
    output_up,
    expand_down,
    expand_up,
    contract_down,
    contract_up,
):
    seq_count, tok_count, model_width = hidden_in.shape
    local_heads = mixing_weight.shape[2] // HEAD_DIM
    local_width = mixing_weight.shape[2]
    rows_all = seq_count * tok_count
    adapter_ids = jnp.arange(NADAPT, dtype=jnp.int32)
    onehot_low = (adapter_index == adapter_ids[None, :]).astype(jnp.bfloat16)
    picks = adapter_index.reshape(-1)
    rank = mixing_down.shape[1]
    mixing_flat = mixing_weight.reshape(mixing_weight.shape[0], 3 * local_width)
    hidden_rows = hidden_in.reshape(rows_all, model_width)
    mixing_up_flat = mixing_up.reshape(NADAPT, rank, 3 * local_width)
    gains = jnp.stack([first_gain, first_shift, second_gain, second_shift])
    (
        out_rows,
        first_low,
        active_low,
        second_low,
        before_low,
        attn_low,
        mixing_full,
        unit_go,
        early_grads,
        part_ranks,
        full_ranks,
        context,
        unit_qkv,
        unit_out,
    ) = middle(
        hidden_rows,
        output_cotangent.reshape(rows_all, model_width),
        (mixing_flat, output_weight, expand_weight, contract_weight),
        (
            mixing_down,
            mixing_up_flat,
            output_down,
            output_up,
            expand_down,
            expand_up,
            contract_down,
            contract_up,
        ),
        gains,
        tok_count,
        picks,
    )
    row_hot = jnp.repeat(onehot_low.T, tok_count, axis=1)

    def table_grad(ranks, values):
        wide = (row_hot[:, None, :] * ranks[None, :, :]).reshape(-1, rows_all)
        part = jnp.einsum("kn,nd->kd", wide, values, preferred_element_type=jnp.float32)
        return part.astype(jnp.bfloat16).reshape(NADAPT, rank, values.shape[1])

    early = (
        table_grad(part_ranks[6], context),
        table_grad(full_ranks[0], attn_low),
        table_grad(full_ranks[2], first_low),
        table_grad(part_ranks[4], before_low),
        table_grad(part_ranks[5], active_low),
        table_grad(full_ranks[1], second_low),
    )
    early, unit_go = lax.optimization_barrier((early, unit_go))
    input_rows, late = mixing_back(
        unit_go,
        early_grads,
        unit_qkv,
        unit_out,
        mixing_full,
        (mixing_up_flat, mixing_down),
        attn_low,
        hidden_rows,
        part_ranks[3],
        row_hot.astype(jnp.float32),
        picks,
    )
    early = lax.psum(early, ("dp", "ctx"))
    late = late.reshape(NADAPT, -1, rank, late.shape[2]).swapaxes(1, 2).reshape(NADAPT, rank, -1)
    late = (
        late[:, :, :model_width],
        late[:, :, model_width:].reshape(NADAPT, rank, 3, local_width),
    )
    summed = tuple(part.astype(jnp.float32) for part in late + early)
    return (
        out_rows.reshape(hidden_in.shape),
        input_rows.reshape(hidden_in.shape),
    ) + summed


def solution(mesh):
    return jax.shard_map(
        per_device,
        mesh=mesh,
        in_specs=(
            P("dp", "ctx", None),
            P("dp", "ctx", None),
            P("dp", None),
            P(("dp", "ctx"), None, "tensor"),
            P("tensor", ("dp", "ctx")),
            P(("dp", "ctx"), "tensor"),
            P("tensor", ("dp", "ctx")),
            P(),
            P(),
            P(),
            P(),
            P(),
            P(None, None, None, "tensor"),
            P(None, None, "tensor"),
            P(),
            P(),
            P(None, None, "tensor"),
            P(None, None, "tensor"),
            P(),
        ),
        out_specs=(
            P("dp", "ctx", None),
            P("dp", "ctx", None),
            P(),
            P(None, None, None, "tensor"),
            P(None, None, "tensor"),
            P(),
            P(),
            P(None, None, "tensor"),
            P(None, None, "tensor"),
            P(),
        ),
        check_vma=False,
    )
```

```python
import functools
import math

import jax
import jax.numpy as jnp
from jax import lax
from jax.experimental import pallas as pl
from jax.experimental.pallas import tpu as pltpu
from jax.sharding import PartitionSpec as P

HEAD_DIM = 128
NADAPT = 8
CHUNK_ROWS = 128
LAST_ROWS = 128
VMEM_BYTES = 62 * 2**20
VMEM_LAST = 56 * 2**20
PIECES = 4
EARLY_AT = 3


BF = jnp.bfloat16
F32 = jnp.float32
MESH_IDS = pl.DeviceIdType.MESH
RANK_ROWS = 16
GELU_C = 0.7978845608028654
GELU_A = 0.044715


def dot_nn(a, b):
    return lax.dot_general(a, b, (((1,), (0,)), ((), ())), preferred_element_type=F32)


def dot_nt(a, b):
    return lax.dot_general(a, b, (((1,), (1,)), ((), ())), preferred_element_type=F32)


def dot_tn(a, b):
    return lax.dot_general(a, b, (((0,), (0,)), ((), ())), preferred_element_type=F32)


def tile(index, size):
    return pl.ds(pl.multiple_of(index * size, size), size)


def chain(
    ranks, half, block, me, acc, red_up, red_down, red_send, red_recv, cast_send, cast_recv, job_of
):
    def comm(tick, way):
        upward = way == 0
        place = me if upward else ranks - 1 - me
        ahead = me + 1 if upward else me - 1
        behind = me - 1 if upward else me + 1
        red = red_up if upward else red_down
        part = pl.ds(way * half, half)

        def red_copy(c):
            return pltpu.make_async_remote_copy(
                src_ref=red.at[c],
                dst_ref=red.at[c],
                send_sem=red_send.at[way, c],
                recv_sem=red_recv.at[way, c],
                device_id={"tensor": ahead},
                device_id_type=MESH_IDS,
            )

        def cast_copy(c):
            return pltpu.make_async_remote_copy(
                src_ref=acc.at[c, part],
                dst_ref=acc.at[c, part],
                send_sem=cast_send.at[way, c],
                recv_sem=cast_recv.at[way, c],
                device_id={"tensor": behind},
                device_id_type=MESH_IDS,
            )

        old_red, c_old = job_of(tick - 2 - place)

        @pl.when(old_red & (place < ranks - 1))
        def _():
            red_copy(c_old).wait_send()

        old_cast, c_cast = job_of(tick - 2 * ranks + place)

        @pl.when(old_cast & (place > 0))
        def _():
            cast_copy(c_cast).wait_send()

        now_red, c = job_of(tick - 1 - place)

        @pl.when(now_red & (place == 0))
        def _():
            red[c] = acc[c, part, :]

        @pl.when(now_red & (place > 0))
        def _():
            red_copy(c).wait_recv()

        @pl.when(now_red & (place > 0) & (place < ranks - 1))
        def _():
            @pl.loop(0, half // block)
            def _(i):
                rs = tile(i, block)
                own = acc[c, pl.ds(pl.multiple_of(way * half + i * block, block), block), :]
                red[c, rs, :] = (red[c, rs, :].astype(F32) + own.astype(F32)).astype(BF)

        @pl.when(now_red & (place < ranks - 1))
        def _():
            red_copy(c).start()

        @pl.when(now_red & (place == ranks - 1))
        def _():
            @pl.loop(0, half // block)
            def _(i):
                rs = tile(i, block)
                own_rs = pl.ds(pl.multiple_of(way * half + i * block, block), block)
                acc[c, own_rs, :] = (
                    red[c, rs, :].astype(F32) + acc[c, own_rs, :].astype(F32)
                ).astype(BF)

            cast_copy(c).start()

        now_cast, cc = job_of(tick - (2 * ranks - 1 - place))

        @pl.when(now_cast & (place < ranks - 1))
        def _():
            cast_copy(cc).wait_recv()

        @pl.when(now_cast & (place > 0) & (place < ranks - 1))
        def _():
            cast_copy(cc).start()
    return comm


def attention_back(unit_qkv, unit_go, unit_out, unit_grad, sum_k, sum_v, u, v):
    seq_all = unit_qkv.shape[2]
    scale = HEAD_DIM ** (-0.5)
    part = math.gcd(seq_all, 256)
    sum_k[...] = jnp.zeros_like(sum_k)
    sum_v[...] = jnp.zeros_like(sum_v)

    @pl.loop(0, seq_all // part)
    def _(i):
        rs = tile(i, part)
        queries = unit_qkv[u, 0, rs, :]
        go = unit_go[u, rs, :]
        scores = dot_nt(queries, unit_qkv[u, 1]) * scale
        raised = jnp.exp(scores - jnp.max(scores, axis=-1, keepdims=True))
        probs = raised * (1.0 / jnp.sum(raised, axis=-1, keepdims=True))
        delta = jnp.sum(
            go.astype(F32) * unit_out[u, rs, :].astype(F32), axis=-1, keepdims=True
        )
        dscores = (probs * (dot_nt(go, unit_qkv[u, 2]) - delta)).astype(BF)
        unit_grad[v, 0, rs, :] = (scale * dot_nn(dscores, unit_qkv[u, 1])).astype(BF)
        sum_k[...] += dot_tn(dscores, queries)
        sum_v[...] += dot_tn(probs.astype(BF), go)

    unit_grad[v, 1] = (scale * sum_k[...]).astype(BF)
    unit_grad[v, 2] = sum_v[...].astype(BF)


def early_units(total, tok, units):
    rows = math.gcd(tok, CHUNK_ROWS)
    return int(units == total // tok and tok // rows >= 2 and units >= 2)


def middle_kernel(
    sizes,
    hidden,
    cotangent,
    shard_mix,
    shard_out,
    shard_exp,
    shard_con,
    md,
    mu,
    od,
    ou,
    ed,
    eu,
    cd,
    cu,
    gains,
    unit_rank,
    picks,
    hidden_out,
    first_low,
    active,
    second_low,
    before_grad,
    attn_low,
    mixing,
    unit_go,
    early_grads,
    part_ranks,
    full_ranks,
    context,
    unit_qkv,
    unit_out,
    context_grad,
    unit_grad,
    sum_k,
    sum_v,
    local_qkv,
    w_out,
    w_exp,
    w_con,
    acc,
    red_up,
    red_down,
    stash,
    spreads,
    rank_in,
    stage_d,
    stage_f,
    rows_in,
    rank_buf,
    in_sem,
    out_sem,
    red_send,
    red_recv,
    cast_send,
    cast_recv,
    peer_send,
    peer_recv,
    twin_send,
    twin_recv,
    side_send,
    side_recv,
    own_sem,
    rank_send,
    rank_recv,
    mix_sem,
    qkv_send,
    qkv_recv,
    ctx_send,
    ctx_recv,
    go_send,
    go_recv,
    early_send,
    early_recv,
    unit_sem,
):
    ranks, dps, ctxs, chunks, rows, per_seq, period = sizes
    half = rows // 2
    width = hidden.shape[1]
    hidden_units = w_exp.shape[1]
    heads = w_out.shape[0]
    block = min(16, half)
    tile_f = math.gcd(hidden_units, 512)
    tile_d = math.gcd(width, 512)
    tile_h = math.gcd(heads, 256)
    me = lax.axis_index("tensor")
    dp = lax.axis_index("dp")
    ctx = lax.axis_index("ctx")
    pairs = ctxs // 2
    core = ctx % 2
    chips = dps * pairs
    chip = dp * pairs + ctx // 2
    twin = {"ctx": ctx + 1 - 2 * core}
    lead = per_seq
    units, seq_all = unit_qkv.shape[0], unit_qkv.shape[2]
    tok = seq_all // ctxs
    local_heads = local_qkv.shape[1]

    def chip_block(step, which):
        row, column = step // pairs, step % pairs
        from_dp = (dp + dps - row) % dps
        from_chip = (ctx // 2 + pairs - column) % pairs
        return from_dp * ctxs + from_chip * 2 + which

    total = chunks * rows
    enter(
        [{"tensor": (me + d) % ranks} for d in range(1, ranks)]
        + [{"ctx": (ctx + d) % ctxs} for d in range(1, ctxs)]
        + [{"dp": (dp + d) % dps} for d in range(1, dps)]
    )

    shards = (shard_mix, shard_out, shard_exp, shard_con)
    fulls = (stash, w_out, w_exp, w_con)
    mix_width = shard_mix.shape[1]
    mix_half = shard_mix.shape[0] // 2

    def piece_of(w, p):
        if w < 2:
            return shards[w]
        return shards[w].at[tile(p, shards[w].shape[0] // PIECES)]

    def block_of(w, index, p):
        deep, wide = shards[w].shape
        if w == 0:
            return stash.at[tile(index, deep), pl.ds(0, mix_width)]
        if w == 1:
            return w_out.at[:, tile(index, wide)]
        if w == 2:
            return w_exp.at[tile(index * PIECES + p, deep // PIECES)]
        return w_con.at[tile(p, deep // PIECES), tile(index, wide)]

    def mix_piece(step, lower):
        start = chip_block(step, core) * (2 * mix_half) + lower * mix_half
        return stash.at[pl.ds(pl.multiple_of(start, mix_half), mix_half), pl.ds(0, mix_width)]

    def peer_copy(w, step, p=0):
        row, column = step // pairs, step % pairs
        block = block_of(w, chip_block(column, core), p)
        if row:
            target = {"dp": (dp + row) % dps}
        else:
            target = {"ctx": (ctx + 2 * column) % ctxs}
        own = block_of(w, chip_block(0, core), p)
        if w == 0 and row and column:
            block = mix_piece(column, 0)
        return pltpu.make_async_remote_copy(
            src_ref=block if row and column else piece_of(w, p),
            dst_ref=block if row else own,
            send_sem=peer_send.at[w, step, p],
            recv_sem=peer_recv.at[w, step, p],
            device_id=target,
            device_id_type=MESH_IDS,
        )

    def peer_arrival(w, step, p=0):
        row = step // pairs
        if row:
            target = {"dp": (dp + row) % dps}
        else:
            target = {"ctx": (ctx + 2 * step) % ctxs}
        block = block_of(w, chip_block(step, core), p)
        if w == 0 and row and step % pairs:
            block = mix_piece(step, 0)
        return pltpu.make_async_remote_copy(
            src_ref=block,
            dst_ref=block,
            send_sem=peer_send.at[w, step, p],
            recv_sem=peer_recv.at[w, step, p],
            device_id=target,
            device_id_type=MESH_IDS,
        )

    def twin_copy(w, step, p=0):
        block = block_of(w, chip_block(step, core), p)
        return pltpu.make_async_remote_copy(
            src_ref=piece_of(w, p) if step == 0 else block,
            dst_ref=block,
            send_sem=twin_send.at[w, step, p],
            recv_sem=twin_recv.at[w, step, p],
            device_id=twin,
            device_id_type=MESH_IDS,
        )

    def twin_arrival(w, step, p=0):
        block = block_of(w, chip_block(step, 1 - core), p)
        return pltpu.make_async_remote_copy(
            src_ref=block,
            dst_ref=block,
            send_sem=twin_send.at[w, step, p],
            recv_sem=twin_recv.at[w, step, p],
            device_id=twin,
            device_id_type=MESH_IDS,
        )

    def own_copy(w, p=0):
        return pltpu.make_async_copy(piece_of(w, p), block_of(w, chip_block(0, core), p), own_sem.at[w, p])

    def side_copy(step):
        row, column = step // pairs, step % pairs
        piece = mix_piece(row * pairs, 1)
        return pltpu.make_async_remote_copy(
            src_ref=piece,
            dst_ref=piece,
            send_sem=side_send.at[step],
            recv_sem=side_recv.at[step],
            device_id={"ctx": (ctx + 2 * column) % ctxs},
            device_id_type=MESH_IDS,
        )

    def side_arrival(step):
        piece = mix_piece(step, 1)
        return pltpu.make_async_remote_copy(
            src_ref=piece,
            dst_ref=piece,
            send_sem=side_send.at[step],
            recv_sem=side_recv.at[step],
            device_id={"ctx": (ctx + 2 * (step % pairs)) % ctxs},
            device_id_type=MESH_IDS,
        )

    def across_start(w, p=0):
        for step in range(pairs, chips, pairs):
            peer_copy(w, step, p).start()
        twin_copy(w, 0, p).start()
        own_copy(w, p).start()

    def along_start(w, p=0):
        for step in range(1, pairs):
            peer_copy(w, step, p).start()

    def weight_relay(w, p=0):
        for step in range(1, pairs):
            peer_arrival(w, step, p).wait_recv()
            for row in range(1, dps):
                peer_copy(w, row * pairs + step, p).start()
            twin_copy(w, step, p).start()

    def weight_forward(w, p=0):
        for step in range(pairs, chips):
            peer_arrival(w, step, p).wait_recv()
            twin_copy(w, step, p).start()

    def mixing_gather():
        along_start(0)
        across_start(0)
        weight_relay(0)
        for row in range(1, dps):
            peer_arrival(0, row * pairs).wait_recv()
            for column in range(1, pairs):
                side_copy(row * pairs + column).start()
            twin_copy(0, row * pairs).start()
        for row in range(1, dps):
            for column in range(1, pairs):
                step = row * pairs + column
                peer_arrival(0, step).wait_recv()
                side_arrival(step).wait_recv()
                twin_copy(0, step).start()

    def weight_finish(w, p=0):
        own_copy(w, p).wait()
        for step in range(chips):
            twin_arrival(w, step, p).wait_recv()

    def side_sent():
        for row in range(1, dps):
            for column in range(1, pairs):
                side_copy(row * pairs + column).wait_send()

    def weight_sent(w, p=0):
        for step in range(1, chips):
            peer_copy(w, step, p).wait_send()
        for step in range(chips):
            twin_copy(w, step, p).wait_send()

    def unit_place(device, u):
        return (device // local_heads) * units + u, device % local_heads

    def qkv_copy(u, step):
        peer = (ctx + step) % ctxs
        s, h = unit_place(peer, u)
        return pltpu.make_async_remote_copy(
            src_ref=local_qkv.at[s, h],
            dst_ref=unit_qkv.at[u, :, tile(ctx, tok)],
            send_sem=qkv_send.at[u, step],
            recv_sem=qkv_recv.at[u, step],
            device_id={"ctx": peer},
            device_id_type=MESH_IDS,
        )

    def qkv_arrival(u, step):
        return pltpu.make_async_remote_copy(
            src_ref=local_qkv.at[0, 0],
            dst_ref=unit_qkv.at[u, :, tile((ctx + ctxs - step) % ctxs, tok)],
            send_sem=qkv_send.at[u, step],
            recv_sem=qkv_recv.at[u, step],
            device_id={"ctx": (ctx + step) % ctxs},
            device_id_type=MESH_IDS,
        )

    def qkv_own(u):
        s, h = unit_place(ctx, u)
        return pltpu.make_async_copy(
            local_qkv.at[s, h], unit_qkv.at[u, :, tile(ctx, tok)], unit_sem.at[0, u]
        )

    def context_place(device, u):
        s, h = unit_place(device, u)
        return context.at[tile(s, tok), tile(h, HEAD_DIM)]

    def context_copy(u, step):
        peer = (ctx + step) % ctxs
        return pltpu.make_async_remote_copy(
            src_ref=unit_out.at[u, tile(peer, tok)],
            dst_ref=context_place(ctx, u),
            send_sem=ctx_send.at[u, step],
            recv_sem=ctx_recv.at[u, step],
            device_id={"ctx": peer},
            device_id_type=MESH_IDS,
        )

    def context_arrival(u, step):
        return pltpu.make_async_remote_copy(
            src_ref=unit_out.at[u, tile(ctx, tok)],
            dst_ref=context_place((ctx + ctxs - step) % ctxs, u),
            send_sem=ctx_send.at[u, step],
            recv_sem=ctx_recv.at[u, step],
            device_id={"ctx": (ctx + step) % ctxs},
            device_id_type=MESH_IDS,
        )

    def context_own(u):
        return pltpu.make_async_copy(
            unit_out.at[u, tile(ctx, tok)], context_place(ctx, u), unit_sem.at[1, u]
        )

    def go_copy(u, step):
        peer = (ctx + step) % ctxs
        s, h = unit_place(peer, u)
        return pltpu.make_async_remote_copy(
            src_ref=context_grad.at[tile(s, tok), tile(h, HEAD_DIM)],
            dst_ref=unit_go.at[u, tile(ctx, tok)],
            send_sem=go_send.at[u, step],
            recv_sem=go_recv.at[u, step],
            device_id={"ctx": peer},
            device_id_type=MESH_IDS,
        )

    def go_arrival(u, step):
        return pltpu.make_async_remote_copy(
            src_ref=context_grad.at[tile(0, tok), tile(0, HEAD_DIM)],
            dst_ref=unit_go.at[u, tile((ctx + ctxs - step) % ctxs, tok)],
            send_sem=go_send.at[u, step],
            recv_sem=go_recv.at[u, step],
            device_id={"ctx": (ctx + step) % ctxs},
            device_id_type=MESH_IDS,
        )

    def go_own(u):
        s, h = unit_place(ctx, u)
        return pltpu.make_async_copy(
            context_grad.at[tile(s, tok), tile(h, HEAD_DIM)],
            unit_go.at[u, tile(ctx, tok)],
            unit_sem.at[2, u],
        )

    def go_start(u):
        for step in range(1, ctxs):
            go_copy(u, step).start()
        go_own(u).start()

    early = early_units(total, tok, units)

    def go_ready(u):
        go_own(u).wait()
        for step in range(1, ctxs):
            go_arrival(u, step).wait_recv()

    def early_place(device):
        return early_grads.at[:, :, tile(unit_place(device, 0)[1], HEAD_DIM)]

    def early_copy(step):
        peer = (ctx + step) % ctxs
        return pltpu.make_async_remote_copy(
            src_ref=unit_grad.at[0, :, tile(peer, tok)],
            dst_ref=early_place(ctx),
            send_sem=early_send.at[step],
            recv_sem=early_recv.at[step],
            device_id={"ctx": peer},
            device_id_type=MESH_IDS,
        )

    def early_arrival(step):
        return pltpu.make_async_remote_copy(
            src_ref=unit_grad.at[0, :, tile(ctx, tok)],
            dst_ref=early_place((ctx + ctxs - step) % ctxs),
            send_sem=early_send.at[step],
            recv_sem=early_recv.at[step],
            device_id={"ctx": (ctx + step) % ctxs},
            device_id_type=MESH_IDS,
        )

    def early_own():
        return pltpu.make_async_copy(
            unit_grad.at[0, :, tile(ctx, tok)], early_place(ctx), unit_sem.at[3, 0]
        )

    def early_back():
        go_ready(0)
        attention_back(unit_qkv, unit_go, unit_out, unit_grad, sum_k, sum_v, 0, 0)
        for step in range(1, ctxs):
            early_copy(step).start()
        early_own().start()

    def attend(u):
        qkv_own(u).wait()
        for step in range(1, ctxs):
            qkv_arrival(u, step).wait_recv()
        part = math.gcd(seq_all, 256)

        @pl.loop(0, seq_all // part)
        def _(i):
            rs = tile(i, part)
            scores = dot_nt(unit_qkv[u, 0, rs, :], unit_qkv[u, 1]) * (HEAD_DIM ** (-0.5))
            largest = jnp.max(scores, axis=-1, keepdims=True)
            raised = jnp.exp(scores - largest)
            total = jnp.sum(raised, axis=-1, keepdims=True)
            mixed = dot_nn(raised.astype(BF), unit_qkv[u, 2])
            unit_out[u, rs, :] = (mixed / total).astype(BF)

        for step in range(1, ctxs):
            context_copy(u, step).start()
        context_own(u).start()

    def context_ready(u):
        context_own(u).wait()
        for step in range(1, ctxs):
            context_arrival(u, step).wait_recv()

    def project_chunk(c):
        bring(hidden, c).wait()
        following = (c + 1) % chunks
        s = c // per_seq
        rs = tile(c % per_seq, rows)
        low = dot_nt(rows_in[...], md[picks[s]]).astype(BF)
        put_rank(3, c, low)
        rank_buf[...] = low
        heads_at_once = math.gcd(local_heads, 2)
        step = heads_at_once * HEAD_DIM

        @pl.loop(0, mix_width // step)
        def _(i):
            cs = tile(i, step)
            values = dot_nn(rows_in[...], stash[0:width, cs]) + dot_nn(rank_buf[...], mu[picks[s], :, cs])
            values = values.astype(BF)
            first = i * heads_at_once
            for k in range(heads_at_once):
                local_qkv[s, (first + k) % local_heads, (first + k) // local_heads, rs, :] = values[
                    :, k * HEAD_DIM : (k + 1) * HEAD_DIM
                ]

        bring(hidden, following).start()

    def project(s):
        @pl.loop(0, per_seq)
        def _(i):
            project_chunk(s * per_seq + i)

    def send_unit(u):
        qkv_own(u).start()
        for step in range(1, ctxs):
            qkv_copy(u, step).start()

    def job_of(number, rounds):
        safe = jnp.maximum(number, 0)
        chunk = safe % period
        valid = (number >= 0) & (chunk < chunks) & (safe < rounds * period)
        return valid, jnp.minimum(chunk, chunks - 1)

    comm = chain(
        ranks,
        half,
        block,
        me,
        acc,
        red_up,
        red_down,
        red_send,
        red_recv,
        cast_send,
        cast_recv,
        lambda number: job_of(number, 3),
    )

    def rows_of(c):
        return tile(c, rows)

    def spot(t, c, i=None):
        start = t * total + c * rows
        if i is None:
            return pl.ds(pl.multiple_of(start, rows), rows)
        return pl.ds(pl.multiple_of(start + i * block, block), block)

    def mixing_keep():
        return pltpu.make_async_copy(
            stash.at[pl.ds(0, width), pl.ds(0, mix_width)], mixing, mix_sem
        )

    def bring(source, c):
        return pltpu.make_async_copy(source.at[rows_of(c)], rows_in, in_sem)

    def keep(index, source, target, c):
        return pltpu.make_async_copy(source, target.at[rows_of(c)], out_sem.at[index])

    def put_rank(t, c, low):
        part_ranks[t, :, tile(c, rows)] = dot_nt(unit_rank[...], low).astype(BF)

    def rank_copy(t, step):
        return pltpu.make_async_remote_copy(
            src_ref=part_ranks.at[t],
            dst_ref=rank_in.at[t, step],
            send_sem=rank_send.at[t, step],
            recv_sem=rank_recv.at[t, step],
            device_id={"tensor": (me + step) % ranks},
            device_id_type=MESH_IDS,
        )

    def mean(values):
        return jnp.sum(values, axis=-1, keepdims=True) * (1.0 / width)

    def attend_part(c, s):
        mine = context[rows_of(c), :]
        low = dot_nt(mine, od[picks[s]]).astype(BF)
        put_rank(0, c, low)

        @pl.loop(0, width // tile_d)
        def _(i):
            cs = tile(i, tile_d)
            acc[c, :, cs] = (dot_nn(mine, w_out[:, cs]) + dot_nn(low, ou[picks[s], :, cs])).astype(BF)

    def forward_first(c, s):
        bring(hidden, c).wait()

        @pl.loop(0, rows // block)
        def _(i):
            rs = tile(i, block)
            total = rows_in[rs, :].astype(F32) + acc[c, rs, :].astype(F32)
            centred = total - mean(total)
            spread = lax.rsqrt(mean(centred * centred) + 1e-06)
            n = centred * spread
            stash[spot(0, c, i), :] = n.astype(BF)
            spreads[c, rs, :] = jnp.broadcast_to(spread, (block, 128))
            stage_d[rs, :] = (n * gains[0:1, :] + gains[1:2, :]).astype(BF)

        low = dot_nt(stage_d[...], ed[picks[s]]).astype(BF)
        put_rank(4, c, low)
        rank_buf[...] = low

        @pl.loop(0, hidden_units // tile_f)
        def _(i):
            cs = tile(i, tile_f)
            b = dot_nn(stage_d[...], w_exp[:, cs]) + dot_nn(rank_buf[...], eu[picks[s], :, cs])
            square = b * b
            t = jnp.tanh(GELU_C * b * (1.0 + GELU_A * square))
            upper = 0.5 * (1.0 + t)
            stage_f[:, cs] = (b * upper).astype(BF)
            stash[spot(1, c), cs] = (
                upper
                + (0.5 * GELU_C) * b * (1.0 - t * t) * (1.0 + (3.0 * GELU_A) * square)
            ).astype(BF)

    def forward_second(c, s):
        low = dot_nt(stage_f[...], cd[picks[s]]).astype(BF)
        put_rank(1, c, low)
        rank_buf[...] = low

        @pl.loop(0, width // tile_d)
        def _(i):
            cs = tile(i, tile_d)
            acc[c, :, cs] = (
                dot_nn(stage_f[...], w_con[:, cs]) + dot_nn(rank_buf[...], cu[picks[s], :, cs])
            ).astype(BF)

        keep(0, stage_d, first_low, c).start()
        keep(1, stage_f, active, c).start()

    def back_first(c, s):
        bring(cotangent, c).wait()

        @pl.loop(0, rows // block)
        def _(i):
            rs = tile(i, block)
            first = stash[spot(0, c, i), :].astype(F32) * gains[0:1, :] + gains[1:2, :]
            total = first + acc[c, rs, :].astype(F32)
            centred = total - mean(total)
            spread = lax.rsqrt(mean(centred * centred) + 1e-06)
            n = centred * spread
            stage_d[rs, :] = (n * gains[2:3, :] + gains[3:4, :]).astype(BF)
            g = rows_in[rs, :].astype(F32) * gains[2:3, :]
            stash[spot(2, c, i), :] = (spread * (g - mean(g) - n * mean(g * n))).astype(BF)

        low = dot_nt(stash[spot(2, c), :], cu[picks[s]]).astype(BF)
        put_rank(5, c, low)
        rank_buf[...] = low

        @pl.loop(0, hidden_units // tile_f)
        def _(i):
            cs = tile(i, tile_f)
            da = dot_nt(stash[spot(2, c), :], w_con[cs, :]) + dot_nn(rank_buf[...], cd[picks[s], :, cs])
            stage_f[:, cs] = (da * stash[spot(1, c), cs].astype(F32)).astype(BF)

    def back_second(c, s):
        low = dot_nt(stage_f[...], eu[picks[s]]).astype(BF)
        put_rank(2, c, low)
        rank_buf[...] = low

        @pl.loop(0, width // tile_d)
        def _(i):
            cs = tile(i, tile_d)
            acc[c, :, cs] = (
                dot_nt(stage_f[...], w_exp[cs, :]) + dot_nn(rank_buf[...], ed[picks[s], :, cs])
            ).astype(BF)

        keep(0, stage_d, hidden_out, c).start()
        keep(1, stage_f, before_grad, c).start()
        keep(2, stash.at[spot(2, c)], second_low, c).start()

    def last_first(c, s):
        @pl.loop(0, rows // block)
        def _(i):
            rs = tile(i, block)
            n = stash[spot(0, c, i), :].astype(F32)
            g = (stash[spot(2, c, i), :].astype(F32) + acc[c, rs, :].astype(F32)) * gains[0:1, :]
            spread = spreads[c, rs, 0:1]
            stage_d[rs, :] = (spread * (g - mean(g) - n * mean(g * n))).astype(BF)

    def last_second(c, s):
        low = dot_nt(stage_d[...], ou[picks[s]]).astype(BF)
        put_rank(6, c, low)
        rank_buf[...] = low

        @pl.loop(0, heads // tile_h)
        def _(i):
            cs = tile(i, tile_h)
            context_grad[rows_of(c), cs] = (
                dot_nt(stage_d[...], w_out[cs, :]) + dot_nn(rank_buf[...], od[picks[s], :, cs])
            ).astype(BF)

        keep(0, stage_d, attn_low, c).start()

    seqs = chunks // per_seq
    flowing = units == seqs
    bring(hidden, 0).start()
    mixing_gather()
    weight_finish(0)
    along_start(1)
    across_start(1)
    mixing_keep().start()
    if flowing:
        for u in range(min(2, units)):
            project(u)
            send_unit(u)
    else:
        pl.loop(0, seqs)(project)
        for u in range(units):
            send_unit(u)
    weight_relay(1)

    @pl.loop(0, lead + 3 * period + chunks)
    def _(now):
        tick = now - lead
        stage = jnp.maximum(tick, 0) // period
        valid, c = job_of(tick, 4)
        s = c // per_seq
        last_valid, last_c = job_of(tick - 1, 4)
        last_stage = jnp.maximum(tick - 1, 0) // period

        comm(tick, 0)

        @pl.when(last_valid & (last_stage >= 1))
        def _():
            keep(0, stage_d, first_low, last_c).wait()

        @pl.when(last_valid & (last_stage >= 1) & (last_stage <= 2))
        def _():
            keep(1, stage_f, active, last_c).wait()

        @pl.when(last_valid & (last_stage == 2))
        def _():
            keep(2, stash.at[spot(2, last_c)], second_low, last_c).wait()

        pl.when(now == 1)(lambda: weight_forward(1))
        pl.when((now % per_seq == 0) & (now < units * per_seq))(lambda: attend(now // per_seq))
        if flowing:

            @pl.when((now % per_seq == 1) & (now < (units - 2) * per_seq))
            def _():
                project(now // per_seq + 2)
                send_unit(now // per_seq + 2)

        @pl.when((now % per_seq == 1) & (now > per_seq) & (now <= PIECES * per_seq + 1))
        def _():
            p = now // per_seq - 1
            weight_relay(2, p)
            weight_relay(3, p)

        @pl.when((now % per_seq == 1) & (now < PIECES * per_seq))
        def _():
            for w in (2, 3):
                along_start(w, now // per_seq)
                across_start(w, now // per_seq)

        @pl.when((now % per_seq == 0) & (now > per_seq) & (now <= (PIECES + 1) * per_seq))
        def _():
            p = now // per_seq - 2
            weight_forward(2, p)
            weight_forward(3, p)

        @pl.when(now == lead + period)
        def _():
            for p in range(PIECES):
                weight_finish(2, p)
                weight_finish(3, p)

        pl.when(now == lead)(lambda: weight_finish(1))

        @pl.when(now == lead + period - 2)
        def _():
            mixing_keep().wait()
            weight_sent(0)
            side_sent()

        for t in range(3):

            @pl.when(tick == (t + 1) * period)
            def _(t=t):
                for step in range(1, ranks):
                    rank_copy(t, step).start()

        pl.when((tick >= 0) & (tick % per_seq == 0) & (tick < units * per_seq))(
            lambda: context_ready(s)
        )

        pl.when(valid & (stage == 1))(lambda: forward_first(c, s))
        pl.when(valid & (stage == 2))(lambda: back_first(c, s))
        pl.when(valid & (stage == 3))(lambda: last_first(c, s))

        comm(tick, 1)

        pl.when(valid & (stage == 0))(lambda: attend_part(c, s))
        pl.when(valid & (stage == 1))(lambda: forward_second(c, s))
        pl.when(valid & (stage == 2))(lambda: back_second(c, s))
        pl.when(valid & (stage == 3))(lambda: last_second(c, s))
        if flowing:
            pl.when(valid & (stage == 3) & (c % per_seq == per_seq - 1))(lambda: go_start(s))
        if early:
            pl.when(tick == 3 * period + EARLY_AT)(early_back)

        next_valid, next_c = job_of(tick + 1, 4)
        next_stage = jnp.maximum(tick + 1, 0) // period
        pl.when(next_valid & (next_stage == 1) & (next_c > 0))(
            lambda: bring(hidden, next_c).start()
        )
        pl.when(next_valid & (next_stage == 2))(lambda: bring(cotangent, next_c).start())

    keep(0, stage_d, attn_low, chunks - 1).wait()
    for t in range(3):
        value = part_ranks[t].astype(F32)
        for step in range(1, ranks):
            rank_copy(t, step).wait_recv()
            value = value + rank_in[t, step].astype(F32)
        full_ranks[t] = value.astype(BF)
    for t in range(3):
        for step in range(1, ranks):
            rank_copy(t, step).wait_send()
    weight_sent(1)
    for p in range(PIECES):
        weight_sent(2, p)
        weight_sent(3, p)
    for u in range(units):
        if not flowing:
            go_start(u)
        for step in range(1, ctxs):
            qkv_copy(u, step).wait_send()
            context_copy(u, step).wait_send()
    for u in range(units):
        if u >= early:
            go_ready(u)
        for step in range(1, ctxs):
            go_copy(u, step).wait_send()
    if early:
        early_own().wait()
        for step in range(1, ctxs):
            early_arrival(step).wait_recv()
            early_copy(step).wait_send()


def enter(others):
    barrier = pltpu.get_barrier_semaphore()
    for other in others:
        pl.semaphore_signal(barrier, inc=1, device_id=other, device_id_type=MESH_IDS)
    pl.semaphore_wait(barrier, len(others))


def middle(hidden, cotangent, shards, picked, gains, tok, picks):
    total, width = hidden.shape
    mix_width = shards[0].shape[1]
    heads, hidden_units = shards[1].shape[0], shards[2].shape[1]
    ranks, dps, ctxs = (lax.axis_size(name) for name in ("tensor", "dp", "ctx"))
    seqs, rank = picks.shape[0], picked[0].shape[1]
    local_heads = heads // HEAD_DIM
    units = seqs * local_heads // ctxs
    rows = math.gcd(tok, CHUNK_ROWS)
    chunks = total // rows
    period = max(chunks, 2 * ranks)
    sizes = (ranks, dps, ctxs, chunks, rows, tok // rows, period)
    chips = dps * ctxs // 2
    vm = pl.BlockSpec(memory_space=pltpu.VMEM)
    hb = pl.BlockSpec(memory_space=pl.ANY)
    sm = pl.BlockSpec(memory_space=pltpu.SMEM)
    half = rows // 2
    dma = pltpu.SemaphoreType.DMA

    def shape(*dims):
        return jax.ShapeDtypeStruct(dims, BF)

    return pl.pallas_call(
        functools.partial(middle_kernel, sizes),
        out_shape=(
            shape(total, width),
            shape(total, width),
            shape(total, hidden_units),
            shape(total, width),
            shape(total, hidden_units),
            shape(total, width),
            shape(width, mix_width),
            shape(units, tok * ctxs, HEAD_DIM),
            shape(3, tok, heads),
            shape(7, rank, total),
            shape(3, rank, total),
            shape(total, heads),
            shape(units, 3, tok * ctxs, HEAD_DIM),
            shape(units, tok * ctxs, HEAD_DIM),
        ),
        in_specs=[hb] * 6 + [vm] * 10 + [sm],
        out_specs=(hb,) * 7 + (vm,) * 7,
        scratch_shapes=[
            pltpu.VMEM((total, heads), BF),
            pltpu.VMEM((1, 3, tok * ctxs, HEAD_DIM), BF),
            pltpu.VMEM((tok * ctxs, HEAD_DIM), F32),
            pltpu.VMEM((tok * ctxs, HEAD_DIM), F32),
            pltpu.VMEM((seqs, local_heads, 3, tok, HEAD_DIM), BF),
            pltpu.VMEM((heads, width), BF),
            pltpu.VMEM((width, hidden_units), BF),
            pltpu.VMEM((hidden_units, width), BF),
            pltpu.VMEM((chunks, rows, width), BF),
            pltpu.VMEM((chunks, half, width), BF),
            pltpu.VMEM((chunks, half, width), BF),
            pltpu.VMEM((3 * total, width), BF),
            pltpu.VMEM((chunks, rows, 128), F32),
            pltpu.VMEM((3, ranks, rank, total), BF),
            pltpu.VMEM((rows, width), BF),
            pltpu.VMEM((rows, hidden_units), BF),
            pltpu.VMEM((rows, width), BF),
            pltpu.VMEM((rows, rank), BF),
            dma(()),
            dma((3,)),
            dma((2, chunks)),
            dma((2, chunks)),
            dma((2, chunks)),
            dma((2, chunks)),
            dma((4, chips, PIECES)),
            dma((4, chips, PIECES)),
            dma((4, chips, PIECES)),
            dma((4, chips, PIECES)),
            dma((chips,)),
            dma((chips,)),
            dma((4, PIECES)),
            dma((3, ranks)),
            dma((3, ranks)),
            dma(()),
            dma((units, ctxs)),
            dma((units, ctxs)),
            dma((units, ctxs)),
            dma((units, ctxs)),
            dma((units, ctxs)),
            dma((units, ctxs)),
            dma((ctxs,)),
            dma((ctxs,)),
            dma((4, units)),
        ],
        compiler_params=pltpu.CompilerParams(
            collective_id=0, has_side_effects=True, vmem_limit_bytes=VMEM_BYTES
        ),
        cost_estimate=pl.CostEstimate(
            flops=8 * total * width * hidden_units + 4 * total * width * heads,
            bytes_accessed=16 * total * width,
            transcendentals=total * hidden_units,
        ),
    )(hidden, cotangent, *shards, *picked, gains, jnp.eye(rank, dtype=BF), picks)


def mixing_kernel(
    sizes,
    unit_go,
    unit_qkv,
    unit_out,
    mixing_far,
    mu,
    md,
    attn_low,
    unit_rank,
    early_grads,
    hidden_far,
    mix_rank,
    row_hot,
    picks,
    input_grad,
    table_sum,
    grads,
    mixing,
    hidden,
    rank_part,
    rank_in,
    wide,
    table_part,
    table_in,
    unit_grad,
    sum_k,
    sum_v,
    acc,
    red_up,
    red_down,
    stage_d,
    rows_in,
    rank_buf,
    in_sem,
    out_sem,
    red_send,
    red_recv,
    cast_send,
    cast_recv,
    far_sem,
    grad_send,
    grad_recv,
    unit_sem,
    rank_send,
    rank_recv,
    part_send,
    part_recv,
    whole_send,
    whole_recv,
):
    ranks, dps, ctxs, chunks, rows, per_seq, group = sizes
    half = rows // 2
    width = mixing.shape[0]
    heads = grads.shape[2]
    local_heads = heads // HEAD_DIM
    units, seq_all = unit_go.shape[0], unit_go.shape[1]
    tok = seq_all // ctxs
    block = min(16, half)
    tile_d = math.gcd(width, 512)
    scale = HEAD_DIM ** (-0.5)
    me = lax.axis_index("tensor")
    ctx = lax.axis_index("ctx")
    dp = lax.axis_index("dp")
    parts = dps * ctxs
    index = dp * ctxs + ctx
    rank = mu.shape[1]
    tables, _, part_width = table_part.shape
    segments = parts // NADAPT
    tile_g = math.gcd(part_width, 256)

    def part_place(step):
        other = (index + step) % parts
        return {"dp": other // ctxs, "ctx": other % ctxs}

    enter(
        [{"tensor": (me + d) % ranks} for d in range(1, ranks)]
        + [part_place(d) for d in range(1, parts)]
    )

    def unit_place(device, u):
        return (device // local_heads) * units + u, device % local_heads

    def mixing_load():
        return pltpu.make_async_copy(mixing_far, mixing, far_sem.at[0])

    def early_load():
        return pltpu.make_async_copy(early_grads, grads.at[:, pl.ds(0, tok)], far_sem.at[2])

    def hidden_load():
        return pltpu.make_async_copy(hidden_far, hidden, far_sem.at[1])

    def grads_place(device, u):
        s, h = unit_place(device, u)
        return grads.at[:, tile(s, tok), tile(h, HEAD_DIM)]

    def grad_copy(u, step):
        peer = (ctx + step) % ctxs
        return pltpu.make_async_remote_copy(
            src_ref=unit_grad.at[u, :, tile(peer, tok)],
            dst_ref=grads_place(ctx, u),
            send_sem=grad_send.at[u, step],
            recv_sem=grad_recv.at[u, step],
            device_id={"ctx": peer},
            device_id_type=MESH_IDS,
        )

    def grad_arrival(u, step):
        return pltpu.make_async_remote_copy(
            src_ref=unit_grad.at[u, :, tile(ctx, tok)],
            dst_ref=grads_place((ctx + ctxs - step) % ctxs, u),
            send_sem=grad_send.at[u, step],
            recv_sem=grad_recv.at[u, step],
            device_id={"ctx": (ctx + step) % ctxs},
            device_id_type=MESH_IDS,
        )

    def grad_own(u):
        return pltpu.make_async_copy(
            unit_grad.at[u, :, tile(ctx, tok)], grads_place(ctx, u), unit_sem.at[u]
        )

    def attend_back(u):
        attention_back(unit_qkv, unit_go, unit_out, unit_grad, sum_k, sum_v, u, u)
        for step in range(1, ctxs):
            grad_copy(u, step).start()
        grad_own(u).start()

    def grads_ready(u):
        grad_own(u).wait()
        for step in range(1, ctxs):
            grad_arrival(u, step).wait_recv()

    early = early_units(chunks * rows, tok, units)
    lead = per_seq * (1 - early)
    if early:
        early_load().start()
    mixing_load().start()
    hidden_load().start()

    def job_of(number):
        return (number >= 0) & (number < chunks), jnp.clip(number, 0, chunks - 1)

    comm = chain(
        ranks, half, block, me, acc, red_up, red_down, red_send, red_recv, cast_send, cast_recv, job_of
    )

    def rows_of(c):
        return tile(c, rows)

    def bring(c):
        return pltpu.make_async_copy(attn_low.at[rows_of(c)], rows_in, in_sem)

    def keep(c):
        return pltpu.make_async_copy(stage_d, input_grad.at[rows_of(c)], out_sem)

    def back_part(c, s):
        rs = pl.ds(pl.multiple_of(c * rows, group * rows), group * rows)
        low = jnp.zeros((group * rows, mu.shape[1]), F32)
        for j in range(3):
            low = low + dot_nt(grads[j, rs, :], mu[picks[s], :, pl.ds(j * heads, heads)])
        low = low.astype(BF)
        rank_part[:, pl.ds(pl.multiple_of(c * rows, group * rows), group * rows)] = dot_nt(
            unit_rank[...], low
        ).astype(BF)
        rank_buf[...] = low

        @pl.loop(0, width // tile_d)
        def _(i):
            cs = tile(i, tile_d)
            total = dot_nn(rank_buf[...], md[picks[s], :, cs])
            for j in range(3):
                total = total + dot_nt(grads[j, rs, :], mixing[cs, pl.ds(j * heads, heads)])
            total = total.astype(BF)
            for k in range(group):
                acc[c + k, :, cs] = total[k * rows : (k + 1) * rows, :]

    def final_part(c):
        bring(c).wait()

        @pl.loop(0, rows // block)
        def _(i):
            rs = tile(i, block)
            stage_d[rs, :] = (rows_in[rs, :].astype(F32) + acc[c, rs, :].astype(F32)).astype(BF)

        keep(c).start()

    def rank_copy(step):
        return pltpu.make_async_remote_copy(
            src_ref=rank_part,
            dst_ref=rank_in.at[step],
            send_sem=rank_send.at[step],
            recv_sem=rank_recv.at[step],
            device_id={"tensor": (me + step) % ranks},
            device_id_type=MESH_IDS,
        )

    def part_copy(step):
        return pltpu.make_async_remote_copy(
            src_ref=table_part.at[(index + step) % parts],
            dst_ref=table_in.at[step],
            send_sem=part_send.at[step],
            recv_sem=part_recv.at[step],
            device_id=part_place(step),
            device_id_type=MESH_IDS,
        )

    def whole_copy(step):
        return pltpu.make_async_remote_copy(
            src_ref=table_sum.at[index],
            dst_ref=table_sum.at[index],
            send_sem=whole_send.at[step],
            recv_sem=whole_recv.at[step],
            device_id=part_place(step),
            device_id_type=MESH_IDS,
        )

    def whole_arrival(step):
        return pltpu.make_async_remote_copy(
            src_ref=table_sum.at[index],
            dst_ref=table_sum.at[(index + parts - step) % parts],
            send_sem=whole_send.at[step],
            recv_sem=whole_recv.at[step],
            device_id=part_place(step),
            device_id_type=MESH_IDS,
        )

    def put_table(column, values):
        segment = column // part_width
        cs = pl.ds(pl.multiple_of(column % part_width, tile_g), tile_g)
        for n in range(NADAPT):
            table_part[n * segments + segment, :, cs] = values[n * rank : (n + 1) * rank, :].astype(
                BF
            )

    def make_tables():
        value = rank_part[...].astype(F32)
        for step in range(1, ranks):
            rank_copy(step).wait_recv()
            value = value + rank_in[step].astype(F32)
        for n in range(NADAPT):
            hot = row_hot[n : n + 1, :]
            wide[0, pl.ds(n * rank, rank), :] = (value * hot).astype(BF)
            wide[1, pl.ds(n * rank, rank), :] = (mix_rank[...].astype(F32) * hot).astype(BF)

        @pl.loop(0, width // tile_g)
        def _(i):
            put_table(i * tile_g, dot_nn(wide[0], hidden[:, tile(i, tile_g)]))

        for j in range(3):

            @pl.loop(0, heads // tile_g)
            def _(i):
                put_table(
                    width + j * heads + i * tile_g, dot_nn(wide[1], grads[j, :, tile(i, tile_g)])
                )

        for step in range(1, parts):
            part_copy(step).start()

    def sum_tables():
        value = table_part[index].astype(F32)
        for step in range(1, parts):
            part_copy(step).wait_recv()
            value = value + table_in[step].astype(F32)
        table_sum[index] = value.astype(BF)
        for step in range(1, parts):
            whole_copy(step).start()

    delay = max(2 * ranks - 1, 4)

    @pl.loop(0, lead + chunks + delay)
    def _(now):
        tick = now - lead

        @pl.when(tick == chunks)
        def _():
            for step in range(1, ranks):
                rank_copy(step).start()

        valid, c = job_of(tick)
        final, c_final = job_of(tick - delay)
        before, c_before = job_of(tick - delay - 1)
        coming, c_coming = job_of(tick - delay + 1)
        s = c // per_seq

        comm(tick, 0)

        pl.when(
            (tick >= early * per_seq) & (tick % per_seq == 0) & (tick < units * per_seq)
        )(lambda: grads_ready(s))
        if not early:
            pl.when((now % per_seq == 0) & (now < units * per_seq))(
                lambda: attend_back(now // per_seq)
            )
        comm(tick, 1)
        if early:
            pl.when((now % per_seq == 0) & (now < (units - 1) * per_seq))(
                lambda: attend_back(now // per_seq + 1)
            )
            pl.when(tick == 0)(lambda: early_load().wait())

        pl.when(tick == 0)(lambda: mixing_load().wait())
        pl.when(valid & (tick % group == 0))(lambda: back_part(c, s))

        @pl.when(tick == chunks + 1)
        def _():
            hidden_load().wait()
            make_tables()

        pl.when(tick == chunks + 3)(sum_tables)

        pl.when(before)(lambda: keep(c_before).wait())
        pl.when(final)(lambda: final_part(c_final))
        pl.when(coming)(lambda: bring(c_coming).start())

    keep(chunks - 1).wait()
    for step in range(1, ranks):
        rank_copy(step).wait_send()
    for step in range(1, parts):
        whole_arrival(step).wait_recv()
    for step in range(1, parts):
        part_copy(step).wait_send()
        whole_copy(step).wait_send()
    for u in range(early, units):
        for step in range(1, ctxs):
            grad_copy(u, step).wait_send()


def mixing_back(
    unit_go, early_grads, unit_qkv, unit_out, mixing, picked, attn_low, hidden, mix_rank, row_hot, picks
):
    mu, md = picked
    total, width = attn_low.shape
    heads = mixing.shape[1] // 3
    ranks, dps, ctxs = (lax.axis_size(name) for name in ("tensor", "dp", "ctx"))
    parts = dps * ctxs
    part_width = (width + 3 * heads) * NADAPT // parts
    units, _, seq_all, _ = unit_qkv.shape
    tok = seq_all // ctxs
    rank = mu.shape[1]
    rows = math.gcd(tok, LAST_ROWS)
    chunks = total // rows
    per_seq = tok // rows
    group = math.gcd(per_seq, 2)
    half = rows // 2
    sizes = (ranks, dps, ctxs, chunks, rows, per_seq, group)
    vm = pl.BlockSpec(memory_space=pltpu.VMEM)
    hb = pl.BlockSpec(memory_space=pl.ANY)
    sm = pl.BlockSpec(memory_space=pltpu.SMEM)
    dma = pltpu.SemaphoreType.DMA
    return pl.pallas_call(
        functools.partial(mixing_kernel, sizes),
        out_shape=(
            jax.ShapeDtypeStruct((total, width), BF),
            jax.ShapeDtypeStruct((parts, rank, part_width), BF),
        ),
        in_specs=[vm] * 3 + [hb] + [vm] * 2 + [hb, vm, hb, hb] + [vm] * 2 + [sm],
        out_specs=(hb, vm),
        scratch_shapes=[
            pltpu.VMEM((3, total, heads), BF),
            pltpu.VMEM((width, 3 * heads), BF),
            pltpu.VMEM((total, width), BF),
            pltpu.VMEM((rank, total), BF),
            pltpu.VMEM((ranks, rank, total), BF),
            pltpu.VMEM((2, NADAPT * rank, total), BF),
            pltpu.VMEM((parts, rank, part_width), BF),
            pltpu.VMEM((parts, rank, part_width), BF),
            pltpu.VMEM((units, 3, seq_all, HEAD_DIM), BF),
            pltpu.VMEM((seq_all, HEAD_DIM), F32),
            pltpu.VMEM((seq_all, HEAD_DIM), F32),
            pltpu.VMEM((chunks, rows, width), BF),
            pltpu.VMEM((chunks, half, width), BF),
            pltpu.VMEM((chunks, half, width), BF),
            pltpu.VMEM((rows, width), BF),
            pltpu.VMEM((rows, width), BF),
            pltpu.VMEM((group * rows, rank), BF),
            dma(()),
            dma(()),
            dma((2, chunks)),
            dma((2, chunks)),
            dma((2, chunks)),
            dma((2, chunks)),
            dma((3,)),
            dma((units, ctxs)),
            dma((units, ctxs)),
            dma((units,)),
            dma((ranks,)),
            dma((ranks,)),
            dma((parts,)),
            dma((parts,)),
            dma((parts,)),
            dma((parts,)),
        ],
        compiler_params=pltpu.CompilerParams(
            collective_id=1, has_side_effects=True, vmem_limit_bytes=VMEM_LAST
        ),
        cost_estimate=pl.CostEstimate(
            flops=6 * total * width * heads + 10 * units * seq_all * seq_all * HEAD_DIM,
            bytes_accessed=8 * total * width,
            transcendentals=units * seq_all * seq_all,
        ),
    )(
        unit_go,
        unit_qkv,
        unit_out,
        mixing,
        mu,
        md,
        attn_low,
        jnp.eye(rank, dtype=BF),
        early_grads,
        hidden,
        mix_rank,
        row_hot,
        picks,
    )


def per_device(
    hidden_in,
    output_cotangent,
    adapter_index,
    mixing_weight,
    output_weight,
    expand_weight,
    contract_weight,
    first_gain,
    first_shift,
    second_gain,
    second_shift,
    mixing_down,
    mixing_up,
    output_down,
    output_up,
    expand_down,
    expand_up,
    contract_down,
    contract_up,
):
    seq_count, tok_count, model_width = hidden_in.shape
    local_heads = mixing_weight.shape[2] // HEAD_DIM
    local_width = mixing_weight.shape[2]
    rows_all = seq_count * tok_count
    adapter_ids = jnp.arange(NADAPT, dtype=jnp.int32)
    onehot_low = (adapter_index == adapter_ids[None, :]).astype(jnp.bfloat16)
    picks = adapter_index.reshape(-1)
    rank = mixing_down.shape[1]
    mixing_flat = mixing_weight.reshape(mixing_weight.shape[0], 3 * local_width)
    hidden_rows = hidden_in.reshape(rows_all, model_width)
    mixing_up_flat = mixing_up.reshape(NADAPT, rank, 3 * local_width)
    gains = jnp.stack([first_gain, first_shift, second_gain, second_shift])
    (
        out_rows,
        first_low,
        active_low,
        second_low,
        before_low,
        attn_low,
        mixing_full,
        unit_go,
        early_grads,
        part_ranks,
        full_ranks,
        context,
        unit_qkv,
        unit_out,
    ) = middle(
        hidden_rows,
        output_cotangent.reshape(rows_all, model_width),
        (mixing_flat, output_weight, expand_weight, contract_weight),
        (
            mixing_down,
            mixing_up_flat,
            output_down,
            output_up,
            expand_down,
            expand_up,
            contract_down,
            contract_up,
        ),
        gains,
        tok_count,
        picks,
    )
    row_hot = jnp.repeat(onehot_low.T, tok_count, axis=1)

    def table_grad(ranks, values):
        wide = (row_hot[:, None, :] * ranks[None, :, :]).reshape(-1, rows_all)
        part = jnp.einsum("kn,nd->kd", wide, values, preferred_element_type=jnp.float32)
        return part.astype(jnp.bfloat16).reshape(NADAPT, rank, values.shape[1])

    early = (
        table_grad(part_ranks[6], context),
        table_grad(full_ranks[0], attn_low),
        table_grad(full_ranks[2], first_low),
        table_grad(part_ranks[4], before_low),
        table_grad(part_ranks[5], active_low),
        table_grad(full_ranks[1], second_low),
    )
    early, unit_go = lax.optimization_barrier((early, unit_go))
    input_rows, late = mixing_back(
        unit_go,
        early_grads,
        unit_qkv,
        unit_out,
        mixing_full,
        (mixing_up_flat, mixing_down),
        attn_low,
        hidden_rows,
        part_ranks[3],
        row_hot.astype(jnp.float32),
        picks,
    )
    early = lax.psum(early, ("dp", "ctx"))
    late = late.reshape(NADAPT, -1, rank, late.shape[2]).swapaxes(1, 2).reshape(NADAPT, rank, -1)
    late = (
        late[:, :, :model_width],
        late[:, :, model_width:].reshape(NADAPT, rank, 3, local_width),
    )
    summed = tuple(part.astype(jnp.float32) for part in late + early)
    return (
        out_rows.reshape(hidden_in.shape),
        input_rows.reshape(hidden_in.shape),
    ) + summed


def solution(mesh):
    return jax.shard_map(
        per_device,
        mesh=mesh,
        in_specs=(
            P("dp", "ctx", None),
            P("dp", "ctx", None),
            P("dp", None),
            P(("dp", "ctx"), None, "tensor"),
            P("tensor", ("dp", "ctx")),
            P(("dp", "ctx"), "tensor"),
            P("tensor", ("dp", "ctx")),
            P(),
            P(),
            P(),
            P(),
            P(),
            P(None, None, None, "tensor"),
            P(None, None, "tensor"),
            P(),
            P(),
            P(None, None, "tensor"),
            P(None, None, "tensor"),
            P(),
        ),
        out_specs=(
            P("dp", "ctx", None),
            P("dp", "ctx", None),
            P(),
            P(None, None, None, "tensor"),
            P(None, None, "tensor"),
            P(),
            P(),
            P(None, None, "tensor"),
            P(None, None, "tensor"),
            P(),
        ),
        check_vma=False,
    )
```
